32 devices in a mesh: narrow: 8 (over z, y), wide: 4 (over x, core).
Axes of the slice: x: 2, y: 2, z: 4, core: 2. Of those that a mesh axis runs over, the one named last changes fastest.
Arguments:
- frame_tokens: bfloat16 [96, 197, 768], P('narrow', None, 'wide'), may hold values from -6 to 6
- cotangent: bfloat16 [96, 197, 768], P('narrow', None, 'wide'), may hold values from -6 to 6
- caption_count: int32 [12], replicated, may hold values from 1 to 5, as said below
- caption_len: int32 [12, 5], replicated, may hold values from 1 to 77, as said below
- message_weight: bfloat16 [768, 768], replicated, may hold values from -0.21875 to 0.21875
- message_bias: float32 [768], replicated, may hold values from -3 to 3
- message_gain: float32 [768], replicated, may hold values from 0.5 to 1.5
- message_shift: float32 [768], replicated, may hold values from -2 to 2
- cross_qkv: bfloat16 [768, 3, 768], P(None, None, 'wide'), may hold values from -0.21875 to 0.21875
- cross_bias: float32 [2, 768], P(None, 'wide'), may hold values from -3 to 3
- cross_proj: bfloat16 [768, 768], P('wide'), may hold values from -0.4375 to 0.4375
- cross_offset: float32 [768], replicated, may hold values from -2 to 2
- attn_gain: float32 [768], replicated, may hold values from 0.5 to 1.5
- attn_shift: float32 [768], replicated, may hold values from -2 to 2
- qkv_weight: bfloat16 [768, 3, 768], P(None, None, 'wide'), may hold values from -0.21875 to 0.21875
- qkv_bias: float32 [2, 768], P(None, 'wide'), may hold values from -3 to 3
- out_weight: bfloat16 [768, 768], P('wide'), may hold values from -1.25 to 1.25
- out_bias: float32 [768], P('wide'), may hold values from -2 to 2
- mlp_gain: float32 [768], replicated, may hold values from 0.5 to 1.5
- mlp_shift: float32 [768], replicated, may hold values from -2 to 2
- up_weight: bfloat16 [768, 3072], P(None, 'wide'), may hold values from -0.21650635 to 0.21650635
- up_bias: float32 [3072], P('wide'), may hold values from -3 to 3
- down_weight: bfloat16 [3072, 768], P('wide'), may hold values from -0.109375 to 0.109375
- down_bias: float32 [768], P('wide'), may hold values from -2 to 2
Outputs:
- output_tokens: bfloat16 [96, 197, 768], P('narrow', None, 'wide')
- grad_tokens: bfloat16 [96, 197, 768], P('narrow', None, 'wide')
- grad_message_weight: float32 [768, 768], replicated
- grad_message_bias: float32 [768], replicated
- grad_message_gain: float32 [768], replicated
- grad_message_shift: float32 [768], replicated
- grad_cross_qkv: float32 [768, 3, 768], P(None, None, 'wide')
- grad_cross_bias: float32 [2, 768], P(None, 'wide')
- grad_cross_proj: float32 [768, 768], P('wide')
- grad_cross_offset: float32 [768], replicated
- grad_attn_gain: float32 [768], replicated
- grad_attn_shift: float32 [768], replicated
- grad_qkv_weight: float32 [768, 3, 768], P(None, None, 'wide')
- grad_qkv_bias: float32 [2, 768], P(None, 'wide')
- grad_out_weight: float32 [768, 768], P('wide')
- grad_out_bias: float32 [768], P('wide')
- grad_mlp_gain: float32 [768], replicated
- grad_mlp_shift: float32 [768], replicated
- grad_up_weight: float32 [768, 3072], P(None, 'wide')
- grad_up_bias: float32 [3072], P('wide')
- grad_down_weight: float32 [3072, 768], P('wide')
- grad_down_bias: float32 [768], P('wide')
The draws below stay inside these ranges and needn't reach their ends.
Inputs may be any that keep to these rules, and one draw needn't show every extreme that they name: Captions of each video; a video uses its first caption_count slots. `caption_len`: words of a caption slot; slots at or after a video's caption_count are unused and hold a value too.
All inputs are finite; a program needn't handle non-finite values.
Results may differ from the reference program's by a relative error of at most 0.02.
Values may be sent and summed in bfloat16 or wider, within the bound.
No kernel may reach another device: no remote copies, remote signals or barrier semaphores. Data moves between devices by JAX's collectives and lax.ppermute only.
A program may use at most 192 MiB of HBM per device.

```python
import jax
import jax.numpy as jnp
from jax import lax

D = 768
HEADS = 12
FF = 3072
PATCHES = 197
VIDEO_FRAMES = 8
CAPS = 5
MAX_WORDS = 77
HD = 64
FRAMES = 96
VIDEOS = 12


def caption_plan(key):
    plan_key = jax.random.fold_in(key, 11)
    counts = jax.random.randint(plan_key, (VIDEOS,), 1, CAPS + 1)
    chosen = jax.random.randint(jax.random.fold_in(plan_key, 1), (), 0, VIDEOS)
    video_slot = jnp.arange(VIDEOS)
    counts = jnp.where(video_slot == chosen, CAPS, counts)
    counts = jnp.where(video_slot == (chosen + 1) % VIDEOS, 1, counts)
    return (counts.astype(jnp.int32), chosen)


def draw_caption_count(key, part):
    counts, chosen = caption_plan(key)
    return counts


def draw_caption_len(key, part):
    counts, chosen = caption_plan(key)
    key = jax.random.fold_in(key, 23)
    lengths = jax.random.randint(key, (VIDEOS, CAPS), MAX_WORDS // 2, MAX_WORDS + 1)
    video_slot = jnp.arange(VIDEOS)[:, None]
    caption_slot = jnp.arange(CAPS)[None, :]
    lengths = jnp.where((video_slot == chosen) & (caption_slot == 0), MAX_WORDS, lengths)
    single = (chosen + 1) % VIDEOS
    lengths = jnp.where((video_slot == single) & (caption_slot == CAPS - 1), 1, lengths)
    return lengths.astype(jnp.int32)


def draw_up_weight(key, part):
    key = jax.random.fold_in(key, 37)
    limit = 6.0 * D ** (-0.5)
    values = jax.random.normal(key, (D, FF), jnp.float32) * D ** (-0.5)
    return jnp.clip(values, -limit, limit).astype(jnp.bfloat16)


def levels(rng, shape, pieces, low, top_value):
    def one(axis_at, shards_of):
        heights = jax.random.uniform(jax.random.fold_in(jax.random.fold_in(rng, 6), axis_at), (shards_of,), jnp.float32, low / len(pieces), top_value / len(pieces))
        return jnp.repeat(jnp.exp(heights), shape[axis_at] // shards_of).reshape((-1,) + (1,) * (len(shape) - axis_at - 1))

    level = one(*pieces[0])
    for cut in pieces[1:]:
        level = level * one(*cut)
    return level


def gaussian(key, dims, scale, bound, shards=(), dtype=jnp.bfloat16):
    drawn = scale * jax.random.normal(key, dims, jnp.float32)
    if shards:
        drawn = drawn * levels(key, dims, shards, -0.22, 0.18)
    return jnp.clip(drawn, -bound, bound).astype(dtype)


def setup_inputs(seed: int = 0) -> dict:
    arg_keys = jax.random.split(jax.random.key(seed), 25)
    return {
        "frame_tokens": gaussian(arg_keys[0], (FRAMES, PATCHES, D), 1.0, 6.0, ((0, 8), (2, 4))),
        "cotangent": gaussian(arg_keys[1], (FRAMES, PATCHES, D), 1.0, 6.0, ((0, 8), (2, 4))),
        "caption_count": draw_caption_count(jax.random.fold_in(arg_keys[24], 71), 0),
        "caption_len": draw_caption_len(jax.random.fold_in(arg_keys[24], 71), 0),
        "message_weight": gaussian(arg_keys[4], (D, D), D ** -0.5, 0.21875),
        "message_bias": gaussian(arg_keys[5], (D,), 0.5, 3.0, (), jnp.float32),
        "message_gain": jnp.clip(1.0 + 0.1 * jax.random.normal(arg_keys[6], (D,), jnp.float32), 0.5, 1.5),
        "message_shift": gaussian(arg_keys[7], (D,), 0.3, 2.0, (), jnp.float32),
        "cross_qkv": gaussian(arg_keys[8], (D, 3, D), D ** -0.5, 0.21875, ((2, 4),)),
        "cross_bias": gaussian(arg_keys[9], (2, D), 0.5, 3.0, ((1, 4),), jnp.float32),
        "cross_proj": gaussian(arg_keys[10], (D, D), (D // 4) ** -0.5, 0.4375, ((0, 4),)),
        "cross_offset": gaussian(arg_keys[11], (D,), 0.3, 2.0, (), jnp.float32),
        "attn_gain": jnp.clip(1.0 + 0.1 * jax.random.normal(arg_keys[12], (D,), jnp.float32), 0.5, 1.5),
        "attn_shift": gaussian(arg_keys[13], (D,), 0.3, 2.0, (), jnp.float32),
        "qkv_weight": gaussian(arg_keys[14], (D, 3, D), D ** -0.5, 0.21875, ((2, 4),)),
        "qkv_bias": gaussian(arg_keys[15], (2, D), 0.5, 3.0, ((1, 4),), jnp.float32),
        "out_weight": gaussian(arg_keys[16], (D, D), (D // 32) ** -0.5, 1.25, ((0, 4),)),
        "out_bias": gaussian(arg_keys[17], (D,), 0.3, 2.0, ((0, 4),), jnp.float32),
        "mlp_gain": jnp.clip(1.0 + 0.1 * jax.random.normal(arg_keys[18], (D,), jnp.float32), 0.5, 1.5),
        "mlp_shift": gaussian(arg_keys[19], (D,), 0.3, 2.0, (), jnp.float32),
        "up_weight": draw_up_weight(jax.random.fold_in(arg_keys[24], 71), 0),
        "up_bias": gaussian(arg_keys[21], (FF,), 0.5, 3.0, ((0, 4),), jnp.float32),
        "down_weight": gaussian(arg_keys[22], (FF, D), FF ** -0.5, 0.109375, ((0, 4),)),
        "down_bias": gaussian(arg_keys[23], (D,), 0.3, 2.0, ((0, 4),), jnp.float32),
    }


@jax.custom_vjp
def low(v):
    return lax.optimization_barrier(v.astype(jnp.bfloat16)).astype(jnp.float32)

@jax.custom_vjp
def low_back(v):
    return v

def low_keep(v):
    return (low(v), None)

def low_pass(kept, grad):
    return (grad,)

def back_keep(v):
    return (v, None)

def back_low(kept, grad):
    return (low(grad),)
low.defvjp(low_keep, low_pass)
low_back.defvjp(back_keep, back_low)
eps_norm = 1e-05

def layer_norm(values, norm_gain, norm_bias):
    row_mean = lax.optimization_barrier(jnp.mean(values, axis=-1, keepdims=True))
    centred = values - row_mean
    variance = lax.optimization_barrier(jnp.mean(centred * centred, axis=-1, keepdims=True))
    return centred * lax.rsqrt(variance + eps_norm) * norm_gain + norm_bias

def mat_high(left, right):
    return jnp.dot(left, right, precision=lax.Precision.HIGHEST)

def video_forward(params, frames):
    message_weight, message_bias, message_gain, message_shift, cross_qkv, cross_bias, cross_proj, cross_offset, attn_gain, attn_shift, qkv_weight, qkv_bias, out_weight, out_bias, mlp_gain, mlp_shift, up_weight, up_bias, down_weight, down_bias = params
    score_scale = HD ** (-0.5)
    frame_count = frames.shape[0]
    message = low_back(mat_high(frames[:, 0, :], message_weight) + message_bias)
    msg_in = low(layer_norm(message, message_gain, message_shift))
    cross_query = low(low_back(mat_high(msg_in, cross_qkv[:, 0]) + cross_bias[0])).reshape(frame_count, HEADS, HD)
    cross_key = low(low_back(mat_high(msg_in, cross_qkv[:, 1]))).reshape(frame_count, HEADS, HD)
    cross_value = low(low_back(mat_high(msg_in, cross_qkv[:, 2]) + cross_bias[1])).reshape(frame_count, HEADS, HD)
    cross_score = jnp.einsum('thd,uhd->htu', cross_query, cross_key, precision=lax.Precision.HIGHEST) * score_scale
    cross_prob = jax.nn.softmax(cross_score, axis=-1)
    cross_mix = jnp.einsum('htu,uhd->thd', cross_prob, cross_value, precision=lax.Precision.HIGHEST)
    cross_mix = low(low_back(cross_mix.reshape(frame_count, D)))
    cross_branch = low_back(mat_high(cross_mix, cross_proj) + cross_offset)
    message_two = message + cross_branch
    full_cat = jnp.concatenate([frames, message_two[:, None, :]], axis=1)
    seq_len = full_cat.shape[1]
    attn_in = low(layer_norm(full_cat, attn_gain, attn_shift))
    queries = low(low_back(mat_high(attn_in, qkv_weight[:, 0]) + qkv_bias[0])).reshape(frame_count, seq_len, HEADS, HD)
    key_rows = low(low_back(mat_high(attn_in, qkv_weight[:, 1]))).reshape(frame_count, seq_len, HEADS, HD)
    value_rows = low(low_back(mat_high(attn_in, qkv_weight[:, 2]) + qkv_bias[1])).reshape(frame_count, seq_len, HEADS, HD)
    scores = low_back(jnp.einsum('tshd,tuhd->thsu', queries, key_rows, precision=lax.Precision.HIGHEST) * score_scale)
    prob = low(jax.nn.softmax(scores, axis=-1))
    attn_mix = jnp.einsum('thsu,tuhd->tshd', prob, value_rows, precision=lax.Precision.HIGHEST)
    attn_mix = low(low_back(attn_mix.reshape(frame_count, seq_len, D)))
    hidden_res = full_cat + low_back(mat_high(attn_mix, out_weight)) + out_bias
    mlp_in = low(layer_norm(low(hidden_res), mlp_gain, mlp_shift))
    pre_act = low_back(mat_high(mlp_in, up_weight) + up_bias)
    activated = low(pre_act * jax.nn.sigmoid(1.702 * pre_act))
    result = hidden_res + low_back(mat_high(activated, down_weight)) + down_bias
    return result[:, :PATCHES, :]

def reference(frame_tokens, cotangent, caption_count, caption_len, message_weight, message_bias, message_gain, message_shift, cross_qkv, cross_bias, cross_proj, cross_offset, attn_gain, attn_shift, qkv_weight, qkv_bias, out_weight, out_bias, mlp_gain, mlp_shift, up_weight, up_bias, down_weight, down_bias):
    caption_slot = jnp.arange(CAPS)
    word_total = lax.optimization_barrier(jnp.sum(jnp.where(caption_slot[None, :] < caption_count[:, None], caption_len, 0), axis=1))
    word_total = word_total.astype(jnp.float32)
    video_scale = word_total / jnp.mean(word_total)
    params = tuple((param_item.astype(jnp.float32) for param_item in (message_weight, message_bias, message_gain, message_shift, cross_qkv, cross_bias, cross_proj, cross_offset, attn_gain, attn_shift, qkv_weight, qkv_bias, out_weight, out_bias, mlp_gain, mlp_shift, up_weight, up_bias, down_weight, down_bias)))
    frames = frame_tokens.astype(jnp.float32).reshape(VIDEOS, VIDEO_FRAMES, PATCHES, D)
    weighted = cotangent.astype(jnp.float32).reshape(VIDEOS, VIDEO_FRAMES, PATCHES, D) * video_scale[:, None, None, None]

    def one_video(totals, inputs):
        video_frames, video_cot = inputs
        outputs, pull_back = jax.vjp(video_forward, params, video_frames)
        grad_params, grad_frames = pull_back(video_cot)
        totals = tuple((grad_total + grad_item for grad_total, grad_item in zip(totals, grad_params)))
        return (totals, (outputs, grad_frames))
    zero_grads = tuple((jnp.zeros_like(param_item) for param_item in params))
    totals, (outputs, grad_frames) = lax.scan(one_video, zero_grads, (frames, weighted))
    return (outputs.reshape(FRAMES, PATCHES, D).astype(jnp.bfloat16), grad_frames.reshape(FRAMES, PATCHES, D).astype(jnp.bfloat16), totals[0], totals[1], totals[2], totals[3], totals[4], totals[5], totals[6], totals[7], totals[8], totals[9], totals[10], totals[11], totals[12], totals[13], totals[14], totals[15], totals[16], totals[17], totals[18], totals[19])
```

```python
import jax
import jax.numpy as jnp
from jax import lax
from jax.sharding import PartitionSpec as P


VIDEO_FRAMES = 8
HD = 64
EPS = 1e-05
ROW_TILE = 16
LOW = jnp.bfloat16
F32 = jnp.float32


def dot(left, right, dims):
    return lax.dot_general(left, right, (dims, ((), ())), preferred_element_type=F32)


def mat_mul(left, right):
    return dot(left, right, ((1,), (0,)))


def mat_tn(left, right):
    return dot(left, right, ((0,), (0,)))


def mat_nt(left, right):
    return dot(left, right, ((1,), (1,)))


def normalize(values):
    row_mean = jnp.mean(values, axis=-1, keepdims=True)
    centred = values - row_mean
    inv_std = lax.rsqrt(jnp.mean(centred * centred, axis=-1, keepdims=True) + EPS)
    return (centred * inv_std, inv_std)


def norm_back(grad_norm, normed, inv_std, norm_gain):
    scaled = grad_norm * norm_gain
    return inv_std * (
        scaled
        - jnp.mean(scaled, axis=-1, keepdims=True)
        - normed * jnp.mean(scaled * normed, axis=-1, keepdims=True)
    )


def swap(block, axis, flip):
    return lax.ppermute(block, axis, [(i, i ^ flip) for i in range(lax.axis_size(axis))])


def bits_of(size):
    return [1 << b for b in range(size.bit_length() - 1)]


def reorder(parts, index):
    parts = list(parts)
    for bit in bits_of(len(parts)):
        odd = (index & bit) != 0
        parts = [jnp.where(odd, parts[k ^ bit], parts[k]) for k in range(len(parts))]
    return parts


def gather_all(block, axis, order):
    index = lax.axis_index(axis)
    for bit in order:
        other = swap(block, axis, bit)
        odd = (index & bit) != 0
        block = jnp.concatenate(
            [jnp.where(odd, other, block), jnp.where(odd, block, other)], axis=0
        )
    return block


def sum_all(block, axis):
    for bit in bits_of(lax.axis_size(axis)):
        block = block + swap(block, axis, bit)
    return block


def frames_in(block, count, index):
    part = block.shape[0] // count
    pieces = []
    for k in range(count):
        piece = lax.dynamic_slice_in_dim(block, (index ^ k) * part, part, 0)
        pieces.append(piece if k == 0 else swap(piece, "wide", k))
    return jnp.concatenate(reorder(pieces, index), axis=2)


def frames_out(block, count, index):
    width = block.shape[2] // count
    pieces = reorder([block[:, :, j * width : (j + 1) * width] for j in range(count)], index)
    pieces = [piece if k == 0 else swap(piece, "wide", k) for k, piece in enumerate(pieces)]
    return jnp.concatenate(reorder(pieces, index), axis=0)


def shards_in(block, count):
    shards = {0: block}
    for bit in reversed(bits_of(count)):
        for k in list(shards):
            shards[k ^ bit] = swap(shards[k], "wide", bit)
    return [shards[k] for k in range(count)]


def reduce_grad(parts):
    parts = {k: part for k, part in enumerate(parts)}
    for bit in bits_of(len(parts)):
        away = [k for k in parts if k & bit]
        sent = swap(jnp.concatenate([parts[k] for k in away], axis=0), "wide", bit)
        size = parts[0].shape[0]
        parts = {
            k ^ bit: (
                parts[k ^ bit].astype(F32) + sent[at * size : (at + 1) * size].astype(F32)
            ).astype(LOW)
            for at, k in enumerate(away)
        }
    block = parts[0]
    index = lax.axis_index("narrow")
    bits = bits_of(lax.axis_size("narrow"))
    for bit in bits:
        odd = (index & bit) != 0
        half = block.shape[0] // 2
        low, high = block[:half], block[half:]
        other = swap(jnp.where(odd, low, high), "narrow", bit)
        block = (jnp.where(odd, high, low).astype(F32) + other.astype(F32)).astype(LOW)
    for bit in reversed(bits):
        odd = (index & bit) != 0
        other = swap(block, "narrow", bit)
        block = jnp.concatenate(
            [jnp.where(odd, other, block), jnp.where(odd, block, other)], axis=0
        )
    return block.astype(F32)


def body(
    frame_tokens,
    cotangent,
    caption_count,
    caption_len,
    message_weight,
    message_bias,
    message_gain,
    message_shift,
    cross_qkv,
    cross_bias,
    cross_proj,
    cross_offset,
    attn_gain,
    attn_shift,
    qkv_weight,
    qkv_bias,
    out_weight,
    out_bias,
    mlp_gain,
    mlp_shift,
    up_weight,
    up_bias,
    down_weight,
    down_bias,
):
    group_frames, patches, width_part = frame_tokens.shape
    model_width = message_weight.shape[0]
    hidden_part = up_weight.shape[1]
    wide = lax.axis_size("wide")
    narrow = lax.axis_size("narrow")
    wide_idx = lax.axis_index("wide")
    narrow_idx = lax.axis_index("narrow")
    frames = group_frames // wide
    seq_len = patches + 1
    seq_pad = -(-seq_len // ROW_TILE) * ROW_TILE
    rows = frames * seq_pad
    part_heads = width_part // HD
    score_scale = HD ** (-0.5)
    all_frames = group_frames * narrow
    first_group = narrow_idx * group_frames
    first_frame = first_group + wide_idx * frames

    tokens = frames_in(frame_tokens, wide, wide_idx)
    cls_part = frame_tokens[:, 0, :]
    cls_rows = jnp.concatenate(
        reorder([cls_part] + [swap(cls_part, "wide", k) for k in range(1, wide)], wide_idx), axis=1
    )
    cls_rows = gather_all(cls_rows, "narrow", bits_of(narrow))
    qkv_shards = shards_in(qkv_weight.reshape(model_width, 3 * width_part), wide)
    rest_shards = shards_in(jnp.concatenate([out_weight, up_weight, down_weight], axis=0), wide)
    cot = frames_in(cotangent, wide, wide_idx)

    message = mat_mul(cls_rows, message_weight) + message_bias
    msg_normed, msg_inv = normalize(message)
    msg_in = (msg_normed * message_gain + message_shift).astype(LOW)
    cross_flat = cross_qkv.reshape(model_width, 3 * width_part)
    cross_all = mat_mul(msg_in, cross_flat)
    cross_query = (cross_all[:, :width_part] + cross_bias[0]).astype(LOW)
    cross_key = cross_all[:, width_part : 2 * width_part].astype(LOW)
    cross_value = (cross_all[:, 2 * width_part :] + cross_bias[1]).astype(LOW)
    chunk = max(c for c in range(VIDEO_FRAMES, 129, VIDEO_FRAMES) if all_frames % c == 0)
    chunks = all_frames // chunk

    def by_head(values):
        return values.reshape(chunks, chunk, part_heads, HD)

    def from_head(values):
        return values.reshape(all_frames, width_part)

    def ein(expr, left, right):
        return jnp.einsum(expr, left, right, preferred_element_type=F32)

    video_of = jnp.arange(chunk) // VIDEO_FRAMES
    same_video = video_of[:, None] == video_of[None, :]
    query_heads, key_heads, value_heads = by_head(cross_query), by_head(cross_key), by_head(cross_value)
    cross_score = ein("cthd,cuhd->chtu", query_heads, key_heads) * score_scale
    cross_prob = jax.nn.softmax(jnp.where(same_video, cross_score, -1e30), axis=-1)
    cross_mix = from_head(ein("chtu,cuhd->cthd", cross_prob.astype(LOW), value_heads)).astype(LOW)
    group_mix = lax.dynamic_slice_in_dim(cross_mix, first_group, group_frames, 0)
    group_sum = mat_mul(group_mix, cross_proj)
    message_two = lax.dynamic_slice_in_dim(message, first_frame, frames, 0) + cross_offset
    for k in range(wide):
        piece = lax.dynamic_slice_in_dim(group_sum, (wide_idx ^ k) * frames, frames, 0)
        message_two = message_two + (piece if k == 0 else swap(piece, "wide", k))

    full_cat = jnp.concatenate(
        [
            tokens.astype(F32),
            message_two[:, None, :],
            jnp.zeros((frames, seq_pad - seq_len, model_width), F32),
        ],
        axis=1,
    ).reshape(rows, model_width)
    attn_normed, attn_inv = normalize(full_cat)
    attn_in = (attn_normed * attn_gain + attn_shift).astype(LOW)
    qkv_full = jnp.concatenate(qkv_shards, axis=1)
    qkv_bias_all = jnp.stack(shards_in(qkv_bias, wide))
    up_bias_all = jnp.concatenate(shards_in(up_bias, wide))
    out_bias_all = jnp.concatenate(reorder(shards_in(out_bias, wide), wide_idx))
    down_bias_all = jnp.concatenate(reorder(shards_in(down_bias, wide), wide_idx))
    heads = wide * part_heads
    proj = mat_mul(attn_in, qkv_full).reshape(rows, wide, 3, width_part)

    def heads_of(values):
        return values.astype(LOW).reshape(frames, seq_pad, heads, HD)

    queries = heads_of(proj[:, :, 0] + qkv_bias_all[:, 0])
    keys = heads_of(proj[:, :, 1])
    values = heads_of(proj[:, :, 2] + qkv_bias_all[:, 1])
    scores = ein("tshd,tuhd->thsu", queries, keys) * score_scale
    scores = jnp.where(jnp.arange(seq_pad) < seq_len, scores, -1e30)
    prob = jax.nn.softmax(scores, axis=-1)
    prob_low = prob.astype(LOW)
    attn_mix = ein("thsu,tuhd->tshd", prob_low, values).astype(LOW).reshape(rows, model_width)
    out_full = jnp.concatenate([s[:width_part] for s in rest_shards], axis=0)
    up_full = jnp.concatenate([s[width_part : width_part + model_width] for s in rest_shards], axis=1)
    down_full = jnp.concatenate([s[width_part + model_width :] for s in rest_shards], axis=0)
    hidden_res = full_cat + mat_mul(attn_mix, out_full) + out_bias_all
    mlp_normed, mlp_inv = normalize(hidden_res.astype(LOW).astype(F32))
    mlp_in = (mlp_normed * mlp_gain + mlp_shift).astype(LOW)
    pre_act = mat_mul(mlp_in, up_full) + up_bias_all
    gate_sig = jax.nn.sigmoid(1.702 * pre_act)
    activated = (pre_act * gate_sig).astype(LOW)
    result = hidden_res + mat_mul(activated, down_full) + down_bias_all
    result = result.reshape(frames, seq_pad, model_width)[:, :patches].astype(LOW)
    output_tokens = frames_out(result, wide, wide_idx)

    caption_slot = jnp.arange(caption_len.shape[1])
    word_total = jnp.sum(
        jnp.where(caption_slot[None, :] < caption_count[:, None], caption_len, 0), axis=1
    ).astype(F32)
    video_scale = word_total / jnp.mean(word_total)
    own_video = (first_frame + jnp.arange(frames)) // VIDEO_FRAMES
    video_match = own_video[:, None] == jnp.arange(video_scale.shape[0])[None, :]
    frame_weight = jnp.sum(jnp.where(video_match, video_scale[None, :], 0.0), axis=1)
    grad_res = jnp.concatenate(
        [
            cot.astype(F32) * frame_weight[:, None, None],
            jnp.zeros((frames, seq_pad - patches, model_width), F32),
        ],
        axis=1,
    ).reshape(rows, model_width)
    grad_rows = grad_res.astype(LOW)
    sum_down_bias = jnp.sum(grad_res, axis=0)
    grad_down = mat_tn(activated, grad_rows).astype(LOW)
    grad_act = mat_nt(grad_rows, down_full)
    grad_pre = (grad_act * (gate_sig + 1.702 * pre_act * gate_sig * (1.0 - gate_sig))).astype(LOW)
    sum_up_bias = jnp.sum(grad_pre, axis=0, dtype=F32)
    grad_up = mat_tn(mlp_in, grad_pre).astype(LOW)
    grad_down_own = reduce_grad([grad_down[k * hidden_part : (k + 1) * hidden_part] for k in range(wide)])
    grad_up_own = reduce_grad([grad_up[:, k * hidden_part : (k + 1) * hidden_part] for k in range(wide)])
    grad_mlp_in = mat_nt(grad_pre, up_full)
    sum_mlp_gain = jnp.sum(grad_mlp_in * mlp_normed, axis=0)
    sum_mlp_shift = jnp.sum(grad_mlp_in, axis=0)
    grad_hidden = grad_res + norm_back(grad_mlp_in, mlp_normed, mlp_inv, mlp_gain)
    sum_out_bias = jnp.sum(grad_hidden, axis=0)
    grad_low = grad_hidden.astype(LOW)
    grad_out = mat_tn(attn_mix, grad_low).astype(LOW)
    grad_out_own = reduce_grad([grad_out[k * width_part : (k + 1) * width_part] for k in range(wide)])
    grad_mix = mat_nt(grad_low, out_full).astype(LOW).reshape(frames, seq_pad, heads, HD)
    grad_value = ein("thsu,tshd->tuhd", prob_low, grad_mix)
    grad_prob = ein("tshd,tuhd->thsu", grad_mix, values)
    grad_score = (prob * (grad_prob - jnp.sum(prob * grad_prob, axis=-1, keepdims=True))).astype(LOW)
    grad_query = ein("thsu,tuhd->tshd", grad_score, keys) * score_scale
    grad_key = ein("thsu,tshd->tuhd", grad_score, queries) * score_scale
    grad_proj = (
        jnp.stack(
            [g.reshape(rows, wide, width_part) for g in (grad_query, grad_key, grad_value)], axis=2
        )
        .astype(LOW)
        .reshape(rows, wide * 3 * width_part)
    )
    sum_proj = jnp.sum(grad_proj, axis=0, dtype=F32).reshape(wide, 3, width_part)
    grad_qkv = mat_tn(attn_in, grad_proj).astype(LOW)
    grad_qkv_own = reduce_grad(
        [grad_qkv[:, k * 3 * width_part : (k + 1) * 3 * width_part] for k in range(wide)]
    )
    grad_attn_in = mat_nt(grad_proj, qkv_full)
    sum_attn_gain = jnp.sum(grad_attn_in * attn_normed, axis=0)
    sum_attn_shift = jnp.sum(grad_attn_in, axis=0)
    grad_total = (
        norm_back(grad_attn_in, attn_normed, attn_inv, attn_gain) + grad_hidden
    ).reshape(frames, seq_pad, model_width)
    grad_tokens = frames_out(grad_total[:, :patches].astype(LOW), wide, wide_idx)

    sums = jnp.concatenate(
        [sum_down_bias, sum_mlp_gain, sum_mlp_shift, sum_out_bias, sum_attn_gain, sum_attn_shift]
        + reorder([sum_up_bias[k * hidden_part : (k + 1) * hidden_part] for k in range(wide)], wide_idx)
        + reorder([sum_proj[k, 0] for k in range(wide)], wide_idx)
        + reorder([sum_proj[k, 2] for k in range(wide)], wide_idx)
    )
    sums = sum_all(sum_all(sums.reshape(-1, 128), "wide"), "narrow").reshape(-1)
    sums = [sums[at : at + model_width] for at in range(0, sums.shape[0], model_width)]
    grad_down_bias, grad_mlp_gain, grad_mlp_shift, grad_out_bias, grad_attn_gain, grad_attn_shift = sums[:6]
    hidden_sums = jnp.concatenate(sums[6:-2])
    grad_up_bias = lax.dynamic_slice_in_dim(hidden_sums, wide_idx * hidden_part, hidden_part, 0)
    col_start = wide_idx * width_part

    def own_cols(values):
        return lax.dynamic_slice_in_dim(values, col_start, width_part, values.ndim - 1)

    grad_qkv_bias = own_cols(jnp.stack(sums[-2:]))

    grad_message_two = gather_all(
        gather_all(grad_total[:, patches], "wide", bits_of(wide)), "narrow", bits_of(narrow)
    )
    grad_cross = grad_message_two.astype(LOW)
    grad_cross_offset = jnp.sum(grad_cross, axis=0, dtype=F32)
    grad_cross_proj = mat_tn(cross_mix, grad_cross)
    grad_cross_mix = by_head(mat_nt(grad_cross, cross_proj).astype(LOW))
    grad_cross_prob = ein("cthd,cuhd->chtu", grad_cross_mix, value_heads)
    grad_cross_score = cross_prob * (
        grad_cross_prob - jnp.sum(cross_prob * grad_cross_prob, axis=-1, keepdims=True)
    )
    score_low = grad_cross_score.astype(LOW)
    grad_cross_all = jnp.concatenate(
        [
            from_head(ein("chtu,cuhd->cthd", score_low, key_heads)) * score_scale,
            from_head(ein("chtu,cthd->cuhd", score_low, query_heads)) * score_scale,
            from_head(ein("chtu,cthd->cuhd", cross_prob.astype(LOW), grad_cross_mix)),
        ],
        axis=1,
    ).astype(LOW)
    cross_sums = jnp.sum(grad_cross_all, axis=0, dtype=F32).reshape(3, width_part)
    grad_cross_bias = jnp.stack([cross_sums[0], cross_sums[2]])
    grad_cross_qkv = mat_tn(msg_in, grad_cross_all).reshape(model_width, 3, width_part)
    grad_msg_in = sum_all(mat_nt(grad_cross_all, cross_flat), "wide")
    grad_message_gain = jnp.sum(grad_msg_in * msg_normed, axis=0)
    grad_message_shift = jnp.sum(grad_msg_in, axis=0)
    grad_message = (
        grad_message_two + norm_back(grad_msg_in, msg_normed, msg_inv, message_gain)
    ).astype(LOW)
    grad_message_bias = jnp.sum(grad_message, axis=0, dtype=F32)
    grad_message_weight = mat_tn(cls_rows, grad_message)
    group_message = lax.dynamic_slice_in_dim(grad_message, first_group, group_frames, 0)
    grad_cls = own_cols(mat_nt(group_message, message_weight))
    grad_tokens = grad_tokens.astype(F32).at[:, 0].add(grad_cls).astype(LOW)

    return (
        output_tokens,
        grad_tokens,
        grad_message_weight,
        grad_message_bias,
        grad_message_gain,
        grad_message_shift,
        grad_cross_qkv,
        grad_cross_bias,
        grad_cross_proj,
        grad_cross_offset,
        grad_attn_gain,
        grad_attn_shift,
        grad_qkv_own.reshape(model_width, 3, width_part),
        grad_qkv_bias,
        grad_out_own,
        own_cols(grad_out_bias),
        grad_mlp_gain,
        grad_mlp_shift,
        grad_up_own,
        grad_up_bias,
        grad_down_own,
        own_cols(grad_down_bias),
    )


def solution(mesh):
    return jax.shard_map(
        body,
        mesh=mesh,
        in_specs=(
            P("narrow", None, "wide"),
            P("narrow", None, "wide"),
            P(),
            P(),
            P(),
            P(),
            P(),
            P(),
            P(None, None, "wide"),
            P(None, "wide"),
            P("wide", None),
            P(),
            P(),
            P(),
            P(None, None, "wide"),
            P(None, "wide"),
            P("wide", None),
            P("wide"),
            P(),
            P(),
            P(None, "wide"),
            P("wide"),
            P("wide", None),
            P("wide"),
        ),
        out_specs=(
            P("narrow", None, "wide"),
            P("narrow", None, "wide"),
            P(),
            P(),
            P(),
            P(),
            P(None, None, "wide"),
            P(None, "wide"),
            P("wide", None),
            P(),
            P(),
            P(),
            P(None, None, "wide"),
            P(None, "wide"),
            P("wide", None),
            P("wide"),
            P(),
            P(),
            P(None, "wide"),
            P("wide"),
            P("wide", None),
            P("wide"),
        ),
        check_vma=False,
    )
```

```python
import functools
import jax
import jax.numpy as jnp
from jax import lax
from jax.experimental import pallas as pl
from jax.experimental.pallas import tpu as pltpu
from jax.sharding import PartitionSpec as P

VIDEO_FRAMES = 8
HD = 64
EPS = 1e-05
ROW_TILE = 16
LOW = jnp.bfloat16
F32 = jnp.float32
VMEM_LIMIT = 56 * 1024 * 1024


def dot(left, right, dims):
    return lax.dot_general(left, right, (dims, ((), ())), preferred_element_type=F32)


def mat_mul(left, right):
    return dot(left, right, ((1,), (0,)))


def mat_tn(left, right):
    return dot(left, right, ((0,), (0,)))


def mat_nt(left, right):
    return dot(left, right, ((1,), (1,)))


def normalize(values):
    row_mean = jnp.mean(values, axis=-1, keepdims=True)
    centred = values - row_mean
    inv_std = lax.rsqrt(jnp.mean(centred * centred, axis=-1, keepdims=True) + EPS)
    return (centred * inv_std, inv_std)


def norm_back(grad_norm, normed, inv_std, norm_gain):
    scaled = grad_norm * norm_gain
    return inv_std * (
        scaled
        - jnp.mean(scaled, axis=-1, keepdims=True)
        - normed * jnp.mean(scaled * normed, axis=-1, keepdims=True)
    )


def params(limit=VMEM_LIMIT):
    return pltpu.CompilerParams(vmem_limit_bytes=limit)


def cost(micros):
    return pl.CostEstimate(flops=int(micros * 1.0e9), bytes_accessed=int(micros * 1.0e6), transcendentals=0)


def whole(array):
    return pl.BlockSpec(array.shape, lambda *_: (0,) * array.ndim)


def per_frame(shape):
    return pl.BlockSpec((1,) + tuple(shape[1:]), lambda f: (f,) + (0,) * (len(shape) - 1))


def head_masks(width):
    lane = lax.broadcasted_iota(jnp.int32, (1, width), 1) // HD
    return [lane == h for h in range(width // HD)]


def stack_heads(values, masks, scale=1.0):
    return jnp.concatenate([values * jnp.where(m, scale, 0.0).astype(values.dtype) for m in masks], axis=0)


def pick_heads(values, masks):
    size = values.shape[0] // len(masks)
    picked = values[:size]
    for h in range(1, len(masks)):
        picked = jnp.where(masks[h], values[h * size : (h + 1) * size], picked)
    return picked


def attn_forward_kernel(seq_len, tok_ref, msg_ref, vec_ref, out_bias_ref, qkv_bias_ref, *refs):
    shards = qkv_bias_ref.shape[0]
    qkv_refs, out_refs = refs[:shards], refs[shards : 2 * shards]
    (normed_ref, inv_ref, attn_in_ref, heads_ref, prob_ref, mix_ref, hidden_ref, mlp_normed_ref,
     mlp_inv_ref, mlp_in_ref, cat) = refs[2 * shards :]
    gain, shift, mlp_gain, mlp_shift = (vec_ref[i : i + 1] for i in range(4))
    patches = tok_ref.shape[1]
    seq_pad, width = cat.shape
    part = out_refs[0].shape[0]
    cat[:patches] = tok_ref[0].astype(F32)
    cat[patches:seq_len] = msg_ref[0, :1]
    cat[seq_len:] = jnp.zeros((seq_pad - seq_len, width), F32)
    full = cat[...]
    normed, inv = normalize(full)
    normed_ref[0] = normed
    inv_ref[0] = inv
    attn_in = (normed * gain + shift).astype(LOW)
    attn_in_ref[0] = attn_in
    masks = head_masks(part)
    live = lax.broadcasted_iota(jnp.int32, (1, seq_pad), 1) < seq_len
    total = full + out_bias_ref[...]
    for k in range(shards):
        proj = mat_mul(attn_in, qkv_refs[k][...])
        queries = (proj[:, :part] + qkv_bias_ref[k, 0:1]).astype(LOW)
        keys = proj[:, part : 2 * part].astype(LOW)
        values = (proj[:, 2 * part :] + qkv_bias_ref[k, 1:2]).astype(LOW)
        heads_ref[0, k, 0] = queries
        heads_ref[0, k, 1] = keys
        heads_ref[0, k, 2] = values
        scores = mat_nt(stack_heads(queries, masks, HD ** (-0.5)), keys)
        scores = jnp.where(live, scores, -1e30)
        exps = jnp.exp(scores - jnp.max(scores, axis=-1, keepdims=True))
        prob = (exps * (1.0 / jnp.sum(exps, axis=-1, keepdims=True))).astype(LOW)
        prob_ref[0, k] = prob
        mix_low = pick_heads(mat_mul(prob, values), masks).astype(LOW)
        mix_ref[0, k] = mix_low
        total += mat_mul(mix_low, out_refs[k][...])
    hidden_ref[0] = total
    mlp_normed, mlp_inv = normalize(total.astype(LOW).astype(F32))
    mlp_normed_ref[0] = mlp_normed
    mlp_inv_ref[0] = mlp_inv
    mlp_in_ref[0] = (mlp_normed * mlp_gain + mlp_shift).astype(LOW)


def attn_forward(seq_pad, tokens, msg, vecs, out_bias, qkv_bias, qkv, out):
    frames, patches, width = tokens.shape
    shards = len(qkv)
    part = qkv[0].shape[1] // 3
    heads = part // HD
    shapes = [
        ((frames, seq_pad, width), F32),
        ((frames, seq_pad, 1), F32),
        ((frames, seq_pad, width), LOW),
        ((frames, shards, 3, seq_pad, part), LOW),
        ((frames, shards, heads * seq_pad, seq_pad), LOW),
        ((frames, shards, seq_pad, part), LOW),
        ((frames, seq_pad, width), F32),
        ((frames, seq_pad, width), F32),
        ((frames, seq_pad, 1), F32),
        ((frames, seq_pad, width), LOW),
    ]
    ins = [tokens, msg, vecs, out_bias, qkv_bias]
    return pl.pallas_call(
        functools.partial(attn_forward_kernel, patches + 1),
        grid=(frames,),
        in_specs=[per_frame(tokens.shape), per_frame(msg.shape)]
        + [whole(v) for v in ins[2:]]
        + [whole(v) for v in list(qkv) + list(out)],
        out_specs=[per_frame(s) for s, _ in shapes],
        out_shape=[jax.ShapeDtypeStruct(s, d) for s, d in shapes],
        scratch_shapes=[pltpu.VMEM((seq_pad, width), F32)],
        compiler_params=params(),
        cost_estimate=cost(20),
        name="attn_forward",
    )(*ins, *qkv, *out)


def mlp_kernel(frames, has_acc, mlp_in_ref, grad_ref, bias_ref, *refs):
    count = bias_ref.shape[0]
    w_refs, refs = refs[: 2 * count], refs[2 * count :]
    if has_acc:
        acc_in, gacc_in, refs = refs[0], refs[1], refs[2:]
    acc_ref, gacc_ref, sums_ref = refs[:3]
    g_refs, refs = refs[3 : 3 + 2 * count], refs[3 + 2 * count :]
    w_buf, g_buf, act_buf, pre_buf, in_sem, out_sem = refs
    rows, width = mlp_in_ref.shape
    hidden = bias_ref.shape[2]
    step = rows // frames
    loads = [pltpu.make_async_copy(w_refs[j], w_buf.at[j], in_sem.at[j]) for j in range(2 * count)]
    stores = [pltpu.make_async_copy(g_buf.at[j], g_refs[j], out_sem.at[j]) for j in range(2 * count)]
    for load in loads:
        load.start()
    for i in range(count):
        up, down = 2 * i, 2 * i + 1
        loads[up].wait()
        loads[down].wait()
        total = jnp.zeros((1, hidden), F32)
        for f in range(frames):
            at = slice(f * step, (f + 1) * step)
            rows_in = mlp_in_ref[at]
            pre = mat_mul(rows_in, w_buf[up]) + bias_ref[i]
            sig = 0.5 + 0.5 * jnp.tanh(0.851 * pre)
            act = (pre * sig).astype(LOW)
            act_buf[at] = act
            grad_act = mat_nt(grad_ref[at], w_buf[down])
            grad_pre = (grad_act * (sig + 1.702 * pre * sig * (1.0 - sig))).astype(LOW)
            pre_buf[at] = grad_pre
            total += jnp.sum(grad_pre.astype(F32), axis=0, keepdims=True)
            out = mat_mul(act, w_buf[down])
            back = mat_nt(grad_pre, w_buf[up])
            if i == 0 and not has_acc:
                acc_ref[at] = out
                gacc_ref[at] = back
            elif i == 0:
                acc_ref[at] = acc_in[at] + out
                gacc_ref[at] = gacc_in[at] + back
            else:
                acc_ref[at] += out
                gacc_ref[at] += back
        sums_ref[i] = total
        for c in range(0, width, 256):
            g_buf[up, c : c + 256] = mat_tn(mlp_in_ref[:, c : c + 256], pre_buf[...]).astype(LOW)
        stores[up].start()
        for c in range(0, hidden, 256):
            g_buf[down, c : c + 256] = mat_tn(act_buf[:, c : c + 256], grad_ref[...]).astype(LOW)
        stores[down].start()
    for store in stores:
        store.wait()


def mlp_step(frames, mlp_in, grad, bias, weights, acc=None):
    rows, width = mlp_in.shape
    count, _, hidden = bias.shape
    vmem = pl.BlockSpec(memory_space=pltpu.VMEM)
    anywhere = pl.BlockSpec(memory_space=pl.ANY)
    acc = list(acc) if acc is not None else []
    return pl.pallas_call(
        functools.partial(mlp_kernel, frames, bool(acc)),
        in_specs=[vmem] * 3 + [anywhere] * (2 * count) + [vmem] * len(acc),
        out_specs=[vmem] * 3 + [anywhere] * (2 * count),
        out_shape=[
            jax.ShapeDtypeStruct((rows, width), F32),
            jax.ShapeDtypeStruct((rows, width), F32),
            jax.ShapeDtypeStruct((count, 1, hidden), F32),
        ]
        + [jax.ShapeDtypeStruct(w.shape, LOW) for w in weights],
        scratch_shapes=[
            pltpu.VMEM((2 * count,) + weights[0].shape, LOW),
            pltpu.VMEM((2 * count,) + weights[0].shape, LOW),
            pltpu.VMEM((rows, hidden), LOW),
            pltpu.VMEM((rows, hidden), LOW),
            pltpu.SemaphoreType.DMA((2 * count,)),
            pltpu.SemaphoreType.DMA((2 * count,)),
        ],
        compiler_params=params(),
        cost_estimate=cost(20),
        name="mlp",
    )(mlp_in, grad, bias, *weights, *acc)


def attn_backward_kernel(
    weight_ref, res_ref, acc_ref, gacc_ref, mlp_normed_ref, mlp_inv_ref, cot_ref, normed_ref, inv_ref,
    heads_ref, prob_ref, vec_ref, down_bias_ref, *refs
):
    shards = heads_ref.shape[1]
    part = heads_ref.shape[4]
    qkv_refs, out_refs = refs[:shards], refs[shards : 2 * shards]
    (tok_ref, grad_tok_ref, msg_ref, proj_ref, low_ref, sum_norm_ref, sum_proj_ref, cat) = refs[2 * shards :]
    patches = cot_ref.shape[1]
    gain, mlp_gain = vec_ref[0:1], vec_ref[2:3]
    frame = pl.program_id(0)

    @pl.when(frame == 0)
    def _():
        sum_norm_ref[...] = jnp.zeros_like(sum_norm_ref)
        sum_proj_ref[...] = jnp.zeros_like(sum_proj_ref)

    result = (res_ref[0] + acc_ref[0] + down_bias_ref[...]).astype(LOW)
    for j in range(shards):
        tok_ref[j, 0] = result[:patches, j * part : (j + 1) * part]
    cat[:patches] = cot_ref[0].astype(F32) * weight_ref[frame]
    cat[patches:] = jnp.zeros((cat.shape[0] - patches, cat.shape[1]), F32)
    grad_res = cat[...]
    gacc, mlp_normed = gacc_ref[0], mlp_normed_ref[0]
    hidden = grad_res + norm_back(gacc, mlp_normed, mlp_inv_ref[0], mlp_gain)

    def add_sum(row, values):
        sum_norm_ref[row : row + 1] += jnp.sum(values, axis=0, keepdims=True)

    add_sum(0, grad_res)
    add_sum(1, gacc * mlp_normed)
    add_sum(2, gacc)
    add_sum(3, hidden)
    low = hidden.astype(LOW)
    low_ref[0] = low
    masks = head_masks(part)
    scale = HD ** (-0.5)
    back = jnp.zeros(hidden.shape, F32)
    for k in range(shards):
        grad_mix = mat_nt(low, out_refs[k][...]).astype(LOW)
        queries, keys, values = heads_ref[0, k, 0], heads_ref[0, k, 1], heads_ref[0, k, 2]
        prob_low = prob_ref[0, k]
        prob = prob_low.astype(F32)
        mix_heads = stack_heads(grad_mix, masks)
        grad_value = mat_tn(prob_low, mix_heads)
        grad_prob = mat_nt(mix_heads, values)
        grad_score = (
            prob * (grad_prob - jnp.sum(prob * grad_prob, axis=-1, keepdims=True))
        ).astype(LOW)
        grad_query = pick_heads(mat_mul(grad_score, keys), masks)
        grad_key = mat_tn(grad_score, stack_heads(queries, masks))
        proj = jnp.concatenate([grad_query * scale, grad_key * scale, grad_value], axis=1).astype(LOW)
        proj_ref[0, k] = proj
        sum_proj_ref[k] += jnp.sum(proj.astype(F32), axis=0, keepdims=True)
        back += mat_nt(proj, qkv_refs[k][...])
    normed = normed_ref[0]
    add_sum(4, back * normed)
    add_sum(5, back)
    total = hidden + norm_back(back, normed, inv_ref[0], gain)
    msg_ref[0] = total[patches : patches + 1]
    for j in range(shards):
        grad_tok_ref[j, 0] = total[:patches, j * part : (j + 1) * part].astype(LOW)


def attn_backward(weight, res, acc, gacc, mlp_normed, mlp_inv, cot, normed, inv, heads, prob, vecs, down_bias,
                  qkv, out):
    frames, seq_pad, width = res.shape
    patches = cot.shape[1]
    shards, part = heads.shape[1], heads.shape[4]
    blocks = (shards, frames, patches, part)
    block_spec = pl.BlockSpec((shards, 1, patches, part), lambda f: (0, f, 0, 0))
    ins = (res, acc, gacc, mlp_normed, mlp_inv, cot, normed, inv, heads, prob)
    return pl.pallas_call(
        attn_backward_kernel,
        grid=(frames,),
        in_specs=[pl.BlockSpec(memory_space=pltpu.SMEM)]
        + [per_frame(v.shape) for v in ins]
        + [whole(v) for v in [vecs, down_bias] + list(qkv) + list(out)],
        out_specs=[
            block_spec,
            block_spec,
            per_frame((frames, 1, width)),
            per_frame((frames, shards, seq_pad, 3 * part)),
            per_frame(res.shape),
            pl.BlockSpec((8, width), lambda f: (0, 0)),
            pl.BlockSpec((shards, 1, 3 * part), lambda f: (0, 0, 0)),
        ],
        out_shape=[
            jax.ShapeDtypeStruct(blocks, LOW),
            jax.ShapeDtypeStruct(blocks, LOW),
            jax.ShapeDtypeStruct((frames, 1, width), F32),
            jax.ShapeDtypeStruct((frames, shards, seq_pad, 3 * part), LOW),
            jax.ShapeDtypeStruct(res.shape, LOW),
            jax.ShapeDtypeStruct((8, width), F32),
            jax.ShapeDtypeStruct((shards, 1, 3 * part), F32),
        ],
        scratch_shapes=[pltpu.VMEM((seq_pad, width), F32)],
        compiler_params=params(),
        cost_estimate=cost(21),
        name="attn_backward",
    )(weight, *ins, vecs, down_bias, *qkv, *out)


def attn_grads_kernel(attn_in_ref, low_ref, proj_ref, mix_ref, *refs):
    count = len(refs) - 2
    grad_refs, (proj_buf, mix_buf) = refs[:count], refs[count:]
    rows, width = attn_in_ref.shape
    frames, seq_pad = mix_ref.shape[0], mix_ref.shape[2]
    for i in range(count):
        for f in range(frames):
            at = slice(f * seq_pad, (f + 1) * seq_pad)
            proj_buf[at] = proj_ref[f, i]
            mix_buf[at] = mix_ref[f, i]
        for c in range(0, width, 256):
            qkv = mat_tn(attn_in_ref[:, c : c + 256], proj_buf[...])
            out = mat_tn(low_ref[:, c : c + 256], mix_buf[...])
            grad_refs[i][c : c + 256] = jnp.concatenate([qkv, out], axis=1).astype(LOW)


def attn_grads(attn_in, proj, low, mix, pair):
    frames, shards, seq_pad, part = mix.shape
    width = attn_in.shape[-1]
    rows = frames * seq_pad
    count = min(2, shards)

    def shard(array):
        return pl.BlockSpec((frames, count) + array.shape[2:], lambda i: (0, pair, 0, 0))

    full = pl.BlockSpec((rows, width), lambda i: (0, 0))
    return pl.pallas_call(
        attn_grads_kernel,
        grid=(1,),
        in_specs=[full, full, shard(proj), shard(mix)],
        out_specs=[pl.BlockSpec((width, 4 * part), lambda i: (0, 0))] * count,
        out_shape=[jax.ShapeDtypeStruct((width, 4 * part), LOW)] * count,
        scratch_shapes=[pltpu.VMEM((rows, 3 * part), LOW), pltpu.VMEM((rows, part), LOW)],
        compiler_params=params(),
        cost_estimate=cost(6),
        name="attn_grads",
    )(attn_in.reshape(rows, width), low.reshape(rows, width), proj, mix)


def same_video(rows, columns):
    row = lax.broadcasted_iota(jnp.int32, (rows, columns), 0)
    column = lax.broadcasted_iota(jnp.int32, (rows, columns), 1)
    return (row % columns) // VIDEO_FRAMES == column // VIDEO_FRAMES


def message_forward_kernel(
    cls_ref, weight_ref, vec_ref, flat_ref, bias_ref, proj_ref,
    message_ref, normed_ref, inv_ref, in_ref, heads_ref, prob_ref, mix_ref, sum_ref
):
    part = proj_ref.shape[0]
    chunk = cls_ref.shape[0]
    message = mat_mul(cls_ref[...], weight_ref[...]) + vec_ref[4:5]
    message_ref[...] = message
    normed, inv = normalize(message)
    normed_ref[...] = normed
    inv_ref[...] = inv
    msg_in = (normed * vec_ref[5:6] + vec_ref[6:7]).astype(LOW)
    in_ref[...] = msg_in
    proj = mat_mul(msg_in, flat_ref[...])
    queries = (proj[:, :part] + bias_ref[0:1]).astype(LOW)
    keys = proj[:, part : 2 * part].astype(LOW)
    values = (proj[:, 2 * part :] + bias_ref[1:2]).astype(LOW)
    heads_ref[0, 0] = queries
    heads_ref[0, 1] = keys
    heads_ref[0, 2] = values
    masks = head_masks(part)
    scores = mat_nt(stack_heads(queries, masks, HD ** (-0.5)), keys)
    scores = jnp.where(same_video(len(masks) * chunk, chunk), scores, -1e30)
    exps = jnp.exp(scores - jnp.max(scores, axis=-1, keepdims=True))
    prob = exps / jnp.sum(exps, axis=-1, keepdims=True)
    prob_ref[0] = prob
    mix = pick_heads(mat_mul(prob.astype(LOW), values), masks).astype(LOW)
    mix_ref[...] = mix
    sum_ref[...] = mat_mul(mix, proj_ref[...])


def message_forward(chunk, cls_rows, weight, vecs, flat, bias, proj):
    count, width = cls_rows.shape
    part = proj.shape[0]
    heads = part // HD
    chunks = count // chunk
    rows = lambda columns: pl.BlockSpec((chunk, columns), lambda c: (c, 0))
    return pl.pallas_call(
        message_forward_kernel,
        grid=(chunks,),
        in_specs=[rows(width)] + [whole(v) for v in (weight, vecs, flat, bias, proj)],
        out_specs=[
            rows(width), rows(width), rows(1), rows(width),
            per_frame((chunks, 3, chunk, part)), per_frame((chunks, heads * chunk, chunk)),
            rows(part), rows(width),
        ],
        out_shape=[
            jax.ShapeDtypeStruct((count, width), F32),
            jax.ShapeDtypeStruct((count, width), F32),
            jax.ShapeDtypeStruct((count, 1), F32),
            jax.ShapeDtypeStruct((count, width), LOW),
            jax.ShapeDtypeStruct((chunks, 3, chunk, part), LOW),
            jax.ShapeDtypeStruct((chunks, heads * chunk, chunk), F32),
            jax.ShapeDtypeStruct((count, part), LOW),
            jax.ShapeDtypeStruct((count, width), F32),
        ],
        compiler_params=params(),
        cost_estimate=cost(5),
        name="message_forward",
    )(cls_rows, weight, vecs, flat, bias, proj)


def message_backward_kernel(
    grad_ref, in_ref, heads_ref, prob_ref, mix_ref, flat_ref, proj_ref,
    grad_flat_ref, grad_proj_ref, sum_grad_ref, sum_cross_ref, back_ref
):
    @pl.when(pl.program_id(0) == 0)
    def _():
        for ref in (grad_flat_ref, grad_proj_ref, sum_grad_ref, sum_cross_ref):
            ref[...] = jnp.zeros_like(ref)

    part = proj_ref.shape[0]
    chunk = grad_ref.shape[0]
    masks = head_masks(part)
    grad = grad_ref[...].astype(LOW)
    sum_grad_ref[...] += jnp.sum(grad.astype(F32), axis=0, keepdims=True)
    grad_proj_ref[...] += mat_tn(mix_ref[...], grad)
    grad_mix = mat_nt(grad, proj_ref[...]).astype(LOW)
    mix_heads = stack_heads(grad_mix, masks)
    queries, keys, values = heads_ref[0, 0], heads_ref[0, 1], heads_ref[0, 2]
    prob = prob_ref[0]
    grad_prob = mat_nt(mix_heads, values)
    grad_score = prob * (grad_prob - jnp.sum(prob * grad_prob, axis=-1, keepdims=True))
    score_low = grad_score.astype(LOW)
    grad_query = pick_heads(mat_mul(score_low, keys), masks) * HD ** (-0.5)
    grad_key = mat_tn(score_low, stack_heads(queries, masks)) * HD ** (-0.5)
    grad_value = mat_tn(prob.astype(LOW), mix_heads)
    cross = jnp.concatenate([grad_query, grad_key, grad_value], axis=1).astype(LOW)
    sum_cross_ref[...] += jnp.sum(cross.astype(F32), axis=0, keepdims=True)
    grad_flat_ref[...] += mat_tn(in_ref[...], cross)
    back_ref[...] = mat_nt(cross, flat_ref[...])


def message_backward(grad, msg_in, heads, prob, mix, flat, proj):
    count, width = grad.shape
    part = proj.shape[0]
    chunks, _, chunk, _ = heads.shape
    rows = lambda columns: pl.BlockSpec((chunk, columns), lambda c: (c, 0))
    fixed = lambda shape: pl.BlockSpec(shape, lambda c: (0, 0))
    shapes = [(width, 3 * part), (part, width), (1, width), (1, 3 * part)]
    return pl.pallas_call(
        message_backward_kernel,
        grid=(chunks,),
        in_specs=[
            rows(width), rows(width), per_frame(heads.shape), per_frame(prob.shape), rows(part),
            whole(flat), whole(proj),
        ],
        out_specs=[fixed(s) for s in shapes] + [rows(width)],
        out_shape=[jax.ShapeDtypeStruct(s, F32) for s in shapes + [(count, width)]],
        compiler_params=params(),
        cost_estimate=cost(6),
        name="message_backward",
    )(grad, msg_in, heads, prob, mix, flat, proj)


def message_end_kernel(
    grad_ref, back_ref, other_ref, normed_ref, inv_ref, vec_ref, cls_ref, weight_ref, grad_weight_ref,
    sums_ref, grad_cls_ref
):
    @pl.when(pl.program_id(0) == 0)
    def _():
        grad_weight_ref[...] = jnp.zeros_like(grad_weight_ref)
        sums_ref[...] = jnp.zeros_like(sums_ref)

    back = back_ref[...] + other_ref[...]
    normed = normed_ref[...]
    grad = grad_ref[...] + norm_back(back, normed, inv_ref[...], vec_ref[5:6])
    low = grad.astype(LOW)
    for row, values in enumerate((low.astype(F32), back * normed, back)):
        sums_ref[row : row + 1] += jnp.sum(values, axis=0, keepdims=True)
    grad_weight_ref[...] += mat_tn(cls_ref[...], low)
    grad_cls_ref[...] = mat_nt(low, weight_ref[...])


def message_end(chunk, grad, back, other, normed, inv, vecs, cls_rows, weight):
    count, width = grad.shape
    rows = lambda columns: pl.BlockSpec((chunk, columns), lambda c: (c, 0))
    fixed = lambda shape: pl.BlockSpec(shape, lambda c: (0, 0))
    return pl.pallas_call(
        message_end_kernel,
        grid=(count // chunk,),
        in_specs=[rows(width)] * 4 + [rows(1), whole(vecs), rows(width), whole(weight)],
        out_specs=[fixed((width, width)), fixed((8, width)), rows(width)],
        out_shape=[
            jax.ShapeDtypeStruct((width, width), F32),
            jax.ShapeDtypeStruct((8, width), F32),
            jax.ShapeDtypeStruct((count, width), F32),
        ],
        compiler_params=params(),
        cost_estimate=cost(5),
        name="message_end",
    )(grad, back, other, normed, inv, vecs, cls_rows, weight)


def swap(block, axis, flip):
    return lax.ppermute(block, axis, [(i, i ^ flip) for i in range(lax.axis_size(axis))])


def bits_of(size):
    return [1 << b for b in range(size.bit_length() - 1)]


def reorder(parts, index):
    parts = list(parts)
    for bit in bits_of(len(parts)):
        odd = (index & bit) != 0
        parts = [jnp.where(odd, parts[k ^ bit], parts[k]) for k in range(len(parts))]
    return parts


def join(block, other, odd):
    return jnp.concatenate([jnp.where(odd, other, block), jnp.where(odd, block, other)], axis=0)


def gather_all(block, axis):
    index = lax.axis_index(axis)
    for bit in bits_of(lax.axis_size(axis)):
        block = join(block, swap(block, axis, bit), (index & bit) != 0)
    return block


def frames_in(block, count, index):
    part = block.shape[0] // count
    pieces = []
    for k in range(count):
        piece = lax.dynamic_slice_in_dim(block, (index ^ k) * part, part, 0)
        pieces.append(piece if k == 0 else swap(piece, "wide", k))
    return jnp.concatenate(reorder(pieces, index), axis=2)


def frames_out(blocks, index):
    pieces = []
    for k in range(blocks.shape[0]):
        piece = lax.dynamic_index_in_dim(blocks, index ^ k, 0, keepdims=False)
        pieces.append(piece if k == 0 else swap(piece, "wide", k))
    return jnp.concatenate(reorder(pieces, index), axis=0)


def shards_in(block, count):
    shards = {0: block}
    for bit in reversed(bits_of(count)):
        for k in list(shards):
            shards[k ^ bit] = swap(shards[k], "wide", bit)
    return [shards[k] for k in range(count)]


def added(terms, start, size):
    total = sum(
        lax.dynamic_slice_in_dim(array, begin + start, size, 0).astype(F32) for array, begin in terms
    )
    return total.astype(LOW)


def reduce_narrow(terms, size, bits):
    index = lax.axis_index("narrow")
    for bit in bits:
        odd = (index & bit) != 0
        size = size // 2
        away = added(terms, jnp.where(odd, 0, size), size)
        keep = jnp.where(odd, size, 0)
        terms = [(array, begin + keep) for array, begin in terms] + [(swap(away, "narrow", bit), 0)]
    block = added(terms, 0, size)
    for bit in reversed(bits):
        block = join(block, swap(block, "narrow", bit), (index & bit) != 0)
    return block


def reduce_grad(parts):
    size = parts[0].shape[0]
    terms = {k: [(part, 0)] for k, part in enumerate(parts)}
    for bit in bits_of(len(parts)):
        for k in sorted(terms, reverse=True):
            if k & bit:
                own = terms.pop(k)
                value = own[0][0] if len(own) == 1 else added(own, 0, size)
                terms[k ^ bit].append((swap(value, "wide", bit), 0))
    bits = bits_of(lax.axis_size("narrow"))
    half = size // 2
    low = reduce_narrow(terms[0], half, bits)
    high = reduce_narrow([(array, begin + half) for array, begin in terms[0]], half, bits[1:] + bits[:1])
    return jnp.concatenate([low, high], axis=0).astype(F32)


def body(
    frame_tokens,
    cotangent,
    caption_count,
    caption_len,
    message_weight,
    message_bias,
    message_gain,
    message_shift,
    cross_qkv,
    cross_bias,
    cross_proj,
    cross_offset,
    attn_gain,
    attn_shift,
    qkv_weight,
    qkv_bias,
    out_weight,
    out_bias,
    mlp_gain,
    mlp_shift,
    up_weight,
    up_bias,
    down_weight,
    down_bias,
):
    group_frames, patches, width_part = frame_tokens.shape
    model_width = message_weight.shape[0]
    hidden_part = up_weight.shape[1]
    wide = lax.axis_size("wide")
    narrow = lax.axis_size("narrow")
    wide_idx = lax.axis_index("wide")
    narrow_idx = lax.axis_index("narrow")
    frames = group_frames // wide
    seq_pad = -(-(patches + 1) // ROW_TILE) * ROW_TILE
    rows = frames * seq_pad
    all_frames = group_frames * narrow
    first_group = narrow_idx * group_frames
    first_frame = first_group + wide_idx * frames
    chunk = max(c for c in range(VIDEO_FRAMES, 129, VIDEO_FRAMES) if all_frames % c == 0)

    def own_cols(values):
        return lax.dynamic_slice_in_dim(values, wide_idx * width_part, width_part, values.ndim - 1)

    tokens = frames_in(frame_tokens, wide, wide_idx)
    small_parts = [qkv_bias, up_bias, out_bias, down_bias, frame_tokens[:, 0, :].astype(F32)]
    small = jnp.concatenate([v.reshape(-1) for v in small_parts])
    small = [small] + [swap(small, "wide", k) for k in range(1, wide)]
    at = 0
    gathered = []
    for part in small_parts:
        gathered.append([v[at : at + part.size].reshape(part.shape) for v in small])
        at += part.size
    qkv_biases = jnp.stack(gathered[0])
    up_biases = [v.reshape(1, 1, hidden_part) for v in gathered[1]]
    out_bias_row = jnp.concatenate(reorder(gathered[2], wide_idx)).reshape(1, model_width)
    down_bias_row = jnp.concatenate(reorder(gathered[3], wide_idx)).reshape(1, model_width)
    cls_rows = gather_all(jnp.concatenate(reorder(gathered[4], wide_idx), axis=1).astype(LOW), "narrow")
    qkv = shards_in(qkv_weight.reshape(model_width, 3 * width_part), wide)
    out = shards_in(out_weight, wide)
    cot = frames_in(cotangent, wide, wide_idx)
    up = shards_in(up_weight, wide)
    down = shards_in(down_weight, wide)
    vecs = jnp.stack(
        [attn_gain, attn_shift, mlp_gain, mlp_shift, message_bias, message_gain, message_shift, cross_offset]
    )

    caption_slot = jnp.arange(caption_len.shape[1])
    word_total = jnp.sum(
        jnp.where(caption_slot[None, :] < caption_count[:, None], caption_len, 0), axis=1
    ).astype(F32)
    video_scale = word_total / jnp.mean(word_total)
    own_video = (first_frame + jnp.arange(frames)) // VIDEO_FRAMES
    video_match = own_video[:, None] == jnp.arange(video_scale.shape[0])[None, :]
    frame_weight = jnp.sum(jnp.where(video_match, video_scale[None, :], 0.0), axis=1)

    cross_flat = cross_qkv.reshape(model_width, 3 * width_part)
    message, msg_normed, msg_inv, msg_in, cross_heads, cross_prob, cross_mix, cross_sum = message_forward(
        chunk, cls_rows, message_weight, vecs, cross_flat, cross_bias, cross_proj
    )
    message_two = lax.dynamic_slice_in_dim(message, first_frame, frames, 0) + cross_offset
    for k in range(wide):
        piece = lax.dynamic_slice_in_dim(cross_sum, first_group + (wide_idx ^ k) * frames, frames, 0)
        message_two = message_two + (piece if k == 0 else swap(piece, "wide", k))

    (normed, inv, attn_in, heads, prob, mix, hidden_res, mlp_normed, mlp_inv, mlp_in) = attn_forward(
        seq_pad, tokens, message_two.reshape(frames, 1, model_width), vecs, out_bias_row, qkv_biases, qkv, out
    )
    grad_rows = jnp.pad(
        (cot.astype(F32) * frame_weight[:, None, None]).astype(LOW),
        ((0, 0), (0, seq_pad - patches), (0, 0)),
    ).reshape(rows, model_width)
    mlp_in = mlp_in.reshape(rows, model_width)
    acc = None
    sum_up, grad_up, grad_down = [], [], []
    for k in range(0, wide, 2):
        shards = range(k, k + 2)
        weights = [w for j in shards for w in (up[j], down[j])]
        done = mlp_step(
            frames, mlp_in, grad_rows, jnp.concatenate([up_biases[j] for j in shards]), weights, acc
        )
        acc = done[:2]
        sum_up += [done[2][j, 0] for j in range(len(shards))]
        grad_up += done[3::2]
        grad_down += done[4::2]
    grad_up_own = reduce_grad(grad_up)
    grad_down_own = reduce_grad(grad_down)

    shape = (frames, seq_pad, model_width)
    out_blocks, grad_blocks, grad_msg, proj, low, sum_norm, sum_proj = attn_backward(
        frame_weight, hidden_res, acc[0].reshape(shape), acc[1].reshape(shape), mlp_normed, mlp_inv, cot,
        normed, inv, heads, prob, vecs, down_bias_row, qkv, out,
    )
    grad_attn = [g for pair in reversed(range(wide // 2)) for g in reversed(attn_grads(attn_in, proj, low, mix, pair))]
    grad_attn = reduce_grad(grad_attn[::-1])
    output_tokens = frames_out(out_blocks, wide_idx)
    grad_tokens = frames_out(grad_blocks, wide_idx)

    sums = jnp.concatenate(
        [sum_norm[i] for i in range(6)]
        + reorder(sum_up, wide_idx)
        + reorder([sum_proj[k, 0, :width_part] for k in range(wide)], wide_idx)
        + reorder([sum_proj[k, 0, 2 * width_part :] for k in range(wide)], wide_idx)
    ).reshape(-1, model_width)
    grad_msg = grad_msg.reshape(frames, model_width)
    for axis in ("wide", "narrow"):
        index = lax.axis_index(axis)
        for bit in bits_of(lax.axis_size(axis)):
            other = swap(jnp.concatenate([sums, grad_msg], axis=0), axis, bit)
            sums = sums + other[: sums.shape[0]]
            grad_msg = join(grad_msg, other[sums.shape[0] :], (index & bit) != 0)
    grad_up_bias = lax.dynamic_slice_in_dim(sums[6:-2].reshape(-1), wide_idx * hidden_part, hidden_part, 0)

    grad_cross_flat, grad_cross_proj, sum_cross_grad, sum_cross, back = message_backward(
        grad_msg, msg_in, cross_heads, cross_prob, cross_mix, cross_flat, cross_proj
    )
    bits = bits_of(wide)
    for bit in bits[:-1]:
        back = back + swap(back, "wide", bit)
    grad_message_weight, msg_sums, grad_cls = message_end(
        chunk, grad_msg, back, swap(back, "wide", bits[-1]), msg_normed, msg_inv, vecs, cls_rows, message_weight
    )
    grad_cls = own_cols(lax.dynamic_slice_in_dim(grad_cls, first_group, group_frames, 0))
    grad_tokens = grad_tokens.at[:, 0].set((grad_tokens[:, 0].astype(F32) + grad_cls).astype(LOW))
    grad_cross_bias = jnp.stack([sum_cross[0, :width_part], sum_cross[0, 2 * width_part :]])

    return (
        output_tokens,
        grad_tokens,
        grad_message_weight,
        msg_sums[0],
        msg_sums[1],
        msg_sums[2],
        grad_cross_flat.reshape(model_width, 3, width_part),
        grad_cross_bias,
        grad_cross_proj,
        sum_cross_grad[0],
        sums[4],
        sums[5],
        grad_attn[:, : 3 * width_part].reshape(model_width, 3, width_part),
        own_cols(sums[-2:]),
        grad_attn[:, 3 * width_part :].T,
        own_cols(sums[3]),
        sums[1],
        sums[2],
        grad_up_own,
        grad_up_bias,
        grad_down_own,
        own_cols(sums[0]),
    )


def solution(mesh):
    return jax.shard_map(
        body,
        mesh=mesh,
        in_specs=(
            P("narrow", None, "wide"),
            P("narrow", None, "wide"),
            P(),
            P(),
            P(),
            P(),
            P(),
            P(),
            P(None, None, "wide"),
            P(None, "wide"),
            P("wide", None),
            P(),
            P(),
            P(),
            P(None, None, "wide"),
            P(None, "wide"),
            P("wide", None),
            P("wide"),
            P(),
            P(),
            P(None, "wide"),
            P("wide"),
            P("wide", None),
            P("wide"),
        ),
        out_specs=(
            P("narrow", None, "wide"),
            P("narrow", None, "wide"),
            P(),
            P(),
            P(),
            P(),
            P(None, None, "wide"),
            P(None, "wide"),
            P("wide", None),
            P(),
            P(),
            P(),
            P(None, None, "wide"),
            P(None, "wide"),
            P("wide", None),
            P("wide"),
            P(),
            P(),
            P(None, "wide"),
            P("wide"),
            P("wide", None),
            P("wide"),
        ),
        check_vma=False,
    )
```

```python
import functools
import jax
import jax.numpy as jnp
from jax import lax
from jax.experimental import pallas as pl
from jax.experimental.pallas import tpu as pltpu
from jax.sharding import PartitionSpec as P

VIDEO_FRAMES = 8
HD = 64
EPS = 1e-05
ROW_TILE = 16
LOW = jnp.bfloat16
F32 = jnp.float32
VMEM_LIMIT = 56 * 1024 * 1024


def dot(left, right, dims):
    return lax.dot_general(left, right, (dims, ((), ())), preferred_element_type=F32)


def mat_mul(left, right):
    return dot(left, right, ((1,), (0,)))


def mat_tn(left, right):
    return dot(left, right, ((0,), (0,)))


def mat_nt(left, right):
    return dot(left, right, ((1,), (1,)))


def normalize(values):
    row_mean = jnp.mean(values, axis=-1, keepdims=True)
    centred = values - row_mean
    inv_std = lax.rsqrt(jnp.mean(centred * centred, axis=-1, keepdims=True) + EPS)
    return (centred * inv_std, inv_std)


def norm_back(grad_norm, normed, inv_std, norm_gain):
    scaled = grad_norm * norm_gain
    return inv_std * (
        scaled
        - jnp.mean(scaled, axis=-1, keepdims=True)
        - normed * jnp.mean(scaled * normed, axis=-1, keepdims=True)
    )


def params(limit=VMEM_LIMIT):
    return pltpu.CompilerParams(vmem_limit_bytes=limit)


def cost(micros):
    return pl.CostEstimate(flops=int(micros * 1.0e6), bytes_accessed=int(micros * 1.0e3), transcendentals=0)


def whole(array):
    return pl.BlockSpec(array.shape, lambda *_: (0,) * array.ndim)


def per_frame(shape):
    return pl.BlockSpec((1,) + tuple(shape[1:]), lambda f: (f,) + (0,) * (len(shape) - 1))


def head_masks(width):
    lane = lax.broadcasted_iota(jnp.int32, (1, width), 1) // HD
    return [lane == h for h in range(width // HD)]


def stack_heads(values, masks, scale=1.0):
    return jnp.concatenate([values * jnp.where(m, scale, 0.0).astype(values.dtype) for m in masks], axis=0)


def pick_heads(values, masks):
    size = values.shape[0] // len(masks)
    picked = values[:size]
    for h in range(1, len(masks)):
        picked = jnp.where(masks[h], values[h * size : (h + 1) * size], picked)
    return picked


def attn_forward_kernel(seq_len, tok_ref, msg_ref, vec_ref, out_bias_ref, qkv_bias_ref, *refs):
    shards = qkv_bias_ref.shape[0]
    qkv_refs, out_refs = refs[:shards], refs[shards : 2 * shards]
    (normed_ref, inv_ref, attn_in_ref, heads_ref, prob_ref, mix_ref, hidden_ref, mlp_normed_ref,
     mlp_inv_ref, mlp_in_ref, cat) = refs[2 * shards :]
    gain, shift, mlp_gain, mlp_shift = (vec_ref[i : i + 1] for i in range(4))
    patches = tok_ref.shape[1]
    seq_pad, width = cat.shape
    part = out_refs[0].shape[0]
    cat[:patches] = tok_ref[0].astype(F32)
    cat[patches:seq_len] = msg_ref[0, :1]
    cat[seq_len:] = jnp.zeros((seq_pad - seq_len, width), F32)
    full = cat[...]
    normed, inv = normalize(full)
    normed_ref[0] = normed
    inv_ref[0] = inv
    attn_in = (normed * gain + shift).astype(LOW)
    attn_in_ref[0] = attn_in
    masks = head_masks(part)
    live = lax.broadcasted_iota(jnp.int32, (1, seq_pad), 1) < seq_len
    total = full + out_bias_ref[...]
    for k in range(shards):
        proj = mat_mul(attn_in, qkv_refs[k][...])
        queries = (proj[:, :part] + qkv_bias_ref[k, 0:1]).astype(LOW)
        keys = proj[:, part : 2 * part].astype(LOW)
        values = (proj[:, 2 * part :] + qkv_bias_ref[k, 1:2]).astype(LOW)
        heads_ref[0, k, 0] = queries
        heads_ref[0, k, 1] = keys
        heads_ref[0, k, 2] = values
        scores = mat_nt(stack_heads(queries, masks, HD ** (-0.5)), keys)
        scores = jnp.where(live, scores, -1e30)
        exps = jnp.exp(scores - jnp.max(scores, axis=-1, keepdims=True))
        prob = (exps * (1.0 / jnp.sum(exps, axis=-1, keepdims=True))).astype(LOW)
        prob_ref[0, k] = prob
        mix_low = pick_heads(mat_mul(prob, values), masks).astype(LOW)
        mix_ref[0, k] = mix_low
        total += mat_mul(mix_low, out_refs[k][...])
    hidden_ref[0] = total
    mlp_normed, mlp_inv = normalize(total.astype(LOW).astype(F32))
    mlp_normed_ref[0] = mlp_normed
    mlp_inv_ref[0] = mlp_inv
    mlp_in_ref[0] = (mlp_normed * mlp_gain + mlp_shift).astype(LOW)


def attn_forward(seq_pad, tokens, msg, vecs, out_bias, qkv_bias, qkv, out):
    frames, patches, width = tokens.shape
    shards = len(qkv)
    part = qkv[0].shape[1] // 3
    heads = part // HD
    shapes = [
        ((frames, seq_pad, width), F32),
        ((frames, seq_pad, 1), F32),
        ((frames, seq_pad, width), LOW),
        ((frames, shards, 3, seq_pad, part), LOW),
        ((frames, shards, heads * seq_pad, seq_pad), LOW),
        ((frames, shards, seq_pad, part), LOW),
        ((frames, seq_pad, width), F32),
        ((frames, seq_pad, width), F32),
        ((frames, seq_pad, 1), F32),
        ((frames, seq_pad, width), LOW),
    ]
    ins = [tokens, msg, vecs, out_bias, qkv_bias]
    return pl.pallas_call(
        functools.partial(attn_forward_kernel, patches + 1),
        grid=(frames,),
        in_specs=[per_frame(tokens.shape), per_frame(msg.shape)]
        + [whole(v) for v in ins[2:]]
        + [whole(v) for v in list(qkv) + list(out)],
        out_specs=[per_frame(s) for s, _ in shapes],
        out_shape=[jax.ShapeDtypeStruct(s, d) for s, d in shapes],
        scratch_shapes=[pltpu.VMEM((seq_pad, width), F32)],
        compiler_params=params(),
        cost_estimate=cost(20),
        name="attn_forward",
    )(*ins, *qkv, *out)


def mlp_kernel(frames, has_acc, mlp_in_ref, grad_ref, bias_ref, *refs):
    count = bias_ref.shape[0]
    w_refs, refs = refs[: 2 * count], refs[2 * count :]
    if has_acc:
        acc_in, gacc_in, refs = refs[0], refs[1], refs[2:]
    acc_ref, gacc_ref, sums_ref = refs[:3]
    g_refs, refs = refs[3 : 3 + 2 * count], refs[3 + 2 * count :]
    w_buf, g_buf, act_buf, pre_buf, in_sem, out_sem = refs
    rows, width = mlp_in_ref.shape
    hidden = bias_ref.shape[2]
    step = rows // frames
    loads = [pltpu.make_async_copy(w_refs[j], w_buf.at[j], in_sem.at[j]) for j in range(2 * count)]
    stores = [pltpu.make_async_copy(g_buf.at[j], g_refs[j], out_sem.at[j]) for j in range(2 * count)]
    for load in loads:
        load.start()
    for i in range(count):
        up, down = 2 * i, 2 * i + 1
        loads[up].wait()
        loads[down].wait()
        total = jnp.zeros((1, hidden), F32)
        for f in range(frames):
            at = slice(f * step, (f + 1) * step)
            rows_in = mlp_in_ref[at]
            pre = mat_mul(rows_in, w_buf[up]) + bias_ref[i]
            sig = 0.5 + 0.5 * jnp.tanh(0.851 * pre)
            act = (pre * sig).astype(LOW)
            act_buf[at] = act
            grad_act = mat_nt(grad_ref[at], w_buf[down])
            grad_pre = (grad_act * (sig + 1.702 * pre * sig * (1.0 - sig))).astype(LOW)
            pre_buf[at] = grad_pre
            total += jnp.sum(grad_pre.astype(F32), axis=0, keepdims=True)
            out = mat_mul(act, w_buf[down])
            back = mat_nt(grad_pre, w_buf[up])
            if i == 0 and not has_acc:
                acc_ref[at] = out
                gacc_ref[at] = back
            elif i == 0:
                acc_ref[at] = acc_in[at] + out
                gacc_ref[at] = gacc_in[at] + back
            else:
                acc_ref[at] += out
                gacc_ref[at] += back
        sums_ref[i] = total
        for c in range(0, width, 256):
            g_buf[up, c : c + 256] = mat_tn(mlp_in_ref[:, c : c + 256], pre_buf[...]).astype(LOW)
        stores[up].start()
        for c in range(0, hidden, 256):
            g_buf[down, c : c + 256] = mat_tn(act_buf[:, c : c + 256], grad_ref[...]).astype(LOW)
        stores[down].start()
    for store in stores:
        store.wait()


def mlp_step(frames, mlp_in, grad, bias, weights, acc=None):
    rows, width = mlp_in.shape
    count, _, hidden = bias.shape
    vmem = pl.BlockSpec(memory_space=pltpu.VMEM)
    anywhere = pl.BlockSpec(memory_space=pl.ANY)
    acc = list(acc) if acc is not None else []
    return pl.pallas_call(
        functools.partial(mlp_kernel, frames, bool(acc)),
        in_specs=[vmem] * 3 + [anywhere] * (2 * count) + [vmem] * len(acc),
        out_specs=[vmem] * 3 + [anywhere] * (2 * count),
        out_shape=[
            jax.ShapeDtypeStruct((rows, width), F32),
            jax.ShapeDtypeStruct((rows, width), F32),
            jax.ShapeDtypeStruct((count, 1, hidden), F32),
        ]
        + [jax.ShapeDtypeStruct(w.shape, LOW) for w in weights],
        scratch_shapes=[
            pltpu.VMEM((2 * count,) + weights[0].shape, LOW),
            pltpu.VMEM((2 * count,) + weights[0].shape, LOW),
            pltpu.VMEM((rows, hidden), LOW),
            pltpu.VMEM((rows, hidden), LOW),
            pltpu.SemaphoreType.DMA((2 * count,)),
            pltpu.SemaphoreType.DMA((2 * count,)),
        ],
        compiler_params=params(),
        cost_estimate=cost(20),
        name="mlp",
    )(mlp_in, grad, bias, *weights, *acc)


def attn_backward_kernel(
    weight_ref, res_ref, acc_ref, gacc_ref, mlp_normed_ref, mlp_inv_ref, cot_ref, normed_ref, inv_ref,
    heads_ref, prob_ref, vec_ref, down_bias_ref, *refs
):
    shards = heads_ref.shape[1]
    part = heads_ref.shape[4]
    qkv_refs, out_refs = refs[:shards], refs[shards : 2 * shards]
    (tok_ref, grad_tok_ref, msg_ref, proj_ref, low_ref, sum_norm_ref, sum_proj_ref, cat) = refs[2 * shards :]
    patches = cot_ref.shape[1]
    gain, mlp_gain = vec_ref[0:1], vec_ref[2:3]
    frame = pl.program_id(0)

    @pl.when(frame == 0)
    def _():
        sum_norm_ref[...] = jnp.zeros_like(sum_norm_ref)
        sum_proj_ref[...] = jnp.zeros_like(sum_proj_ref)

    result = (res_ref[0] + acc_ref[0] + down_bias_ref[...]).astype(LOW)
    for j in range(shards):
        tok_ref[j, 0] = result[:patches, j * part : (j + 1) * part]
    cat[:patches] = cot_ref[0].astype(F32) * weight_ref[frame]
    cat[patches:] = jnp.zeros((cat.shape[0] - patches, cat.shape[1]), F32)
    grad_res = cat[...]
    gacc, mlp_normed = gacc_ref[0], mlp_normed_ref[0]
    hidden = grad_res + norm_back(gacc, mlp_normed, mlp_inv_ref[0], mlp_gain)

    def add_sum(row, values):
        sum_norm_ref[row : row + 1] += jnp.sum(values, axis=0, keepdims=True)

    add_sum(0, grad_res)
    add_sum(1, gacc * mlp_normed)
    add_sum(2, gacc)
    add_sum(3, hidden)
    low = hidden.astype(LOW)
    low_ref[0] = low
    masks = head_masks(part)
    scale = HD ** (-0.5)
    back = jnp.zeros(hidden.shape, F32)
    for k in range(shards):
        grad_mix = mat_nt(low, out_refs[k][...]).astype(LOW)
        queries, keys, values = heads_ref[0, k, 0], heads_ref[0, k, 1], heads_ref[0, k, 2]
        prob_low = prob_ref[0, k]
        prob = prob_low.astype(F32)
        mix_heads = stack_heads(grad_mix, masks)
        grad_value = mat_tn(prob_low, mix_heads)
        grad_prob = mat_nt(mix_heads, values)
        grad_score = (
            prob * (grad_prob - jnp.sum(prob * grad_prob, axis=-1, keepdims=True))
        ).astype(LOW)
        grad_query = pick_heads(mat_mul(grad_score, keys), masks)
        grad_key = mat_tn(grad_score, stack_heads(queries, masks))
        proj = jnp.concatenate([grad_query * scale, grad_key * scale, grad_value], axis=1).astype(LOW)
        proj_ref[0, k] = proj
        sum_proj_ref[k] += jnp.sum(proj.astype(F32), axis=0, keepdims=True)
        back += mat_nt(proj, qkv_refs[k][...])
    normed = normed_ref[0]
    add_sum(4, back * normed)
    add_sum(5, back)
    total = hidden + norm_back(back, normed, inv_ref[0], gain)
    msg_ref[0] = total[patches : patches + 1]
    for j in range(shards):
        grad_tok_ref[j, 0] = total[:patches, j * part : (j + 1) * part].astype(LOW)


def attn_backward(weight, res, acc, gacc, mlp_normed, mlp_inv, cot, normed, inv, heads, prob, vecs, down_bias,
                  qkv, out):
    frames, seq_pad, width = res.shape
    patches = cot.shape[1]
    shards, part = heads.shape[1], heads.shape[4]
    blocks = (shards, frames, patches, part)
    block_spec = pl.BlockSpec((shards, 1, patches, part), lambda f: (0, f, 0, 0))
    ins = (res, acc, gacc, mlp_normed, mlp_inv, cot, normed, inv, heads, prob)
    return pl.pallas_call(
        attn_backward_kernel,
        grid=(frames,),
        in_specs=[pl.BlockSpec(memory_space=pltpu.SMEM)]
        + [per_frame(v.shape) for v in ins]
        + [whole(v) for v in [vecs, down_bias] + list(qkv) + list(out)],
        out_specs=[
            block_spec,
            block_spec,
            per_frame((frames, 1, width)),
            per_frame((frames, shards, seq_pad, 3 * part)),
            per_frame(res.shape),
            pl.BlockSpec((8, width), lambda f: (0, 0)),
            pl.BlockSpec((shards, 1, 3 * part), lambda f: (0, 0, 0)),
        ],
        out_shape=[
            jax.ShapeDtypeStruct(blocks, LOW),
            jax.ShapeDtypeStruct(blocks, LOW),
            jax.ShapeDtypeStruct((frames, 1, width), F32),
            jax.ShapeDtypeStruct((frames, shards, seq_pad, 3 * part), LOW),
            jax.ShapeDtypeStruct(res.shape, LOW),
            jax.ShapeDtypeStruct((8, width), F32),
            jax.ShapeDtypeStruct((shards, 1, 3 * part), F32),
        ],
        scratch_shapes=[pltpu.VMEM((seq_pad, width), F32)],
        compiler_params=params(),
        cost_estimate=cost(21),
        name="attn_backward",
    )(weight, *ins, vecs, down_bias, *qkv, *out)


def attn_grads_kernel(attn_in_ref, low_ref, proj_ref, mix_ref, after_ref, *refs):
    count = len(refs) - 2
    grad_refs, (proj_buf, mix_buf) = refs[:count], refs[count:]
    rows, width = attn_in_ref.shape
    frames, seq_pad = mix_ref.shape[0], mix_ref.shape[2]
    for i in range(count):
        for f in range(frames):
            at = slice(f * seq_pad, (f + 1) * seq_pad)
            proj_buf[at] = proj_ref[f, i]
            mix_buf[at] = mix_ref[f, i]
        for c in range(0, width, 256):
            qkv = mat_tn(attn_in_ref[:, c : c + 256], proj_buf[...])
            out = mat_tn(low_ref[:, c : c + 256], mix_buf[...])
            grad_refs[i][c : c + 256] = jnp.concatenate([qkv, out], axis=1).astype(LOW)


def attn_grads(attn_in, proj, low, mix, pair, after):
    frames, shards, seq_pad, part = mix.shape
    width = attn_in.shape[-1]
    rows = frames * seq_pad
    count = min(2, shards)

    def shard(array):
        return pl.BlockSpec((frames, count) + array.shape[2:], lambda i: (0, pair, 0, 0))

    full = pl.BlockSpec((rows, width), lambda i: (0, 0))
    return pl.pallas_call(
        attn_grads_kernel,
        grid=(1,),
        in_specs=[full, full, shard(proj), shard(mix), pl.BlockSpec(memory_space=pl.ANY)],
        out_specs=[pl.BlockSpec((width, 4 * part), lambda i: (0, 0))] * count,
        out_shape=[jax.ShapeDtypeStruct((width, 4 * part), LOW)] * count,
        scratch_shapes=[pltpu.VMEM((rows, 3 * part), LOW), pltpu.VMEM((rows, part), LOW)],
        compiler_params=params(),
        cost_estimate=cost(6),
        name="attn_grads",
    )(attn_in.reshape(rows, width), low.reshape(rows, width), proj, mix, after)


def same_video(rows, columns):
    row = lax.broadcasted_iota(jnp.int32, (rows, columns), 0)
    column = lax.broadcasted_iota(jnp.int32, (rows, columns), 1)
    return (row % columns) // VIDEO_FRAMES == column // VIDEO_FRAMES


def message_forward_kernel(
    cls_ref, weight_ref, vec_ref, flat_ref, bias_ref, proj_ref,
    message_ref, normed_ref, inv_ref, in_ref, heads_ref, prob_ref, mix_ref, sum_ref
):
    part = proj_ref.shape[0]
    chunk = cls_ref.shape[0]
    message = mat_mul(cls_ref[...], weight_ref[...]) + vec_ref[4:5]
    message_ref[...] = message
    normed, inv = normalize(message)
    normed_ref[...] = normed
    inv_ref[...] = inv
    msg_in = (normed * vec_ref[5:6] + vec_ref[6:7]).astype(LOW)
    in_ref[...] = msg_in
    proj = mat_mul(msg_in, flat_ref[...])
    queries = (proj[:, :part] + bias_ref[0:1]).astype(LOW)
    keys = proj[:, part : 2 * part].astype(LOW)
    values = (proj[:, 2 * part :] + bias_ref[1:2]).astype(LOW)
    heads_ref[0, 0] = queries
    heads_ref[0, 1] = keys
    heads_ref[0, 2] = values
    masks = head_masks(part)
    scores = mat_nt(stack_heads(queries, masks, HD ** (-0.5)), keys)
    scores = jnp.where(same_video(len(masks) * chunk, chunk), scores, -1e30)
    exps = jnp.exp(scores - jnp.max(scores, axis=-1, keepdims=True))
    prob = exps / jnp.sum(exps, axis=-1, keepdims=True)
    prob_ref[0] = prob
    mix = pick_heads(mat_mul(prob.astype(LOW), values), masks).astype(LOW)
    mix_ref[...] = mix
    sum_ref[...] = mat_mul(mix, proj_ref[...])


def message_forward(chunk, cls_rows, weight, vecs, flat, bias, proj):
    count, width = cls_rows.shape
    part = proj.shape[0]
    heads = part // HD
    chunks = count // chunk
    rows = lambda columns: pl.BlockSpec((chunk, columns), lambda c: (c, 0))
    return pl.pallas_call(
        message_forward_kernel,
        grid=(chunks,),
        in_specs=[rows(width)] + [whole(v) for v in (weight, vecs, flat, bias, proj)],
        out_specs=[
            rows(width), rows(width), rows(1), rows(width),
            per_frame((chunks, 3, chunk, part)), per_frame((chunks, heads * chunk, chunk)),
            rows(part), rows(width),
        ],
        out_shape=[
            jax.ShapeDtypeStruct((count, width), F32),
            jax.ShapeDtypeStruct((count, width), F32),
            jax.ShapeDtypeStruct((count, 1), F32),
            jax.ShapeDtypeStruct((count, width), LOW),
            jax.ShapeDtypeStruct((chunks, 3, chunk, part), LOW),
            jax.ShapeDtypeStruct((chunks, heads * chunk, chunk), F32),
            jax.ShapeDtypeStruct((count, part), LOW),
            jax.ShapeDtypeStruct((count, width), F32),
        ],
        compiler_params=params(),
        cost_estimate=cost(5),
        name="message_forward",
    )(cls_rows, weight, vecs, flat, bias, proj)


def message_backward_kernel(
    grad_ref, in_ref, heads_ref, prob_ref, mix_ref, flat_ref, proj_ref,
    grad_flat_ref, grad_proj_ref, sum_grad_ref, sum_cross_ref, back_ref
):
    @pl.when(pl.program_id(0) == 0)
    def _():
        for ref in (grad_flat_ref, grad_proj_ref, sum_grad_ref, sum_cross_ref):
            ref[...] = jnp.zeros_like(ref)

    part = proj_ref.shape[0]
    chunk = grad_ref.shape[0]
    masks = head_masks(part)
    grad = grad_ref[...].astype(LOW)
    sum_grad_ref[...] += jnp.sum(grad.astype(F32), axis=0, keepdims=True)
    grad_proj_ref[...] += mat_tn(mix_ref[...], grad)
    grad_mix = mat_nt(grad, proj_ref[...]).astype(LOW)
    mix_heads = stack_heads(grad_mix, masks)
    queries, keys, values = heads_ref[0, 0], heads_ref[0, 1], heads_ref[0, 2]
    prob = prob_ref[0]
    grad_prob = mat_nt(mix_heads, values)
    grad_score = prob * (grad_prob - jnp.sum(prob * grad_prob, axis=-1, keepdims=True))
    score_low = grad_score.astype(LOW)
    grad_query = pick_heads(mat_mul(score_low, keys), masks) * HD ** (-0.5)
    grad_key = mat_tn(score_low, stack_heads(queries, masks)) * HD ** (-0.5)
    grad_value = mat_tn(prob.astype(LOW), mix_heads)
    cross = jnp.concatenate([grad_query, grad_key, grad_value], axis=1).astype(LOW)
    sum_cross_ref[...] += jnp.sum(cross.astype(F32), axis=0, keepdims=True)
    grad_flat_ref[...] += mat_tn(in_ref[...], cross)
    back_ref[...] = mat_nt(cross, flat_ref[...])


def message_backward(grad, msg_in, heads, prob, mix, flat, proj):
    count, width = grad.shape
    part = proj.shape[0]
    chunks, _, chunk, _ = heads.shape
    rows = lambda columns: pl.BlockSpec((chunk, columns), lambda c: (c, 0))
    fixed = lambda shape: pl.BlockSpec(shape, lambda c: (0, 0))
    shapes = [(width, 3 * part), (part, width), (1, width), (1, 3 * part)]
    return pl.pallas_call(
        message_backward_kernel,
        grid=(chunks,),
        in_specs=[
            rows(width), rows(width), per_frame(heads.shape), per_frame(prob.shape), rows(part),
            whole(flat), whole(proj),
        ],
        out_specs=[fixed(s) for s in shapes] + [rows(width)],
        out_shape=[jax.ShapeDtypeStruct(s, F32) for s in shapes + [(count, width)]],
        compiler_params=params(),
        cost_estimate=cost(6),
        name="message_backward",
    )(grad, msg_in, heads, prob, mix, flat, proj)


def message_end_kernel(
    grad_ref, back_ref, other_ref, normed_ref, inv_ref, vec_ref, cls_ref, weight_ref, grad_weight_ref,
    sums_ref, grad_cls_ref
):
    @pl.when(pl.program_id(0) == 0)
    def _():
        grad_weight_ref[...] = jnp.zeros_like(grad_weight_ref)
        sums_ref[...] = jnp.zeros_like(sums_ref)

    back = back_ref[...] + other_ref[...]
    normed = normed_ref[...]
    grad = grad_ref[...] + norm_back(back, normed, inv_ref[...], vec_ref[5:6])
    low = grad.astype(LOW)
    for row, values in enumerate((low.astype(F32), back * normed, back)):
        sums_ref[row : row + 1] += jnp.sum(values, axis=0, keepdims=True)
    grad_weight_ref[...] += mat_tn(cls_ref[...], low)
    grad_cls_ref[...] = mat_nt(low, weight_ref[...])


def message_end(chunk, grad, back, other, normed, inv, vecs, cls_rows, weight):
    count, width = grad.shape
    rows = lambda columns: pl.BlockSpec((chunk, columns), lambda c: (c, 0))
    fixed = lambda shape: pl.BlockSpec(shape, lambda c: (0, 0))
    return pl.pallas_call(
        message_end_kernel,
        grid=(count // chunk,),
        in_specs=[rows(width)] * 4 + [rows(1), whole(vecs), rows(width), whole(weight)],
        out_specs=[fixed((width, width)), fixed((8, width)), rows(width)],
        out_shape=[
            jax.ShapeDtypeStruct((width, width), F32),
            jax.ShapeDtypeStruct((8, width), F32),
            jax.ShapeDtypeStruct((count, width), F32),
        ],
        compiler_params=params(),
        cost_estimate=cost(5),
        name="message_end",
    )(grad, back, other, normed, inv, vecs, cls_rows, weight)


def swap(block, axis, flip):
    return lax.ppermute(block, axis, [(i, i ^ flip) for i in range(lax.axis_size(axis))])


def bits_of(size):
    return [1 << b for b in range(size.bit_length() - 1)]


def reorder(parts, index):
    parts = list(parts)
    for bit in bits_of(len(parts)):
        odd = (index & bit) != 0
        parts = [jnp.where(odd, parts[k ^ bit], parts[k]) for k in range(len(parts))]
    return parts


def join(block, other, odd):
    return jnp.concatenate([jnp.where(odd, other, block), jnp.where(odd, block, other)], axis=0)


def gather_all(block, axis):
    index = lax.axis_index(axis)
    for bit in bits_of(lax.axis_size(axis)):
        block = join(block, swap(block, axis, bit), (index & bit) != 0)
    return block


def frames_in(block, count, index, after):
    part = block.shape[0] // count
    begin = zero_of(after)
    pieces = []
    for k in range(count):
        piece = lax.dynamic_slice_in_dim(block, (index ^ k) * part + begin, part, 0)
        pieces.append(piece if k == 0 else swap(piece, "wide", k))
    return pieces


def frames_out(blocks, index, after):
    pieces = []
    begin = zero_of(after)
    for k in range(blocks.shape[0]):
        piece = lax.dynamic_index_in_dim(blocks, (index ^ k) + begin, 0, keepdims=False)
        pieces.append(piece if k == 0 else swap(piece, "wide", k))
    return jnp.concatenate(reorder(pieces, index), axis=0)


def nothing(array):
    one = lax.slice(array, (0,) * array.ndim, (1,) * array.ndim).reshape(()).astype(F32)
    return jnp.minimum(jnp.abs(one), 0.0)


def zero_of(array):
    return nothing(array).astype(jnp.int32)


def send_half(block, after):
    odd = lax.axis_index("narrow") & 1
    half = block.shape[0] // 2
    sent = lax.dynamic_slice_in_dim(block, odd * half + zero_of(after), half, 0)
    return [swap(sent, "wide", bit) for bit in bits_of(lax.axis_size("wide"))[1:]]


def shards_in(block, near, after=None):
    odd = lax.axis_index("narrow") & 1
    far = [swap(half, "narrow", 1) for half in near]
    if after is not None:
        odd = odd + zero_of(after)
    own = [block] + [join(*pair, odd != 0) for pair in zip(near, far)]
    return [piece for shard in own for piece in (shard, swap(shard, "wide", 1))]


def added(terms, start, size):
    total = sum(
        lax.dynamic_slice_in_dim(array, begin + start, size, 0).astype(F32) for array, begin in terms
    )
    return total.astype(LOW)


def reduce_narrow(terms, size):
    index = lax.axis_index("narrow")
    bits = bits_of(lax.axis_size("narrow"))
    groups = [bits[:1]] + [bits[i : i + 2] for i in range(1, len(bits), 2)]
    groups = [(group[0], 1 << len(group)) for group in groups if group]
    for low, count in groups:
        size = size // count
        place = (index // low) % count
        away = [added(terms, (place ^ flip) * size, size) for flip in range(1, count)]
        terms = [(array, begin + place * size) for array, begin in terms]
        terms += [(swap(block, "narrow", (at + 1) * low), 0) for at, block in enumerate(away)]
    block = added(terms, 0, size)
    for low, count in reversed(groups):
        place = (index // low) % count
        blocks = [block] + [swap(block, "narrow", flip * low) for flip in range(1, count)]
        block = jnp.concatenate(reorder(blocks, place), axis=0)
    return block


def reduce_grad(parts, after=None):
    size = parts[0].shape[0]
    terms = {k: [(part, 0)] for k, part in enumerate(parts)}
    for bit in bits_of(len(parts)):
        for k in sorted(terms, reverse=True):
            if k & bit:
                own = terms.pop(k)
                value = own[0][0]
                if len(own) > 1:
                    value = sum(array.astype(F32) for array, _ in own)
                    if after is not None:
                        value = value + nothing(after)
                    value = value.astype(LOW)
                last = swap(value, "wide", bit)
                terms[k ^ bit].append((last, 0))
    return terms[0], last


def body(
    frame_tokens,
    cotangent,
    caption_count,
    caption_len,
    message_weight,
    message_bias,
    message_gain,
    message_shift,
    cross_qkv,
    cross_bias,
    cross_proj,
    cross_offset,
    attn_gain,
    attn_shift,
    qkv_weight,
    qkv_bias,
    out_weight,
    out_bias,
    mlp_gain,
    mlp_shift,
    up_weight,
    up_bias,
    down_weight,
    down_bias,
):
    group_frames, patches, width_part = frame_tokens.shape
    model_width = message_weight.shape[0]
    hidden_part = up_weight.shape[1]
    wide = lax.axis_size("wide")
    narrow = lax.axis_size("narrow")
    wide_idx = lax.axis_index("wide")
    narrow_idx = lax.axis_index("narrow")
    frames = group_frames // wide
    seq_pad = -(-(patches + 1) // ROW_TILE) * ROW_TILE
    rows = frames * seq_pad
    all_frames = group_frames * narrow
    first_group = narrow_idx * group_frames
    first_frame = first_group + wide_idx * frames
    chunk = max(c for c in range(VIDEO_FRAMES, 129, VIDEO_FRAMES) if all_frames % c == 0)

    def own_cols(values):
        return lax.dynamic_slice_in_dim(values, wide_idx * width_part, width_part, values.ndim - 1)

    small_parts = [qkv_bias, up_bias, out_bias, down_bias, frame_tokens[:, 0, :].astype(F32)]
    small = jnp.concatenate([v.reshape(-1) for v in small_parts])
    small = [small] + [swap(small, "wide", k) for k in range(1, wide)]
    at = 0
    gathered = []
    for part in small_parts:
        gathered.append([v[at : at + part.size].reshape(part.shape) for v in small])
        at += part.size
    qkv_biases = jnp.stack(gathered[0])
    up_biases = [v.reshape(1, 1, hidden_part) for v in gathered[1]]
    out_bias_row = jnp.concatenate(reorder(gathered[2], wide_idx)).reshape(1, model_width)
    down_bias_row = jnp.concatenate(reorder(gathered[3], wide_idx)).reshape(1, model_width)
    cls_rows = gather_all(jnp.concatenate(reorder(gathered[4], wide_idx), axis=1).astype(LOW), "narrow")
    tokens = frames_in(frame_tokens, wide, wide_idx, small[-1])
    qkv_own = qkv_weight.reshape(model_width, 3 * width_part)
    qkv = shards_in(qkv_own, send_half(qkv_own, small[-1]))
    out = shards_in(out_weight, send_half(out_weight, small[-1]))
    tokens = jnp.concatenate(reorder(tokens, wide_idx), axis=2)
    vecs = jnp.stack(
        [attn_gain, attn_shift, mlp_gain, mlp_shift, message_bias, message_gain, message_shift, cross_offset]
    )

    caption_slot = jnp.arange(caption_len.shape[1])
    word_total = jnp.sum(
        jnp.where(caption_slot[None, :] < caption_count[:, None], caption_len, 0), axis=1
    ).astype(F32)
    video_scale = word_total / jnp.mean(word_total)
    own_video = (first_frame + jnp.arange(frames)) // VIDEO_FRAMES
    video_match = own_video[:, None] == jnp.arange(video_scale.shape[0])[None, :]
    frame_weight = jnp.sum(jnp.where(video_match, video_scale[None, :], 0.0), axis=1)

    cross_flat = cross_qkv.reshape(model_width, 3 * width_part)
    message, msg_normed, msg_inv, msg_in, cross_heads, cross_prob, cross_mix, cross_sum = message_forward(
        chunk, cls_rows, message_weight, vecs, cross_flat, cross_bias, cross_proj
    )
    message_two = lax.dynamic_slice_in_dim(message, first_frame, frames, 0) + cross_offset
    for k in range(wide):
        piece = lax.dynamic_slice_in_dim(cross_sum, first_group + (wide_idx ^ k) * frames, frames, 0)
        message_two = message_two + (piece if k == 0 else swap(piece, "wide", k))

    up_near = send_half(up_weight, message_two)
    cot_parts = frames_in(cotangent, wide, wide_idx, message_two)
    down_near = send_half(down_weight, message_two)

    (normed, inv, attn_in, heads, prob, mix, hidden_res, mlp_normed, mlp_inv, mlp_in) = attn_forward(
        seq_pad, tokens, message_two.reshape(frames, 1, model_width), vecs, out_bias_row, qkv_biases, qkv, out
    )
    cot = jnp.concatenate(reorder(cot_parts, wide_idx + zero_of(mlp_in)), axis=2)
    down_near = [half + nothing(mlp_in).astype(LOW) for half in down_near]
    grad_rows = jnp.pad(
        (cot.astype(F32) * frame_weight[:, None, None]).astype(LOW),
        ((0, 0), (0, seq_pad - patches), (0, 0)),
    ).reshape(rows, model_width)
    mlp_in = mlp_in.reshape(rows, model_width)
    acc = None
    sum_up, grad_up, grad_down = [], [], []
    near_up = [up_weight, swap(up_weight, "wide", 1)]
    near_down = [down_weight, swap(down_weight, "wide", 1)]
    up, down = near_up, near_down
    for k in range(0, wide, 2):
        if k == 2:
            up = shards_in(up_weight, up_near, acc[0])
            down = shards_in(down_weight, down_near, acc[0])
        shards = range(k, k + 2)
        weights = [w for j in shards for w in (up[j], down[j])]
        done = mlp_step(
            frames, mlp_in, grad_rows, jnp.concatenate([up_biases[j] for j in shards]), weights, acc
        )
        acc = done[:2]
        sum_up += [done[2][j, 0] for j in range(len(shards))]
        grad_up += done[3::2]
        grad_down += done[4::2]
    up_terms, up_last = reduce_grad(grad_up)
    down_terms, down_last = reduce_grad(grad_down)
    grad_up_own = reduce_narrow(up_terms, hidden_part).astype(F32)

    shape = (frames, seq_pad, model_width)
    out_blocks, grad_blocks, grad_msg, proj, low, sum_norm, sum_proj = attn_backward(
        frame_weight, hidden_res, acc[0].reshape(shape), acc[1].reshape(shape), mlp_normed, mlp_inv, cot,
        normed, inv, heads, prob, vecs, down_bias_row, qkv, out,
    )
    grad_attn = []
    after = up_last
    for pair in reversed(range(wide // 2)):
        grad_attn = list(attn_grads(attn_in, proj, low, mix, pair, after)) + grad_attn
        after = grad_attn[0]
    begin = zero_of(after)
    grad_down_own = reduce_narrow([(t, b + begin) for t, b in down_terms], hidden_part).astype(F32)
    attn_terms, attn_last = reduce_grad(grad_attn, down_last)
    half = model_width // 2
    grad_attn = jnp.concatenate(
        [reduce_narrow([(t, b + at) for t, b in attn_terms], half) for at in (0, half)], axis=0
    ).astype(F32)
    output_tokens = frames_out(out_blocks, wide_idx, attn_last)
    grad_tokens = frames_out(grad_blocks, wide_idx, attn_last)

    sums = jnp.concatenate(
        [sum_norm[i] for i in range(6)]
        + reorder(sum_up, wide_idx)
        + reorder([sum_proj[k, 0, :width_part] for k in range(wide)], wide_idx)
        + reorder([sum_proj[k, 0, 2 * width_part :] for k in range(wide)], wide_idx)
    ).reshape(-1, model_width) + nothing(up_last)
    grad_msg = grad_msg.reshape(frames, model_width) + nothing(up_last)
    for axis in ("wide", "narrow"):
        index = lax.axis_index(axis)
        for bit in bits_of(lax.axis_size(axis)):
            other = swap(jnp.concatenate([sums, grad_msg], axis=0), axis, bit)
            sums = sums + other[: sums.shape[0]]
            grad_msg = join(grad_msg, other[sums.shape[0] :], (index & bit) != 0)
    grad_up_bias = lax.dynamic_slice_in_dim(sums[6:-2].reshape(-1), wide_idx * hidden_part, hidden_part, 0)

    grad_cross_flat, grad_cross_proj, sum_cross_grad, sum_cross, back = message_backward(
        grad_msg, msg_in, cross_heads, cross_prob, cross_mix, cross_flat, cross_proj
    )
    bits = bits_of(wide)
    for bit in bits[:-1]:
        back = back + swap(back, "wide", bit)
    grad_message_weight, msg_sums, grad_cls = message_end(
        chunk, grad_msg, back, swap(back, "wide", bits[-1]), msg_normed, msg_inv, vecs, cls_rows, message_weight
    )
    grad_cls = own_cols(lax.dynamic_slice_in_dim(grad_cls, first_group, group_frames, 0))
    grad_tokens = grad_tokens.at[:, 0].set((grad_tokens[:, 0].astype(F32) + grad_cls).astype(LOW))
    grad_cross_bias = jnp.stack([sum_cross[0, :width_part], sum_cross[0, 2 * width_part :]])

    return (
        output_tokens,
        grad_tokens,
        grad_message_weight,
        msg_sums[0],
        msg_sums[1],
        msg_sums[2],
        grad_cross_flat.reshape(model_width, 3, width_part),
        grad_cross_bias,
        grad_cross_proj,
        sum_cross_grad[0],
        sums[4],
        sums[5],
        grad_attn[:, : 3 * width_part].reshape(model_width, 3, width_part),
        own_cols(sums[-2:]),
        grad_attn[:, 3 * width_part :].T,
        own_cols(sums[3]),
        sums[1],
        sums[2],
        grad_up_own,
        grad_up_bias,
        grad_down_own,
        own_cols(sums[0]),
    )


def solution(mesh):
    return jax.shard_map(
        body,
        mesh=mesh,
        in_specs=(
            P("narrow", None, "wide"),
            P("narrow", None, "wide"),
            P(),
            P(),
            P(),
            P(),
            P(),
            P(),
            P(None, None, "wide"),
            P(None, "wide"),
            P("wide", None),
            P(),
            P(),
            P(),
            P(None, None, "wide"),
            P(None, "wide"),
            P("wide", None),
            P("wide"),
            P(),
            P(),
            P(None, "wide"),
            P("wide"),
            P("wide", None),
            P("wide"),
        ),
        out_specs=(
            P("narrow", None, "wide"),
            P("narrow", None, "wide"),
            P(),
            P(),
            P(),
            P(),
            P(None, None, "wide"),
            P(None, "wide"),
            P("wide", None),
            P(),
            P(),
            P(),
            P(None, None, "wide"),
            P(None, "wide"),
            P("wide", None),
            P("wide"),
            P(),
            P(),
            P(None, "wide"),
            P("wide"),
            P("wide", None),
            P("wide"),
        ),
        check_vma=False,
    )
```

```python
import functools
import jax
import jax.numpy as jnp
from jax import lax
from jax.experimental import pallas as pl
from jax.experimental.pallas import tpu as pltpu
from jax.sharding import PartitionSpec as P

VIDEO_FRAMES = 8
HD = 64
EPS = 1e-05
ROW_TILE = 16
LOW = jnp.bfloat16
F32 = jnp.float32
VMEM_LIMIT = 56 * 1024 * 1024
ANY = pl.BlockSpec(memory_space=pl.ANY)
VMEM = pl.BlockSpec(memory_space=pltpu.VMEM)
SMEM = pl.BlockSpec(memory_space=pltpu.SMEM)


def dot(left, right, dims):
    return lax.dot_general(left, right, (dims, ((), ())), preferred_element_type=F32)


def mat_mul(left, right):
    return dot(left, right, ((1,), (0,)))


def mat_tn(left, right):
    return dot(left, right, ((0,), (0,)))


def mat_nt(left, right):
    return dot(left, right, ((1,), (1,)))


def normalize(values):
    row_mean = jnp.mean(values, axis=-1, keepdims=True)
    centred = values - row_mean
    inv_std = lax.rsqrt(jnp.mean(centred * centred, axis=-1, keepdims=True) + EPS)
    return (centred * inv_std, inv_std)


def norm_back(grad_norm, normed, inv_std, norm_gain):
    scaled = grad_norm * norm_gain
    return inv_std * (
        scaled
        - jnp.mean(scaled, axis=-1, keepdims=True)
        - normed * jnp.mean(scaled * normed, axis=-1, keepdims=True)
    )


def bits_of(size):
    return [1 << b for b in range(size.bit_length() - 1)]


def reorder(parts, index):
    parts = list(parts)
    for bit in bits_of(len(parts)):
        odd = (index & bit) != 0
        parts = [jnp.where(odd, parts[k ^ bit], parts[k]) for k in range(len(parts))]
    return parts


def call(kernel, name, micros=0.0, **options):
    return pl.pallas_call(
        kernel,
        name=name,
        compiler_params=pltpu.CompilerParams(vmem_limit_bytes=VMEM_LIMIT),
        cost_estimate=pl.CostEstimate(
            flops=int(micros * 1.0e6), bytes_accessed=int(micros * 1.0e3), transcendentals=0
        ),
        **options,
    )


def shaped(shape, dtype):
    return jax.ShapeDtypeStruct(tuple(shape), dtype)


def whole(array):
    return pl.BlockSpec(array.shape, lambda *_: (0,) * array.ndim)


def fixed(shape):
    return pl.BlockSpec(tuple(shape), lambda *_: (0,) * len(shape))


def per_step(shape):
    return pl.BlockSpec((1,) + tuple(shape[1:]), lambda f: (f,) + (0,) * (len(shape) - 1))


def head_masks(width):
    lane = lax.broadcasted_iota(jnp.int32, (1, width), 1) // HD
    return [lane == h for h in range(width // HD)]


def stack_heads(values, masks, scale=1.0):
    return jnp.concatenate([values * jnp.where(m, scale, 0.0).astype(values.dtype) for m in masks], axis=0)


def pick_heads(values, masks):
    size = values.shape[0] // len(masks)
    picked = values[:size]
    for h in range(1, len(masks)):
        picked = jnp.where(masks[h], values[h * size : (h + 1) * size], picked)
    return picked


def weight_copies(refs, shards, place_ref, buf, sem):
    whole_count = 2 * shards - len(refs)
    odd = place_ref[1]
    copies = []
    for j in range(whole_count):
        copies.append([pltpu.make_async_copy(refs[j], buf.at[j], sem.at[j, 0])])
    rest = refs[whole_count:]
    for i in range(len(rest) // 2):
        half = rest[2 * i].shape[0]
        at = pl.multiple_of(odd * half, half)
        other = pl.multiple_of((1 - odd) * half, half)
        j = whole_count + i
        copies.append([
            pltpu.make_async_copy(rest[2 * i], buf.at[j, pl.ds(at, half)], sem.at[j, 0]),
            pltpu.make_async_copy(rest[2 * i + 1], buf.at[j, pl.ds(other, half)], sem.at[j, 1]),
        ])
    return copies


def start_all(copies):
    for group in copies:
        for copy in group:
            copy.start()


def wait_all(copies):
    for group in copies:
        for copy in group:
            copy.wait()


def attn_forward_kernel(waits, place_ref, vec_ref, base_ref, *refs):
    shards = refs[-3].shape[0]
    toks, refs = refs[:shards], refs[shards:]
    sums, refs = refs[:shards], refs[shards:]
    packs, refs = refs[:shards], refs[shards:]
    weights, refs = refs[: -14 - waits], refs[-14:]
    (normed_ref, inv_ref, attn_in_ref, heads_ref, prob_ref, mix_ref, hidden_ref, mlp_normed_ref,
     mlp_inv_ref, mlp_in_ref, tok_buf, w_buf, w_sem, msg_buf) = refs
    part, patches = toks[0].shape[1], toks[0].shape[2]
    seq_pad, width = normed_ref.shape[1], normed_ref.shape[2]
    frames = pl.num_programs(0)
    frame = pl.program_id(0)
    wide_idx = place_ref[0]
    copies = weight_copies(weights, shards, place_ref, w_buf, w_sem)

    @pl.when(frame == 0)
    def _():
        start_all(copies)
        tok_buf[...] = jnp.zeros_like(tok_buf)
        total = base_ref[...]
        for ref in sums:
            total += ref[...]
        msg_buf[...] = total

    for k in range(shards):
        at = pl.multiple_of((wide_idx ^ k) * part, part)
        tok_buf[pl.ds(at, part), :patches] = toks[k][0]
    tokens = tok_buf[...].T[:seq_pad].astype(F32)
    group = msg_buf[...]
    own = lax.broadcasted_iota(jnp.int32, (group.shape[0], 1), 0) == wide_idx * frames + frame
    message = jnp.sum(jnp.where(own, group, 0.0), axis=0, keepdims=True)
    row = lax.broadcasted_iota(jnp.int32, (seq_pad, 1), 0)
    full = jnp.where(row == patches, message, tokens)
    normed, inv = normalize(full)
    normed_ref[0] = normed
    inv_ref[0] = inv
    gain, shift, mlp_gain, mlp_shift = (vec_ref[i : i + 1] for i in range(4))
    attn_in = (normed * gain + shift).astype(LOW)
    attn_in_ref[0] = attn_in
    masks = head_masks(part)
    live = lax.broadcasted_iota(jnp.int32, (1, seq_pad), 1) <= patches
    total = full + jnp.concatenate(reorder([p[1:2, 2 * part : 3 * part] for p in packs], wide_idx), axis=1)

    @pl.when(frame == 0)
    def _():
        wait_all(copies)

    for k in range(shards):
        proj = mat_nt(attn_in, w_buf[k, : 3 * part])
        queries = (proj[:, :part] + packs[k][1:2, :part]).astype(LOW)
        keys = proj[:, part : 2 * part].astype(LOW)
        values = (proj[:, 2 * part :] + packs[k][1:2, part : 2 * part]).astype(LOW)
        heads_ref[0, k, 0] = queries
        heads_ref[0, k, 1] = keys
        heads_ref[0, k, 2] = values
        scores = mat_nt(stack_heads(queries, masks, HD ** (-0.5)), keys)
        scores = jnp.where(live, scores, -1e30)
        exps = jnp.exp(scores - jnp.max(scores, axis=-1, keepdims=True))
        prob = (exps * (1.0 / jnp.sum(exps, axis=-1, keepdims=True))).astype(LOW)
        prob_ref[0, k] = prob
        mix_low = pick_heads(mat_mul(prob, values), masks).astype(LOW)
        mix_ref[0, k] = mix_low
        total += mat_mul(mix_low, w_buf[k, 3 * part :])
    hidden_ref[0] = total
    mlp_normed, mlp_inv = normalize(total.astype(LOW).astype(F32))
    mlp_normed_ref[0] = mlp_normed
    mlp_inv_ref[0] = mlp_inv
    mlp_in_ref[0] = (mlp_normed * mlp_gain + mlp_shift).astype(LOW)


def attn_forward(seq_pad, place, vecs, base, toks, sums, packs, weights, after):
    frames, part, patches = toks[0].shape
    shards = len(toks)
    width = part * shards
    heads = part // HD
    seq_lanes = -(-seq_pad // 128) * 128
    shapes = [
        ((frames, seq_pad, width), F32),
        ((frames, seq_pad, 1), F32),
        ((frames, seq_pad, width), LOW),
        ((frames, shards, 3, seq_pad, part), LOW),
        ((frames, shards, heads * seq_pad, seq_pad), LOW),
        ((frames, shards, seq_pad, part), LOW),
        ((frames, seq_pad, width), F32),
        ((frames, seq_pad, width), F32),
        ((frames, seq_pad, 1), F32),
        ((frames, seq_pad, width), LOW),
    ]
    return call(
        functools.partial(attn_forward_kernel, len(after)),
        "attn_forward",
        grid=(frames,),
        in_specs=[SMEM, whole(vecs), whole(base)]
        + [per_step(v.shape) for v in toks]
        + [whole(v) for v in list(sums) + list(packs)]
        + [ANY] * (len(weights) + len(after)),
        out_specs=[per_step(s) for s, _ in shapes],
        out_shape=[shaped(s, d) for s, d in shapes],
        scratch_shapes=[
            pltpu.VMEM((width, seq_lanes), LOW),
            pltpu.VMEM((shards, 4 * part, width), LOW),
            pltpu.SemaphoreType.DMA((shards, 2)),
            pltpu.VMEM(base.shape, F32),
        ],
    )(place, vecs, base, *toks, *sums, *packs, *weights, *after)


def mlp_kernel(frames, count, first, place_ref, scale_ref, mlp_in_ref, *refs):
    packs, refs = refs[:count], refs[count:]
    if first:
        shards = 2 * count
        cots, refs = refs[:shards], refs[shards:]
    else:
        (grad_ref, acc_in, gacc_in), refs = refs[:3], refs[3:]
    outs = 3 + 2 * count + (2 if first else 0)
    w_total = len(refs) - outs - 6 - first
    weights, refs = refs[:w_total], refs[w_total:]
    if first:
        (cot_ref, grad_ref), refs = refs[:2], refs[2:]
    acc_ref, gacc_ref, sums_ref = refs[:3]
    g_refs, refs = refs[3 : 3 + 2 * count], refs[3 + 2 * count :]
    w_buf, g_buf, act_buf, pre_buf, in_sem, out_sem = refs[:6]
    rows, width = mlp_in_ref.shape
    hidden = act_buf.shape[1]
    step = rows // frames
    loads = []
    for i in range(count):
        if first:
            for j, ref in ((2 * i, weights[i]), (2 * i + 1, weights[count + i])):
                loads.append([pltpu.make_async_copy(ref, w_buf.at[j], in_sem.at[j, 0])])
        else:
            half = weights[2 * i].shape[0] // 2
            for j in range(2):
                load = []
                for n, odd in enumerate((place_ref[1], 1 - place_ref[1])):
                    to = w_buf.at[2 * i + j, pl.ds(pl.multiple_of(odd * half, half), half)]
                    load.append(
                        pltpu.make_async_copy(weights[2 * i + n].at[pl.ds(j * half, half)], to, in_sem.at[2 * i + j, n])
                    )
                loads.append(load)
    start_all(loads)
    stores = [pltpu.make_async_copy(g_buf.at[j], g_refs[j], out_sem.at[j]) for j in range(2 * count)]
    if first:
        cot_buf = refs[6]
        cot_buf[...] = jnp.zeros_like(cot_buf)
        part, patches = cots[0].shape[1:]
        for f in range(frames):
            for k in range(shards):
                at = pl.multiple_of((place_ref[0] ^ k) * part, part)
                cot_buf[pl.ds(at, part), :patches] = cots[k][f]
            cot = cot_buf[...].T[:step]
            cot_ref[f] = cot
            grad_ref[f * step : (f + 1) * step] = (cot.astype(F32) * scale_ref[f]).astype(LOW)
    for i in range(count):
        up, down = 2 * i, 2 * i + 1
        wait_all(loads[up : down + 1])
        bias = packs[i][0:1]
        total = jnp.zeros((1, hidden), F32)
        for f in range(frames):
            at = slice(f * step, (f + 1) * step)
            pre = mat_mul(mlp_in_ref[at], w_buf[up]) + bias
            sig = 0.5 + 0.5 * jnp.tanh(0.851 * pre)
            act = (pre * sig).astype(LOW)
            act_buf[at] = act
            grad_act = mat_nt(grad_ref[at], w_buf[down])
            grad_pre = (grad_act * (sig + 1.702 * pre * sig * (1.0 - sig))).astype(LOW)
            pre_buf[at] = grad_pre
            total += jnp.sum(grad_pre.astype(F32), axis=0, keepdims=True)
            out = mat_mul(act, w_buf[down])
            back = mat_nt(grad_pre, w_buf[up])
            if i > 0:
                acc_ref[at] += out
                gacc_ref[at] += back
            elif first:
                acc_ref[at] = out
                gacc_ref[at] = back
            else:
                acc_ref[at] = acc_in[at] + out
                gacc_ref[at] = gacc_in[at] + back
        sums_ref[i] = total
        for c in range(0, width, 256):
            g_buf[up, c : c + 256] = mat_tn(mlp_in_ref[:, c : c + 256], pre_buf[...]).astype(LOW)
        stores[up].start()
        for c in range(0, hidden, 256):
            g_buf[down, c : c + 256] = mat_tn(act_buf[:, c : c + 256], grad_ref[...]).astype(LOW)
        stores[down].start()
    for store in stores:
        store.wait()


def mlp_step(frames, place, scale, mlp_in, packs, ups, downs, cots=None, carried=None):
    rows, width = mlp_in.shape
    count = len(packs)
    first = cots is not None
    hidden = packs[0].shape[1]
    step = rows // frames
    ins = [place, scale, mlp_in, *packs, *(cots if first else carried), *ups, *downs]
    shapes = [shaped((frames, step, width), LOW), shaped((rows, width), LOW)] if first else []
    shapes += [shaped((rows, width), F32)] * 2 + [shaped((count, 1, hidden), F32)]
    grads = [shaped((width, hidden), LOW), shaped((hidden, width), LOW)] * count
    scratch = [
        pltpu.VMEM((2 * count, width, hidden), LOW),
        pltpu.VMEM((2 * count, width, hidden), LOW),
        pltpu.VMEM((rows, hidden), LOW),
        pltpu.VMEM((rows, hidden), LOW),
        pltpu.SemaphoreType.DMA((2 * count, 2)),
        pltpu.SemaphoreType.DMA((2 * count,)),
    ]
    if first:
        scratch.append(pltpu.VMEM((width, -(-step // 128) * 128), LOW))
    return call(
        functools.partial(mlp_kernel, frames, count, first),
        "mlp",
        in_specs=[SMEM, SMEM, VMEM] + [VMEM] * (len(ins) - 3 - len(ups) - len(downs)) + [ANY] * (len(ups) + len(downs)),
        out_specs=[VMEM] * len(shapes) + [ANY] * len(grads),
        out_shape=shapes + grads,
        scratch_shapes=scratch,
    )(*ins)


def attn_backward_kernel(
    shards, place_ref, scale_ref, vec_ref, res_ref, acc_ref, gacc_ref, mlp_normed_ref, mlp_inv_ref, cot_ref,
    normed_ref, inv_ref, heads_ref, prob_ref, *refs
):
    packs, refs = refs[:shards], refs[shards:]
    ups, refs = refs[: shards // 2], refs[shards // 2 :]
    outs = 2 * shards + 3 + 2
    weights, refs = refs[: len(refs) - outs], refs[len(refs) - outs :]
    toks, grad_toks, refs = refs[:shards], refs[shards : 2 * shards], refs[2 * shards :]
    proj_ref, low_ref, sums_ref, w_buf, w_sem = refs
    part = heads_ref.shape[4]
    patches = toks[0].shape[2]
    seq_pad, width = res_ref.shape[1:]
    gain, mlp_gain = vec_ref[0:1], vec_ref[2:3]
    frame = pl.program_id(0)
    wide_idx = place_ref[0]
    copies = weight_copies(weights, shards, place_ref, w_buf, w_sem)

    @pl.when(frame == 0)
    def _():
        start_all(copies)
        sums_ref[...] = jnp.zeros_like(sums_ref)
        rows = [ref[i] for ref in ups for i in range(2)]
        for k, values in enumerate(reorder(rows, wide_idx)):
            sums_ref[6 + k] = values

    def columns(values, out_refs):
        blocks = values.T
        blocks = reorder([blocks[j * part : (j + 1) * part, :patches] for j in range(shards)], wide_idx)
        for ref, block in zip(out_refs, blocks):
            ref[0] = block

    down_bias = jnp.concatenate(reorder([p[1:2, 3 * part : 4 * part] for p in packs], wide_idx), axis=1)
    columns((res_ref[0] + acc_ref[0] + down_bias).astype(LOW), toks)
    grad_res = cot_ref[0].astype(F32) * scale_ref[frame]
    gacc, mlp_normed = gacc_ref[0], mlp_normed_ref[0]
    hidden = grad_res + norm_back(gacc, mlp_normed, mlp_inv_ref[0], mlp_gain)

    def add_sum(row, values):
        sums_ref[row] += jnp.sum(values, axis=0, keepdims=True)

    add_sum(0, grad_res)
    add_sum(1, gacc * mlp_normed)
    add_sum(2, gacc)
    add_sum(3, hidden)
    low = hidden.astype(LOW)
    low_ref[0] = low
    masks = head_masks(part)
    scale = HD ** (-0.5)
    back = jnp.zeros(hidden.shape, F32)
    bias_sums = []

    @pl.when(frame == 0)
    def _():
        wait_all(copies)

    for k in range(shards):
        grad_mix = mat_nt(low, w_buf[k, 3 * part :]).astype(LOW)
        queries, keys, values = heads_ref[0, k, 0], heads_ref[0, k, 1], heads_ref[0, k, 2]
        prob_low = prob_ref[0, k]
        prob = prob_low.astype(F32)
        mix_heads = stack_heads(grad_mix, masks)
        grad_value = mat_tn(prob_low, mix_heads)
        grad_prob = mat_nt(mix_heads, values)
        grad_score = (
            prob * (grad_prob - jnp.sum(prob * grad_prob, axis=-1, keepdims=True))
        ).astype(LOW)
        grad_query = pick_heads(mat_mul(grad_score, keys), masks)
        grad_key = mat_tn(grad_score, stack_heads(queries, masks))
        proj = jnp.concatenate([grad_query * scale, grad_key * scale, grad_value], axis=1).astype(LOW)
        proj_ref[0, k] = proj
        bias_sums.append(jnp.sum(proj.astype(F32), axis=0, keepdims=True))
        back += mat_mul(proj, w_buf[k, : 3 * part])
    for i, at in ((6 + shards, 0), (7 + shards, 2 * part)):
        own = reorder([values[:, at : at + part] for values in bias_sums], wide_idx)
        sums_ref[i] += jnp.concatenate(own, axis=1)
    normed = normed_ref[0]
    add_sum(4, back * normed)
    add_sum(5, back)
    total = hidden + norm_back(back, normed, inv_ref[0], gain)
    row = lax.broadcasted_iota(jnp.int32, (seq_pad, 1), 0)
    sums_ref[8 + shards + frame] = jnp.sum(jnp.where(row == patches, total, 0.0), axis=0, keepdims=True)
    columns(total.astype(LOW), grad_toks)


def attn_backward(patches, place, scale, vecs, per_frame, packs, ups, weights):
    frames, seq_pad, width = per_frame[0].shape
    heads = per_frame[8]
    shards, part = heads.shape[1], heads.shape[4]
    blocks = [(frames, part, patches)] * (2 * shards)
    proj = (frames, shards, seq_pad, 3 * part)
    return call(
        functools.partial(attn_backward_kernel, shards),
        "attn_backward",
        grid=(frames,),
        in_specs=[SMEM, SMEM, whole(vecs)]
        + [per_step(v.shape) for v in per_frame]
        + [whole(v) for v in list(packs) + list(ups)]
        + [ANY] * len(weights),
        out_specs=[per_step(b) for b in blocks]
        + [per_step(proj), per_step((frames, seq_pad, width)), fixed((8 + shards + frames, 1, width))],
        out_shape=[shaped(b, LOW) for b in blocks]
        + [
            shaped(proj, LOW),
            shaped((frames, seq_pad, width), LOW),
            shaped((8 + shards + frames, 1, width), F32),
        ],
        scratch_shapes=[
            pltpu.VMEM((shards, 4 * part, width), LOW),
            pltpu.SemaphoreType.DMA((shards, 2)),
        ],
    )(place, scale, vecs, *per_frame, *packs, *ups, *weights)


def attn_grads_kernel(waits, attn_in_ref, low_ref, proj_ref, mix_ref, *refs):
    grad_refs, (proj_buf, mix_buf) = refs[waits:-2], refs[-2:]
    count = len(grad_refs)
    frames, seq_pad, part = mix_ref.shape[0], mix_ref.shape[2], mix_ref.shape[3]
    for i in range(count):
        for f in range(frames):
            at = slice(f * seq_pad, (f + 1) * seq_pad)
            proj_buf[at] = proj_ref[f, i]
            mix_buf[at] = mix_ref[f, i]
        for c in range(0, 3 * part, part):
            grad_refs[i][c : c + part] = mat_tn(proj_buf[:, c : c + part], attn_in_ref[...]).astype(LOW)
        grad_refs[i][3 * part :] = mat_tn(mix_buf[...], low_ref[...]).astype(LOW)


def attn_grads(attn_in, proj, low, mix, pair, after):
    frames, shards, seq_pad, part = mix.shape
    width = attn_in.shape[-1]
    rows = frames * seq_pad
    count = min(2, shards)

    def shard(array):
        return pl.BlockSpec((frames, count) + array.shape[2:], lambda i: (0, pair, 0, 0))

    return call(
        functools.partial(attn_grads_kernel, len(after)),
        "attn_grads",
        grid=(1,),
        in_specs=[fixed((rows, width)), fixed((rows, width)), shard(proj), shard(mix)] + [ANY] * len(after),
        out_specs=[fixed((4 * part, width))] * count,
        out_shape=[shaped((4 * part, width), LOW)] * count,
        scratch_shapes=[pltpu.VMEM((rows, 3 * part), LOW), pltpu.VMEM((rows, part), LOW)],
    )(attn_in.reshape(rows, width), low.reshape(rows, width), proj, mix, *after)


def same_video(place_ref, group, rows, columns):
    first = pl.program_id(0) * columns

    def video(position):
        position = position + first
        return (((position // group) ^ place_ref[2]) * group + position % group) // VIDEO_FRAMES

    row = lax.broadcasted_iota(jnp.int32, (rows, columns), 0) % columns
    column = lax.broadcasted_iota(jnp.int32, (rows, columns), 1)
    return video(row) == video(column)


def message_forward_kernel(
    group, waits, place_ref, cls_ref, weight_ref, vec_ref, flat_ref, bias_ref, proj_ref, *refs
):
    normed_ref, inv_ref, in_ref, heads_ref, prob_ref, mix_ref, base_ref, sum_ref = refs[waits:]
    part = proj_ref.shape[0]
    chunk = cls_ref.shape[0]
    message = mat_mul(cls_ref[...], weight_ref[...]) + vec_ref[4:5]
    normed, inv = normalize(message)
    normed_ref[...] = normed
    inv_ref[...] = inv
    msg_in = (normed * vec_ref[5:6] + vec_ref[6:7]).astype(LOW)
    in_ref[...] = msg_in
    proj = mat_nt(msg_in, flat_ref[...])
    queries = (proj[:, :part] + bias_ref[0:1]).astype(LOW)
    keys = proj[:, part : 2 * part].astype(LOW)
    values = (proj[:, 2 * part :] + bias_ref[1:2]).astype(LOW)
    heads_ref[0, 0] = queries
    heads_ref[0, 1] = keys
    heads_ref[0, 2] = values
    masks = head_masks(part)
    scores = mat_nt(stack_heads(queries, masks, HD ** (-0.5)), keys)
    scores = jnp.where(same_video(place_ref, group, len(masks) * chunk, chunk), scores, -1e30)
    exps = jnp.exp(scores - jnp.max(scores, axis=-1, keepdims=True))
    prob = exps / jnp.sum(exps, axis=-1, keepdims=True)
    prob_ref[0] = prob
    mix = pick_heads(mat_mul(prob.astype(LOW), values), masks).astype(LOW)
    mix_ref[...] = mix

    @pl.when(pl.program_id(0) == 0)
    def _():
        base_ref[...] = message[:group] + vec_ref[7:8]
        sum_ref[...] = mat_mul(mix, proj_ref[...])[:group]


def message_forward(chunk, group, place, cls_rows, weight, vecs, flat, bias, proj, after):
    count, width = cls_rows.shape
    part = proj.shape[0]
    heads = part // HD
    chunks = count // chunk
    rows = lambda columns: pl.BlockSpec((chunk, columns), lambda c: (c, 0))
    return call(
        functools.partial(message_forward_kernel, group, len(after)),
        "message_forward",
        grid=(chunks,),
        in_specs=[SMEM, rows(width)]
        + [whole(v) for v in (weight, vecs, flat, bias, proj)]
        + [ANY] * len(after),
        out_specs=[
            rows(width), rows(1), rows(width),
            per_step((chunks, 3, chunk, part)), per_step((chunks, heads * chunk, chunk)),
            rows(part), fixed((group, width)), fixed((group, width)),
        ],
        out_shape=[
            shaped((count, width), F32),
            shaped((count, 1), F32),
            shaped((count, width), LOW),
            shaped((chunks, 3, chunk, part), LOW),
            shaped((chunks, heads * chunk, chunk), F32),
            shaped((count, part), LOW),
            shaped((group, width), F32),
            shaped((group, width), F32),
        ],
    )(place, cls_rows, weight, vecs, flat, bias, proj, *after)


def message_backward_kernel(
    waits, grad_ref, in_ref, heads_ref, prob_ref, mix_ref, flat_ref, proj_ref, *refs
):
    grad_flat_ref, grad_proj_ref, sum_grad_ref, sum_cross_ref, back_ref = refs[waits:]

    @pl.when(pl.program_id(0) == 0)
    def _():
        for ref in (grad_flat_ref, grad_proj_ref, sum_grad_ref, sum_cross_ref):
            ref[...] = jnp.zeros_like(ref)

    part = proj_ref.shape[0]
    masks = head_masks(part)
    grad = grad_ref[:, 0].astype(LOW)
    sum_grad_ref[...] += jnp.sum(grad.astype(F32), axis=0, keepdims=True)
    grad_proj_ref[...] += mat_tn(mix_ref[...], grad)
    grad_mix = mat_nt(grad, proj_ref[...]).astype(LOW)
    mix_heads = stack_heads(grad_mix, masks)
    queries, keys, values = heads_ref[0, 0], heads_ref[0, 1], heads_ref[0, 2]
    prob = prob_ref[0]
    grad_prob = mat_nt(mix_heads, values)
    grad_score = prob * (grad_prob - jnp.sum(prob * grad_prob, axis=-1, keepdims=True))
    score_low = grad_score.astype(LOW)
    grad_query = pick_heads(mat_mul(score_low, keys), masks) * HD ** (-0.5)
    grad_key = mat_tn(score_low, stack_heads(queries, masks)) * HD ** (-0.5)
    grad_value = mat_tn(prob.astype(LOW), mix_heads)
    cross = jnp.concatenate([grad_query, grad_key, grad_value], axis=1).astype(LOW)
    sum_cross_ref[...] += jnp.sum(cross.astype(F32), axis=0, keepdims=True)
    grad_flat_ref[...] += mat_tn(cross, in_ref[...])
    back_ref[...] = mat_mul(cross, flat_ref[...])


def message_backward(grad, msg_in, heads, prob, mix, flat, proj, after):
    count, _, width = grad.shape
    part = proj.shape[0]
    chunks, _, chunk, _ = heads.shape
    rows = lambda columns: pl.BlockSpec((chunk, columns), lambda c: (c, 0))
    shapes = [(3 * part, width), (part, width), (1, width), (1, 3 * part)]
    return call(
        functools.partial(message_backward_kernel, len(after)),
        "message_backward",
        grid=(chunks,),
        in_specs=[
            pl.BlockSpec((chunk, 1, width), lambda c: (c, 0, 0)),
            rows(width), per_step(heads.shape), per_step(prob.shape), rows(part), whole(flat), whole(proj),
        ]
        + [ANY] * len(after),
        out_specs=[fixed(s) for s in shapes] + [rows(width)],
        out_shape=[shaped(s, F32) for s in shapes + [(count, width)]],
    )(grad, msg_in, heads, prob, mix, flat, proj, *after)


def message_end_kernel(
    group, passed, grad_ref, back_ref, other_ref, normed_ref, inv_ref, vec_ref, cls_ref, weight_ref, *refs
):
    grad_weight_ref, sums_ref, grad_cls_ref = refs[passed : passed + 3]

    @pl.when(pl.program_id(0) == 0)
    def _():
        grad_weight_ref[...] = jnp.zeros_like(grad_weight_ref)
        sums_ref[...] = jnp.zeros_like(sums_ref)

    back = back_ref[...] + other_ref[...].astype(F32)
    normed = normed_ref[...]
    grad = grad_ref[:, 0] + norm_back(back, normed, inv_ref[...], vec_ref[5:6])
    low = grad.astype(LOW)
    for row, values in enumerate((low.astype(F32), back * normed, back)):
        sums_ref[row : row + 1] += jnp.sum(values, axis=0, keepdims=True)
    grad_weight_ref[...] += mat_tn(cls_ref[...], low)

    @pl.when(pl.program_id(0) == 0)
    def _():
        grad_cls_ref[...] = mat_nt(weight_ref[...], low)[:, :group]


def message_end(chunk, group, grad, back, other, normed, inv, vecs, cls_rows, weight, passed):
    count, _, width = grad.shape
    rows = lambda columns: pl.BlockSpec((chunk, columns), lambda c: (c, 0))
    return call(
        functools.partial(message_end_kernel, group, len(passed)),
        "message_end",
        grid=(count // chunk,),
        in_specs=[pl.BlockSpec((chunk, 1, width), lambda c: (c, 0, 0))] + [rows(width)] * 3 + [rows(1), whole(vecs), rows(width), whole(weight)]
        + [ANY] * len(passed),
        out_specs=[fixed((width, width)), fixed((8, width)), fixed((width, group))] + [ANY] * len(passed),
        out_shape=[shaped((width, width), F32), shaped((8, width), F32), shaped((width, group), F32)]
        + [shaped(v.shape, v.dtype) for v in passed],
        input_output_aliases={8 + i: 3 + i for i in range(len(passed))},
    )(grad, back, other, normed, inv, vecs, cls_rows, weight, *passed)


def collect_kernel(place_ref, *refs):
    *pieces, grad_cls_ref, out_ref = refs
    frames, part, patches = pieces[0].shape
    own = grad_cls_ref[pl.ds(pl.multiple_of(place_ref[0] * part, part), part), :]
    lane = lax.broadcasted_iota(jnp.int32, (part, patches), 1)
    for j, piece in enumerate(reorder([ref[...] for ref in pieces], place_ref[0])):
        for f in range(frames):
            i = j * frames + f
            out_ref[i] = jnp.where(lane == 0, piece[f].astype(F32) + own[:, i : i + 1], piece[f].astype(F32)).astype(LOW)


def collect(place, pieces, grad_cls):
    frames, part, patches = pieces[0].shape
    shape = (frames * len(pieces), part, patches)
    return call(
        collect_kernel,
        "collect",
        in_specs=[SMEM] + [VMEM] * (len(pieces) + 1),
        out_specs=VMEM,
        out_shape=shaped(shape, LOW),
    )(place, *pieces, grad_cls)


def swap(block, axis, flip):
    return lax.ppermute(block, axis, [(i, i ^ flip) for i in range(lax.axis_size(axis))])


def nothing(array):
    one = lax.slice(array, (0,) * array.ndim, (1,) * array.ndim).reshape(()).astype(F32)
    return one * 0.0


def zero_of(array):
    return nothing(array).astype(jnp.int32)


def frames_in(block, after):
    count = lax.axis_size("wide")
    index = lax.axis_index("wide")
    part = block.shape[0] // count
    begin = zero_of(after)
    pieces = [lax.dynamic_slice_in_dim(block, (index ^ k) * part + begin, part, 0) for k in range(count)]
    return [piece if k == 0 else swap(piece, "wide", k) for k, piece in enumerate(pieces)]


def send_half(block, after):
    odd = lax.axis_index("narrow") & 1
    half = block.shape[0] // 2
    sent = lax.dynamic_slice_in_dim(block, odd * half + zero_of(after), half, 0)
    return [swap(sent, "wide", bit) for bit in bits_of(lax.axis_size("wide"))[1:]]


def near_shards(block):
    return [block, swap(block, "wide", 1)]


def far_shards(near, far):
    return [near, far, swap(near, "wide", 1), swap(far, "wide", 1)]


def added(terms, start, size):
    total = sum(
        lax.dynamic_slice_in_dim(array, begin + start, size, 0).astype(F32) for array, begin in terms
    )
    return total.astype(LOW)


def narrow_groups():
    return [(bit, 2) for bit in bits_of(lax.axis_size("narrow"))]


def split_sum(terms, size, group, after=None):
    low, count = group
    begin = 0 if after is None else zero_of(after)
    size = size // count
    place = (lax.axis_index("narrow") // low) % count
    away = [added(terms, (place ^ flip) * size + begin, size) for flip in range(1, count)]
    terms = [(array, start + place * size) for array, start in terms]
    return terms + [(swap(block, "narrow", (at + 1) * low), 0) for at, block in enumerate(away)], size


def join_parts(block, group, after=None):
    odd = lax.axis_index("narrow") & group[0]
    if after is not None:
        odd = odd + zero_of(after)
    other = swap(block, "narrow", group[0])
    return jnp.where(
        odd != 0, jnp.concatenate([other, block], axis=0), jnp.concatenate([block, other], axis=0)
    )


def finish_sum(terms, size, after=None, join_after=None):
    groups = narrow_groups()
    for group in groups[1:]:
        terms, size = split_sum(terms, size, group, after)
    block = added(terms, 0, size)
    for group in reversed(groups):
        block = join_parts(block, group, join_after if group[0] != 1 else None)
    return block


def reduce_wide(parts, after=None):
    terms = {k: [part] for k, part in enumerate(parts)}
    for bit in bits_of(len(parts)):
        for k in sorted(terms, reverse=True):
            if k & bit:
                own = terms.pop(k)
                value = own[0]
                if len(own) > 1:
                    value = sum(array.astype(F32) for array in own)
                    if after is not None:
                        value = value + nothing(after)
                    value = value.astype(LOW)
                last = swap(value, "wide", bit)
                terms[k ^ bit].append(last)
    return terms[0], value, last


def body(
    frame_tokens,
    cotangent,
    caption_count,
    caption_len,
    message_weight,
    message_bias,
    message_gain,
    message_shift,
    cross_qkv,
    cross_bias,
    cross_proj,
    cross_offset,
    attn_gain,
    attn_shift,
    qkv_weight,
    qkv_bias,
    out_weight,
    out_bias,
    mlp_gain,
    mlp_shift,
    up_weight,
    up_bias,
    down_weight,
    down_bias,
):
    group, patches, part = frame_tokens.shape
    width = message_weight.shape[0]
    hidden = up_weight.shape[1]
    wide = lax.axis_size("wide")
    narrow = lax.axis_size("narrow")
    wide_idx = lax.axis_index("wide")
    narrow_idx = lax.axis_index("narrow")
    frames = group // wide
    seq_pad = -(-(patches + 1) // ROW_TILE) * ROW_TILE
    rows = frames * seq_pad
    all_frames = group * narrow
    chunk = max(c for c in range(VIDEO_FRAMES, 129, VIDEO_FRAMES) if all_frames % c == 0 and c % group == 0)
    place = jnp.stack([wide_idx, narrow_idx & 1, narrow_idx]).astype(jnp.int32)

    def own_cols(values):
        return lax.dynamic_slice_in_dim(values, wide_idx * part, part, values.ndim - 1)

    tokens_t = frame_tokens.transpose(0, 2, 1)
    pack = jnp.concatenate(
        [up_bias, qkv_bias.reshape(-1), out_bias, down_bias, frame_tokens[:, 0, :].astype(F32).reshape(-1)]
    ).reshape(-1, width)
    packs = [pack] + [swap(pack, "wide", k) for k in range(1, wide)]
    cls_rows = jnp.concatenate(
        reorder([p[2:].reshape(group, part).astype(LOW) for p in packs], wide_idx), axis=1
    )
    for bit in bits_of(narrow):
        cls_rows = jnp.concatenate([cls_rows, swap(cls_rows, "narrow", bit)], axis=0)
    vecs = jnp.stack(
        [attn_gain, attn_shift, mlp_gain, mlp_shift, message_bias, message_gain, message_shift, cross_offset]
    )

    toks = frames_in(tokens_t, packs[-1])
    attn_own = jnp.concatenate(
        [qkv_weight.transpose(1, 2, 0).reshape(3 * part, width), out_weight], axis=0
    )
    attn_weights = near_shards(attn_own)
    attn_near = send_half(attn_own, packs[-1])
    attn_far = [swap(near, "narrow", 1) for near in attn_near]
    for near, far in zip(attn_near, attn_far):
        attn_weights += far_shards(near, far)

    caption_slot = jnp.arange(caption_len.shape[1])
    word_total = jnp.sum(
        jnp.where(caption_slot[None, :] < caption_count[:, None], caption_len, 0), axis=1
    ).astype(F32)
    video_scale = word_total / jnp.mean(word_total)
    own_video = (narrow_idx * group + wide_idx * frames + jnp.arange(frames)) // VIDEO_FRAMES
    video_match = own_video[:, None] == jnp.arange(video_scale.shape[0])[None, :]
    scale = jnp.sum(jnp.where(video_match, video_scale[None, :], 0.0), axis=1)

    cross_flat = cross_qkv.transpose(1, 2, 0).reshape(3 * part, width)
    msg_normed, msg_inv, msg_in, cross_heads, cross_prob, cross_mix, base, group_sum = message_forward(
        chunk, group, place, cls_rows, message_weight, vecs, cross_flat, cross_bias, cross_proj,
        toks[1:] + attn_far,
    )
    group_sums = [group_sum] + [swap(group_sum, "wide", k) for k in range(1, wide)]

    cots = frames_in(cotangent.transpose(0, 2, 1), attn_near[0])
    odd, begin = narrow_idx & 1, zero_of(cots[-1])
    half = width // 2
    mlp_half = jnp.concatenate(
        [lax.dynamic_slice_in_dim(w, odd * half + begin, half, 0) for w in (up_weight, down_weight)], axis=0
    )
    mlp_near = [swap(mlp_half, "wide", bit) for bit in bits_of(wide)[1:]]
    up_shards, down_shards = near_shards(up_weight), near_shards(down_weight)

    (normed, inv, attn_in, heads, prob, mix, hidden_res, mlp_normed, mlp_inv, mlp_in) = attn_forward(
        seq_pad, place, vecs, base, toks, group_sums, packs, attn_weights,
        [up_shards[1], down_shards[1]] + cots[1:],
    )
    mlp_in = mlp_in.reshape(rows, width)
    cot, grad_rows, acc, gacc, *done = mlp_step(
        frames, place, scale, mlp_in, packs[:2], up_shards, down_shards, cots=cots
    )
    sum_up, grad_up, grad_down = [done[0]], done[1::2], done[2::2]
    mlp_near = [near + nothing(mlp_in).astype(LOW) for near in mlp_near]
    mlp_far = [swap(near, "narrow", 1) + nothing(acc).astype(LOW) for near in mlp_near]
    mlp_weights = [piece for near, far in zip(mlp_near, mlp_far) for piece in far_shards(near, far)]
    acc, gacc, *done = mlp_step(
        frames, place, scale, mlp_in, packs[2:], mlp_weights, [], carried=(grad_rows, acc, gacc)
    )
    sum_up, grad_up, grad_down = sum_up + [done[0]], grad_up + done[1::2], grad_down + done[2::2]
    up_terms, _, up_last = reduce_wide(grad_up)
    down_terms, _, down_last = reduce_wide(grad_down)

    shape = (frames, seq_pad, width)
    per_frame = (
        hidden_res, acc.reshape(shape), gacc.reshape(shape), mlp_normed, mlp_inv, cot, normed, inv, heads, prob
    )
    *blocks, proj, low, sums = attn_backward(patches, place, scale, vecs, per_frame, packs, sum_up, attn_weights)
    first = narrow_groups()[0]
    up_part = split_sum([(term, 0) for term in up_terms], width, first)
    grad_attn = list(attn_grads(attn_in, proj, low, mix, 1, [up_last]))
    grad_attn = list(attn_grads(attn_in, proj, low, mix, 0, [grad_attn[0], down_last])) + grad_attn
    attn_terms, attn_sent, attn_last = reduce_wide(grad_attn)
    down_part = split_sum([(term, 0) for term in down_terms], hidden, first, attn_sent)
    grad_up_own = finish_sum(*up_part, None, attn_last).astype(F32)
    grad_down_own = finish_sum(*down_part, attn_last).astype(F32)
    half = 2 * part
    grad_attn_own = jnp.concatenate(
        [
            finish_sum(*split_sum([(term, at) for term in attn_terms], half, first, attn_last))
            for at in (0, half)
        ],
        axis=0,
    ).astype(F32)

    sums = sums + nothing(up_last)
    count = 8 + wide
    others = [sums] + [swap(sums, "wide", k) for k in range(1, wide)]
    sums = sum(o[:count] for o in others)
    grad_msg = jnp.concatenate(reorder([o[count:] for o in others], wide_idx), axis=0)
    for bit in bits_of(narrow):
        other = swap(jnp.concatenate([sums, grad_msg], axis=0), "narrow", bit)
        sums = sums + other[:count]
        grad_msg = jnp.concatenate([grad_msg, other[count:]], axis=0)
    sums = sums.reshape(count, width)
    grad_up_bias = lax.dynamic_slice_in_dim(sums[6 : 6 + wide].reshape(-1), wide_idx * hidden, hidden, 0)

    grad_cross_flat, grad_cross_proj, sum_cross_grad, sum_cross, back = message_backward(
        grad_msg, msg_in, cross_heads, cross_prob, cross_mix, cross_flat, cross_proj, [attn_last]
    )
    bits = bits_of(wide)
    for bit in bits[:-1]:
        back = back + swap(back, "wide", bit)
    grad_message_weight, msg_sums, grad_cls, *blocks = message_end(
        chunk, group, grad_msg, back, swap(back.astype(LOW), "wide", bits[-1]), msg_normed, msg_inv, vecs, cls_rows,
        message_weight, blocks,
    )

    def frames_out(pieces):
        return [piece if k == 0 else swap(piece, "wide", k) for k, piece in enumerate(pieces)]

    out_pieces = frames_out(blocks[:wide])
    grad_pieces = frames_out(blocks[wide:])
    output_tokens = jnp.concatenate(reorder(out_pieces, wide_idx), axis=0)
    grad_tokens = collect(place, grad_pieces, grad_cls)

    return (
        output_tokens.transpose(0, 2, 1),
        grad_tokens.transpose(0, 2, 1),
        grad_message_weight,
        msg_sums[0],
        msg_sums[1],
        msg_sums[2],
        grad_cross_flat.reshape(3, part, width).transpose(2, 0, 1),
        jnp.stack([sum_cross[0, :part], sum_cross[0, 2 * part :]]),
        grad_cross_proj,
        sum_cross_grad[0],
        sums[4],
        sums[5],
        grad_attn_own[: 3 * part].reshape(3, part, width).transpose(2, 0, 1),
        own_cols(sums[count - 2 :]),
        grad_attn_own[3 * part :],
        own_cols(sums[3]),
        sums[1],
        sums[2],
        grad_up_own,
        grad_up_bias,
        grad_down_own,
        own_cols(sums[0]),
    )


def solution(mesh):
    return jax.shard_map(
        body,
        mesh=mesh,
        in_specs=(
            P("narrow", None, "wide"),
            P("narrow", None, "wide"),
            P(),
            P(),
            P(),
            P(),
            P(),
            P(),
            P(None, None, "wide"),
            P(None, "wide"),
            P("wide", None),
            P(),
            P(),
            P(),
            P(None, None, "wide"),
            P(None, "wide"),
            P("wide", None),
            P("wide"),
            P(),
            P(),
            P(None, "wide"),
            P("wide"),
            P("wide", None),
            P("wide"),
        ),
        out_specs=(
            P("narrow", None, "wide"),
            P("narrow", None, "wide"),
            P(),
            P(),
            P(),
            P(),
            P(None, None, "wide"),
            P(None, "wide"),
            P("wide", None),
            P(),
            P(),
            P(),
            P(None, None, "wide"),
            P(None, "wide"),
            P("wide", None),
            P("wide"),
            P(),
            P(),
            P(None, "wide"),
            P("wide"),
            P("wide", None),
            P("wide"),
        ),
        check_vma=False,
    )
```

```python
import functools
import jax
import jax.numpy as jnp
from jax import lax
from jax.experimental import pallas as pl
from jax.experimental.pallas import tpu as pltpu
from jax.sharding import PartitionSpec as P

VIDEO_FRAMES = 8
HD = 64
EPS = 1e-05
ROW_TILE = 16
LOW = jnp.bfloat16
F32 = jnp.float32
VMEM_LIMIT = 56 * 1024 * 1024
ANY = pl.BlockSpec(memory_space=pl.ANY)
VMEM = pl.BlockSpec(memory_space=pltpu.VMEM)
SMEM = pl.BlockSpec(memory_space=pltpu.SMEM)


def dot(left, right, dims):
    return lax.dot_general(left, right, (dims, ((), ())), preferred_element_type=F32)


def mat_mul(left, right):
    return dot(left, right, ((1,), (0,)))


def mat_tn(left, right):
    return dot(left, right, ((0,), (0,)))


def mat_nt(left, right):
    return dot(left, right, ((1,), (1,)))


def normalize(values):
    row_mean = jnp.mean(values, axis=-1, keepdims=True)
    centred = values - row_mean
    inv_std = lax.rsqrt(jnp.mean(centred * centred, axis=-1, keepdims=True) + EPS)
    return (centred * inv_std, inv_std)


def norm_back(grad_norm, normed, inv_std, norm_gain):
    scaled = grad_norm * norm_gain
    return inv_std * (
        scaled
        - jnp.mean(scaled, axis=-1, keepdims=True)
        - normed * jnp.mean(scaled * normed, axis=-1, keepdims=True)
    )


def bits_of(size):
    return [1 << b for b in range(size.bit_length() - 1)]


def reorder(parts, index):
    parts = list(parts)
    for bit in bits_of(len(parts)):
        odd = (index & bit) != 0
        parts = [jnp.where(odd, parts[k ^ bit], parts[k]) for k in range(len(parts))]
    return parts


def call(kernel, name, micros=0.0, **options):
    return pl.pallas_call(
        kernel,
        name=name,
        compiler_params=pltpu.CompilerParams(vmem_limit_bytes=VMEM_LIMIT),
        cost_estimate=pl.CostEstimate(
            flops=int(micros * 1.0e9), bytes_accessed=int(micros * 3.0e6), transcendentals=0
        ),
        **options,
    )


def shaped(shape, dtype):
    return jax.ShapeDtypeStruct(tuple(shape), dtype)


def whole(array):
    return pl.BlockSpec(array.shape, lambda *_: (0,) * array.ndim)


def fixed(shape):
    return pl.BlockSpec(tuple(shape), lambda *_: (0,) * len(shape))


def per_step(shape):
    return pl.BlockSpec((1,) + tuple(shape[1:]), lambda f: (f,) + (0,) * (len(shape) - 1))


def row_of(ref):
    return ref[...].reshape(1, -1)


def head_masks(width):
    lane = lax.broadcasted_iota(jnp.int32, (1, width), 1) // HD
    return [lane == h for h in range(width // HD)]


def stack_heads(values, masks, scale=1.0):
    return jnp.concatenate([values * jnp.where(m, scale, 0.0).astype(values.dtype) for m in masks], axis=0)


def pick_heads(values, masks):
    size = values.shape[0] // len(masks)
    picked = values[:size]
    for h in range(1, len(masks)):
        picked = jnp.where(masks[h], values[h * size : (h + 1) * size], picked)
    return picked


def weight_copies(refs, shards, place_ref, buf, sem):
    whole_count = 2 * shards - len(refs)
    odd = place_ref[1]
    copies = []
    for j in range(whole_count):
        copies.append([pltpu.make_async_copy(refs[j], buf.at[j], sem.at[j, 0])])
    rest = refs[whole_count:]
    for i in range(len(rest) // 2):
        half = rest[2 * i].shape[0]
        at = pl.multiple_of(odd * half, half)
        other = pl.multiple_of((1 - odd) * half, half)
        j = whole_count + i
        copies.append([
            pltpu.make_async_copy(rest[2 * i], buf.at[j, pl.ds(at, half)], sem.at[j, 0]),
            pltpu.make_async_copy(rest[2 * i + 1], buf.at[j, pl.ds(other, half)], sem.at[j, 1]),
        ])
    return copies


def start_all(copies):
    for group in copies:
        for copy in group:
            copy.start()


def wait_all(copies):
    for group in copies:
        for copy in group:
            copy.wait()


def attn_forward_kernel(waits, place_ref, gain_ref, shift_ref, mlp_gain_ref, mlp_shift_ref, base_ref, *refs):
    shards = refs[-3].shape[0]
    toks, refs = refs[:shards], refs[shards:]
    sums, refs = refs[:shards], refs[shards:]
    packs, refs = refs[:shards], refs[shards:]
    weights, refs = refs[: -14 - waits], refs[-14:]
    (normed_ref, inv_ref, attn_in_ref, heads_ref, prob_ref, mix_ref, hidden_ref, mlp_normed_ref,
     mlp_inv_ref, mlp_in_ref, tok_buf, w_buf, w_sem, msg_buf) = refs
    part, patches = toks[0].shape[1], toks[0].shape[2]
    seq_pad, width = normed_ref.shape[1], normed_ref.shape[2]
    frames = pl.num_programs(0)
    frame = pl.program_id(0)
    wide_idx = place_ref[0]
    copies = weight_copies(weights, shards, place_ref, w_buf, w_sem)

    @pl.when(frame == 0)
    def _():
        start_all(copies)
        tok_buf[...] = jnp.zeros_like(tok_buf)
        total = base_ref[...]
        for ref in sums:
            total += ref[...]
        msg_buf[...] = total

    for k in range(shards):
        at = pl.multiple_of((wide_idx ^ k) * part, part)
        tok_buf[pl.ds(at, part), :patches] = toks[k][0]
    tokens = tok_buf[...].T[:seq_pad].astype(F32)
    group = msg_buf[...]
    own = lax.broadcasted_iota(jnp.int32, (group.shape[0], 1), 0) == wide_idx * frames + frame
    message = jnp.sum(jnp.where(own, group, 0.0), axis=0, keepdims=True)
    row = lax.broadcasted_iota(jnp.int32, (seq_pad, 1), 0)
    full = jnp.where(row == patches, message, tokens)
    normed, inv = normalize(full)
    normed_ref[0] = normed
    inv_ref[0] = inv
    gain, shift, mlp_gain, mlp_shift = map(row_of, (gain_ref, shift_ref, mlp_gain_ref, mlp_shift_ref))
    attn_in = (normed * gain + shift).astype(LOW)
    attn_in_ref[0] = attn_in
    masks = head_masks(part)
    live = lax.broadcasted_iota(jnp.int32, (1, seq_pad), 1) <= patches
    total = full + jnp.concatenate(reorder([p[1:2, 2 * part : 3 * part] for p in packs], wide_idx), axis=1)

    @pl.when(frame == 0)
    def _():
        wait_all(copies)

    for k in range(shards):
        proj = mat_nt(attn_in, w_buf[k, : 3 * part])
        queries = (proj[:, :part] + packs[k][1:2, :part]).astype(LOW)
        keys = proj[:, part : 2 * part].astype(LOW)
        values = (proj[:, 2 * part :] + packs[k][1:2, part : 2 * part]).astype(LOW)
        heads_ref[0, k, 0] = queries
        heads_ref[0, k, 1] = keys
        heads_ref[0, k, 2] = values
        scores = mat_nt(stack_heads(queries, masks, HD ** (-0.5)), keys)
        scores = jnp.where(live, scores, -1e30)
        exps = jnp.exp(scores - jnp.max(scores, axis=-1, keepdims=True))
        prob = (exps * (1.0 / jnp.sum(exps, axis=-1, keepdims=True))).astype(LOW)
        prob_ref[0, k] = prob
        mix_low = pick_heads(mat_mul(prob, values), masks).astype(LOW)
        mix_ref[0, k] = mix_low
        total += mat_mul(mix_low, w_buf[k, 3 * part :])
    hidden_ref[0] = total
    mlp_normed, mlp_inv = normalize(total.astype(LOW).astype(F32))
    mlp_normed_ref[0] = mlp_normed
    mlp_inv_ref[0] = mlp_inv
    mlp_in_ref[0] = (mlp_normed * mlp_gain + mlp_shift).astype(LOW)


def attn_forward(seq_pad, place, vecs, base, toks, sums, packs, weights, after):
    frames, part, patches = toks[0].shape
    shards = len(toks)
    width = part * shards
    heads = part // HD
    seq_lanes = -(-seq_pad // 128) * 128
    shapes = [
        ((frames, seq_pad, width), F32),
        ((frames, seq_pad, 1), F32),
        ((frames, seq_pad, width), LOW),
        ((frames, shards, 3, seq_pad, part), LOW),
        ((frames, shards, heads * seq_pad, seq_pad), LOW),
        ((frames, shards, seq_pad, part), LOW),
        ((frames, seq_pad, width), F32),
        ((frames, seq_pad, width), F32),
        ((frames, seq_pad, 1), F32),
        ((frames, seq_pad, width), LOW),
    ]
    return call(
        functools.partial(attn_forward_kernel, len(after)),
        "attn_forward",
        grid=(frames,),
        in_specs=[SMEM] + [whole(v) for v in vecs] + [whole(base)]
        + [per_step(v.shape) for v in toks]
        + [whole(v) for v in list(sums) + list(packs)]
        + [ANY] * (len(weights) + len(after)),
        out_specs=[per_step(s) for s, _ in shapes],
        out_shape=[shaped(s, d) for s, d in shapes],
        scratch_shapes=[
            pltpu.VMEM((width, seq_lanes), LOW),
            pltpu.VMEM((shards, 4 * part, width), LOW),
            pltpu.SemaphoreType.DMA((shards, 2)),
            pltpu.VMEM(base.shape, F32),
        ],
    )(place, *vecs, base, *toks, *sums, *packs, *weights, *after)


def mlp_kernel(frames, count, first, waits, place_ref, scale_ref, mlp_in_ref, *refs):
    packs, refs = refs[:count], refs[count:]
    if first:
        shards = 2 * count
        cots, refs = refs[:shards], refs[shards:]
    else:
        (grad_ref, acc_in, gacc_in), refs = refs[:3], refs[3:]
    weights, refs = refs[: 2 * count], refs[2 * count + waits :]
    if first:
        (cot_ref, grad_ref), refs = refs[:2], refs[2:]
    acc_ref, gacc_ref, sums_ref = refs[:3]
    g_refs, refs = refs[3 : 3 + count], refs[3 + count :]
    w_buf, g_buf, act_buf, pre_buf, in_sem, out_sem = refs[:6]
    rows, width = mlp_in_ref.shape
    hidden = act_buf.shape[1]
    step = rows // frames
    loads = []
    for i in range(count):
        if first:
            for j, ref in ((2 * i, weights[i]), (2 * i + 1, weights[count + i])):
                loads.append([pltpu.make_async_copy(ref, w_buf.at[j], in_sem.at[j, 0])])
        else:
            half = weights[2 * i].shape[0] // 2
            for j in range(2):
                load = []
                for n, odd in enumerate((place_ref[1], 1 - place_ref[1])):
                    to = w_buf.at[2 * i + j, pl.ds(pl.multiple_of(odd * half, half), half)]
                    load.append(
                        pltpu.make_async_copy(weights[2 * i + n].at[pl.ds(j * half, half)], to, in_sem.at[2 * i + j, n])
                    )
                loads.append(load)
    start_all(loads)
    stores = [
        pltpu.make_async_copy(g_buf.at[2 * i + j], g_refs[i].at[pl.ds(j * width, width)], out_sem.at[2 * i + j])
        for i in range(count) for j in range(2)
    ]
    if first:
        cot_buf = refs[6]
        cot_buf[...] = jnp.zeros_like(cot_buf)
        part, patches = cots[0].shape[1:]
        for f in range(frames):
            for k in range(shards):
                at = pl.multiple_of((place_ref[0] ^ k) * part, part)
                cot_buf[pl.ds(at, part), :patches] = cots[k][f]
            cot = cot_buf[...].T[:step]
            cot_ref[f] = cot
            grad_ref[f * step : (f + 1) * step] = (cot.astype(F32) * scale_ref[f]).astype(LOW)
    for i in range(count):
        up, down = 2 * i, 2 * i + 1
        wait_all(loads[up : down + 1])
        bias = packs[i][0:1]

        def one(f, total, i=i, up=up, down=down, bias=bias):
            at = pl.ds(pl.multiple_of(f * step, step), step)
            pre = mat_mul(mlp_in_ref[at], w_buf[up]) + bias
            sig = 0.5 + 0.5 * jnp.tanh(0.851 * pre)
            act = (pre * sig).astype(LOW)
            act_buf[at] = act
            grad_act = mat_nt(grad_ref[at], w_buf[down])
            grad_pre = (grad_act * (sig + 1.702 * pre * sig * (1.0 - sig))).astype(LOW)
            pre_buf[at] = grad_pre
            out = mat_mul(act, w_buf[down])
            back = mat_nt(grad_pre, w_buf[up])
            if i > 0:
                acc_ref[at] += out
                gacc_ref[at] += back
            elif first:
                acc_ref[at] = out
                gacc_ref[at] = back
            else:
                acc_ref[at] = acc_in[at] + out
                gacc_ref[at] = gacc_in[at] + back
            return total + jnp.sum(grad_pre.astype(F32), axis=0, keepdims=True)

        sums_ref[i] = lax.fori_loop(0, frames, one, jnp.zeros((1, hidden), F32))
        for c in range(0, width, 256):
            g_buf[up, c : c + 256] = mat_tn(mlp_in_ref[:, c : c + 256], pre_buf[...]).astype(LOW)
        stores[up].start()
        for c in range(0, hidden, 256):
            g_buf[down, c : c + 256] = mat_tn(act_buf[:, c : c + 256], grad_ref[...]).astype(LOW)
        stores[down].start()
    for store in stores:
        store.wait()


def mlp_step(frames, place, scale, mlp_in, packs, weights, cots=None, carried=None, after=()):
    rows, width = mlp_in.shape
    count = len(packs)
    first = cots is not None
    hidden = packs[0].shape[1]
    step = rows // frames
    ins = [place, scale, mlp_in, *packs, *(cots if first else carried)]
    shapes = [shaped((frames, step, width), LOW), shaped((rows, width), LOW)] if first else []
    shapes += [shaped((rows, width), F32)] * 2 + [shaped((count, 1, hidden), F32)]
    grads = [shaped((width + hidden, width), LOW)] * count
    scratch = [
        pltpu.VMEM((2 * count, width, hidden), LOW),
        pltpu.VMEM((2 * count, width, hidden), LOW),
        pltpu.VMEM((rows, hidden), LOW),
        pltpu.VMEM((rows, hidden), LOW),
        pltpu.SemaphoreType.DMA((2 * count, 2)),
        pltpu.SemaphoreType.DMA((2 * count,)),
    ]
    if first:
        scratch.append(pltpu.VMEM((width, -(-step // 128) * 128), LOW))
    return call(
        functools.partial(mlp_kernel, frames, count, first, len(after)),
        "mlp",
        in_specs=[SMEM, SMEM, VMEM] + [VMEM] * (len(ins) - 3) + [ANY] * (len(weights) + len(after)),
        out_specs=[VMEM] * len(shapes) + [ANY] * len(grads),
        out_shape=shapes + grads,
        scratch_shapes=scratch,
    )(*ins, *weights, *after)


def attn_backward_kernel(
    shards, waits, place_ref, scale_ref, gain_ref, mlp_gain_ref, res_ref, acc_ref, gacc_ref, mlp_normed_ref, mlp_inv_ref, cot_ref,
    normed_ref, inv_ref, heads_ref, prob_ref, *refs
):
    packs, refs = refs[:shards], refs[shards:]
    ups, refs = refs[: shards // 2], refs[shards // 2 :]
    outs = 2 * shards + 3 + 2
    weights, refs = refs[: len(refs) - outs - waits], refs[len(refs) - outs :]
    toks, grad_toks, refs = refs[:shards], refs[shards : 2 * shards], refs[2 * shards :]
    proj_ref, low_ref, sums_ref, w_buf, w_sem = refs
    part = heads_ref.shape[4]
    patches = toks[0].shape[2]
    seq_pad, width = res_ref.shape[1:]
    gain, mlp_gain = row_of(gain_ref), row_of(mlp_gain_ref)
    frame = pl.program_id(0)
    wide_idx = place_ref[0]
    copies = weight_copies(weights, shards, place_ref, w_buf, w_sem)

    @pl.when(frame == 0)
    def _():
        start_all(copies)
        sums_ref[...] = jnp.zeros_like(sums_ref)
        rows = [ref[i] for ref in ups for i in range(2)]
        for k, values in enumerate(reorder(rows, wide_idx)):
            sums_ref[6 + k] = values

    def columns(values, out_refs):
        blocks = values.T
        blocks = reorder([blocks[j * part : (j + 1) * part, :patches] for j in range(shards)], wide_idx)
        for ref, block in zip(out_refs, blocks):
            ref[0] = block

    down_bias = jnp.concatenate(reorder([p[1:2, 3 * part : 4 * part] for p in packs], wide_idx), axis=1)
    columns((res_ref[0] + acc_ref[0] + down_bias).astype(LOW), toks)
    grad_res = cot_ref[0].astype(F32) * scale_ref[frame]
    gacc, mlp_normed = gacc_ref[0], mlp_normed_ref[0]
    hidden = grad_res + norm_back(gacc, mlp_normed, mlp_inv_ref[0], mlp_gain)

    def add_sum(row, values):
        sums_ref[row] += jnp.sum(values, axis=0, keepdims=True)

    add_sum(0, grad_res)
    add_sum(1, gacc * mlp_normed)
    add_sum(2, gacc)
    add_sum(3, hidden)
    low = hidden.astype(LOW)
    low_ref[0] = low
    masks = head_masks(part)
    scale = HD ** (-0.5)
    back = jnp.zeros(hidden.shape, F32)
    bias_sums = []

    @pl.when(frame == 0)
    def _():
        wait_all(copies)

    for k in range(shards):
        grad_mix = mat_nt(low, w_buf[k, 3 * part :]).astype(LOW)
        queries, keys, values = heads_ref[0, k, 0], heads_ref[0, k, 1], heads_ref[0, k, 2]
        prob_low = prob_ref[0, k]
        prob = prob_low.astype(F32)
        mix_heads = stack_heads(grad_mix, masks)
        grad_value = mat_tn(prob_low, mix_heads)
        grad_prob = mat_nt(mix_heads, values)
        grad_score = (
            prob * (grad_prob - jnp.sum(prob * grad_prob, axis=-1, keepdims=True))
        ).astype(LOW)
        grad_query = pick_heads(mat_mul(grad_score, keys), masks)
        grad_key = mat_tn(grad_score, stack_heads(queries, masks))
        proj = jnp.concatenate([grad_query * scale, grad_key * scale, grad_value], axis=1).astype(LOW)
        proj_ref[0, k] = proj
        bias_sums.append(jnp.sum(proj.astype(F32), axis=0, keepdims=True))
        back += mat_mul(proj, w_buf[k, : 3 * part])
    for i, at in ((6 + shards, 0), (7 + shards, 2 * part)):
        own = reorder([values[:, at : at + part] for values in bias_sums], wide_idx)
        sums_ref[i] += jnp.concatenate(own, axis=1)
    normed = normed_ref[0]
    add_sum(4, back * normed)
    add_sum(5, back)
    total = hidden + norm_back(back, normed, inv_ref[0], gain)
    row = lax.broadcasted_iota(jnp.int32, (seq_pad, 1), 0)
    sums_ref[8 + shards + frame] = jnp.sum(jnp.where(row == patches, total, 0.0), axis=0, keepdims=True)
    columns(total.astype(LOW), grad_toks)


def attn_backward(patches, place, scale, vecs, per_frame, packs, ups, weights, after):
    frames, seq_pad, width = per_frame[0].shape
    heads = per_frame[8]
    shards, part = heads.shape[1], heads.shape[4]
    blocks = [(frames, part, patches)] * (2 * shards)
    proj = (frames, shards, seq_pad, 3 * part)
    return call(
        functools.partial(attn_backward_kernel, shards, len(after)),
        "attn_backward",
        grid=(frames,),
        in_specs=[SMEM, SMEM]
        + [whole(v) for v in vecs]
        + [per_step(v.shape) for v in per_frame]
        + [whole(v) for v in list(packs) + list(ups)]
        + [ANY] * (len(weights) + len(after)),
        out_specs=[per_step(b) for b in blocks]
        + [per_step(proj), per_step((frames, seq_pad, width)), fixed((8 + shards + frames, 1, width))],
        out_shape=[shaped(b, LOW) for b in blocks]
        + [
            shaped(proj, LOW),
            shaped((frames, seq_pad, width), LOW),
            shaped((8 + shards + frames, 1, width), F32),
        ],
        scratch_shapes=[
            pltpu.VMEM((shards, 4 * part, width), LOW),
            pltpu.SemaphoreType.DMA((shards, 2)),
        ],
    )(place, scale, *vecs, *per_frame, *packs, *ups, *weights, *after)


def attn_grads_kernel(waits, attn_in_ref, low_ref, proj_ref, mix_ref, *refs):
    grad_refs, (proj_buf, mix_buf) = refs[waits:-2], refs[-2:]
    count = len(grad_refs)
    frames, seq_pad, part = mix_ref.shape[0], mix_ref.shape[2], mix_ref.shape[3]
    for i in range(count):
        for f in range(frames):
            at = slice(f * seq_pad, (f + 1) * seq_pad)
            proj_buf[at] = proj_ref[f, i]
            mix_buf[at] = mix_ref[f, i]
        for c in range(0, 3 * part, part):
            grad_refs[i][c : c + part] = mat_tn(proj_buf[:, c : c + part], attn_in_ref[...]).astype(LOW)
        grad_refs[i][3 * part :] = mat_tn(mix_buf[...], low_ref[...]).astype(LOW)


def attn_grads(attn_in, proj, low, mix, pair, after):
    frames, shards, seq_pad, part = mix.shape
    width = attn_in.shape[-1]
    rows = frames * seq_pad
    count = min(2, shards)

    def shard(array):
        return pl.BlockSpec((frames, count) + array.shape[2:], lambda i: (0, pair, 0, 0))

    return call(
        functools.partial(attn_grads_kernel, len(after)),
        "attn_grads",
        grid=(1,),
        in_specs=[fixed((rows, width)), fixed((rows, width)), shard(proj), shard(mix)] + [ANY] * len(after),
        out_specs=[fixed((4 * part, width))] * count,
        out_shape=[shaped((4 * part, width), LOW)] * count,
        scratch_shapes=[pltpu.VMEM((rows, 3 * part), LOW), pltpu.VMEM((rows, part), LOW)],
    )(attn_in.reshape(rows, width), low.reshape(rows, width), proj, mix, *after)


def same_video(place_ref, group, rows, columns):
    first = pl.program_id(0) * columns

    def video(position):
        position = position + first
        return (((position // group) ^ place_ref[2]) * group + position % group) // VIDEO_FRAMES

    row = lax.broadcasted_iota(jnp.int32, (rows, columns), 0) % columns
    column = lax.broadcasted_iota(jnp.int32, (rows, columns), 1)
    return video(row) == video(column)


def message_forward_kernel(
    group, waits, place_ref, cls_ref, weight_ref, m_bias_ref, gain_ref, shift_ref, offset_ref, flat_ref, bias_ref,
    proj_ref, *refs
):
    normed_ref, inv_ref, in_ref, heads_ref, prob_ref, mix_ref, base_ref, sum_ref = refs[waits:]
    part = proj_ref.shape[0]
    chunk = cls_ref.shape[0]
    message = mat_mul(cls_ref[...], weight_ref[...]) + row_of(m_bias_ref)
    normed, inv = normalize(message)
    normed_ref[...] = normed
    inv_ref[...] = inv
    msg_in = (normed * row_of(gain_ref) + row_of(shift_ref)).astype(LOW)
    in_ref[...] = msg_in
    proj = mat_nt(msg_in, flat_ref[...])
    queries = (proj[:, :part] + bias_ref[0:1]).astype(LOW)
    keys = proj[:, part : 2 * part].astype(LOW)
    values = (proj[:, 2 * part :] + bias_ref[1:2]).astype(LOW)
    heads_ref[0, 0] = queries
    heads_ref[0, 1] = keys
    heads_ref[0, 2] = values
    masks = head_masks(part)
    scores = mat_nt(stack_heads(queries, masks, HD ** (-0.5)), keys)
    scores = jnp.where(same_video(place_ref, group, len(masks) * chunk, chunk), scores, -1e30)
    exps = jnp.exp(scores - jnp.max(scores, axis=-1, keepdims=True))
    prob = exps / jnp.sum(exps, axis=-1, keepdims=True)
    prob_ref[0] = prob
    mix = pick_heads(mat_mul(prob.astype(LOW), values), masks).astype(LOW)
    mix_ref[...] = mix

    @pl.when(pl.program_id(0) == 0)
    def _():
        base_ref[...] = message[:group] + row_of(offset_ref)
        sum_ref[...] = mat_mul(mix, proj_ref[...])[:group]


def message_forward(chunk, group, place, cls_rows, weight, vecs, flat, bias, proj, after):
    count, width = cls_rows.shape
    part = proj.shape[0]
    heads = part // HD
    chunks = count // chunk
    rows = lambda columns: pl.BlockSpec((chunk, columns), lambda c: (c, 0))
    return call(
        functools.partial(message_forward_kernel, group, len(after)),
        "message_forward",
        grid=(chunks,),
        in_specs=[SMEM, rows(width)]
        + [whole(v) for v in (weight, *vecs, flat, bias, proj)]
        + [ANY] * len(after),
        out_specs=[
            rows(width), rows(1), rows(width),
            per_step((chunks, 3, chunk, part)), per_step((chunks, heads * chunk, chunk)),
            rows(part), fixed((group, width)), fixed((group, width)),
        ],
        out_shape=[
            shaped((count, width), F32),
            shaped((count, 1), F32),
            shaped((count, width), LOW),
            shaped((chunks, 3, chunk, part), LOW),
            shaped((chunks, heads * chunk, chunk), F32),
            shaped((count, part), LOW),
            shaped((group, width), F32),
            shaped((group, width), F32),
        ],
    )(place, cls_rows, weight, *vecs, flat, bias, proj, *after)


def message_backward_kernel(
    waits, grad_ref, in_ref, heads_ref, prob_ref, mix_ref, flat_ref, proj_ref, *refs
):
    grad_flat_ref, grad_proj_ref, sum_grad_ref, sum_cross_ref, back_ref = refs[waits:]

    @pl.when(pl.program_id(0) == 0)
    def _():
        for ref in (grad_flat_ref, grad_proj_ref, sum_grad_ref, sum_cross_ref):
            ref[...] = jnp.zeros_like(ref)

    part = proj_ref.shape[0]
    masks = head_masks(part)
    grad = grad_ref[:, 0].astype(LOW)
    sum_grad_ref[...] += jnp.sum(grad.astype(F32), axis=0, keepdims=True)
    grad_proj_ref[...] += mat_tn(mix_ref[...], grad)
    grad_mix = mat_nt(grad, proj_ref[...]).astype(LOW)
    mix_heads = stack_heads(grad_mix, masks)
    queries, keys, values = heads_ref[0, 0], heads_ref[0, 1], heads_ref[0, 2]
    prob = prob_ref[0]
    grad_prob = mat_nt(mix_heads, values)
    grad_score = prob * (grad_prob - jnp.sum(prob * grad_prob, axis=-1, keepdims=True))
    score_low = grad_score.astype(LOW)
    grad_query = pick_heads(mat_mul(score_low, keys), masks) * HD ** (-0.5)
    grad_key = mat_tn(score_low, stack_heads(queries, masks)) * HD ** (-0.5)
    grad_value = mat_tn(prob.astype(LOW), mix_heads)
    cross = jnp.concatenate([grad_query, grad_key, grad_value], axis=1).astype(LOW)
    sum_cross_ref[...] += jnp.sum(cross.astype(F32), axis=0, keepdims=True)
    grad_flat_ref[...] += mat_tn(cross, in_ref[...])
    back_ref[...] = mat_mul(cross, flat_ref[...])


def message_backward(grad, msg_in, heads, prob, mix, flat, proj, after):
    count, _, width = grad.shape
    part = proj.shape[0]
    chunks, _, chunk, _ = heads.shape
    rows = lambda columns: pl.BlockSpec((chunk, columns), lambda c: (c, 0))
    shapes = [(3 * part, width), (part, width), (1, width), (1, 3 * part)]
    return call(
        functools.partial(message_backward_kernel, len(after)),
        "message_backward",
        grid=(chunks,),
        in_specs=[
            pl.BlockSpec((chunk, 1, width), lambda c: (c, 0, 0)),
            rows(width), per_step(heads.shape), per_step(prob.shape), rows(part), whole(flat), whole(proj),
        ]
        + [ANY] * len(after),
        out_specs=[fixed(s) for s in shapes] + [rows(width)],
        out_shape=[shaped(s, F32) for s in shapes + [(count, width)]],
    )(grad, msg_in, heads, prob, mix, flat, proj, *after)


def message_end_kernel(
    group, passed, grad_ref, back_ref, other_ref, normed_ref, inv_ref, gain_ref, cls_ref, weight_ref, *refs
):
    grad_weight_ref, sums_ref, grad_cls_ref = refs[passed : passed + 3]

    @pl.when(pl.program_id(0) == 0)
    def _():
        grad_weight_ref[...] = jnp.zeros_like(grad_weight_ref)
        sums_ref[...] = jnp.zeros_like(sums_ref)

    back = back_ref[...] + other_ref[...].astype(F32)
    normed = normed_ref[...]
    grad = grad_ref[:, 0] + norm_back(back, normed, inv_ref[...], row_of(gain_ref))
    low = grad.astype(LOW)
    for row, values in enumerate((low.astype(F32), back * normed, back)):
        sums_ref[row : row + 1] += jnp.sum(values, axis=0, keepdims=True)
    grad_weight_ref[...] += mat_tn(cls_ref[...], low)

    @pl.when(pl.program_id(0) == 0)
    def _():
        grad_cls_ref[...] = mat_nt(weight_ref[...], low)[:, :group]


def message_end(chunk, group, grad, back, other, normed, inv, gain, cls_rows, weight, passed):
    count, _, width = grad.shape
    rows = lambda columns: pl.BlockSpec((chunk, columns), lambda c: (c, 0))
    return call(
        functools.partial(message_end_kernel, group, len(passed)),
        "message_end",
        grid=(count // chunk,),
        in_specs=[pl.BlockSpec((chunk, 1, width), lambda c: (c, 0, 0))] + [rows(width)] * 3 + [rows(1), whole(gain), rows(width), whole(weight)]
        + [ANY] * len(passed),
        out_specs=[fixed((width, width)), fixed((8, width)), fixed((width, group))] + [ANY] * len(passed),
        out_shape=[shaped((width, width), F32), shaped((8, width), F32), shaped((width, group), F32)]
        + [shaped(v.shape, v.dtype) for v in passed],
        input_output_aliases={8 + i: 3 + i for i in range(len(passed))},
    )(grad, back, other, normed, inv, gain, cls_rows, weight, *passed)


def gate_kernel(*refs):
    pass


def gate(arrays, after, micros=0.0):
    count = len(arrays)
    return call(
        gate_kernel,
        "gate",
        micros,
        in_specs=[ANY] * (count + len(after)),
        out_specs=[ANY] * count,
        out_shape=[shaped(v.shape, v.dtype) for v in arrays],
        input_output_aliases={i: i for i in range(count)},
    )(*arrays, *after)


def merge_kernel(count, ordered, place_ref, *refs):
    refs, out_ref = refs[:-1], refs[-1]
    size = refs[0].shape[0] - count
    total = refs[0][:count]
    for ref in refs[1:]:
        total += ref[:count]
    out_ref[:count] = total
    for k, ref in enumerate(refs):
        at = (place_ref[0] ^ k) if ordered else k
        out_ref[pl.ds(count + at * size, size)] = ref[count:]


def merge(place, count, buffers, ordered=False):
    rows, one, width = buffers[0].shape
    return call(
        functools.partial(merge_kernel, count, ordered),
        "merge",
        in_specs=[SMEM] + [VMEM] * len(buffers),
        out_specs=VMEM,
        out_shape=shaped((count + (rows - count) * len(buffers), one, width), F32),
    )(place, *buffers)


def collect_kernel(place_ref, *refs):
    *pieces, grad_cls_ref, out_ref = refs
    frames, part, patches = pieces[0].shape
    own = grad_cls_ref[pl.ds(pl.multiple_of(place_ref[0] * part, part), part), :]
    lane = lax.broadcasted_iota(jnp.int32, (part, patches), 1)
    for j, piece in enumerate(reorder([ref[...] for ref in pieces], place_ref[0])):
        for f in range(frames):
            i = j * frames + f
            out_ref[i] = jnp.where(lane == 0, piece[f].astype(F32) + own[:, i : i + 1], piece[f].astype(F32)).astype(LOW)


def collect(place, pieces, grad_cls):
    frames, part, patches = pieces[0].shape
    shape = (frames * len(pieces), part, patches)
    return call(
        collect_kernel,
        "collect",
        in_specs=[SMEM] + [VMEM] * (len(pieces) + 1),
        out_specs=VMEM,
        out_shape=shaped(shape, LOW),
    )(place, *pieces, grad_cls)


def swap(block, axis, flip):
    return lax.ppermute(block, axis, [(i, i ^ flip) for i in range(lax.axis_size(axis))])


def nothing(array):
    one = lax.slice(array, (0,) * array.ndim, (1,) * array.ndim).reshape(()).astype(F32)
    return one * 0.0


def zero_of(array):
    return nothing(array).astype(jnp.int32)


def frames_in(block, after):
    count = lax.axis_size("wide")
    index = lax.axis_index("wide")
    part = block.shape[0] // count
    begin = zero_of(after)
    pieces = [lax.dynamic_slice_in_dim(block, (index ^ k) * part + begin, part, 0) for k in range(count)]
    return [piece if k == 0 else swap(piece, "wide", k) for k, piece in enumerate(pieces)]


def send_half(block, after):
    odd = lax.axis_index("narrow") & 1
    half = block.shape[0] // 2
    sent = lax.dynamic_slice_in_dim(block, odd * half + zero_of(after), half, 0)
    return [swap(sent, "wide", bit) for bit in bits_of(lax.axis_size("wide"))[1:]]


def near_shards(block):
    return [block, swap(block, "wide", 1)]


def far_shards(near, far):
    return [near, far, swap(near, "wide", 1), swap(far, "wide", 1)]


def added(terms, start, size):
    total = sum(
        lax.dynamic_slice_in_dim(array, begin + start, size, 0).astype(F32) for array, begin in terms
    )
    return total.astype(LOW)


def halve(terms, size, bit):
    size = size // 2
    odd = ((lax.axis_index("narrow") & bit) != 0).astype(jnp.int32)
    sent = added(terms, (1 - odd) * size, size)
    received = swap(sent, "narrow", bit)
    return [(array, start + odd * size) for array, start in terms] + [(received, 0)], size, sent, received


def halve_all(terms, size, bits):
    for bit in bits:
        terms, size, _, _ = halve(terms, size, bit)
    return terms, size


def join_all(block, bits):
    for bit in reversed(bits):
        odd = (lax.axis_index("narrow") & bit) != 0
        other = swap(block, "narrow", bit)
        block = jnp.where(
            odd, jnp.concatenate([other, block], axis=0), jnp.concatenate([block, other], axis=0)
        )
    return block


def body(
    frame_tokens,
    cotangent,
    caption_count,
    caption_len,
    message_weight,
    message_bias,
    message_gain,
    message_shift,
    cross_qkv,
    cross_bias,
    cross_proj,
    cross_offset,
    attn_gain,
    attn_shift,
    qkv_weight,
    qkv_bias,
    out_weight,
    out_bias,
    mlp_gain,
    mlp_shift,
    up_weight,
    up_bias,
    down_weight,
    down_bias,
):
    group, patches, part = frame_tokens.shape
    width = message_weight.shape[0]
    hidden = up_weight.shape[1]
    wide = lax.axis_size("wide")
    narrow = lax.axis_size("narrow")
    wide_idx = lax.axis_index("wide")
    narrow_idx = lax.axis_index("narrow")
    frames = group // wide
    seq_pad = -(-(patches + 1) // ROW_TILE) * ROW_TILE
    rows = frames * seq_pad
    all_frames = group * narrow
    chunk = max(c for c in range(VIDEO_FRAMES, 129, VIDEO_FRAMES) if all_frames % c == 0 and c % group == 0)
    place = jnp.stack([wide_idx, narrow_idx & 1, narrow_idx]).astype(jnp.int32)

    def own_cols(values):
        return lax.dynamic_slice_in_dim(values, wide_idx * part, part, values.ndim - 1)

    tokens_t = frame_tokens.transpose(0, 2, 1)
    pack = jnp.concatenate(
        [up_bias, qkv_bias.reshape(-1), out_bias, down_bias, frame_tokens[:, 0, :].astype(F32).reshape(-1)]
    ).reshape(-1, width)
    packs = [pack] + [swap(pack, "wide", k) for k in range(1, wide)]
    cls_rows = jnp.concatenate(
        reorder([p[2:].reshape(group, part).astype(LOW) for p in packs], wide_idx), axis=1
    )
    for bit in bits_of(narrow):
        cls_rows = jnp.concatenate([cls_rows, swap(cls_rows, "narrow", bit)], axis=0)
    toks = frames_in(tokens_t, packs[-1])
    attn_own = jnp.concatenate(
        [qkv_weight.transpose(1, 2, 0).reshape(3 * part, width), out_weight], axis=0
    )
    attn_weights = near_shards(attn_own)
    attn_near = send_half(attn_own, packs[-1])
    attn_far = [swap(near, "narrow", 1) for near in attn_near]
    for near, far in zip(attn_near, attn_far):
        attn_weights += far_shards(near, far)

    cots = frames_in(cotangent.transpose(0, 2, 1), attn_far[0])

    caption_slot = jnp.arange(caption_len.shape[1])
    word_total = jnp.sum(
        jnp.where(caption_slot[None, :] < caption_count[:, None], caption_len, 0), axis=1
    ).astype(F32)
    video_scale = word_total / jnp.mean(word_total)
    own_video = (narrow_idx * group + wide_idx * frames + jnp.arange(frames)) // VIDEO_FRAMES
    video_match = own_video[:, None] == jnp.arange(video_scale.shape[0])[None, :]
    scale = jnp.sum(jnp.where(video_match, video_scale[None, :], 0.0), axis=1)

    cross_flat = cross_qkv.transpose(1, 2, 0).reshape(3 * part, width)
    msg_normed, msg_inv, msg_in, cross_heads, cross_prob, cross_mix, base, group_sum = message_forward(
        chunk, group, place, cls_rows, message_weight,
        (message_bias, message_gain, message_shift, cross_offset), cross_flat, cross_bias, cross_proj,
        attn_far + toks[1:] + cots[1:],
    )
    group_sums = [group_sum] + [swap(group_sum, "wide", k) for k in range(1, wide)]

    odd, begin = narrow_idx & 1, zero_of(group_sums[-1])
    half = width // 2
    mlp_half = jnp.concatenate(
        [lax.dynamic_slice_in_dim(w, odd * half + begin, half, 0) for w in (up_weight, down_weight)], axis=0
    )
    mlp_near = [swap(mlp_half, "wide", bit) for bit in bits_of(wide)[1:]]
    up_shards, down_shards = near_shards(up_weight), near_shards(down_weight)

    (normed, inv, attn_in, heads, prob, mix, hidden_res, mlp_normed, mlp_inv, mlp_in) = attn_forward(
        seq_pad, place, (attn_gain, attn_shift, mlp_gain, mlp_shift), base, toks, group_sums, packs, attn_weights,
        [up_shards[1], down_shards[1]],
    )
    mlp_in = mlp_in.reshape(rows, width)
    bits = bits_of(narrow)
    size = width + hidden
    mlp_near = gate(mlp_near, [mlp_in])
    cot, grad_rows, acc, gacc, sum_up, *grad_own = mlp_step(
        frames, place, scale, mlp_in, packs[:2], up_shards + down_shards, cots=cots, after=mlp_near
    )
    *mlp_far, grad_next = gate([swap(near, "narrow", 1) for near in mlp_near] + [grad_own[1]], [acc])
    own_terms = [(grad_own[0], 0), (swap(grad_next, "wide", 1), 0)]
    own_terms, own_size, own_sent, own_received = halve(own_terms, size, bits[0])
    mlp_weights = [piece for near, far in zip(mlp_near, mlp_far) for piece in far_shards(near, far)]
    acc, gacc, sum_up_far, *grad_far = mlp_step(
        frames, place, scale, mlp_in, packs[2:], mlp_weights, carried=(grad_rows, acc, gacc), after=[own_sent]
    )
    grad_far = gate(grad_far, [own_received])
    own_terms, own_size, own_sent, own_next = halve(own_terms, own_size, bits[1])
    far_terms = [(grad_far[0], 0), (swap(grad_far[1], "wide", 1), 0)]
    far_terms, far_size, far_sent, far_received = halve(far_terms, size, bits[0])

    shape = (frames, seq_pad, width)
    per_frame = (
        hidden_res, acc.reshape(shape), gacc.reshape(shape), mlp_normed, mlp_inv, cot, normed, inv, heads, prob
    )
    *blocks, proj, low, sums = attn_backward(
        patches, place, scale, (attn_gain, mlp_gain), per_frame, packs, [sum_up, sum_up_far], attn_weights,
        [own_sent, far_sent],
    )
    grad_attn = list(attn_grads(attn_in, proj, low, mix, 1, [far_received, own_next]))
    half = 2 * part
    attn_far = [(grad_attn[0], 0), (swap(grad_attn[1], "wide", 1), 0)]
    attn_sent = added(attn_far, 0, 2 * half)
    attn_received = swap(attn_sent, "wide", 2)
    grad_attn = gate(attn_grads(attn_in, proj, low, mix, 0, [attn_sent]), [attn_received])
    attn_own = [(grad_attn[0], 0), (swap(grad_attn[1], "wide", 1), 0)]

    own_terms, own_size = halve_all(own_terms, own_size, bits[2:])
    far_terms, far_size = halve_all(far_terms, far_size, bits[1:])
    crossed = swap(added(far_terms, 0, far_size), "wide", 2)
    grad_mlp = join_all(added(own_terms + [(crossed, 0)], 0, own_size), bits).astype(F32)
    grad_attn_own = []
    for at in (0, half):
        terms, left = halve_all([(array, at) for array, _ in attn_own + [(attn_received, 0)]], half, bits)
        grad_attn_own.append(join_all(added(terms, 0, left), bits))
    grad_attn_own = jnp.concatenate(grad_attn_own, axis=0).astype(F32)

    (sums,) = gate([sums], [far_received, own_next])
    count = 8 + wide
    sums = merge(place, count, [sums] + [swap(sums, "wide", k) for k in range(1, wide)], True)
    for bit in bits:
        sums = merge(place, count, [sums, swap(sums, "narrow", bit)])
    grad_msg = sums[count:]
    sums = sums[:count].reshape(count, width)
    grad_up_bias = lax.dynamic_slice_in_dim(sums[6 : 6 + wide].reshape(-1), wide_idx * hidden, hidden, 0)

    grad_cross_flat, grad_cross_proj, sum_cross_grad, sum_cross, back = message_backward(
        grad_msg, msg_in, cross_heads, cross_prob, cross_mix, cross_flat, cross_proj, [attn_received]
    )
    bits = bits_of(wide)
    for bit in bits[:-1]:
        back = back + swap(back, "wide", bit)
    grad_message_weight, msg_sums, grad_cls, *blocks = message_end(
        chunk, group, grad_msg, back, swap(back.astype(LOW), "wide", bits[-1]), msg_normed, msg_inv, message_gain, cls_rows,
        message_weight, blocks,
    )

    def frames_out(pieces):
        return [piece if k == 0 else swap(piece, "wide", k) for k, piece in enumerate(pieces)]

    out_pieces = frames_out(blocks[:wide])
    grad_pieces = frames_out(blocks[wide:])
    output_tokens = jnp.concatenate(reorder(out_pieces, wide_idx), axis=0)
    grad_tokens = collect(place, grad_pieces, grad_cls)

    return (
        output_tokens.transpose(0, 2, 1),
        grad_tokens.transpose(0, 2, 1),
        grad_message_weight,
        msg_sums[0],
        msg_sums[1],
        msg_sums[2],
        grad_cross_flat.reshape(3, part, width).transpose(2, 0, 1),
        jnp.stack([sum_cross[0, :part], sum_cross[0, 2 * part :]]),
        grad_cross_proj,
        sum_cross_grad[0],
        sums[4],
        sums[5],
        grad_attn_own[: 3 * part].reshape(3, part, width).transpose(2, 0, 1),
        own_cols(sums[count - 2 :]),
        grad_attn_own[3 * part :],
        own_cols(sums[3]),
        sums[1],
        sums[2],
        grad_mlp[:width],
        grad_up_bias,
        grad_mlp[width:],
        own_cols(sums[0]),
    )


def solution(mesh):
    return jax.shard_map(
        body,
        mesh=mesh,
        in_specs=(
            P("narrow", None, "wide"),
            P("narrow", None, "wide"),
            P(),
            P(),
            P(),
            P(),
            P(),
            P(),
            P(None, None, "wide"),
            P(None, "wide"),
            P("wide", None),
            P(),
            P(),
            P(),
            P(None, None, "wide"),
            P(None, "wide"),
            P("wide", None),
            P("wide"),
            P(),
            P(),
            P(None, "wide"),
            P("wide"),
            P("wide", None),
            P("wide"),
        ),
        out_specs=(
            P("narrow", None, "wide"),
            P("narrow", None, "wide"),
            P(),
            P(),
            P(),
            P(),
            P(None, None, "wide"),
            P(None, "wide"),
            P("wide", None),
            P(),
            P(),
            P(),
            P(None, None, "wide"),
            P(None, "wide"),
            P("wide", None),
            P("wide"),
            P(),
            P(),
            P(None, "wide"),
            P("wide"),
            P("wide", None),
            P("wide"),
        ),
        check_vma=False,
    )
```

```python
import functools
import jax
import jax.numpy as jnp
from jax import lax
from jax.experimental import pallas as pl
from jax.experimental.pallas import tpu as pltpu
from jax.sharding import PartitionSpec as P

VIDEO_FRAMES = 8
HD = 64
EPS = 1e-05
ROW_TILE = 16
LOW = jnp.bfloat16
F32 = jnp.float32
VMEM_LIMIT = 56 * 1024 * 1024
ANY = pl.BlockSpec(memory_space=pl.ANY)
VMEM = pl.BlockSpec(memory_space=pltpu.VMEM)
SMEM = pl.BlockSpec(memory_space=pltpu.SMEM)


def dot(left, right, dims):
    return lax.dot_general(left, right, (dims, ((), ())), preferred_element_type=F32)


def mat_mul(left, right):
    return dot(left, right, ((1,), (0,)))


def mat_tn(left, right):
    return dot(left, right, ((0,), (0,)))


def mat_nt(left, right):
    return dot(left, right, ((1,), (1,)))


def normalize(values):
    row_mean = jnp.mean(values, axis=-1, keepdims=True)
    centred = values - row_mean
    inv_std = lax.rsqrt(jnp.mean(centred * centred, axis=-1, keepdims=True) + EPS)
    return (centred * inv_std, inv_std)


def norm_back(grad_norm, normed, inv_std, norm_gain):
    scaled = grad_norm * norm_gain
    return inv_std * (
        scaled
        - jnp.mean(scaled, axis=-1, keepdims=True)
        - normed * jnp.mean(scaled * normed, axis=-1, keepdims=True)
    )


def bits_of(size):
    return [1 << b for b in range(size.bit_length() - 1)]


def reorder(parts, index):
    parts = list(parts)
    for bit in bits_of(len(parts)):
        odd = (index & bit) != 0
        parts = [jnp.where(odd, parts[k ^ bit], parts[k]) for k in range(len(parts))]
    return parts


def call(kernel, name, micros=0.0, **options):
    return pl.pallas_call(
        kernel,
        name=name,
        compiler_params=pltpu.CompilerParams(vmem_limit_bytes=VMEM_LIMIT),
        cost_estimate=pl.CostEstimate(
            flops=int(micros * 1.0e9), bytes_accessed=int(micros * 3.0e6), transcendentals=0
        ),
        **options,
    )


def shaped(shape, dtype):
    return jax.ShapeDtypeStruct(tuple(shape), dtype)


def whole(array):
    return pl.BlockSpec(array.shape, lambda *_: (0,) * array.ndim)


def fixed(shape):
    return pl.BlockSpec(tuple(shape), lambda *_: (0,) * len(shape))


def per_step(shape):
    return pl.BlockSpec((1,) + tuple(shape[1:]), lambda f: (f,) + (0,) * (len(shape) - 1))


def row_of(ref):
    return ref[...].reshape(1, -1)


def head_masks(width):
    lane = lax.broadcasted_iota(jnp.int32, (1, width), 1) // HD
    return [lane == h for h in range(width // HD)]


def stack_heads(values, masks, scale=1.0):
    return jnp.concatenate([values * jnp.where(m, scale, 0.0).astype(values.dtype) for m in masks], axis=0)


def pick_heads(values, masks):
    size = values.shape[0] // len(masks)
    picked = values[:size]
    for h in range(1, len(masks)):
        picked = jnp.where(masks[h], values[h * size : (h + 1) * size], picked)
    return picked


def weight_copies(refs, shards, place_ref, buf, sem):
    whole_count = 2 * shards - len(refs)
    odd = place_ref[1]
    copies = []
    for j in range(whole_count):
        copies.append([pltpu.make_async_copy(refs[j], buf.at[j], sem.at[j, 0])])
    rest = refs[whole_count:]
    for i in range(len(rest) // 2):
        half = rest[2 * i].shape[0]
        at = pl.multiple_of(odd * half, half)
        other = pl.multiple_of((1 - odd) * half, half)
        j = whole_count + i
        copies.append([
            pltpu.make_async_copy(rest[2 * i], buf.at[j, pl.ds(at, half)], sem.at[j, 0]),
            pltpu.make_async_copy(rest[2 * i + 1], buf.at[j, pl.ds(other, half)], sem.at[j, 1]),
        ])
    return copies


def start_all(copies):
    for group in copies:
        for copy in group:
            copy.start()


def wait_all(copies):
    for group in copies:
        for copy in group:
            copy.wait()


def attn_forward_kernel(waits, place_ref, gain_ref, shift_ref, mlp_gain_ref, mlp_shift_ref, base_ref, *refs):
    shards = refs[-3].shape[0]
    toks, refs = refs[:shards], refs[shards:]
    sums, refs = refs[:shards], refs[shards:]
    packs, refs = refs[:shards], refs[shards:]
    weights, refs = refs[: -14 - waits], refs[-14:]
    (normed_ref, inv_ref, attn_in_ref, heads_ref, prob_ref, mix_ref, hidden_ref, mlp_normed_ref,
     mlp_inv_ref, mlp_in_ref, tok_buf, w_buf, w_sem, msg_buf) = refs
    part, patches = toks[0].shape[1], toks[0].shape[2]
    seq_pad, width = normed_ref.shape[1], normed_ref.shape[2]
    frames = pl.num_programs(0)
    frame = pl.program_id(0)
    wide_idx = place_ref[0]
    copies = weight_copies(weights, shards, place_ref, w_buf, w_sem)

    @pl.when(frame == 0)
    def _():
        start_all(copies)
        tok_buf[...] = jnp.zeros_like(tok_buf)
        total = base_ref[...]
        for ref in sums:
            total += ref[...]
        msg_buf[...] = total

    for k in range(shards):
        at = pl.multiple_of((wide_idx ^ k) * part, part)
        tok_buf[pl.ds(at, part), :patches] = toks[k][0]
    tokens = tok_buf[...].T[:seq_pad].astype(F32)
    group = msg_buf[...]
    own = lax.broadcasted_iota(jnp.int32, (group.shape[0], 1), 0) == wide_idx * frames + frame
    message = jnp.sum(jnp.where(own, group, 0.0), axis=0, keepdims=True)
    row = lax.broadcasted_iota(jnp.int32, (seq_pad, 1), 0)
    full = jnp.where(row == patches, message, tokens)
    normed, inv = normalize(full)
    normed_ref[0] = normed
    inv_ref[0] = inv
    gain, shift, mlp_gain, mlp_shift = map(row_of, (gain_ref, shift_ref, mlp_gain_ref, mlp_shift_ref))
    attn_in = (normed * gain + shift).astype(LOW)
    attn_in_ref[0] = attn_in
    masks = head_masks(part)
    live = lax.broadcasted_iota(jnp.int32, (1, seq_pad), 1) <= patches
    total = full + jnp.concatenate(reorder([p[1:2, 2 * part : 3 * part] for p in packs], wide_idx), axis=1)

    @pl.when(frame == 0)
    def _():
        wait_all(copies)

    for k in range(shards):
        proj = mat_nt(attn_in, w_buf[k, : 3 * part])
        queries = (proj[:, :part] + packs[k][1:2, :part]).astype(LOW)
        keys = proj[:, part : 2 * part].astype(LOW)
        values = (proj[:, 2 * part :] + packs[k][1:2, part : 2 * part]).astype(LOW)
        heads_ref[0, k, 0] = queries
        heads_ref[0, k, 1] = keys
        heads_ref[0, k, 2] = values
        scores = mat_nt(stack_heads(queries, masks, HD ** (-0.5)), keys)
        scores = jnp.where(live, scores, -1e30)
        exps = jnp.exp(scores - jnp.max(scores, axis=-1, keepdims=True))
        prob = (exps * (1.0 / jnp.sum(exps, axis=-1, keepdims=True))).astype(LOW)
        prob_ref[0, k] = prob
        mix_low = pick_heads(mat_mul(prob, values), masks).astype(LOW)
        mix_ref[0, k] = mix_low
        total += mat_mul(mix_low, w_buf[k, 3 * part :])
    hidden_ref[0] = total
    mlp_normed, mlp_inv = normalize(total.astype(LOW).astype(F32))
    mlp_normed_ref[0] = mlp_normed
    mlp_inv_ref[0] = mlp_inv
    mlp_in_ref[0] = (mlp_normed * mlp_gain + mlp_shift).astype(LOW)


def attn_forward(seq_pad, place, vecs, base, toks, sums, packs, weights, after):
    frames, part, patches = toks[0].shape
    shards = len(toks)
    width = part * shards
    heads = part // HD
    seq_lanes = -(-seq_pad // 128) * 128
    shapes = [
        ((frames, seq_pad, width), F32),
        ((frames, seq_pad, 1), F32),
        ((frames, seq_pad, width), LOW),
        ((frames, shards, 3, seq_pad, part), LOW),
        ((frames, shards, heads * seq_pad, seq_pad), LOW),
        ((frames, shards, seq_pad, part), LOW),
        ((frames, seq_pad, width), F32),
        ((frames, seq_pad, width), F32),
        ((frames, seq_pad, 1), F32),
        ((frames, seq_pad, width), LOW),
    ]
    return call(
        functools.partial(attn_forward_kernel, len(after)),
        "attn_forward",
        23.0,
        grid=(frames,),
        in_specs=[SMEM] + [whole(v) for v in vecs] + [whole(base)]
        + [per_step(v.shape) for v in toks]
        + [whole(v) for v in list(sums) + list(packs)]
        + [ANY] * (len(weights) + len(after)),
        out_specs=[per_step(s) for s, _ in shapes],
        out_shape=[shaped(s, d) for s, d in shapes],
        scratch_shapes=[
            pltpu.VMEM((width, seq_lanes), LOW),
            pltpu.VMEM((shards, 4 * part, width), LOW),
            pltpu.SemaphoreType.DMA((shards, 2)),
            pltpu.VMEM(base.shape, F32),
        ],
    )(place, *vecs, base, *toks, *sums, *packs, *weights, *after)


def mlp_kernel(frames, count, first, waits, place_ref, scale_ref, mlp_in_ref, *refs):
    packs, refs = refs[:count], refs[count:]
    if first:
        shards = 2 * count
        cots, refs = refs[:shards], refs[shards:]
    else:
        (grad_ref, acc_in, gacc_in), refs = refs[:3], refs[3:]
    weights, refs = refs[: 2 * count], refs[2 * count + waits :]
    if first:
        (cot_ref, grad_ref), refs = refs[:2], refs[2:]
    acc_ref, gacc_ref, sums_ref = refs[:3]
    g_refs, refs = refs[3 : 3 + count], refs[3 + count :]
    w_buf, g_buf, act_buf, pre_buf, in_sem, out_sem = refs[:6]
    rows, width = mlp_in_ref.shape
    hidden = act_buf.shape[1]
    step = rows // frames
    loads = []
    for i in range(count):
        if first:
            for j, ref in ((2 * i, weights[i]), (2 * i + 1, weights[count + i])):
                loads.append([pltpu.make_async_copy(ref, w_buf.at[j], in_sem.at[j, 0])])
        else:
            half = weights[2 * i].shape[0] // 2
            for j in range(2):
                load = []
                for n, odd in enumerate((place_ref[1], 1 - place_ref[1])):
                    to = w_buf.at[2 * i + j, pl.ds(pl.multiple_of(odd * half, half), half)]
                    load.append(
                        pltpu.make_async_copy(weights[2 * i + n].at[pl.ds(j * half, half)], to, in_sem.at[2 * i + j, n])
                    )
                loads.append(load)
    start_all(loads)
    stores = [
        pltpu.make_async_copy(g_buf.at[2 * i + j], g_refs[i].at[pl.ds(j * width, width)], out_sem.at[2 * i + j])
        for i in range(count) for j in range(2)
    ]
    if first:
        cot_buf = refs[6]
        cot_buf[...] = jnp.zeros_like(cot_buf)
        part, patches = cots[0].shape[1:]
        for f in range(frames):
            for k in range(shards):
                at = pl.multiple_of((place_ref[0] ^ k) * part, part)
                cot_buf[pl.ds(at, part), :patches] = cots[k][f]
            cot = cot_buf[...].T[:step]
            cot_ref[f] = cot
            grad_ref[f * step : (f + 1) * step] = (cot.astype(F32) * scale_ref[f]).astype(LOW)
    for i in range(count):
        up, down = 2 * i, 2 * i + 1
        wait_all(loads[up : down + 1])
        bias = packs[i][0:1]

        def one(f, total, i=i, up=up, down=down, bias=bias):
            at = pl.ds(pl.multiple_of(f * step, step), step)
            pre = mat_mul(mlp_in_ref[at], w_buf[up]) + bias
            sig = 0.5 + 0.5 * jnp.tanh(0.851 * pre)
            act = (pre * sig).astype(LOW)
            act_buf[at] = act
            grad_act = mat_nt(grad_ref[at], w_buf[down])
            grad_pre = (grad_act * (sig + 1.702 * pre * sig * (1.0 - sig))).astype(LOW)
            pre_buf[at] = grad_pre
            out = mat_mul(act, w_buf[down])
            back = mat_nt(grad_pre, w_buf[up])
            if i > 0:
                acc_ref[at] += out
                gacc_ref[at] += back
            elif first:
                acc_ref[at] = out
                gacc_ref[at] = back
            else:
                acc_ref[at] = acc_in[at] + out
                gacc_ref[at] = gacc_in[at] + back
            return total + jnp.sum(grad_pre.astype(F32), axis=0, keepdims=True)

        sums_ref[i] = lax.fori_loop(0, frames, one, jnp.zeros((1, hidden), F32))
        for c in range(0, width, 256):
            g_buf[up, c : c + 256] = mat_tn(mlp_in_ref[:, c : c + 256], pre_buf[...]).astype(LOW)
        stores[up].start()
        for c in range(0, hidden, 256):
            g_buf[down, c : c + 256] = mat_tn(act_buf[:, c : c + 256], grad_ref[...]).astype(LOW)
        stores[down].start()
    for store in stores:
        store.wait()


def mlp_step(frames, place, scale, mlp_in, packs, weights, cots=None, carried=None, after=()):
    rows, width = mlp_in.shape
    count = len(packs)
    first = cots is not None
    hidden = packs[0].shape[1]
    step = rows // frames
    ins = [place, scale, mlp_in, *packs, *(cots if first else carried)]
    shapes = [shaped((frames, step, width), LOW), shaped((rows, width), LOW)] if first else []
    shapes += [shaped((rows, width), F32)] * 2 + [shaped((count, 1, hidden), F32)]
    grads = [shaped((width + hidden, width), LOW)] * count
    scratch = [
        pltpu.VMEM((2 * count, width, hidden), LOW),
        pltpu.VMEM((2 * count, width, hidden), LOW),
        pltpu.VMEM((rows, hidden), LOW),
        pltpu.VMEM((rows, hidden), LOW),
        pltpu.SemaphoreType.DMA((2 * count, 2)),
        pltpu.SemaphoreType.DMA((2 * count,)),
    ]
    if first:
        scratch.append(pltpu.VMEM((width, -(-step // 128) * 128), LOW))
    return call(
        functools.partial(mlp_kernel, frames, count, first, len(after)),
        "mlp",
        19.5,
        in_specs=[SMEM, SMEM, VMEM] + [VMEM] * (len(ins) - 3) + [ANY] * (len(weights) + len(after)),
        out_specs=[VMEM] * len(shapes) + [ANY] * len(grads),
        out_shape=shapes + grads,
        scratch_shapes=scratch,
    )(*ins, *weights, *after)


def attn_backward_kernel(
    shards, waits, place_ref, scale_ref, gain_ref, mlp_gain_ref, res_ref, acc_ref, gacc_ref, mlp_normed_ref, mlp_inv_ref, cot_ref,
    normed_ref, inv_ref, heads_ref, prob_ref, *refs
):
    packs, refs = refs[:shards], refs[shards:]
    ups, refs = refs[: shards // 2], refs[shards // 2 :]
    outs = shards + 3 + 2
    weights, refs = refs[: len(refs) - outs - waits], refs[len(refs) - outs :]
    pieces, refs = refs[:shards], refs[shards:]
    proj_ref, low_ref, sums_ref, w_buf, w_sem = refs
    part = heads_ref.shape[4]
    patches = pieces[0].shape[3]
    seq_pad, width = res_ref.shape[1:]
    gain, mlp_gain = row_of(gain_ref), row_of(mlp_gain_ref)
    frame = pl.program_id(0)
    wide_idx = place_ref[0]
    copies = weight_copies(weights, shards, place_ref, w_buf, w_sem)

    @pl.when(frame == 0)
    def _():
        start_all(copies)
        sums_ref[...] = jnp.zeros_like(sums_ref)
        rows = [ref[i] for ref in ups for i in range(2)]
        for k, values in enumerate(reorder(rows, wide_idx)):
            sums_ref[6 + k] = values

    def columns(values, i):
        blocks = values.T
        blocks = reorder([blocks[j * part : (j + 1) * part, :patches] for j in range(shards)], wide_idx)
        for ref, block in zip(pieces, blocks):
            ref[0, i] = block

    down_bias = jnp.concatenate(reorder([p[1:2, 3 * part : 4 * part] for p in packs], wide_idx), axis=1)
    columns((res_ref[0] + acc_ref[0] + down_bias).astype(LOW), 0)
    grad_res = cot_ref[0].astype(F32) * scale_ref[frame]
    gacc, mlp_normed = gacc_ref[0], mlp_normed_ref[0]
    hidden = grad_res + norm_back(gacc, mlp_normed, mlp_inv_ref[0], mlp_gain)

    def add_sum(row, values):
        sums_ref[row] += jnp.sum(values, axis=0, keepdims=True)

    add_sum(0, grad_res)
    add_sum(1, gacc * mlp_normed)
    add_sum(2, gacc)
    add_sum(3, hidden)
    low = hidden.astype(LOW)
    low_ref[0] = low
    masks = head_masks(part)
    scale = HD ** (-0.5)
    back = jnp.zeros(hidden.shape, F32)
    bias_sums = []

    @pl.when(frame == 0)
    def _():
        wait_all(copies)

    for k in range(shards):
        grad_mix = mat_nt(low, w_buf[k, 3 * part :]).astype(LOW)
        queries, keys, values = heads_ref[0, k, 0], heads_ref[0, k, 1], heads_ref[0, k, 2]
        prob_low = prob_ref[0, k]
        prob = prob_low.astype(F32)
        mix_heads = stack_heads(grad_mix, masks)
        grad_value = mat_tn(prob_low, mix_heads)
        grad_prob = mat_nt(mix_heads, values)
        grad_score = (
            prob * (grad_prob - jnp.sum(prob * grad_prob, axis=-1, keepdims=True))
        ).astype(LOW)
        grad_query = pick_heads(mat_mul(grad_score, keys), masks)
        grad_key = mat_tn(grad_score, stack_heads(queries, masks))
        proj = jnp.concatenate([grad_query * scale, grad_key * scale, grad_value], axis=1).astype(LOW)
        proj_ref[0, k] = proj
        bias_sums.append(jnp.sum(proj.astype(F32), axis=0, keepdims=True))
        back += mat_mul(proj, w_buf[k, : 3 * part])
    for i, at in ((6 + shards, 0), (7 + shards, 2 * part)):
        own = reorder([values[:, at : at + part] for values in bias_sums], wide_idx)
        sums_ref[i] += jnp.concatenate(own, axis=1)
    normed = normed_ref[0]
    add_sum(4, back * normed)
    add_sum(5, back)
    total = hidden + norm_back(back, normed, inv_ref[0], gain)
    row = lax.broadcasted_iota(jnp.int32, (seq_pad, 1), 0)
    sums_ref[8 + shards + frame] = jnp.sum(jnp.where(row == patches, total, 0.0), axis=0, keepdims=True)
    columns(total.astype(LOW), 1)


def attn_backward(patches, place, scale, vecs, per_frame, packs, ups, weights, after):
    frames, seq_pad, width = per_frame[0].shape
    heads = per_frame[8]
    shards, part = heads.shape[1], heads.shape[4]
    blocks = [(frames, 2, part, patches)] * shards
    proj = (frames, shards, seq_pad, 3 * part)
    return call(
        functools.partial(attn_backward_kernel, shards, len(after)),
        "attn_backward",
        24.0,
        grid=(frames,),
        in_specs=[SMEM, SMEM]
        + [whole(v) for v in vecs]
        + [per_step(v.shape) for v in per_frame]
        + [whole(v) for v in list(packs) + list(ups)]
        + [ANY] * (len(weights) + len(after)),
        out_specs=[per_step(b) for b in blocks]
        + [per_step(proj), per_step((frames, seq_pad, width)), fixed((8 + shards + frames, 1, width))],
        out_shape=[shaped(b, LOW) for b in blocks]
        + [
            shaped(proj, LOW),
            shaped((frames, seq_pad, width), LOW),
            shaped((8 + shards + frames, 1, width), F32),
        ],
        scratch_shapes=[
            pltpu.VMEM((shards, 4 * part, width), LOW),
            pltpu.SemaphoreType.DMA((shards, 2)),
        ],
    )(place, scale, *vecs, *per_frame, *packs, *ups, *weights, *after)


def attn_grads_kernel(waits, attn_in_ref, low_ref, proj_ref, mix_ref, *refs):
    grad_refs, (proj_buf, mix_buf) = refs[waits:-2], refs[-2:]
    count = len(grad_refs)
    frames, seq_pad, part = mix_ref.shape[0], mix_ref.shape[2], mix_ref.shape[3]
    for i in range(count):
        for f in range(frames):
            at = slice(f * seq_pad, (f + 1) * seq_pad)
            proj_buf[at] = proj_ref[f, i]
            mix_buf[at] = mix_ref[f, i]
        for c in range(0, 3 * part, part):
            grad_refs[i][c : c + part] = mat_tn(proj_buf[:, c : c + part], attn_in_ref[...]).astype(LOW)
        grad_refs[i][3 * part :] = mat_tn(mix_buf[...], low_ref[...]).astype(LOW)


def attn_grads(attn_in, proj, low, mix, after):
    frames, shards, seq_pad, part = mix.shape
    width = attn_in.shape[-1]
    rows = frames * seq_pad
    return call(
        functools.partial(attn_grads_kernel, len(after)),
        "attn_grads",
        0.0,
        grid=(1,),
        in_specs=[fixed((rows, width)), fixed((rows, width)), fixed(proj.shape), fixed(mix.shape)] + [ANY] * len(after),
        out_specs=[fixed((4 * part, width))] * shards,
        out_shape=[shaped((4 * part, width), LOW)] * shards,
        scratch_shapes=[pltpu.VMEM((rows, 3 * part), LOW), pltpu.VMEM((rows, part), LOW)],
    )(attn_in.reshape(rows, width), low.reshape(rows, width), proj, mix, *after)


def same_video(place_ref, group, rows, columns):
    first = pl.program_id(0) * columns

    def video(position):
        position = position + first
        return (((position // group) ^ place_ref[2]) * group + position % group) // VIDEO_FRAMES

    row = lax.broadcasted_iota(jnp.int32, (rows, columns), 0) % columns
    column = lax.broadcasted_iota(jnp.int32, (rows, columns), 1)
    return video(row) == video(column)


def message_forward_kernel(
    group, waits, place_ref, cls_ref, weight_ref, m_bias_ref, gain_ref, shift_ref, offset_ref, flat_ref, bias_ref,
    proj_ref, *refs
):
    normed_ref, inv_ref, in_ref, heads_ref, prob_ref, mix_ref, base_ref, sum_ref = refs[waits:]
    part = proj_ref.shape[0]
    chunk = cls_ref.shape[0]
    message = mat_mul(cls_ref[...], weight_ref[...]) + row_of(m_bias_ref)
    normed, inv = normalize(message)
    normed_ref[...] = normed
    inv_ref[...] = inv
    msg_in = (normed * row_of(gain_ref) + row_of(shift_ref)).astype(LOW)
    in_ref[...] = msg_in
    proj = mat_nt(msg_in, flat_ref[...])
    queries = (proj[:, :part] + bias_ref[0:1]).astype(LOW)
    keys = proj[:, part : 2 * part].astype(LOW)
    values = (proj[:, 2 * part :] + bias_ref[1:2]).astype(LOW)
    heads_ref[0, 0] = queries
    heads_ref[0, 1] = keys
    heads_ref[0, 2] = values
    masks = head_masks(part)
    scores = mat_nt(stack_heads(queries, masks, HD ** (-0.5)), keys)
    scores = jnp.where(same_video(place_ref, group, len(masks) * chunk, chunk), scores, -1e30)
    exps = jnp.exp(scores - jnp.max(scores, axis=-1, keepdims=True))
    prob = exps / jnp.sum(exps, axis=-1, keepdims=True)
    prob_ref[0] = prob
    mix = pick_heads(mat_mul(prob.astype(LOW), values), masks).astype(LOW)
    mix_ref[...] = mix

    @pl.when(pl.program_id(0) == 0)
    def _():
        base_ref[...] = message[:group] + row_of(offset_ref)
        sum_ref[...] = mat_mul(mix, proj_ref[...])[:group]


def message_forward(chunk, group, place, cls_rows, weight, vecs, flat, bias, proj, after):
    count, width = cls_rows.shape
    part = proj.shape[0]
    heads = part // HD
    chunks = count // chunk
    rows = lambda columns: pl.BlockSpec((chunk, columns), lambda c: (c, 0))
    return call(
        functools.partial(message_forward_kernel, group, len(after)),
        "message_forward",
        4.2,
        grid=(chunks,),
        in_specs=[SMEM, rows(width)]
        + [whole(v) for v in (weight, *vecs, flat, bias, proj)]
        + [ANY] * len(after),
        out_specs=[
            rows(width), rows(1), rows(width),
            per_step((chunks, 3, chunk, part)), per_step((chunks, heads * chunk, chunk)),
            rows(part), fixed((group, width)), fixed((group, width)),
        ],
        out_shape=[
            shaped((count, width), F32),
            shaped((count, 1), F32),
            shaped((count, width), LOW),
            shaped((chunks, 3, chunk, part), LOW),
            shaped((chunks, heads * chunk, chunk), F32),
            shaped((count, part), LOW),
            shaped((group, width), F32),
            shaped((group, width), F32),
        ],
    )(place, cls_rows, weight, *vecs, flat, bias, proj, *after)


def message_backward_kernel(
    waits, count, wide, place_ref, all_ref, in_ref, heads_ref, prob_ref, mix_ref, flat_ref, proj_ref, *refs
):
    grad_ref, sums_ref, grad_flat_ref, grad_proj_ref, sum_grad_ref, sum_cross_ref, back_ref = refs[waits:]
    frames = all_ref.shape[1] - count
    group = frames * wide
    step = pl.program_id(0)

    @pl.when(step == 0)
    def _():
        for ref in (grad_flat_ref, grad_proj_ref, sum_grad_ref, sum_cross_ref):
            ref[...] = jnp.zeros_like(ref)
        total = all_ref[0, :count]
        for d in range(1, all_ref.shape[0]):
            total += all_ref[d, :count]
        sums_ref[...] = total

    groups = grad_ref.shape[0] // group
    for b in range(groups):
        holder = ((step * groups + b) ^ place_ref[2]) * wide
        for w in range(wide):
            at = b * group + w * frames
            grad_ref[at : at + frames] = all_ref[holder + w, count:]

    part = proj_ref.shape[0]
    masks = head_masks(part)
    grad = grad_ref[:, 0].astype(LOW)
    sum_grad_ref[...] += jnp.sum(grad.astype(F32), axis=0, keepdims=True)
    grad_proj_ref[...] += mat_tn(mix_ref[...], grad)
    grad_mix = mat_nt(grad, proj_ref[...]).astype(LOW)
    mix_heads = stack_heads(grad_mix, masks)
    queries, keys, values = heads_ref[0, 0], heads_ref[0, 1], heads_ref[0, 2]
    prob = prob_ref[0]
    grad_prob = mat_nt(mix_heads, values)
    grad_score = prob * (grad_prob - jnp.sum(prob * grad_prob, axis=-1, keepdims=True))
    score_low = grad_score.astype(LOW)
    grad_query = pick_heads(mat_mul(score_low, keys), masks) * HD ** (-0.5)
    grad_key = mat_tn(score_low, stack_heads(queries, masks)) * HD ** (-0.5)
    grad_value = mat_tn(prob.astype(LOW), mix_heads)
    cross = jnp.concatenate([grad_query, grad_key, grad_value], axis=1).astype(LOW)
    sum_cross_ref[...] += jnp.sum(cross.astype(F32), axis=0, keepdims=True)
    grad_flat_ref[...] += mat_tn(cross, in_ref[...])
    back_ref[...] = mat_mul(cross, flat_ref[...])


def message_backward(place, count, wide, gathered, msg_in, heads, prob, mix, flat, proj, after):
    total, width = msg_in.shape
    part = proj.shape[0]
    chunks, _, chunk, _ = heads.shape
    rows = lambda columns: pl.BlockSpec((chunk, columns), lambda c: (c, 0))
    shapes = [(count, 1, width), (3 * part, width), (part, width), (1, width), (1, 3 * part)]
    return call(
        functools.partial(message_backward_kernel, len(after), count, wide),
        "message_backward",
        0.0,
        grid=(chunks,),
        in_specs=[SMEM, whole(gathered), rows(width), per_step(heads.shape), per_step(prob.shape), rows(part)]
        + [whole(flat), whole(proj)]
        + [ANY] * len(after),
        out_specs=[pl.BlockSpec((chunk, 1, width), lambda c: (c, 0, 0))] + [fixed(s) for s in shapes] + [rows(width)],
        out_shape=[shaped(s, F32) for s in [(total, 1, width)] + shapes + [(total, width)]],
    )(place, gathered, msg_in, heads, prob, mix, flat, proj, *after)


def message_end_kernel(
    group, grad_ref, back_ref, other_ref, normed_ref, inv_ref, gain_ref, cls_ref, weight_ref, grad_weight_ref,
    sums_ref, grad_cls_ref
):
    @pl.when(pl.program_id(0) == 0)
    def _():
        grad_weight_ref[...] = jnp.zeros_like(grad_weight_ref)
        sums_ref[...] = jnp.zeros_like(sums_ref)

    back = back_ref[...] + other_ref[...].astype(F32)
    normed = normed_ref[...]
    grad = grad_ref[:, 0] + norm_back(back, normed, inv_ref[...], row_of(gain_ref))
    low = grad.astype(LOW)
    for row, values in enumerate((low.astype(F32), back * normed, back)):
        sums_ref[row : row + 1] += jnp.sum(values, axis=0, keepdims=True)
    grad_weight_ref[...] += mat_tn(cls_ref[...], low)

    @pl.when(pl.program_id(0) == 0)
    def _():
        grad_cls_ref[...] = mat_nt(weight_ref[...], low)[:, :group]


def message_end(chunk, group, grad, back, other, normed, inv, gain, cls_rows, weight):
    count, _, width = grad.shape
    rows = lambda columns: pl.BlockSpec((chunk, columns), lambda c: (c, 0))
    return call(
        functools.partial(message_end_kernel, group),
        "message_end",
        0.0,
        grid=(count // chunk,),
        in_specs=[pl.BlockSpec((chunk, 1, width), lambda c: (c, 0, 0))] + [rows(width)] * 3 + [rows(1), whole(gain), rows(width), whole(weight)],
        out_specs=[fixed((width, width)), fixed((8, width)), fixed((width, group))],
        out_shape=[shaped((width, width), F32), shaped((8, width), F32), shaped((width, group), F32)],
    )(grad, back, other, normed, inv, gain, cls_rows, weight)


def row_at(place_ref, base, moves):
    at = base
    for bit, rows, flipped in moves:
        is_set = (place_ref[2] // bit) % 2
        at = at + rows * ((1 - is_set) if flipped else is_set)
    return pl.multiple_of(at, ROW_TILE)


def add_kernel(sums, waits, outs, place_ref, *refs):
    count = max(i for _, rows, _ in sums for i, _, _ in rows) + 1
    terms, refs = refs[:count], refs[count + waits :]
    out_refs, sem = refs[:outs], refs[-1]
    bufs = refs[outs:-1]
    copies = []
    for n, (_, rows, size) in enumerate(sums):
        for j, (i, base, moves) in enumerate(rows):
            source = terms[i].at[pl.ds(row_at(place_ref, base, moves), size)]
            copies.append(pltpu.make_async_copy(source, bufs[n].at[j], sem.at[len(copies)]))
    for copy in copies:
        copy.start()
    done = 0
    for n, ((out, at), rows, size) in enumerate(sums):
        for copy in copies[done : done + len(rows)]:
            copy.wait()
        done += len(rows)
        step = size // 2 if size % (2 * ROW_TILE) == 0 else size
        for r in range(0, size, step):
            total = bufs[n][0, r : r + step].astype(F32)
            for j in range(1, len(rows)):
                total += bufs[n][j, r : r + step].astype(F32)
            out_refs[out][at + r : at + r + step] = total.astype(LOW)


def added(place, sums, after=(), together=False):
    arrays, listed = [], []
    for terms, size in sums:
        rows = []
        for array, base, moves in terms:
            known = [i for i, other in enumerate(arrays) if other is array]
            if not known:
                arrays.append(array)
            rows.append((known[0] if known else len(arrays) - 1, base, moves))
        to = (0, sum(other[2] for other in listed)) if together else (len(listed), 0)
        listed.append((to, rows, size))
    width = arrays[0].shape[1]
    sizes = [sum(item[2] for item in listed)] if together else [item[2] for item in listed]
    return call(
        functools.partial(add_kernel, listed, len(after), len(sizes)),
        "added",
        in_specs=[SMEM] + [ANY] * (len(arrays) + len(after)),
        out_specs=[VMEM] * len(sizes),
        out_shape=[shaped((size, width), LOW) for size in sizes],
        scratch_shapes=[pltpu.VMEM((len(rows), size, width), LOW) for _, rows, size in listed]
        + [pltpu.SemaphoreType.DMA((sum(len(rows) for _, rows, _ in listed),))],
    )(place, *arrays, *after)


def join_kernel(bits, waits, place_ref, *refs):
    count = len(bits)
    pairs, refs = [refs[2 * i : 2 * i + 2] for i in range(count)], refs[2 * count + waits :]
    *out_refs, buf, sem = refs
    size = pairs[0][0].shape[0]
    copies = []
    for n, bit in enumerate(bits):
        for i, ref in enumerate(pairs[n]):
            at = row_at(place_ref, n * 2 * size, [(bit, size, i == 1)])
            copies.append(pltpu.make_async_copy(ref, buf.at[pl.ds(at, size)], sem.at[n, i]))
    for copy in copies:
        copy.start()
    for copy in copies:
        copy.wait()
    first = 0
    for ref in out_refs:
        rows = ref.shape[0]
        step = rows // 2 if rows % (2 * ROW_TILE) == 0 else rows
        for at in range(0, rows, step):
            ref[at : at + step] = buf[first + at : first + at + step].astype(ref.dtype)
        first += rows


def joined(place, pairs, bits, dtype, after=(), splits=None):
    size, width = pairs[0][0].shape
    count = len(pairs)
    outs = [(rows, width) for rows in splits or [2 * size] * count]
    return call(
        functools.partial(join_kernel, bits, len(after)),
        "joined",
        in_specs=[SMEM] + [ANY] * (2 * count + len(after)),
        out_specs=[VMEM] * len(outs),
        out_shape=[shaped(out, dtype) for out in outs],
        scratch_shapes=[pltpu.VMEM((2 * size * count, width), LOW), pltpu.SemaphoreType.DMA((count, 2))],
    )(place, *[ref for pair in pairs for ref in pair], *after)


def gate_kernel(*refs):
    pass


def gate(arrays, after, micros=0.0):
    count = len(arrays)
    return list(call(
        gate_kernel,
        "gate",
        micros,
        in_specs=[ANY] * (count + len(after)),
        out_specs=[ANY] * count,
        out_shape=[shaped(v.shape, v.dtype) for v in arrays],
        input_output_aliases={i: i for i in range(count)},
    )(*arrays, *after))


def collect_kernel(place_ref, *refs):
    *pieces, grad_cls_ref, tok_ref, grad_ref = refs
    frames, _, part, patches = pieces[0].shape
    own = grad_cls_ref[pl.ds(pl.multiple_of(place_ref[0] * part, part), part), :]
    lane = lax.broadcasted_iota(jnp.int32, (part, patches), 1)
    for j, piece in enumerate(reorder([ref[...] for ref in pieces], place_ref[0])):
        for f in range(frames):
            i = j * frames + f
            tok_ref[i] = piece[f, 0]
            grad = piece[f, 1].astype(F32)
            grad_ref[i] = jnp.where(lane == 0, grad + own[:, i : i + 1], grad).astype(LOW)


def collect(place, pieces, grad_cls):
    frames, _, part, patches = pieces[0].shape
    shape = (frames * len(pieces), part, patches)
    return call(
        collect_kernel,
        "collect",
        0.0,
        in_specs=[SMEM] + [VMEM] * (len(pieces) + 1),
        out_specs=[VMEM] * 2,
        out_shape=[shaped(shape, LOW)] * 2,
    )(place, *pieces, grad_cls)


def swap(block, axis, flip):
    return lax.ppermute(block, axis, [(i, i ^ flip) for i in range(lax.axis_size(axis))])


def nothing(array):
    one = lax.slice(array, (0,) * array.ndim, (1,) * array.ndim).reshape(()).astype(F32)
    return one * 0.0


def zero_of(*arrays):
    return sum(nothing(array) for array in arrays).astype(jnp.int32)


def frames_in(block, after):
    count = lax.axis_size("wide")
    index = lax.axis_index("wide")
    part = block.shape[0] // count
    begin = zero_of(after)
    pieces = [lax.dynamic_slice_in_dim(block, (index ^ k) * part + begin, part, 0) for k in range(count)]
    return [piece if k == 0 else swap(piece, "wide", k) for k, piece in enumerate(pieces)]


def send_half(block, after):
    odd = lax.axis_index("narrow") & 1
    half = block.shape[0] // 2
    sent = lax.dynamic_slice_in_dim(block, odd * half + zero_of(after), half, 0)
    return [swap(sent, "wide", bit) for bit in bits_of(lax.axis_size("wide"))[1:]]


def near_shards(block):
    return [block, swap(block, "wide", 1)]


def far_shards(near, far):
    return [near, far, swap(near, "wide", 1), swap(far, "wide", 1)]


def orders(count):
    bits = bits_of(lax.axis_size("narrow"))[:count]
    return [bits, bits[1:] + bits[:1]]


def regions_of(arrays, base=0):
    half = arrays[0].shape[0] // 2
    return [[(array, n * half, []) for array in arrays] for n in range(2)], half


def halving(place, regions, size, steps):
    after = ()
    for at in range(steps):
        bits = [order[at] for order in orders(steps)]
        size = size // 2
        sums = [
            ([(array, base, moves + [(bit, size, True)]) for array, base, moves in terms], size)
            for bit, terms in zip(bits, regions)
        ]
        sent = added(place, sums, after)
        received, after = yield sent, [swap(block, "narrow", bit) for block, bit in zip(sent, bits)]
        regions = [
            [(array, base, moves + [(bit, size, False)]) for array, base, moves in terms] + [(block, 0, [])]
            for bit, terms, block in zip(bits, regions, received)
        ]
    return regions, size, after


def joining(place, blocks, steps, splits):
    for at in reversed(range(steps)):
        bits = [order[at] for order in orders(steps)]
        others, after = yield blocks, [swap(block, "narrow", bit) for block, bit in zip(blocks, bits)]
        last = at == 0
        blocks = joined(
            place, list(zip(blocks, others)), bits, F32 if last else LOW, after, splits if last else None
        )
    return blocks


def whole_sum(place, blocks, steps):
    for bit in bits_of(lax.axis_size("narrow"))[steps:]:
        others, after = yield blocks, [swap(block, "narrow", bit) for block in blocks]
        blocks = added(
            place, [([(a, 0, []), (b, 0, [])], a.shape[0]) for a, b in zip(blocks, others)], after
        )
    return blocks


class Chain:
    def __init__(self, steps):
        self.steps = steps
        self.value = None
        self.turns = 0
        self.sent, self.received = next(steps)

    def turn(self, *after):
        if self.value is not None:
            return after[0]
        self.turns += 1
        try:
            self.sent, self.received = self.steps.send((self.received, after))
        except StopIteration as end:
            self.value = end.value
            return after[0] if isinstance(self.value, tuple) else self.value[0]
        return self.sent[0]


ORDER = "foAfoaPMBafaEfaCf"


def body(
    frame_tokens,
    cotangent,
    caption_count,
    caption_len,
    message_weight,
    message_bias,
    message_gain,
    message_shift,
    cross_qkv,
    cross_bias,
    cross_proj,
    cross_offset,
    attn_gain,
    attn_shift,
    qkv_weight,
    qkv_bias,
    out_weight,
    out_bias,
    mlp_gain,
    mlp_shift,
    up_weight,
    up_bias,
    down_weight,
    down_bias,
):
    group, patches, part = frame_tokens.shape
    width = message_weight.shape[0]
    hidden = up_weight.shape[1]
    wide = lax.axis_size("wide")
    narrow = lax.axis_size("narrow")
    wide_idx = lax.axis_index("wide")
    narrow_idx = lax.axis_index("narrow")
    frames = group // wide
    seq_pad = -(-(patches + 1) // ROW_TILE) * ROW_TILE
    rows = frames * seq_pad
    all_frames = group * narrow
    chunk = max(c for c in range(VIDEO_FRAMES, 129, VIDEO_FRAMES) if all_frames % c == 0 and c % group == 0)
    place = jnp.stack([wide_idx, narrow_idx & 1, narrow_idx]).astype(jnp.int32)

    def own_cols(values):
        return lax.dynamic_slice_in_dim(values, wide_idx * part, part, values.ndim - 1)

    tokens_t = frame_tokens.transpose(0, 2, 1)
    pack = jnp.concatenate(
        [up_bias, qkv_bias.reshape(-1), out_bias, down_bias, frame_tokens[:, 0, :].astype(F32).reshape(-1)]
    ).reshape(-1, width)
    packs = [pack] + [swap(pack, "wide", k) for k in range(1, wide)]
    cls_rows = jnp.concatenate(
        reorder([p[2:].reshape(group, part).astype(LOW) for p in packs], wide_idx), axis=1
    )
    cls_own = cls_rows
    toks = frames_in(tokens_t, cls_own)
    attn_own = jnp.concatenate(
        [qkv_weight.transpose(1, 2, 0).reshape(3 * part, width), out_weight], axis=0
    )
    attn_near = send_half(attn_own, cls_own)
    narrow_bits = bits_of(narrow)
    cls_next = swap(cls_rows, "narrow", 1)
    cls_rows = jnp.concatenate([cls_rows, cls_next], axis=0)
    attn_near = gate(attn_near, [cls_next, toks[1]])
    attn_far = [swap(near, "narrow", 1) for near in attn_near]
    (cls_rows,) = gate([cls_rows], attn_near)
    for bit in narrow_bits[1:]:
        if bit == narrow_bits[-1]:
            (cls_rows,) = gate([cls_rows], attn_far)
        cls_rows = jnp.concatenate([cls_rows, swap(cls_rows, "narrow", bit)], axis=0)
    attn_weights = near_shards(attn_own)
    for near, far in zip(attn_near, attn_far):
        attn_weights += far_shards(near, far)
    cots = frames_in(cotangent.transpose(0, 2, 1), attn_near[0])

    caption_slot = jnp.arange(caption_len.shape[1])
    word_total = jnp.sum(
        jnp.where(caption_slot[None, :] < caption_count[:, None], caption_len, 0), axis=1
    ).astype(F32)
    video_scale = word_total / jnp.mean(word_total)
    own_video = (narrow_idx * group + wide_idx * frames + jnp.arange(frames)) // VIDEO_FRAMES
    video_match = own_video[:, None] == jnp.arange(video_scale.shape[0])[None, :]
    scale = jnp.sum(jnp.where(video_match, video_scale[None, :], 0.0), axis=1)

    cross_flat = cross_qkv.transpose(1, 2, 0).reshape(3 * part, width)
    msg_normed, msg_inv, msg_in, cross_heads, cross_prob, cross_mix, base, group_sum = message_forward(
        chunk, group, place, cls_rows, message_weight,
        (message_bias, message_gain, message_shift, cross_offset), cross_flat, cross_bias, cross_proj,
        attn_far + toks[1:],
    )
    group_sums = [group_sum] + [swap(group_sum, "wide", k) for k in range(1, wide)]

    odd, begin = narrow_idx & 1, zero_of(*cots[2:])
    half = width // 2
    mlp_half = jnp.concatenate(
        [lax.dynamic_slice_in_dim(w, odd * half + begin, half, 0) for w in (up_weight, down_weight)], axis=0
    )
    mlp_near = [swap(mlp_half, "wide", bit) for bit in bits_of(wide)[1:]]
    up_shards, down_shards = near_shards(up_weight), near_shards(down_weight)

    (normed, inv, attn_in, heads, prob, mix, hidden_res, mlp_normed, mlp_inv, mlp_in) = attn_forward(
        seq_pad, place, (attn_gain, attn_shift, mlp_gain, mlp_shift), base, toks, group_sums, packs, attn_weights,
        [up_shards[1], down_shards[1]] + cots[1:],
    )
    mlp_in = mlp_in.reshape(rows, width)
    bits = bits_of(narrow)
    size = width + hidden
    mlp_near = gate(mlp_near, [mlp_in])
    cot, grad_rows, acc, gacc, sum_up, *grad_own = mlp_step(
        frames, place, scale, mlp_in, packs[:2], up_shards + down_shards, cots=cots, after=mlp_near
    )
    *mlp_far, grad_next = gate([swap(near, "narrow", 1) for near in mlp_near] + [grad_own[1]], [acc])
    def split_steps(rows):
        count = 0
        while count < len(bits) and rows % (2 * ROW_TILE) == 0:
            rows, count = rows // 2, count + 1
        return count

    mlp_steps, attn_count = split_steps(size // 2), split_steps(2 * part)
    own = Chain(halving(place, *regions_of([grad_own[0], swap(grad_next, "wide", 1)]), mlp_steps))
    mlp_weights = [piece for near, far in zip(mlp_near, mlp_far) for piece in far_shards(near, far)]
    acc, gacc, sum_up_far, *grad_far = mlp_step(
        frames, place, scale, mlp_in, packs[2:], mlp_weights, carried=(grad_rows, acc, gacc), after=own.sent
    )

    def far_steps(arrays):
        regions, left, after = yield from halving(place, *regions_of(arrays), mlp_steps)
        value = added(place, [(terms, left) for terms in regions], after, True)
        crossed, after = yield value, [swap(value[0], "wide", 2)]
        blocks = added(
            place,
            [(terms + [(crossed[0], n * left, [])], left) for n, terms in enumerate(own.value[0])],
            after,
        )
        blocks = yield from whole_sum(place, blocks, mlp_steps)
        return (yield from joining(place, blocks, mlp_steps, [width, hidden]))

    def attn_steps(arrays):
        regions, left, after = yield from halving(place, *regions_of(arrays), attn_count)
        blocks = added(place, [(terms, left) for terms in regions], after)
        blocks = yield from whole_sum(place, blocks, attn_count)
        return (yield from joining(place, blocks, attn_count, [3 * part, part]))

    own.turn(acc)
    grad_far = gate(grad_far, own.sent)
    far = Chain(far_steps([grad_far[0], swap(grad_far[1], "wide", 1)]))

    shape = (frames, seq_pad, width)
    per_frame = (
        hidden_res, acc.reshape(shape), gacc.reshape(shape), mlp_normed, mlp_inv, cot, normed, inv, heads, prob
    )
    *blocks, proj, low, sums = attn_backward(
        patches, place, scale, (attn_gain, mlp_gain), per_frame, packs, [sum_up, sum_up_far], attn_weights,
        own.sent + far.sent,
    )
    count = 8 + wide
    gathered = lax.all_gather(sums, ("narrow", "wide"))
    far.turn(own.turn(low))
    grad_attn = attn_grads(attn_in, proj, low, mix, own.sent + far.sent)
    last = grad_attn[0]
    while far.turns < mlp_steps - 1:
        last = far.turn(last)
    grad_attn = gate(grad_attn, [last])
    attn_next, attn_last = (swap(grad_attn[k], "wide", 1) for k in (1, 3))
    last = added(place, [([(grad_attn[2], 0, []), (attn_last, 0, [])], 4 * part)])[0]
    attn_received = swap(last, "wide", 2)
    attn = pieces = None
    for step in ORDER:
        if step == "f":
            while far.turns == mlp_steps and own.value is None:
                last = own.turn(last)
            last = far.turn(last)
        elif step == "o":
            last = own.turn(last)
        elif step == "a":
            last = attn.turn(last)
        elif step == "A":
            attn_received, attn_next = gate([attn_received, attn_next], [last, *own.received])
            attn = Chain(attn_steps([grad_attn[0], attn_next, attn_received]))
            last = attn.sent[0]
        elif step == "P":
            blocks = gate(blocks, [last])
            pieces = [piece if k == 0 else swap(piece, "wide", k) for k, piece in enumerate(blocks)]
        elif step == "M":
            grad_msg, sums, grad_cross_flat, grad_cross_proj, sum_cross_grad, sum_cross, back = message_backward(
                place, count, wide, gathered, msg_in, cross_heads, cross_prob, cross_mix, cross_flat, cross_proj, [last]
            )
            last = back
        elif step == "B":
            for bit in bits_of(wide)[:-1]:
                back = back + gate([swap(back, "wide", bit)], [last])[0]
            other = swap(back.astype(LOW), "wide", bits_of(wide)[-1])
            last = back
        elif step == "E":
            grad_message_weight, msg_sums, grad_cls = message_end(
                chunk, group, grad_msg, back, gate([other], [last])[0], msg_normed, msg_inv, message_gain, cls_rows,
                message_weight,
            )
            last = grad_message_weight
        elif step == "C":
            output_tokens, grad_tokens = collect(place, pieces[:1] + gate(pieces[1:], [last]), grad_cls)
            last = grad_tokens
    while attn.value is None or far.value is None:
        while far.turns == mlp_steps and own.value is None:
            last = own.turn(last)
        last = far.turn(attn.turn(last))
    sums = sums.reshape(count, width)
    grad_up_bias = lax.dynamic_slice_in_dim(sums[6 : 6 + wide].reshape(-1), wide_idx * hidden, hidden, 0)

    return (
        output_tokens.transpose(0, 2, 1),
        grad_tokens.transpose(0, 2, 1),
        grad_message_weight,
        msg_sums[0],
        msg_sums[1],
        msg_sums[2],
        grad_cross_flat.reshape(3, part, width).transpose(2, 0, 1),
        jnp.stack([sum_cross[0, :part], sum_cross[0, 2 * part :]]),
        grad_cross_proj,
        sum_cross_grad[0],
        sums[4],
        sums[5],
        attn.value[0].reshape(3, part, width).transpose(2, 0, 1),
        own_cols(sums[count - 2 :]),
        attn.value[1],
        own_cols(sums[3]),
        sums[1],
        sums[2],
        far.value[0],
        grad_up_bias,
        far.value[1],
        own_cols(sums[0]),
    )


def solution(mesh):
    return jax.shard_map(
        body,
        mesh=mesh,
        in_specs=(
            P("narrow", None, "wide"),
            P("narrow", None, "wide"),
            P(),
            P(),
            P(),
            P(),
            P(),
            P(),
            P(None, None, "wide"),
            P(None, "wide"),
            P("wide", None),
            P(),
            P(),
            P(),
            P(None, None, "wide"),
            P(None, "wide"),
            P("wide", None),
            P("wide"),
            P(),
            P(),
            P(None, "wide"),
            P("wide"),
            P("wide", None),
            P("wide"),
        ),
        out_specs=(
            P("narrow", None, "wide"),
            P("narrow", None, "wide"),
            P(),
            P(),
            P(),
            P(),
            P(None, None, "wide"),
            P(None, "wide"),
            P("wide", None),
            P(),
            P(),
            P(),
            P(None, None, "wide"),
            P(None, "wide"),
            P("wide", None),
            P("wide"),
            P(),
            P(),
            P(None, "wide"),
            P("wide"),
            P("wide", None),
            P("wide"),
        ),
        check_vma=False,
    )
```

```python
import functools
import jax
import jax.numpy as jnp
from jax import lax
from jax.experimental import pallas as pl
from jax.experimental.pallas import tpu as pltpu
from jax.sharding import PartitionSpec as P

VIDEO_FRAMES = 8
HD = 64
EPS = 1e-05
ROW_TILE = 16
LOW = jnp.bfloat16
F32 = jnp.float32
VMEM_LIMIT = 56 * 1024 * 1024
ANY = pl.BlockSpec(memory_space=pl.ANY)
VMEM = pl.BlockSpec(memory_space=pltpu.VMEM)
SMEM = pl.BlockSpec(memory_space=pltpu.SMEM)


def dot(left, right, dims):
    return lax.dot_general(left, right, (dims, ((), ())), preferred_element_type=F32)


def mat_mul(left, right):
    return dot(left, right, ((1,), (0,)))


def mat_tn(left, right):
    return dot(left, right, ((0,), (0,)))


def mat_nt(left, right):
    return dot(left, right, ((1,), (1,)))


def normalize(values):
    row_mean = jnp.mean(values, axis=-1, keepdims=True)
    centred = values - row_mean
    inv_std = lax.rsqrt(jnp.mean(centred * centred, axis=-1, keepdims=True) + EPS)
    return (centred * inv_std, inv_std)


def norm_back(grad_norm, normed, inv_std, norm_gain):
    scaled = grad_norm * norm_gain
    return inv_std * (
        scaled
        - jnp.mean(scaled, axis=-1, keepdims=True)
        - normed * jnp.mean(scaled * normed, axis=-1, keepdims=True)
    )


def bits_of(size):
    return [1 << b for b in range(size.bit_length() - 1)]


def reorder(parts, index):
    parts = list(parts)
    for bit in bits_of(len(parts)):
        odd = (index & bit) != 0
        parts = [jnp.where(odd, parts[k ^ bit], parts[k]) for k in range(len(parts))]
    return parts


def call(kernel, name, micros=0.0, **options):
    return pl.pallas_call(
        kernel,
        name=name,
        compiler_params=pltpu.CompilerParams(vmem_limit_bytes=VMEM_LIMIT),
        cost_estimate=pl.CostEstimate(
            flops=int(micros * 1.0e9), bytes_accessed=int(micros * 3.0e6), transcendentals=0
        ),
        **options,
    )


def shaped(shape, dtype):
    return jax.ShapeDtypeStruct(tuple(shape), dtype)


def whole(array):
    return pl.BlockSpec(array.shape, lambda *_: (0,) * array.ndim)


def fixed(shape):
    return pl.BlockSpec(tuple(shape), lambda *_: (0,) * len(shape))


def per_step(shape):
    return pl.BlockSpec((1,) + tuple(shape[1:]), lambda f: (f,) + (0,) * (len(shape) - 1))


def row_of(ref):
    return ref[...].reshape(1, -1)


def head_masks(width):
    lane = lax.broadcasted_iota(jnp.int32, (1, width), 1) // HD
    return [lane == h for h in range(width // HD)]


def stack_heads(values, masks, scale=1.0):
    return jnp.concatenate([values * jnp.where(m, scale, 0.0).astype(values.dtype) for m in masks], axis=0)


def pick_heads(values, masks):
    size = values.shape[0] // len(masks)
    picked = values[:size]
    for h in range(1, len(masks)):
        picked = jnp.where(masks[h], values[h * size : (h + 1) * size], picked)
    return picked


def weight_copies(refs, shards, place_ref, buf, sem):
    whole_count = 2 * shards - len(refs)
    odd = place_ref[1]
    copies = []
    for j in range(whole_count):
        copies.append([pltpu.make_async_copy(refs[j], buf.at[j], sem.at[j, 0])])
    rest = refs[whole_count:]
    for i in range(len(rest) // 2):
        half = rest[2 * i].shape[0]
        at = pl.multiple_of(odd * half, half)
        other = pl.multiple_of((1 - odd) * half, half)
        j = whole_count + i
        copies.append([
            pltpu.make_async_copy(rest[2 * i], buf.at[j, pl.ds(at, half)], sem.at[j, 0]),
            pltpu.make_async_copy(rest[2 * i + 1], buf.at[j, pl.ds(other, half)], sem.at[j, 1]),
        ])
    return copies


def start_all(copies):
    for group in copies:
        for copy in group:
            copy.start()


def wait_all(copies):
    for group in copies:
        for copy in group:
            copy.wait()


def attn_forward_kernel(waits, place_ref, gain_ref, shift_ref, mlp_gain_ref, mlp_shift_ref, base_ref, *refs):
    shards = refs[-3].shape[0]
    toks, refs = refs[:shards], refs[shards:]
    sums, refs = refs[:shards], refs[shards:]
    packs, refs = refs[:shards], refs[shards:]
    weights, refs = refs[: -14 - waits], refs[-14:]
    (normed_ref, inv_ref, attn_in_ref, heads_ref, prob_ref, mix_ref, hidden_ref, mlp_normed_ref,
     mlp_inv_ref, mlp_in_ref, tok_buf, w_buf, w_sem, msg_buf) = refs
    part, patches = toks[0].shape[1], toks[0].shape[2]
    seq_pad, width = normed_ref.shape[1], normed_ref.shape[2]
    frames = pl.num_programs(0)
    frame = pl.program_id(0)
    wide_idx = place_ref[0]
    copies = weight_copies(weights, shards, place_ref, w_buf, w_sem)

    @pl.when(frame == 0)
    def _():
        start_all(copies)
        tok_buf[...] = jnp.zeros_like(tok_buf)
        total = base_ref[...]
        for ref in sums:
            total += ref[...]
        msg_buf[...] = total

    for k in range(shards):
        at = pl.multiple_of((wide_idx ^ k) * part, part)
        at_frame = (wide_idx & 1) * frames + frame if k == 2 else 0
        tok_buf[pl.ds(at, part), :patches] = toks[k][at_frame]
    tokens = tok_buf[...].T[:seq_pad].astype(F32)
    group = msg_buf[...]
    own = lax.broadcasted_iota(jnp.int32, (group.shape[0], 1), 0) == wide_idx * frames + frame
    message = jnp.sum(jnp.where(own, group, 0.0), axis=0, keepdims=True)
    row = lax.broadcasted_iota(jnp.int32, (seq_pad, 1), 0)
    full = jnp.where(row == patches, message, tokens)
    normed, inv = normalize(full)
    normed_ref[0] = normed
    inv_ref[0] = inv
    gain, shift, mlp_gain, mlp_shift = map(row_of, (gain_ref, shift_ref, mlp_gain_ref, mlp_shift_ref))
    attn_in = (normed * gain + shift).astype(LOW)
    attn_in_ref[0] = attn_in
    masks = head_masks(part)
    live = lax.broadcasted_iota(jnp.int32, (1, seq_pad), 1) <= patches
    total = full + jnp.concatenate(reorder([p[1:2, 2 * part : 3 * part] for p in packs], wide_idx), axis=1)

    @pl.when(frame == 0)
    def _():
        wait_all(copies)

    heads = []
    for k in range(shards):
        proj = mat_nt(attn_in, w_buf[k, : 3 * part])
        queries = (proj[:, :part] + packs[k][1:2, :part]).astype(LOW)
        keys = proj[:, part : 2 * part].astype(LOW)
        values = (proj[:, 2 * part :] + packs[k][1:2, part : 2 * part]).astype(LOW)
        heads_ref[0, k, 0] = queries
        heads_ref[0, k, 1] = keys
        heads_ref[0, k, 2] = values
        heads.append((queries, keys, values))

    def score(k):
        queries, keys, _ = heads[k]
        return mat_nt(stack_heads(queries, masks, HD ** (-0.5)), keys)

    scores = [score(0)]
    for k in range(shards):
        if k + 1 < shards:
            scores.append(score(k + 1))
        live_scores = jnp.where(live, scores[k], -1e30)
        exps = jnp.exp(live_scores - jnp.max(live_scores, axis=-1, keepdims=True))
        prob = (exps * (1.0 / jnp.sum(exps, axis=-1, keepdims=True))).astype(LOW)
        prob_ref[0, k] = prob
        mix_low = pick_heads(mat_mul(prob, heads[k][2]), masks).astype(LOW)
        mix_ref[0, k] = mix_low
    for k in range(shards):
        total += mat_mul(mix_ref[0, k], w_buf[k, 3 * part :])
    hidden_ref[0] = total
    mlp_normed, mlp_inv = normalize(total.astype(LOW).astype(F32))
    mlp_normed_ref[0] = mlp_normed
    mlp_inv_ref[0] = mlp_inv
    mlp_in_ref[0] = (mlp_normed * mlp_gain + mlp_shift).astype(LOW)


def attn_forward(seq_pad, place, vecs, base, toks, sums, packs, weights, after):
    frames, part, patches = toks[0].shape
    shards = len(toks)
    width = part * shards
    heads = part // HD
    seq_lanes = -(-seq_pad // 128) * 128
    shapes = [
        ((frames, seq_pad, width), F32),
        ((frames, seq_pad, 1), F32),
        ((frames, seq_pad, width), LOW),
        ((frames, shards, 3, seq_pad, part), LOW),
        ((frames, shards, heads * seq_pad, seq_pad), LOW),
        ((frames, shards, seq_pad, part), LOW),
        ((frames, seq_pad, width), F32),
        ((frames, seq_pad, width), F32),
        ((frames, seq_pad, 1), F32),
        ((frames, seq_pad, width), LOW),
    ]
    return call(
        functools.partial(attn_forward_kernel, len(after)),
        "attn_forward",
        0.0,
        grid=(frames,),
        in_specs=[SMEM] + [whole(v) for v in vecs] + [whole(base)]
        + [per_step(v.shape) if v.shape[0] == frames else whole(v) for v in toks]
        + [whole(v) for v in list(sums) + list(packs)]
        + [ANY] * (len(weights) + len(after)),
        out_specs=[per_step(s) for s, _ in shapes],
        out_shape=[shaped(s, d) for s, d in shapes],
        scratch_shapes=[
            pltpu.VMEM((width, seq_lanes), LOW),
            pltpu.VMEM((shards, 4 * part, width), LOW),
            pltpu.SemaphoreType.DMA((shards, 2)),
            pltpu.VMEM(base.shape, F32),
        ],
    )(place, *vecs, base, *toks, *sums, *packs, *weights, *after)


def mlp_kernel(frames, count, first, waits, place_ref, scale_ref, mlp_in_ref, *refs):
    packs, refs = refs[:count], refs[count:]
    if first:
        shards = 2 * count
        cots, refs = refs[:shards], refs[shards:]
    else:
        (grad_ref, acc_in, gacc_in), refs = refs[:3], refs[3:]
    each = 2 if first else 3
    weights, refs = refs[: each * count], refs[each * count + waits :]
    if first:
        (cot_ref, grad_ref), refs = refs[:2], refs[2:]
    acc_ref, gacc_ref, sums_ref = refs[:3]
    g_refs, refs = refs[3 : 3 + count], refs[3 + count :]
    w_buf, g_buf, act_buf, pre_buf, in_sem, out_sem = refs[:6]
    rows, width = mlp_in_ref.shape
    hidden = act_buf.shape[1]
    step = rows // frames
    loads = []
    for i in range(count):
        if first:
            for j, ref in ((2 * i, weights[i]), (2 * i + 1, weights[count + i])):
                loads.append([pltpu.make_async_copy(ref, w_buf.at[j], in_sem.at[j, 0])])
        else:
            near, *far = weights[3 * i : 3 * i + 3]
            half = far[0].shape[0]
            at, other = (pl.multiple_of(odd * half, half) for odd in (place_ref[1], 1 - place_ref[1]))
            for j in range(2):
                to = w_buf.at[2 * i + j]
                loads.append([
                    pltpu.make_async_copy(near.at[pl.ds(j * half, half)], to.at[pl.ds(at, half)], in_sem.at[2 * i + j, 0]),
                    pltpu.make_async_copy(far[j], to.at[pl.ds(other, half)], in_sem.at[2 * i + j, 1]),
                ])
    start_all(loads)
    stores = [
        pltpu.make_async_copy(g_buf.at[2 * i + j], g_refs[i].at[pl.ds(j * width, width)], out_sem.at[2 * i + j])
        for i in range(count) for j in range(2)
    ]
    if first:
        cot_buf = refs[6]
        cot_buf[...] = jnp.zeros_like(cot_buf)
        part, patches = cots[0].shape[1:]
        for f in range(frames):
            for k in range(shards):
                at = pl.multiple_of((place_ref[0] ^ k) * part, part)
                at_frame = (place_ref[0] & 1) * frames + f if k == 2 else f
                cot_buf[pl.ds(at, part), :patches] = cots[k][at_frame]
            cot = cot_buf[...].T[:step]
            cot_ref[f] = cot
            grad_ref[f * step : (f + 1) * step] = (cot.astype(F32) * scale_ref[f]).astype(LOW)
    for i in range(count):
        up, down = 2 * i, 2 * i + 1
        wait_all(loads[up : down + 1])
        bias = packs[i][0:1]

        def before(f):
            at = slice(f * step, (f + 1) * step)
            return mat_mul(mlp_in_ref[at], w_buf[up]), mat_nt(grad_ref[at], w_buf[down])

        total = jnp.zeros((1, hidden), F32)
        ahead = [before(0)]
        for f in range(frames):
            at = slice(f * step, (f + 1) * step)
            if f + 1 < frames:
                ahead.append(before(f + 1))
            pre, grad_act = ahead[f]
            pre = pre + bias
            sig = 0.5 + 0.5 * jnp.tanh(0.851 * pre)
            act = pre * sig
            act_buf[at] = act.astype(LOW)
            grad_pre = (grad_act * (sig + 1.702 * act * (1.0 - sig))).astype(LOW)
            pre_buf[at] = grad_pre
            total += jnp.sum(grad_pre.astype(F32), axis=0, keepdims=True)
        sums_ref[i] = total
        for f in range(frames):
            at = slice(f * step, (f + 1) * step)
            out = mat_mul(act_buf[at], w_buf[down])
            back = mat_nt(pre_buf[at], w_buf[up])
            if i > 0:
                acc_ref[at] += out
                gacc_ref[at] += back
            elif first:
                acc_ref[at] = out
                gacc_ref[at] = back
            else:
                acc_ref[at] = acc_in[at] + out
                gacc_ref[at] = gacc_in[at] + back
        for c in range(0, width, 256):
            g_buf[up, c : c + 256] = mat_tn(mlp_in_ref[:, c : c + 256], pre_buf[...]).astype(LOW)
        stores[up].start()
        for c in range(0, hidden, 256):
            g_buf[down, c : c + 256] = mat_tn(act_buf[:, c : c + 256], grad_ref[...]).astype(LOW)
        stores[down].start()
    for store in stores:
        store.wait()


def mlp_step(frames, place, scale, mlp_in, packs, weights, cots=None, carried=None, after=()):
    rows, width = mlp_in.shape
    count = len(packs)
    first = cots is not None
    hidden = packs[0].shape[1]
    step = rows // frames
    ins = [place, scale, mlp_in, *packs, *(cots if first else carried)]
    shapes = [shaped((frames, step, width), LOW), shaped((rows, width), LOW)] if first else []
    shapes += [shaped((rows, width), F32)] * 2 + [shaped((count, 1, hidden), F32)]
    grads = [shaped((width + hidden, width), LOW)] * count
    scratch = [
        pltpu.VMEM((2 * count, width, hidden), LOW),
        pltpu.VMEM((2 * count, width, hidden), LOW),
        pltpu.VMEM((rows, hidden), LOW),
        pltpu.VMEM((rows, hidden), LOW),
        pltpu.SemaphoreType.DMA((2 * count, 2)),
        pltpu.SemaphoreType.DMA((2 * count,)),
    ]
    if first:
        scratch.append(pltpu.VMEM((width, -(-step // 128) * 128), LOW))
    return call(
        functools.partial(mlp_kernel, frames, count, first, len(after)),
        "mlp",
        18.5,
        in_specs=[SMEM, SMEM, VMEM] + [VMEM] * (len(ins) - 3) + [ANY] * (len(weights) + len(after)),
        out_specs=[VMEM] * len(shapes) + [ANY] * len(grads),
        out_shape=shapes + grads,
        scratch_shapes=scratch,
    )(*ins, *weights, *after)


def attn_backward_kernel(
    shards, waits, place_ref, scale_ref, gain_ref, mlp_gain_ref, res_ref, acc_ref, gacc_ref, mlp_normed_ref, mlp_inv_ref, cot_ref,
    normed_ref, inv_ref, heads_ref, prob_ref, *refs
):
    packs, refs = refs[:shards], refs[shards:]
    ups, refs = refs[: shards // 2], refs[shards // 2 :]
    outs = shards + 3 + 2
    weights, refs = refs[: len(refs) - outs - waits], refs[len(refs) - outs :]
    pieces, refs = refs[:shards], refs[shards:]
    proj_ref, low_ref, sums_ref, w_buf, w_sem = refs
    part = heads_ref.shape[4]
    patches = pieces[0].shape[3]
    seq_pad, width = res_ref.shape[1:]
    gain, mlp_gain = row_of(gain_ref), row_of(mlp_gain_ref)
    frame = pl.program_id(0)
    wide_idx = place_ref[0]
    copies = weight_copies(weights, shards, place_ref, w_buf, w_sem)

    @pl.when(frame == 0)
    def _():
        start_all(copies)
        sums_ref[...] = jnp.zeros_like(sums_ref)
        rows = [ref[i] for ref in ups for i in range(2)]
        for k, values in enumerate(reorder(rows, wide_idx)):
            sums_ref[6 + k] = values

    def columns(values, i):
        blocks = values.T
        blocks = reorder([blocks[j * part : (j + 1) * part, :patches] for j in range(shards)], wide_idx)
        for ref, block in zip(pieces, blocks):
            ref[0, i] = block

    down_bias = jnp.concatenate(reorder([p[1:2, 3 * part : 4 * part] for p in packs], wide_idx), axis=1)
    columns((res_ref[0] + acc_ref[0] + down_bias).astype(LOW), 0)
    grad_res = cot_ref[0].astype(F32) * scale_ref[frame]
    gacc, mlp_normed = gacc_ref[0], mlp_normed_ref[0]
    hidden = grad_res + norm_back(gacc, mlp_normed, mlp_inv_ref[0], mlp_gain)

    def add_sum(row, values):
        sums_ref[row] += jnp.sum(values, axis=0, keepdims=True)

    add_sum(0, grad_res)
    add_sum(1, gacc * mlp_normed)
    add_sum(2, gacc)
    add_sum(3, hidden)
    low = hidden.astype(LOW)
    low_ref[0] = low
    masks = head_masks(part)
    scale = HD ** (-0.5)
    back = jnp.zeros(hidden.shape, F32)
    bias_sums = []

    @pl.when(frame == 0)
    def _():
        wait_all(copies)

    mixes = [stack_heads(mat_nt(low, w_buf[k, 3 * part :]).astype(LOW), masks) for k in range(shards)]

    def grad_prob_of(k):
        return mat_nt(mixes[k], heads_ref[0, k, 2])

    grad_probs = [grad_prob_of(0)]
    for k in range(shards):
        if k + 1 < shards:
            grad_probs.append(grad_prob_of(k + 1))
        prob_low = prob_ref[0, k]
        prob = prob_low.astype(F32)
        grad_value = mat_tn(prob_low, mixes[k])
        weighted = prob * grad_probs[k]
        grad_score = (weighted - prob * jnp.sum(weighted, axis=-1, keepdims=True)).astype(LOW)
        grad_query = pick_heads(mat_mul(grad_score, heads_ref[0, k, 1]), masks)
        grad_key = mat_tn(grad_score, stack_heads(heads_ref[0, k, 0], masks))
        proj = jnp.concatenate([grad_query * scale, grad_key * scale, grad_value], axis=1).astype(LOW)
        proj_ref[0, k] = proj
        bias_sums.append(jnp.sum(proj.astype(F32), axis=0, keepdims=True))
    for k in range(shards):
        back += mat_mul(proj_ref[0, k], w_buf[k, : 3 * part])
    for i, at in ((6 + shards, 0), (7 + shards, 2 * part)):
        own = reorder([values[:, at : at + part] for values in bias_sums], wide_idx)
        sums_ref[i] += jnp.concatenate(own, axis=1)
    normed = normed_ref[0]
    add_sum(4, back * normed)
    add_sum(5, back)
    total = hidden + norm_back(back, normed, inv_ref[0], gain)
    row = lax.broadcasted_iota(jnp.int32, (seq_pad, 1), 0)
    sums_ref[8 + shards + frame] = jnp.sum(jnp.where(row == patches, total, 0.0), axis=0, keepdims=True)
    columns(total.astype(LOW), 1)


def attn_backward(patches, place, scale, vecs, per_frame, packs, ups, weights, after):
    frames, seq_pad, width = per_frame[0].shape
    heads = per_frame[8]
    shards, part = heads.shape[1], heads.shape[4]
    blocks = [(frames, 2, part, patches)] * shards
    proj = (frames, shards, seq_pad, 3 * part)
    return call(
        functools.partial(attn_backward_kernel, shards, len(after)),
        "attn_backward",
        20.3,
        grid=(frames,),
        in_specs=[SMEM, SMEM]
        + [whole(v) for v in vecs]
        + [per_step(v.shape) for v in per_frame]
        + [whole(v) for v in list(packs) + list(ups)]
        + [ANY] * (len(weights) + len(after)),
        out_specs=[per_step(b) for b in blocks]
        + [per_step(proj), per_step((frames, seq_pad, width)), fixed((8 + shards + frames, 1, width))],
        out_shape=[shaped(b, LOW) for b in blocks]
        + [
            shaped(proj, LOW),
            shaped((frames, seq_pad, width), LOW),
            shaped((8 + shards + frames, 1, width), F32),
        ],
        scratch_shapes=[
            pltpu.VMEM((shards, 4 * part, width), LOW),
            pltpu.SemaphoreType.DMA((shards, 2)),
        ],
    )(place, scale, *vecs, *per_frame, *packs, *ups, *weights, *after)


def attn_grads_kernel(waits, attn_in_ref, low_ref, proj_ref, mix_ref, *refs):
    grad_refs, (proj_buf, mix_buf) = refs[waits:-2], refs[-2:]
    count = len(grad_refs)
    frames, seq_pad, part = mix_ref.shape[0], mix_ref.shape[2], mix_ref.shape[3]
    for i in range(count):
        for f in range(frames):
            at = slice(f * seq_pad, (f + 1) * seq_pad)
            proj_buf[at] = proj_ref[f, i]
            mix_buf[at] = mix_ref[f, i]
        for c in range(0, 3 * part, part):
            grad_refs[i][c : c + part] = mat_tn(proj_buf[:, c : c + part], attn_in_ref[...]).astype(LOW)
        grad_refs[i][3 * part :] = mat_tn(mix_buf[...], low_ref[...]).astype(LOW)


def attn_grads(attn_in, proj, low, mix, after):
    frames, shards, seq_pad, part = mix.shape
    width = attn_in.shape[-1]
    rows = frames * seq_pad
    return call(
        functools.partial(attn_grads_kernel, len(after)),
        "attn_grads",
        0.0,
        grid=(1,),
        in_specs=[fixed((rows, width)), fixed((rows, width)), fixed(proj.shape), fixed(mix.shape)] + [ANY] * len(after),
        out_specs=[fixed((4 * part, width))] * shards,
        out_shape=[shaped((4 * part, width), LOW)] * shards,
        scratch_shapes=[pltpu.VMEM((rows, 3 * part), LOW), pltpu.VMEM((rows, part), LOW)],
    )(attn_in.reshape(rows, width), low.reshape(rows, width), proj, mix, *after)


def same_video(place_ref, group, rows, columns):
    first = pl.program_id(0) * columns

    def video(position):
        position = position + first
        return (((position // group) ^ place_ref[2]) * group + position % group) // VIDEO_FRAMES

    row = lax.broadcasted_iota(jnp.int32, (rows, columns), 0) % columns
    column = lax.broadcasted_iota(jnp.int32, (rows, columns), 1)
    return video(row) == video(column)


def message_forward_kernel(
    group, waits, place_ref, cls_ref, weight_ref, m_bias_ref, gain_ref, shift_ref, offset_ref, flat_ref, bias_ref,
    proj_ref, *refs
):
    normed_ref, inv_ref, in_ref, heads_ref, prob_ref, mix_ref, base_ref, sum_ref = refs[waits:]
    part = proj_ref.shape[0]
    chunk = cls_ref.shape[0]
    message = mat_mul(cls_ref[...], weight_ref[...]) + row_of(m_bias_ref)
    normed, inv = normalize(message)
    normed_ref[...] = normed
    inv_ref[...] = inv
    msg_in = (normed * row_of(gain_ref) + row_of(shift_ref)).astype(LOW)
    in_ref[...] = msg_in
    proj = mat_nt(msg_in, flat_ref[...])
    queries = (proj[:, :part] + bias_ref[0:1]).astype(LOW)
    keys = proj[:, part : 2 * part].astype(LOW)
    values = (proj[:, 2 * part :] + bias_ref[1:2]).astype(LOW)
    heads_ref[0, 0] = queries
    heads_ref[0, 1] = keys
    heads_ref[0, 2] = values
    masks = head_masks(part)
    scores = mat_nt(stack_heads(queries, masks, HD ** (-0.5)), keys)
    scores = jnp.where(same_video(place_ref, group, len(masks) * chunk, chunk), scores, -1e30)
    exps = jnp.exp(scores - jnp.max(scores, axis=-1, keepdims=True))
    prob = exps / jnp.sum(exps, axis=-1, keepdims=True)
    prob_ref[0] = prob
    mix = pick_heads(mat_mul(prob.astype(LOW), values), masks).astype(LOW)
    mix_ref[...] = mix

    @pl.when(pl.program_id(0) == 0)
    def _():
        base_ref[...] = message[:group] + row_of(offset_ref)
        sum_ref[...] = mat_mul(mix, proj_ref[...])[:group]


def message_forward(chunk, group, place, cls_rows, weight, vecs, flat, bias, proj, after):
    count, width = cls_rows.shape
    part = proj.shape[0]
    heads = part // HD
    chunks = count // chunk
    rows = lambda columns: pl.BlockSpec((chunk, columns), lambda c: (c, 0))
    return call(
        functools.partial(message_forward_kernel, group, len(after)),
        "message_forward",
        4.2,
        grid=(chunks,),
        in_specs=[SMEM, rows(width)]
        + [whole(v) for v in (weight, *vecs, flat, bias, proj)]
        + [ANY] * len(after),
        out_specs=[
            rows(width), rows(1), rows(width),
            per_step((chunks, 3, chunk, part)), per_step((chunks, heads * chunk, chunk)),
            rows(part), fixed((group, width)), fixed((group, width)),
        ],
        out_shape=[
            shaped((count, width), F32),
            shaped((count, 1), F32),
            shaped((count, width), LOW),
            shaped((chunks, 3, chunk, part), LOW),
            shaped((chunks, heads * chunk, chunk), F32),
            shaped((count, part), LOW),
            shaped((group, width), F32),
            shaped((group, width), F32),
        ],
    )(place, cls_rows, weight, *vecs, flat, bias, proj, *after)


def message_rows(all_ref, count, chunk):
    return all_ref[pl.ds(count + pl.program_id(0) * chunk, chunk)][:, 0]


def message_backward_kernel(
    count, all_ref, in_ref, heads_ref, prob_ref, mix_ref, flat_ref, proj_ref, grad_flat_ref, grad_proj_ref,
    sum_grad_ref, sum_cross_ref, back_ref
):
    @pl.when(pl.program_id(0) == 0)
    def _():
        for ref in (grad_flat_ref, grad_proj_ref, sum_grad_ref, sum_cross_ref):
            ref[...] = jnp.zeros_like(ref)

    part = proj_ref.shape[0]
    masks = head_masks(part)
    grad = message_rows(all_ref, count, in_ref.shape[0]).astype(LOW)
    sum_grad_ref[...] += jnp.sum(grad.astype(F32), axis=0, keepdims=True)
    grad_proj_ref[...] += mat_tn(mix_ref[...], grad)
    grad_mix = mat_nt(grad, proj_ref[...]).astype(LOW)
    mix_heads = stack_heads(grad_mix, masks)
    queries, keys, values = heads_ref[0, 0], heads_ref[0, 1], heads_ref[0, 2]
    prob = prob_ref[0]
    grad_prob = mat_nt(mix_heads, values)
    grad_score = prob * (grad_prob - jnp.sum(prob * grad_prob, axis=-1, keepdims=True))
    score_low = grad_score.astype(LOW)
    grad_query = pick_heads(mat_mul(score_low, keys), masks) * HD ** (-0.5)
    grad_key = mat_tn(score_low, stack_heads(queries, masks)) * HD ** (-0.5)
    grad_value = mat_tn(prob.astype(LOW), mix_heads)
    cross = jnp.concatenate([grad_query, grad_key, grad_value], axis=1).astype(LOW)
    sum_cross_ref[...] += jnp.sum(cross.astype(F32), axis=0, keepdims=True)
    grad_flat_ref[...] += mat_tn(cross, in_ref[...])
    back_ref[...] = mat_mul(cross, flat_ref[...])


def message_backward(count, merged, msg_in, heads, prob, mix, flat, proj):
    total, width = msg_in.shape
    part = proj.shape[0]
    chunks, _, chunk, _ = heads.shape
    rows = lambda columns: pl.BlockSpec((chunk, columns), lambda c: (c, 0))
    shapes = [(3 * part, width), (part, width), (1, width), (1, 3 * part)]
    return call(
        functools.partial(message_backward_kernel, count),
        "message_backward",
        0.0,
        grid=(chunks,),
        in_specs=[whole(merged), rows(width), per_step(heads.shape), per_step(prob.shape), rows(part)]
        + [whole(flat), whole(proj)],
        out_specs=[fixed(s) for s in shapes] + [rows(width)],
        out_shape=[shaped(s, F32) for s in shapes + [(total, width)]],
    )(merged, msg_in, heads, prob, mix, flat, proj)


def message_end_kernel(
    group, count, all_ref, back_ref, other_ref, normed_ref, inv_ref, gain_ref, cls_ref, weight_ref, grad_weight_ref,
    sums_ref, grad_cls_ref
):
    @pl.when(pl.program_id(0) == 0)
    def _():
        grad_weight_ref[...] = jnp.zeros_like(grad_weight_ref)
        sums_ref[...] = jnp.zeros_like(sums_ref)

    back = back_ref[...] + other_ref[...].astype(F32)
    normed = normed_ref[...]
    grad = message_rows(all_ref, count, back.shape[0]) + norm_back(back, normed, inv_ref[...], row_of(gain_ref))
    low = grad.astype(LOW)
    for row, values in enumerate((low.astype(F32), back * normed, back)):
        sums_ref[row : row + 1] += jnp.sum(values, axis=0, keepdims=True)
    grad_weight_ref[...] += mat_tn(cls_ref[...], low)

    @pl.when(pl.program_id(0) == 0)
    def _():
        grad_cls_ref[...] = mat_nt(weight_ref[...], low)[:, :group]


def message_end(chunk, group, count, merged, back, other, normed, inv, gain, cls_rows, weight):
    total, width = back.shape
    rows = lambda columns: pl.BlockSpec((chunk, columns), lambda c: (c, 0))
    return call(
        functools.partial(message_end_kernel, group, count),
        "message_end",
        0.0,
        grid=(total // chunk,),
        in_specs=[whole(merged)] + [rows(width)] * 3 + [rows(1), whole(gain), rows(width), whole(weight)],
        out_specs=[fixed((width, width)), fixed((8, width)), fixed((width, group))],
        out_shape=[shaped((width, width), F32), shaped((8, width), F32), shaped((width, group), F32)],
    )(merged, back, other, normed, inv, gain, cls_rows, weight)


def merge_kernel(count, ordered, place_ref, *refs):
    refs, out_ref = refs[:-1], refs[-1]
    size = refs[0].shape[0] - count
    total = refs[0][:count]
    for ref in refs[1:]:
        total += ref[:count]
    out_ref[:count] = total
    for k, ref in enumerate(refs):
        at = (place_ref[0] ^ k) if ordered else k
        out_ref[pl.ds(count + at * size, size)] = ref[count:]


def merge(place, count, buffers, ordered=False):
    rows, one, width = buffers[0].shape
    return call(
        functools.partial(merge_kernel, count, ordered),
        "merge",
        0.0,
        in_specs=[SMEM] + [VMEM] * len(buffers),
        out_specs=VMEM,
        out_shape=shaped((count + (rows - count) * len(buffers), one, width), F32),
    )(place, *buffers)


def collect_kernel(place_ref, *refs):
    *pieces, grad_cls_ref, tok_ref, grad_ref = refs
    frames, _, part, patches = pieces[0].shape
    own = grad_cls_ref[pl.ds(pl.multiple_of(place_ref[0] * part, part), part), :]
    lane = lax.broadcasted_iota(jnp.int32, (part, patches), 1)
    for j, piece in enumerate(reorder([ref[...] for ref in pieces], place_ref[0])):
        for f in range(frames):
            i = j * frames + f
            tok_ref[i] = piece[f, 0]
            grad = piece[f, 1].astype(F32)
            grad_ref[i] = jnp.where(lane == 0, grad + own[:, i : i + 1], grad).astype(LOW)


def collect(place, pieces, grad_cls):
    frames, _, part, patches = pieces[0].shape
    shape = (frames * len(pieces), part, patches)
    return call(
        collect_kernel,
        "collect",
        0.0,
        in_specs=[SMEM] + [VMEM] * (len(pieces) + 1),
        out_specs=[VMEM] * 2,
        out_shape=[shaped(shape, LOW)] * 2,
    )(place, *pieces, grad_cls)


def swap(block, axis, flip):
    return lax.ppermute(block, axis, [(i, i ^ flip) for i in range(lax.axis_size(axis))])


def gate(arrays, after):
    return list(lax.optimization_barrier((tuple(arrays), tuple(after)))[0])


def frames_in(block, after):
    index = lax.axis_index("wide")
    part = block.shape[0] // lax.axis_size("wide")
    (block,) = gate([block], after)
    crossed = swap(lax.dynamic_slice_in_dim(block, ((index ^ 2) & 2) * part, 2 * part, 0), "wide", 2)
    own = lax.dynamic_slice_in_dim(block, index * part, part, 0)
    near = swap(lax.dynamic_slice_in_dim(block, (index ^ 1) * part, part, 0), "wide", 1)
    return [own, near, crossed]


def frames_end(pieces, after):
    own, near, crossed = pieces
    (crossed,) = gate([crossed], after)
    part = own.shape[0]
    index = lax.axis_index("wide")
    far = swap(lax.dynamic_slice_in_dim(crossed, ((index & 1) ^ 1) * part, part, 0), "wide", 1)
    return [own, near, crossed, far]


def send_half(block, after):
    odd = lax.axis_index("narrow") & 1
    half = block.shape[0] // 2
    sent = lax.dynamic_slice_in_dim(gate([block], after)[0], odd * half, half, 0)
    return [swap(sent, "wide", bit) for bit in bits_of(lax.axis_size("wide"))[1:]]


def near_shards(block):
    return [block, swap(block, "wide", 1)]


def far_shards(near, far):
    return [near, far, swap(near, "wide", 1), swap(far, "wide", 1)]


def row_at(base, moves):
    at = base
    for bit, rows, flipped in moves:
        is_set = ((lax.axis_index("narrow") & bit) != 0).astype(jnp.int32)
        at = at + rows * ((1 - is_set) if flipped else is_set)
    return at


def added(sums, together=False):
    blocks = []
    for terms, size in sums:
        rows = [
            array if not moves and array.shape[0] == size else lax.dynamic_slice_in_dim(array, row_at(base, moves), size, 0)
            for array, base, moves in terms
        ]
        blocks.append(sum(row.astype(F32) for row in rows).astype(LOW))
    return [jnp.concatenate(blocks, axis=0)] if together else blocks


def joined(pairs, bits):
    odds = [(lax.axis_index("narrow") & bit) != 0 for bit in bits]
    return [
        jnp.where(odd, jnp.concatenate([other, block], axis=0), jnp.concatenate([block, other], axis=0))
        for (block, other), odd in zip(pairs, odds)
    ]


def orders(count):
    bits = bits_of(lax.axis_size("narrow"))[:count]
    return [bits, bits[1:] + bits[:1]]


def regions_of(arrays, base=0):
    half = arrays[0].shape[0] // 2
    return [[(array, n * half, []) for array in arrays] for n in range(2)], half


def halving(regions, size, steps):
    for at in range(steps):
        bits = [order[at] for order in orders(steps)]
        size = size // 2
        sent = added([
            ([(array, base, moves + [(bit, size, True)]) for array, base, moves in terms], size)
            for bit, terms in zip(bits, regions)
        ])
        received = yield sent, [swap(block, "narrow", bit) for block, bit in zip(sent, bits)]
        regions = [
            [(array, base, moves + [(bit, size, False)]) for array, base, moves in terms] + [(block, 0, [])]
            for bit, terms, block in zip(bits, regions, received)
        ]
    return regions, size


def joining(blocks, steps):
    for at in reversed(range(steps)):
        bits = [order[at] for order in orders(steps)]
        others = yield blocks, [swap(block, "narrow", bit) for block, bit in zip(blocks, bits)]
        blocks = joined(list(zip(blocks, others)), bits)
    return [block.astype(F32) for block in blocks]


def whole_sum(blocks, steps):
    for bit in bits_of(lax.axis_size("narrow"))[steps:]:
        others = yield blocks, [swap(block, "narrow", bit) for block in blocks]
        blocks = added([([(a, 0, []), (b, 0, [])], a.shape[0]) for a, b in zip(blocks, others)])
    return blocks


def narrow_sum(arrays, steps):
    regions, left = yield from halving(*regions_of(arrays), steps)
    blocks = added([(terms, left) for terms in regions])
    blocks = yield from whole_sum(blocks, steps)
    return (yield from joining(blocks, steps))


class Chain:
    def __init__(self, steps):
        self.steps = steps
        self.value = None
        self.sent, self.received = next(steps)

    def turn(self, *after):
        if self.value is not None:
            return list(after)
        received = gate(self.received, after) if after else self.received
        try:
            self.sent, self.received = self.steps.send(received)
        except StopIteration as end:
            self.value = end.value
            return received
        return self.sent


def finish(chain):
    while chain.value is None:
        chain.turn()
    return chain.value


ORDER = "ofTwfgofmAfmamMBfPaEfaCaf"


def body(
    frame_tokens,
    cotangent,
    caption_count,
    caption_len,
    message_weight,
    message_bias,
    message_gain,
    message_shift,
    cross_qkv,
    cross_bias,
    cross_proj,
    cross_offset,
    attn_gain,
    attn_shift,
    qkv_weight,
    qkv_bias,
    out_weight,
    out_bias,
    mlp_gain,
    mlp_shift,
    up_weight,
    up_bias,
    down_weight,
    down_bias,
):
    group, patches, part = frame_tokens.shape
    width = message_weight.shape[0]
    hidden = up_weight.shape[1]
    wide = lax.axis_size("wide")
    narrow = lax.axis_size("narrow")
    wide_idx = lax.axis_index("wide")
    narrow_idx = lax.axis_index("narrow")
    frames = group // wide
    seq_pad = -(-(patches + 1) // ROW_TILE) * ROW_TILE
    rows = frames * seq_pad
    all_frames = group * narrow
    chunk = max(c for c in range(VIDEO_FRAMES, 129, VIDEO_FRAMES) if all_frames % c == 0 and c % group == 0)
    place = jnp.stack([wide_idx, narrow_idx & 1, narrow_idx]).astype(jnp.int32)

    def own_cols(values):
        return lax.dynamic_slice_in_dim(values, wide_idx * part, part, values.ndim - 1)

    tokens_t = frame_tokens.transpose(0, 2, 1)
    pack = jnp.concatenate(
        [up_bias, qkv_bias.reshape(-1), out_bias, down_bias, frame_tokens[:, 0, :].astype(F32).reshape(-1)]
    ).reshape(-1, width)
    packs = [pack] + [swap(pack, "wide", k) for k in range(1, wide)]
    cls_rows = jnp.concatenate(
        reorder([p[2:].reshape(group, part).astype(LOW) for p in packs], wide_idx), axis=1
    )
    cls_own = cls_rows
    toks = frames_in(tokens_t, [cls_own])
    attn_own = jnp.concatenate(
        [qkv_weight.transpose(1, 2, 0).reshape(3 * part, width), out_weight], axis=0
    )
    attn_near = send_half(attn_own, [cls_own])
    narrow_bits = bits_of(narrow)
    cls_rows = jnp.concatenate([cls_rows, swap(cls_rows, "narrow", 1)], axis=0)
    attn_near = gate(attn_near, [cls_rows])
    attn_far = [swap(near, "narrow", 1) for near in attn_near]
    (cls_rows,) = gate([cls_rows], attn_near)
    for bit in narrow_bits[1:]:
        cls_rows = jnp.concatenate([cls_rows, swap(cls_rows, "narrow", bit)], axis=0)
    attn_far = gate(attn_far, [cls_rows])
    toks = frames_end(toks, [cls_rows])
    attn_weights = near_shards(attn_own)
    for near, far in zip(attn_near, attn_far):
        attn_weights += far_shards(near, far)
    cots = frames_in(cotangent.transpose(0, 2, 1), attn_far)

    caption_slot = jnp.arange(caption_len.shape[1])
    word_total = jnp.sum(
        jnp.where(caption_slot[None, :] < caption_count[:, None], caption_len, 0), axis=1
    ).astype(F32)
    video_scale = word_total / jnp.mean(word_total)
    own_video = (narrow_idx * group + wide_idx * frames + jnp.arange(frames)) // VIDEO_FRAMES
    video_match = own_video[:, None] == jnp.arange(video_scale.shape[0])[None, :]
    scale = jnp.sum(jnp.where(video_match, video_scale[None, :], 0.0), axis=1)

    up_shards, down_shards = near_shards(up_weight), near_shards(down_weight)

    cross_flat = cross_qkv.transpose(1, 2, 0).reshape(3 * part, width)
    msg_normed, msg_inv, msg_in, cross_heads, cross_prob, cross_mix, base, group_sum = message_forward(
        chunk, group, place, cls_rows, message_weight,
        (message_bias, message_gain, message_shift, cross_offset), cross_flat, cross_bias, cross_proj,
        toks[1:] + attn_weights[1:2] + attn_weights[4:5] + [up_shards[1], down_shards[1]],
    )
    group_sums = [group_sum] + [swap(group_sum, "wide", k) for k in range(1, wide)]

    odd = narrow_idx & 1
    half = width // 2
    mlp_half = jnp.concatenate(
        [lax.dynamic_slice_in_dim(w, odd * half, half, 0) for w in gate([up_weight, down_weight], toks[2:3])],
        axis=0,
    )
    (mlp_near,) = gate([swap(mlp_half, "wide", 2)], group_sums[2:] + attn_far)
    near_parts = [mlp_near[:half], mlp_near[half:]]
    far_parts = [swap(near, "narrow", 1) for near in near_parts]
    near_other = swap(mlp_near, "wide", 1)

    forward = attn_forward(
        seq_pad, place, (attn_gain, attn_shift, mlp_gain, mlp_shift), base, toks, group_sums, packs, attn_weights,
        [up_shards[1], down_shards[1], near_parts[0], near_other],
    )
    (normed, inv, attn_in, heads, prob, mix, hidden_res, mlp_normed, mlp_inv, mlp_in) = gate(forward, far_parts[:1])
    mlp_in = mlp_in.reshape(rows, width)
    bits = bits_of(narrow)
    size = width + hidden
    cots = frames_end(cots, [mlp_in])
    (near_parts[1],) = gate(near_parts[1:], [mlp_in])
    far_parts[1] = swap(near_parts[1], "narrow", 1)
    (far_parts[0],) = gate(far_parts[:1], [mlp_in])
    far_other = [swap(far_parts[0], "wide", 1)]
    cot, grad_rows, acc, gacc, sum_up, *grad_own = mlp_step(
        frames, place, scale, mlp_in, packs[:2], up_shards + down_shards, cots=cots,
        after=[near_parts[1]] + far_other,
    )
    acc, gacc, grad_rows, cot, *grad_own = gate([acc, gacc, grad_rows, cot] + grad_own, far_parts[1:])
    far_other.append(swap(far_parts[1], "wide", 1))
    grad_next = grad_own[1]

    def split_steps(rows):
        count = 0
        while count < len(bits) and rows % (2 * ROW_TILE) == 0:
            rows, count = rows // 2, count + 1
        return count

    mlp_steps, attn_count = split_steps(size // 2), split_steps(2 * part)
    own = Chain(halving(*regions_of([grad_own[0], swap(grad_next, "wide", 1)]), mlp_steps))
    mlp_weights = [mlp_near] + far_parts + [near_other] + far_other
    acc, gacc, sum_up_far, *grad_far = mlp_step(
        frames, place, scale, mlp_in, packs[2:], mlp_weights, carried=(grad_rows, acc, gacc), after=own.sent
    )

    def far_steps(arrays):
        regions, left = yield from halving(*regions_of(arrays), mlp_steps)
        value = added([(terms, left) for terms in regions], True)
        crossed = yield value, [swap(value[0], "wide", 2)]
        blocks = added([
            (terms + [(crossed[0], n * left, [(0, 0, False)])], left) for n, terms in enumerate(finish(own)[0])
        ])
        blocks = yield from whole_sum(blocks, mlp_steps)
        return (yield from joining(blocks, mlp_steps))

    own.turn()
    grad_far = gate(grad_far, own.sent)
    far = Chain(far_steps([grad_far[0], swap(grad_far[1], "wide", 1)]))

    shape = (frames, seq_pad, width)
    per_frame = (
        hidden_res, acc.reshape(shape), gacc.reshape(shape), mlp_normed, mlp_inv, cot, normed, inv, heads, prob
    )
    *blocks, proj, low, sums = attn_backward(
        patches, place, scale, (attn_gain, mlp_gain), per_frame, packs, [sum_up, sum_up_far], attn_weights,
        own.sent + far.sent,
    )
    count = 8 + wide
    others = [swap(sums, "wide", k) for k in range(1, wide)]
    message_bits = list(bits)
    last, attn = [low], None
    for step in ORDER:
        if step == "o":
            last = own.turn(*last)
        elif step == "f":
            last = far.turn(*last)
        elif step == "a":
            last = attn.turn(*last)
        elif step == "T":
            grad_attn = attn_grads(attn_in, proj, low, mix, last + own.sent + far.sent)
            last = grad_attn[:1]
        elif step == "g":
            grad_attn = gate(grad_attn, last)
            attn_next, attn_last = (swap(grad_attn[k], "wide", 1) for k in (1, 3))
            last = added([([(grad_attn[2], 0, []), (attn_last, 0, [])], 4 * part)])
            attn_received = swap(last[0], "wide", 2)
        elif step == "A":
            attn_received, attn_next = gate([attn_received, attn_next], last)
            attn = Chain(narrow_sum([grad_attn[0], attn_next, attn_received], attn_count))
            last = attn.sent
        elif step == "w":
            merged = merge(place, count, [sums] + gate(others, last), True)
            last = [merged]
        elif step == "m":
            bit = message_bits.pop(0)
            merged = merge(place, count, [merged] + gate([swap(merged, "narrow", bit)], last))
            last = [merged]
        elif step == "M":
            for bit in message_bits:
                merged = merge(place, count, [merged] + gate([swap(merged, "narrow", bit)], last))
            (merged,) = gate([merged], last)
            grad_cross_flat, grad_cross_proj, sum_cross_grad, sum_cross, back = message_backward(
                count, merged, msg_in, cross_heads, cross_prob, cross_mix, cross_flat, cross_proj
            )
            last = [back]
        elif step == "B":
            for bit in bits_of(wide)[:-1]:
                back = back + gate([swap(back, "wide", bit)], last)[0]
            other = swap(back.astype(LOW), "wide", bits_of(wide)[-1])
            last = [back]
        elif step == "P":
            blocks = gate(blocks, last)
            pieces = [piece if k == 0 else swap(piece, "wide", k) for k, piece in enumerate(blocks)]
        elif step == "E":
            grad_message_weight, msg_sums, grad_cls = message_end(
                chunk, group, count, merged, back, gate([other], last)[0], msg_normed, msg_inv, message_gain, cls_rows,
                message_weight,
            )
            last = [grad_message_weight]
        elif step == "C":
            output_tokens, grad_tokens = collect(place, pieces[:1] + gate(pieces[1:], last), grad_cls)
            last = [grad_tokens]
    while attn.value is None or far.value is None:
        last = far.turn(*attn.turn(*last))
    far_value = far.value
    grad_attn_own = jnp.concatenate(attn.value, axis=0)
    sums = merged[:count].reshape(count, width)
    grad_up_bias = lax.dynamic_slice_in_dim(sums[6 : 6 + wide].reshape(-1), wide_idx * hidden, hidden, 0)

    return (
        output_tokens.transpose(0, 2, 1),
        grad_tokens.transpose(0, 2, 1),
        grad_message_weight,
        msg_sums[0],
        msg_sums[1],
        msg_sums[2],
        grad_cross_flat.reshape(3, part, width).transpose(2, 0, 1),
        jnp.stack([sum_cross[0, :part], sum_cross[0, 2 * part :]]),
        grad_cross_proj,
        sum_cross_grad[0],
        sums[4],
        sums[5],
        grad_attn_own[: 3 * part].reshape(3, part, width).transpose(2, 0, 1),
        own_cols(sums[count - 2 :]),
        grad_attn_own[3 * part :],
        own_cols(sums[3]),
        sums[1],
        sums[2],
        far_value[0],
        grad_up_bias,
        far_value[1],
        own_cols(sums[0]),
    )


def solution(mesh):
    return jax.shard_map(
        body,
        mesh=mesh,
        in_specs=(
            P("narrow", None, "wide"),
            P("narrow", None, "wide"),
            P(),
            P(),
            P(),
            P(),
            P(),
            P(),
            P(None, None, "wide"),
            P(None, "wide"),
            P("wide", None),
            P(),
            P(),
            P(),
            P(None, None, "wide"),
            P(None, "wide"),
            P("wide", None),
            P("wide"),
            P(),
            P(),
            P(None, "wide"),
            P("wide"),
            P("wide", None),
            P("wide"),
        ),
        out_specs=(
            P("narrow", None, "wide"),
            P("narrow", None, "wide"),
            P(),
            P(),
            P(),
            P(),
            P(None, None, "wide"),
            P(None, "wide"),
            P("wide", None),
            P(),
            P(),
            P(),
            P(None, None, "wide"),
            P(None, "wide"),
            P("wide", None),
            P("wide"),
            P(),
            P(),
            P(None, "wide"),
            P("wide"),
            P("wide", None),
            P("wide"),
        ),
        check_vma=False,
    )
```

```python
import functools
import jax
import jax.numpy as jnp
from jax import lax
from jax.experimental import pallas as pl
from jax.experimental.pallas import tpu as pltpu
from jax.sharding import PartitionSpec as P

VIDEO_FRAMES = 8
HD = 64
EPS = 1e-05
ROW_TILE = 16
LOW = jnp.bfloat16
F32 = jnp.float32
VMEM_LIMIT = 56 * 1024 * 1024
ANY = pl.BlockSpec(memory_space=pl.ANY)
VMEM = pl.BlockSpec(memory_space=pltpu.VMEM)
SMEM = pl.BlockSpec(memory_space=pltpu.SMEM)


def dot(left, right, dims):
    return lax.dot_general(left, right, (dims, ((), ())), preferred_element_type=F32)


def mat_mul(left, right):
    return dot(left, right, ((1,), (0,)))


def mat_tn(left, right):
    return dot(left, right, ((0,), (0,)))


def mat_nt(left, right):
    return dot(left, right, ((1,), (1,)))


def normalize(values):
    row_mean = jnp.mean(values, axis=-1, keepdims=True)
    centred = values - row_mean
    inv_std = lax.rsqrt(jnp.mean(centred * centred, axis=-1, keepdims=True) + EPS)
    return (centred * inv_std, inv_std)


def norm_back(grad_norm, normed, inv_std, norm_gain):
    scaled = grad_norm * norm_gain
    return inv_std * (
        scaled
        - jnp.mean(scaled, axis=-1, keepdims=True)
        - normed * jnp.mean(scaled * normed, axis=-1, keepdims=True)
    )


def bits_of(size):
    return [1 << b for b in range(size.bit_length() - 1)]


def reorder(parts, index):
    parts = list(parts)
    for bit in bits_of(len(parts)):
        odd = (index & bit) != 0
        parts = [jnp.where(odd, parts[k ^ bit], parts[k]) for k in range(len(parts))]
    return parts


def call(kernel, name, micros=0.0, **options):
    return pl.pallas_call(
        kernel,
        name=name,
        compiler_params=pltpu.CompilerParams(vmem_limit_bytes=VMEM_LIMIT),
        cost_estimate=pl.CostEstimate(
            flops=int(micros * 1.0e9), bytes_accessed=int(micros * 3.0e6), transcendentals=0
        ),
        **options,
    )


def shaped(shape, dtype):
    return jax.ShapeDtypeStruct(tuple(shape), dtype)


def whole(array):
    return pl.BlockSpec(array.shape, lambda *_: (0,) * array.ndim)


def fixed(shape):
    return pl.BlockSpec(tuple(shape), lambda *_: (0,) * len(shape))


def per_step(shape):
    return pl.BlockSpec((1,) + tuple(shape[1:]), lambda f: (f,) + (0,) * (len(shape) - 1))


def row_of(ref):
    return ref[...].reshape(1, -1)


def head_masks(width):
    lane = lax.broadcasted_iota(jnp.int32, (1, width), 1) // HD
    return [lane == h for h in range(width // HD)]


def stack_heads(values, masks, scale=1.0):
    return jnp.concatenate([values * jnp.where(m, scale, 0.0).astype(values.dtype) for m in masks], axis=0)


def pick_heads(values, masks):
    size = values.shape[0] // len(masks)
    picked = values[:size]
    for h in range(1, len(masks)):
        picked = jnp.where(masks[h], values[h * size : (h + 1) * size], picked)
    return picked


def weight_copies(refs, shards, place_ref, buf, sem):
    whole_count = 2 * shards - len(refs)
    odd = place_ref[1]
    copies = []
    for j in range(whole_count):
        copies.append([pltpu.make_async_copy(refs[j], buf.at[j], sem.at[j, 0])])
    rest = refs[whole_count:]
    for i in range(len(rest) // 2):
        half = rest[2 * i].shape[0]
        at = pl.multiple_of(odd * half, half)
        other = pl.multiple_of((1 - odd) * half, half)
        j = whole_count + i
        copies.append([
            pltpu.make_async_copy(rest[2 * i], buf.at[j, pl.ds(at, half)], sem.at[j, 0]),
            pltpu.make_async_copy(rest[2 * i + 1], buf.at[j, pl.ds(other, half)], sem.at[j, 1]),
        ])
    return copies


def start_all(copies):
    for group in copies:
        for copy in group:
            copy.start()


def wait_all(copies):
    for group in copies:
        for copy in group:
            copy.wait()


def attn_forward_kernel(waits, place_ref, gain_ref, shift_ref, mlp_gain_ref, mlp_shift_ref, base_ref, *refs):
    shards = refs[-3].shape[0]
    toks, refs = refs[:shards], refs[shards:]
    sums, refs = refs[:shards], refs[shards:]
    packs, refs = refs[:shards], refs[shards:]
    weights, refs = refs[: -14 - waits], refs[-14:]
    (normed_ref, inv_ref, attn_in_ref, heads_ref, prob_ref, mix_ref, hidden_ref, mlp_normed_ref,
     mlp_inv_ref, mlp_in_ref, tok_buf, w_buf, w_sem, msg_buf) = refs
    part, patches = toks[0].shape[1], toks[0].shape[2]
    seq_pad, width = normed_ref.shape[1], normed_ref.shape[2]
    frames = pl.num_programs(0)
    frame = pl.program_id(0)
    wide_idx = place_ref[0]
    copies = weight_copies(weights, shards, place_ref, w_buf, w_sem)

    @pl.when(frame == 0)
    def _():
        start_all(copies)
        tok_buf[...] = jnp.zeros_like(tok_buf)
        total = base_ref[...]
        for ref in sums:
            total += ref[...]
        msg_buf[...] = total

    for k in range(shards):
        at = pl.multiple_of((wide_idx ^ k) * part, part)
        at_frame = (wide_idx & 1) * frames + frame if k == 2 else 0
        tok_buf[pl.ds(at, part), :patches] = toks[k][at_frame]
    tokens = tok_buf[...].T[:seq_pad].astype(F32)
    group = msg_buf[...]
    own = lax.broadcasted_iota(jnp.int32, (group.shape[0], 1), 0) == wide_idx * frames + frame
    message = jnp.sum(jnp.where(own, group, 0.0), axis=0, keepdims=True)
    row = lax.broadcasted_iota(jnp.int32, (seq_pad, 1), 0)
    full = jnp.where(row == patches, message, tokens)
    normed, inv = normalize(full)
    normed_ref[0] = normed
    inv_ref[0] = inv
    gain, shift, mlp_gain, mlp_shift = map(row_of, (gain_ref, shift_ref, mlp_gain_ref, mlp_shift_ref))
    attn_in = (normed * gain + shift).astype(LOW)
    attn_in_ref[0] = attn_in
    masks = head_masks(part)
    live = lax.broadcasted_iota(jnp.int32, (1, seq_pad), 1) <= patches
    total = full + jnp.concatenate(reorder([p[1:2, 2 * part : 3 * part] for p in packs], wide_idx), axis=1)

    @pl.when(frame == 0)
    def _():
        wait_all(copies)

    heads = []
    for k in range(shards):
        proj = mat_nt(attn_in, w_buf[k, : 3 * part])
        queries = (proj[:, :part] + packs[k][1:2, :part]).astype(LOW)
        keys = proj[:, part : 2 * part].astype(LOW)
        values = (proj[:, 2 * part :] + packs[k][1:2, part : 2 * part]).astype(LOW)
        heads_ref[0, k, 0] = queries
        heads_ref[0, k, 1] = keys
        heads_ref[0, k, 2] = values
        heads.append((queries, keys, values))

    def score(k):
        queries, keys, _ = heads[k]
        return mat_nt(stack_heads(queries, masks, HD ** (-0.5)), keys)

    scores = [score(0)]
    for k in range(shards):
        if k + 1 < shards:
            scores.append(score(k + 1))
        live_scores = jnp.where(live, scores[k], -1e30)
        exps = jnp.exp(live_scores - jnp.max(live_scores, axis=-1, keepdims=True))
        prob = (exps * (1.0 / jnp.sum(exps, axis=-1, keepdims=True))).astype(LOW)
        prob_ref[0, k] = prob
        mix_low = pick_heads(mat_mul(prob, heads[k][2]), masks).astype(LOW)
        mix_ref[0, k] = mix_low
    for k in range(shards):
        total += mat_mul(mix_ref[0, k], w_buf[k, 3 * part :])
    hidden_ref[0] = total
    mlp_normed, mlp_inv = normalize(total.astype(LOW).astype(F32))
    mlp_normed_ref[0] = mlp_normed
    mlp_inv_ref[0] = mlp_inv
    mlp_in_ref[0] = (mlp_normed * mlp_gain + mlp_shift).astype(LOW)


def attn_forward(seq_pad, place, vecs, base, toks, sums, packs, weights, after):
    frames, part, patches = toks[0].shape
    shards = len(toks)
    width = part * shards
    heads = part // HD
    seq_lanes = -(-seq_pad // 128) * 128
    shapes = [
        ((frames, seq_pad, width), F32),
        ((frames, seq_pad, 1), F32),
        ((frames, seq_pad, width), LOW),
        ((frames, shards, 3, seq_pad, part), LOW),
        ((frames, shards, heads * seq_pad, seq_pad), LOW),
        ((frames, shards, seq_pad, part), LOW),
        ((frames, seq_pad, width), F32),
        ((frames, seq_pad, width), F32),
        ((frames, seq_pad, 1), F32),
        ((frames, seq_pad, width), LOW),
    ]
    return call(
        functools.partial(attn_forward_kernel, len(after)),
        "attn_forward",
        0.0,
        grid=(frames,),
        in_specs=[SMEM] + [whole(v) for v in vecs] + [whole(base)]
        + [per_step(v.shape) if v.shape[0] == frames else whole(v) for v in toks]
        + [whole(v) for v in list(sums) + list(packs)]
        + [ANY] * (len(weights) + len(after)),
        out_specs=[per_step(s) for s, _ in shapes],
        out_shape=[shaped(s, d) for s, d in shapes],
        scratch_shapes=[
            pltpu.VMEM((width, seq_lanes), LOW),
            pltpu.VMEM((shards, 4 * part, width), LOW),
            pltpu.SemaphoreType.DMA((shards, 2)),
            pltpu.VMEM(base.shape, F32),
        ],
    )(place, *vecs, base, *toks, *sums, *packs, *weights, *after)


def mlp_kernel(frames, count, first, waits, place_ref, scale_ref, mlp_in_ref, *refs):
    packs, refs = refs[:count], refs[count:]
    if first:
        shards = 2 * count
        cots, refs = refs[:shards], refs[shards:]
    else:
        (grad_ref, acc_in, gacc_in), refs = refs[:3], refs[3:]
    each = 2 if first else 4
    weights, refs = refs[: each * count], refs[each * count + waits :]
    if first:
        (cot_ref, grad_ref), refs = refs[:2], refs[2:]
    acc_ref, gacc_ref, sums_ref = refs[:3]
    g_refs, refs = refs[3 : 3 + count], refs[3 + count :]
    w_buf, g_buf, act_buf, pre_buf, in_sem, out_sem = refs[:6]
    rows, width = mlp_in_ref.shape
    hidden = act_buf.shape[1]
    step = rows // frames
    loads = []
    for i in range(count):
        if first:
            for j, ref in ((2 * i, weights[i]), (2 * i + 1, weights[count + i])):
                loads.append([pltpu.make_async_copy(ref, w_buf.at[j], in_sem.at[j, 0])])
        else:
            near, far = weights[4 * i : 4 * i + 2], weights[4 * i + 2 : 4 * i + 4]
            half = far[0].shape[0]
            at, other = (pl.multiple_of(odd * half, half) for odd in (place_ref[1], 1 - place_ref[1]))
            for j in range(2):
                to = w_buf.at[2 * i + j]
                loads.append([
                    pltpu.make_async_copy(near[j], to.at[pl.ds(at, half)], in_sem.at[2 * i + j, 0]),
                    pltpu.make_async_copy(far[j], to.at[pl.ds(other, half)], in_sem.at[2 * i + j, 1]),
                ])
    start_all(loads)
    stores = [
        pltpu.make_async_copy(g_buf.at[2 * i + j], g_refs[i].at[pl.ds(j * width, width)], out_sem.at[2 * i + j])
        for i in range(count) for j in range(2)
    ]
    if first:
        cot_buf = refs[6]
        cot_buf[...] = jnp.zeros_like(cot_buf)
        part, patches = cots[0].shape[1:]
        for f in range(frames):
            for k in range(shards):
                at = pl.multiple_of((place_ref[0] ^ k) * part, part)
                at_frame = (place_ref[0] & 1) * frames + f if k == 2 else f
                cot_buf[pl.ds(at, part), :patches] = cots[k][at_frame]
            cot = cot_buf[...].T[:step]
            cot_ref[f] = cot
            grad_ref[f * step : (f + 1) * step] = (cot.astype(F32) * scale_ref[f]).astype(LOW)
    for i in range(count):
        up, down = 2 * i, 2 * i + 1
        wait_all(loads[up : down + 1])
        bias = packs[i][0:1]

        def before(f):
            at = slice(f * step, (f + 1) * step)
            return mat_mul(mlp_in_ref[at], w_buf[up]), mat_nt(grad_ref[at], w_buf[down])

        total = jnp.zeros((1, hidden), F32)
        ahead = [before(0)]
        for f in range(frames):
            at = slice(f * step, (f + 1) * step)
            if f + 1 < frames:
                ahead.append(before(f + 1))
            pre, grad_act = ahead[f]
            pre = pre + bias
            sig = 0.5 + 0.5 * jnp.tanh(0.851 * pre)
            act = pre * sig
            act_buf[at] = act.astype(LOW)
            grad_pre = (grad_act * (sig + 1.702 * act * (1.0 - sig))).astype(LOW)
            pre_buf[at] = grad_pre
            total += jnp.sum(grad_pre.astype(F32), axis=0, keepdims=True)
        sums_ref[i] = total
        for f in range(frames):
            at = slice(f * step, (f + 1) * step)
            out = mat_mul(act_buf[at], w_buf[down])
            back = mat_nt(pre_buf[at], w_buf[up])
            if i > 0:
                acc_ref[at] += out
                gacc_ref[at] += back
            elif first:
                acc_ref[at] = out
                gacc_ref[at] = back
            else:
                acc_ref[at] = acc_in[at] + out
                gacc_ref[at] = gacc_in[at] + back
        for c in range(0, width, 256):
            g_buf[up, c : c + 256] = mat_tn(mlp_in_ref[:, c : c + 256], pre_buf[...]).astype(LOW)
        stores[up].start()
        for c in range(0, hidden, 256):
            g_buf[down, c : c + 256] = mat_tn(act_buf[:, c : c + 256], grad_ref[...]).astype(LOW)
        stores[down].start()
    for store in stores:
        store.wait()


def mlp_step(frames, place, scale, mlp_in, packs, weights, cots=None, carried=None, after=()):
    rows, width = mlp_in.shape
    count = len(packs)
    first = cots is not None
    hidden = packs[0].shape[1]
    step = rows // frames
    ins = [place, scale, mlp_in, *packs, *(cots if first else carried)]
    shapes = [shaped((frames, step, width), LOW), shaped((rows, width), LOW)] if first else []
    shapes += [shaped((rows, width), F32)] * 2 + [shaped((count, 1, hidden), F32)]
    grads = [shaped((width + hidden, width), LOW)] * count
    scratch = [
        pltpu.VMEM((2 * count, width, hidden), LOW),
        pltpu.VMEM((2 * count, width, hidden), LOW),
        pltpu.VMEM((rows, hidden), LOW),
        pltpu.VMEM((rows, hidden), LOW),
        pltpu.SemaphoreType.DMA((2 * count, 2)),
        pltpu.SemaphoreType.DMA((2 * count,)),
    ]
    if first:
        scratch.append(pltpu.VMEM((width, -(-step // 128) * 128), LOW))
    return call(
        functools.partial(mlp_kernel, frames, count, first, len(after)),
        "mlp",
        18.5,
        in_specs=[SMEM, SMEM, VMEM] + [VMEM] * (len(ins) - 3) + [ANY] * (len(weights) + len(after)),
        out_specs=[VMEM] * len(shapes) + [ANY] * len(grads),
        out_shape=shapes + grads,
        scratch_shapes=scratch,
    )(*ins, *weights, *after)


def attn_backward_kernel(
    shards, waits, place_ref, scale_ref, gain_ref, mlp_gain_ref, res_ref, acc_ref, gacc_ref, mlp_normed_ref, mlp_inv_ref, cot_ref,
    normed_ref, inv_ref, heads_ref, prob_ref, *refs
):
    packs, refs = refs[:shards], refs[shards:]
    ups, refs = refs[: shards // 2], refs[shards // 2 :]
    outs = shards + 3 + 2
    weights, refs = refs[: len(refs) - outs - waits], refs[len(refs) - outs :]
    pieces, refs = refs[:shards], refs[shards:]
    proj_ref, low_ref, sums_ref, w_buf, w_sem = refs
    part = heads_ref.shape[4]
    patches = pieces[0].shape[3]
    seq_pad, width = res_ref.shape[1:]
    gain, mlp_gain = row_of(gain_ref), row_of(mlp_gain_ref)
    frame = pl.program_id(0)
    wide_idx = place_ref[0]
    copies = weight_copies(weights, shards, place_ref, w_buf, w_sem)

    @pl.when(frame == 0)
    def _():
        start_all(copies)
        sums_ref[...] = jnp.zeros_like(sums_ref)
        rows = [ref[i] for ref in ups for i in range(2)]
        for k, values in enumerate(reorder(rows, wide_idx)):
            sums_ref[6 + k] = values

    def columns(values, i):
        blocks = values.T
        blocks = reorder([blocks[j * part : (j + 1) * part, :patches] for j in range(shards)], wide_idx)
        for ref, block in zip(pieces, blocks):
            ref[0, i] = block

    down_bias = jnp.concatenate(reorder([p[1:2, 3 * part : 4 * part] for p in packs], wide_idx), axis=1)
    columns((res_ref[0] + acc_ref[0] + down_bias).astype(LOW), 0)
    grad_res = cot_ref[0].astype(F32) * scale_ref[frame]
    gacc, mlp_normed = gacc_ref[0], mlp_normed_ref[0]
    hidden = grad_res + norm_back(gacc, mlp_normed, mlp_inv_ref[0], mlp_gain)

    def add_sum(row, values):
        sums_ref[row] += jnp.sum(values, axis=0, keepdims=True)

    add_sum(0, grad_res)
    add_sum(1, gacc * mlp_normed)
    add_sum(2, gacc)
    add_sum(3, hidden)
    low = hidden.astype(LOW)
    low_ref[0] = low
    masks = head_masks(part)
    scale = HD ** (-0.5)
    back = jnp.zeros(hidden.shape, F32)
    bias_sums = []

    @pl.when(frame == 0)
    def _():
        wait_all(copies)

    mixes = [stack_heads(mat_nt(low, w_buf[k, 3 * part :]).astype(LOW), masks) for k in range(shards)]

    def grad_prob_of(k):
        return mat_nt(mixes[k], heads_ref[0, k, 2])

    grad_probs = [grad_prob_of(0)]
    for k in range(shards):
        if k + 1 < shards:
            grad_probs.append(grad_prob_of(k + 1))
        prob_low = prob_ref[0, k]
        prob = prob_low.astype(F32)
        grad_value = mat_tn(prob_low, mixes[k])
        weighted = prob * grad_probs[k]
        grad_score = (weighted - prob * jnp.sum(weighted, axis=-1, keepdims=True)).astype(LOW)
        grad_query = pick_heads(mat_mul(grad_score, heads_ref[0, k, 1]), masks)
        grad_key = mat_tn(grad_score, stack_heads(heads_ref[0, k, 0], masks))
        proj = jnp.concatenate([grad_query * scale, grad_key * scale, grad_value], axis=1).astype(LOW)
        proj_ref[0, k] = proj
        bias_sums.append(jnp.sum(proj.astype(F32), axis=0, keepdims=True))
    for k in range(shards):
        back += mat_mul(proj_ref[0, k], w_buf[k, : 3 * part])
    for i, at in ((6 + shards, 0), (7 + shards, 2 * part)):
        own = reorder([values[:, at : at + part] for values in bias_sums], wide_idx)
        sums_ref[i] += jnp.concatenate(own, axis=1)
    normed = normed_ref[0]
    add_sum(4, back * normed)
    add_sum(5, back)
    total = hidden + norm_back(back, normed, inv_ref[0], gain)
    row = lax.broadcasted_iota(jnp.int32, (seq_pad, 1), 0)
    sums_ref[8 + shards + frame] = jnp.sum(jnp.where(row == patches, total, 0.0), axis=0, keepdims=True)
    columns(total.astype(LOW), 1)


def attn_backward(patches, place, scale, vecs, per_frame, packs, ups, weights, after):
    frames, seq_pad, width = per_frame[0].shape
    heads = per_frame[8]
    shards, part = heads.shape[1], heads.shape[4]
    blocks = [(frames, 2, part, patches)] * shards
    proj = (frames, shards, seq_pad, 3 * part)
    return call(
        functools.partial(attn_backward_kernel, shards, len(after)),
        "attn_backward",
        20.3,
        grid=(frames,),
        in_specs=[SMEM, SMEM]
        + [whole(v) for v in vecs]
        + [per_step(v.shape) for v in per_frame]
        + [whole(v) for v in list(packs) + list(ups)]
        + [ANY] * (len(weights) + len(after)),
        out_specs=[per_step(b) for b in blocks]
        + [per_step(proj), per_step((frames, seq_pad, width)), fixed((8 + shards + frames, 1, width))],
        out_shape=[shaped(b, LOW) for b in blocks]
        + [
            shaped(proj, LOW),
            shaped((frames, seq_pad, width), LOW),
            shaped((8 + shards + frames, 1, width), F32),
        ],
        scratch_shapes=[
            pltpu.VMEM((shards, 4 * part, width), LOW),
            pltpu.SemaphoreType.DMA((shards, 2)),
        ],
    )(place, scale, *vecs, *per_frame, *packs, *ups, *weights, *after)


def attn_grads_kernel(waits, attn_in_ref, low_ref, proj_ref, mix_ref, *refs):
    grad_refs, (proj_buf, mix_buf) = refs[waits:-2], refs[-2:]
    count = len(grad_refs)
    frames, seq_pad, part = mix_ref.shape[0], mix_ref.shape[2], mix_ref.shape[3]
    for i in range(count):
        for f in range(frames):
            at = slice(f * seq_pad, (f + 1) * seq_pad)
            proj_buf[at] = proj_ref[f, i]
            mix_buf[at] = mix_ref[f, i]
        for c in range(0, 3 * part, part):
            grad_refs[i][c : c + part] = mat_tn(proj_buf[:, c : c + part], attn_in_ref[...]).astype(LOW)
        grad_refs[i][3 * part :] = mat_tn(mix_buf[...], low_ref[...]).astype(LOW)


def attn_grads(attn_in, proj, low, mix, after):
    frames, shards, seq_pad, part = mix.shape
    width = attn_in.shape[-1]
    rows = frames * seq_pad
    return call(
        functools.partial(attn_grads_kernel, len(after)),
        "attn_grads",
        0.0,
        grid=(1,),
        in_specs=[fixed((rows, width)), fixed((rows, width)), fixed(proj.shape), fixed(mix.shape)] + [ANY] * len(after),
        out_specs=[fixed((4 * part, width))] * shards,
        out_shape=[shaped((4 * part, width), LOW)] * shards,
        scratch_shapes=[pltpu.VMEM((rows, 3 * part), LOW), pltpu.VMEM((rows, part), LOW)],
    )(attn_in.reshape(rows, width), low.reshape(rows, width), proj, mix, *after)


def same_video(place_ref, group, rows, columns):
    first = pl.program_id(0) * columns

    def video(position):
        position = position + first
        return (((position // group) ^ place_ref[2]) * group + position % group) // VIDEO_FRAMES

    row = lax.broadcasted_iota(jnp.int32, (rows, columns), 0) % columns
    column = lax.broadcasted_iota(jnp.int32, (rows, columns), 1)
    return video(row) == video(column)


def message_forward_kernel(
    group, waits, place_ref, cls_ref, weight_ref, m_bias_ref, gain_ref, shift_ref, offset_ref, flat_ref, bias_ref,
    proj_ref, *refs
):
    normed_ref, inv_ref, in_ref, heads_ref, prob_ref, mix_ref, base_ref, sum_ref = refs[waits:]
    part = proj_ref.shape[0]
    chunk = cls_ref.shape[0]
    message = mat_mul(cls_ref[...], weight_ref[...]) + row_of(m_bias_ref)
    normed, inv = normalize(message)
    normed_ref[...] = normed
    inv_ref[...] = inv
    msg_in = (normed * row_of(gain_ref) + row_of(shift_ref)).astype(LOW)
    in_ref[...] = msg_in
    proj = mat_nt(msg_in, flat_ref[...])
    queries = (proj[:, :part] + bias_ref[0:1]).astype(LOW)
    keys = proj[:, part : 2 * part].astype(LOW)
    values = (proj[:, 2 * part :] + bias_ref[1:2]).astype(LOW)
    heads_ref[0, 0] = queries
    heads_ref[0, 1] = keys
    heads_ref[0, 2] = values
    masks = head_masks(part)
    scores = mat_nt(stack_heads(queries, masks, HD ** (-0.5)), keys)
    scores = jnp.where(same_video(place_ref, group, len(masks) * chunk, chunk), scores, -1e30)
    exps = jnp.exp(scores - jnp.max(scores, axis=-1, keepdims=True))
    prob = exps / jnp.sum(exps, axis=-1, keepdims=True)
    prob_ref[0] = prob
    mix = pick_heads(mat_mul(prob.astype(LOW), values), masks).astype(LOW)
    mix_ref[...] = mix

    @pl.when(pl.program_id(0) == 0)
    def _():
        base_ref[...] = message[:group] + row_of(offset_ref)
        sum_ref[...] = mat_mul(mix, proj_ref[...])[:group]


def message_forward(chunk, group, place, cls_rows, weight, vecs, flat, bias, proj, after):
    count, width = cls_rows.shape
    part = proj.shape[0]
    heads = part // HD
    chunks = count // chunk
    rows = lambda columns: pl.BlockSpec((chunk, columns), lambda c: (c, 0))
    return call(
        functools.partial(message_forward_kernel, group, len(after)),
        "message_forward",
        4.2,
        grid=(chunks,),
        in_specs=[SMEM, rows(width)]
        + [whole(v) for v in (weight, *vecs, flat, bias, proj)]
        + [ANY] * len(after),
        out_specs=[
            rows(width), rows(1), rows(width),
            per_step((chunks, 3, chunk, part)), per_step((chunks, heads * chunk, chunk)),
            rows(part), fixed((group, width)), fixed((group, width)),
        ],
        out_shape=[
            shaped((count, width), F32),
            shaped((count, 1), F32),
            shaped((count, width), LOW),
            shaped((chunks, 3, chunk, part), LOW),
            shaped((chunks, heads * chunk, chunk), F32),
            shaped((count, part), LOW),
            shaped((group, width), F32),
            shaped((group, width), F32),
        ],
    )(place, cls_rows, weight, *vecs, flat, bias, proj, *after)


def message_rows(all_ref, count, chunk):
    return all_ref[pl.ds(count + pl.program_id(0) * chunk, chunk)][:, 0]


def message_backward_kernel(
    count, all_ref, in_ref, heads_ref, prob_ref, mix_ref, flat_ref, proj_ref, grad_flat_ref, grad_proj_ref,
    sum_grad_ref, sum_cross_ref, back_ref
):
    @pl.when(pl.program_id(0) == 0)
    def _():
        for ref in (grad_flat_ref, grad_proj_ref, sum_grad_ref, sum_cross_ref):
            ref[...] = jnp.zeros_like(ref)

    part = proj_ref.shape[0]
    masks = head_masks(part)
    grad = message_rows(all_ref, count, in_ref.shape[0]).astype(LOW)
    sum_grad_ref[...] += jnp.sum(grad.astype(F32), axis=0, keepdims=True)
    grad_proj_ref[...] += mat_tn(mix_ref[...], grad)
    grad_mix = mat_nt(grad, proj_ref[...]).astype(LOW)
    mix_heads = stack_heads(grad_mix, masks)
    queries, keys, values = heads_ref[0, 0], heads_ref[0, 1], heads_ref[0, 2]
    prob = prob_ref[0]
    grad_prob = mat_nt(mix_heads, values)
    grad_score = prob * (grad_prob - jnp.sum(prob * grad_prob, axis=-1, keepdims=True))
    score_low = grad_score.astype(LOW)
    grad_query = pick_heads(mat_mul(score_low, keys), masks) * HD ** (-0.5)
    grad_key = mat_tn(score_low, stack_heads(queries, masks)) * HD ** (-0.5)
    grad_value = mat_tn(prob.astype(LOW), mix_heads)
    cross = jnp.concatenate([grad_query, grad_key, grad_value], axis=1).astype(LOW)
    sum_cross_ref[...] += jnp.sum(cross.astype(F32), axis=0, keepdims=True)
    grad_flat_ref[...] += mat_tn(cross, in_ref[...])
    back_ref[...] = mat_mul(cross, flat_ref[...])


def message_backward(count, merged, msg_in, heads, prob, mix, flat, proj):
    total, width = msg_in.shape
    part = proj.shape[0]
    chunks, _, chunk, _ = heads.shape
    rows = lambda columns: pl.BlockSpec((chunk, columns), lambda c: (c, 0))
    shapes = [(3 * part, width), (part, width), (1, width), (1, 3 * part)]
    return call(
        functools.partial(message_backward_kernel, count),
        "message_backward",
        0.0,
        grid=(chunks,),
        in_specs=[whole(merged), rows(width), per_step(heads.shape), per_step(prob.shape), rows(part)]
        + [whole(flat), whole(proj)],
        out_specs=[fixed(s) for s in shapes] + [rows(width)],
        out_shape=[shaped(s, F32) for s in shapes + [(total, width)]],
    )(merged, msg_in, heads, prob, mix, flat, proj)


def message_end_kernel(
    group, count, all_ref, back_ref, other_ref, normed_ref, inv_ref, gain_ref, cls_ref, weight_ref, grad_weight_ref,
    sums_ref, grad_cls_ref
):
    @pl.when(pl.program_id(0) == 0)
    def _():
        grad_weight_ref[...] = jnp.zeros_like(grad_weight_ref)
        sums_ref[...] = jnp.zeros_like(sums_ref)

    back = back_ref[...] + other_ref[...].astype(F32)
    normed = normed_ref[...]
    grad = message_rows(all_ref, count, back.shape[0]) + norm_back(back, normed, inv_ref[...], row_of(gain_ref))
    low = grad.astype(LOW)
    for row, values in enumerate((low.astype(F32), back * normed, back)):
        sums_ref[row : row + 1] += jnp.sum(values, axis=0, keepdims=True)
    grad_weight_ref[...] += mat_tn(cls_ref[...], low)

    @pl.when(pl.program_id(0) == 0)
    def _():
        grad_cls_ref[...] = mat_nt(weight_ref[...], low)[:, :group]


def message_end(chunk, group, count, merged, back, other, normed, inv, gain, cls_rows, weight):
    total, width = back.shape
    rows = lambda columns: pl.BlockSpec((chunk, columns), lambda c: (c, 0))
    return call(
        functools.partial(message_end_kernel, group, count),
        "message_end",
        0.0,
        grid=(total // chunk,),
        in_specs=[whole(merged)] + [rows(width)] * 3 + [rows(1), whole(gain), rows(width), whole(weight)],
        out_specs=[fixed((width, width)), fixed((8, width)), fixed((width, group))],
        out_shape=[shaped((width, width), F32), shaped((8, width), F32), shaped((width, group), F32)],
    )(merged, back, other, normed, inv, gain, cls_rows, weight)


def merge_kernel(count, ordered, place_ref, *refs):
    refs, out_ref = refs[:-1], refs[-1]
    size = refs[0].shape[0] - count
    total = refs[0][:count]
    for ref in refs[1:]:
        total += ref[:count]
    out_ref[:count] = total
    for k, ref in enumerate(refs):
        at = (place_ref[0] ^ k) if ordered else k
        out_ref[pl.ds(count + at * size, size)] = ref[count:]


def merge(place, count, buffers, ordered=False):
    rows, one, width = buffers[0].shape
    return call(
        functools.partial(merge_kernel, count, ordered),
        "merge",
        0.0,
        in_specs=[SMEM] + [VMEM] * len(buffers),
        out_specs=VMEM,
        out_shape=shaped((count + (rows - count) * len(buffers), one, width), F32),
    )(place, *buffers)


def collect_kernel(place_ref, *refs):
    *pieces, grad_cls_ref, tok_ref, grad_ref = refs
    frames, _, part, patches = pieces[0].shape
    own = grad_cls_ref[pl.ds(pl.multiple_of(place_ref[0] * part, part), part), :]
    lane = lax.broadcasted_iota(jnp.int32, (part, patches), 1)
    for j, piece in enumerate(reorder([ref[...] for ref in pieces], place_ref[0])):
        for f in range(frames):
            i = j * frames + f
            tok_ref[i] = piece[f, 0]
            grad = piece[f, 1].astype(F32)
            grad_ref[i] = jnp.where(lane == 0, grad + own[:, i : i + 1], grad).astype(LOW)


def collect(place, pieces, grad_cls):
    frames, _, part, patches = pieces[0].shape
    shape = (frames * len(pieces), part, patches)
    return call(
        collect_kernel,
        "collect",
        0.0,
        in_specs=[SMEM] + [VMEM] * (len(pieces) + 1),
        out_specs=[VMEM] * 2,
        out_shape=[shaped(shape, LOW)] * 2,
    )(place, *pieces, grad_cls)


def swap(block, axis, flip):
    return lax.ppermute(block, axis, [(i, i ^ flip) for i in range(lax.axis_size(axis))])


def gate(arrays, after):
    return list(lax.optimization_barrier((tuple(arrays), tuple(after)))[0])


def frames_in(block, after):
    index = lax.axis_index("wide")
    part = block.shape[0] // lax.axis_size("wide")
    (block,) = gate([block], after)
    crossed = swap(lax.dynamic_slice_in_dim(block, ((index ^ 2) & 2) * part, 2 * part, 0), "wide", 2)
    own = lax.dynamic_slice_in_dim(block, index * part, part, 0)
    near = swap(lax.dynamic_slice_in_dim(block, (index ^ 1) * part, part, 0), "wide", 1)
    return [own, near, crossed]


def frames_end(pieces, after):
    own, near, crossed = pieces
    (crossed,) = gate([crossed], after)
    part = own.shape[0]
    index = lax.axis_index("wide")
    far = swap(lax.dynamic_slice_in_dim(crossed, ((index & 1) ^ 1) * part, part, 0), "wide", 1)
    return [own, near, crossed, far]


def send_half(block, after):
    odd = lax.axis_index("narrow") & 1
    half = block.shape[0] // 2
    sent = lax.dynamic_slice_in_dim(gate([block], after)[0], odd * half, half, 0)
    return [swap(sent, "wide", bit) for bit in bits_of(lax.axis_size("wide"))[1:]]


def near_shards(block):
    return [block, swap(block, "wide", 1)]


def far_shards(near, far):
    return [near, far, swap(near, "wide", 1), swap(far, "wide", 1)]


def row_at(base, moves):
    at = base
    for bit, rows, flipped in moves:
        is_set = ((lax.axis_index("narrow") & bit) != 0).astype(jnp.int32)
        at = at + rows * ((1 - is_set) if flipped else is_set)
    return at


def added(sums, together=False):
    blocks = []
    for terms, size in sums:
        rows = [
            array if not moves and array.shape[0] == size else lax.dynamic_slice_in_dim(array, row_at(base, moves), size, 0)
            for array, base, moves in terms
        ]
        blocks.append(sum(row.astype(F32) for row in rows).astype(LOW))
    return [jnp.concatenate(blocks, axis=0)] if together else blocks


def joined(pairs, bits):
    odds = [(lax.axis_index("narrow") & bit) != 0 for bit in bits]
    return [
        jnp.where(odd, jnp.concatenate([other, block], axis=0), jnp.concatenate([block, other], axis=0))
        for (block, other), odd in zip(pairs, odds)
    ]


def orders(count):
    bits = bits_of(lax.axis_size("narrow"))[:count]
    return [bits, bits[1:] + bits[:1]]


def regions_of(arrays, base=0):
    half = arrays[0].shape[0] // 2
    return [[(array, n * half, []) for array in arrays] for n in range(2)], half


def halving(regions, size, steps):
    for at in range(steps):
        bits = [order[at] for order in orders(steps)]
        size = size // 2
        sent = added([
            ([(array, base, moves + [(bit, size, True)]) for array, base, moves in terms], size)
            for bit, terms in zip(bits, regions)
        ])
        received = yield sent, [swap(block, "narrow", bit) for block, bit in zip(sent, bits)]
        regions = [
            [(array, base, moves + [(bit, size, False)]) for array, base, moves in terms] + [(block, 0, [])]
            for bit, terms, block in zip(bits, regions, received)
        ]
    return regions, size


def joining(blocks, steps):
    for at in reversed(range(steps)):
        bits = [order[at] for order in orders(steps)]
        others = yield blocks, [swap(block, "narrow", bit) for block, bit in zip(blocks, bits)]
        blocks = joined(list(zip(blocks, others)), bits)
    return [block.astype(F32) for block in blocks]


def whole_sum(blocks, steps):
    for bit in bits_of(lax.axis_size("narrow"))[steps:]:
        others = yield blocks, [swap(block, "narrow", bit) for block in blocks]
        blocks = added([([(a, 0, []), (b, 0, [])], a.shape[0]) for a, b in zip(blocks, others)])
    return blocks


def narrow_sum(arrays, steps):
    regions, left = yield from halving(*regions_of(arrays), steps)
    blocks = added([(terms, left) for terms in regions])
    blocks = yield from whole_sum(blocks, steps)
    return (yield from joining(blocks, steps))


class Chain:
    def __init__(self, steps):
        self.steps = steps
        self.value = None
        self.sent, self.received = next(steps)

    def turn(self, *after):
        if self.value is not None:
            return list(after)
        received = gate(self.received, after) if after else self.received
        try:
            self.sent, self.received = self.steps.send(received)
        except StopIteration as end:
            self.value = end.value
            return received
        return self.sent


def finish(chain):
    while chain.value is None:
        chain.turn()
    return chain.value


ORDER = "ofTwfmgfmAofmMaBPfaEfaCaf"


def body(
    frame_tokens,
    cotangent,
    caption_count,
    caption_len,
    message_weight,
    message_bias,
    message_gain,
    message_shift,
    cross_qkv,
    cross_bias,
    cross_proj,
    cross_offset,
    attn_gain,
    attn_shift,
    qkv_weight,
    qkv_bias,
    out_weight,
    out_bias,
    mlp_gain,
    mlp_shift,
    up_weight,
    up_bias,
    down_weight,
    down_bias,
):
    group, patches, part = frame_tokens.shape
    width = message_weight.shape[0]
    hidden = up_weight.shape[1]
    wide = lax.axis_size("wide")
    narrow = lax.axis_size("narrow")
    wide_idx = lax.axis_index("wide")
    narrow_idx = lax.axis_index("narrow")
    frames = group // wide
    seq_pad = -(-(patches + 1) // ROW_TILE) * ROW_TILE
    rows = frames * seq_pad
    all_frames = group * narrow
    chunk = max(c for c in range(VIDEO_FRAMES, 129, VIDEO_FRAMES) if all_frames % c == 0 and c % group == 0)
    place = jnp.stack([wide_idx, narrow_idx & 1, narrow_idx]).astype(jnp.int32)

    def own_cols(values):
        return lax.dynamic_slice_in_dim(values, wide_idx * part, part, values.ndim - 1)

    tokens_t = frame_tokens.transpose(0, 2, 1)
    pack = jnp.concatenate(
        [up_bias, qkv_bias.reshape(-1), out_bias, down_bias, frame_tokens[:, 0, :].astype(F32).reshape(-1)]
    ).reshape(-1, width)
    packs = [pack] + [swap(pack, "wide", k) for k in range(1, wide)]
    cls_rows = jnp.concatenate(
        reorder([p[2:].reshape(group, part).astype(LOW) for p in packs], wide_idx), axis=1
    )
    cls_own = cls_rows
    toks = frames_in(tokens_t, [cls_own])
    attn_own = jnp.concatenate(
        [qkv_weight.transpose(1, 2, 0).reshape(3 * part, width), out_weight], axis=0
    )
    attn_near = send_half(attn_own, [cls_own])
    narrow_bits = bits_of(narrow)
    cls_rows = jnp.concatenate([cls_rows, swap(cls_rows, "narrow", 1)], axis=0)
    attn_near = gate(attn_near, [cls_rows])
    attn_far = [swap(near, "narrow", 1) for near in attn_near]
    (cls_rows,) = gate([cls_rows], attn_near)
    for bit in narrow_bits[1:]:
        cls_rows = jnp.concatenate([cls_rows, swap(cls_rows, "narrow", bit)], axis=0)
    attn_far = gate(attn_far, [cls_rows])
    toks = frames_end(toks, [cls_rows])
    attn_weights = near_shards(attn_own)
    for near, far in zip(attn_near, attn_far):
        attn_weights += far_shards(near, far)
    cots = frames_in(cotangent.transpose(0, 2, 1), attn_far)

    caption_slot = jnp.arange(caption_len.shape[1])
    word_total = jnp.sum(
        jnp.where(caption_slot[None, :] < caption_count[:, None], caption_len, 0), axis=1
    ).astype(F32)
    video_scale = word_total / jnp.mean(word_total)
    own_video = (narrow_idx * group + wide_idx * frames + jnp.arange(frames)) // VIDEO_FRAMES
    video_match = own_video[:, None] == jnp.arange(video_scale.shape[0])[None, :]
    scale = jnp.sum(jnp.where(video_match, video_scale[None, :], 0.0), axis=1)

    up_shards, down_shards = near_shards(up_weight), near_shards(down_weight)

    cross_flat = cross_qkv.transpose(1, 2, 0).reshape(3 * part, width)
    msg_normed, msg_inv, msg_in, cross_heads, cross_prob, cross_mix, base, group_sum = message_forward(
        chunk, group, place, cls_rows, message_weight,
        (message_bias, message_gain, message_shift, cross_offset), cross_flat, cross_bias, cross_proj,
        toks[1:] + attn_weights[1:2] + attn_weights[4:5] + [up_shards[1], down_shards[1]],
    )
    group_sums = [group_sum] + [swap(group_sum, "wide", k) for k in range(1, wide)]

    odd = narrow_idx & 1
    half = width // 2

    def half_of(weight, after):
        return lax.dynamic_slice_in_dim(gate([weight], after)[0], odd * half, half, 0)

    near_parts = [
        swap(half_of(up_weight, toks[2:3]), "wide", 2),
        swap(half_of(down_weight, group_sums[2:]), "wide", 2),
    ]
    (near_parts[0],) = gate(near_parts[:1], group_sums[2:] + attn_far)
    near_other = [swap(near_parts[0], "wide", 1)]
    far_parts = [swap(near_parts[0], "narrow", 1)]

    forward = attn_forward(
        seq_pad, place, (attn_gain, attn_shift, mlp_gain, mlp_shift), base, toks, group_sums, packs, attn_weights,
        [up_shards[1], down_shards[1], near_other[0]],
    )
    (normed, inv, attn_in, heads, prob, mix, hidden_res, mlp_normed, mlp_inv, mlp_in) = gate(
        forward, far_parts + near_parts[1:]
    )
    mlp_in = mlp_in.reshape(rows, width)
    bits = bits_of(narrow)
    size = width + hidden
    cots = frames_end(cots, [mlp_in])
    (near_parts[1],) = gate(near_parts[1:], [mlp_in])
    far_parts.append(swap(near_parts[1], "narrow", 1))
    near_other.append(swap(near_parts[1], "wide", 1))
    (far_parts[0],) = gate(far_parts[:1], [mlp_in])
    far_other = [swap(far_parts[0], "wide", 1)]
    cot, grad_rows, acc, gacc, sum_up, *grad_own = mlp_step(
        frames, place, scale, mlp_in, packs[:2], up_shards + down_shards, cots=cots,
        after=[near_other[1]] + far_other,
    )
    acc, gacc, grad_rows, cot, *grad_own = gate([acc, gacc, grad_rows, cot] + grad_own, far_parts[1:])
    far_other.append(swap(far_parts[1], "wide", 1))
    grad_next = grad_own[1]

    def split_steps(rows):
        count = 0
        while count < len(bits) and rows % (2 * ROW_TILE) == 0:
            rows, count = rows // 2, count + 1
        return count

    mlp_steps, attn_count = split_steps(size // 2), split_steps(2 * part)
    own = Chain(halving(*regions_of([grad_own[0], swap(grad_next, "wide", 1)]), mlp_steps))
    mlp_weights = near_parts + far_parts + near_other + far_other
    acc, gacc, sum_up_far, *grad_far = mlp_step(
        frames, place, scale, mlp_in, packs[2:], mlp_weights, carried=(grad_rows, acc, gacc), after=own.sent
    )

    def far_steps(arrays):
        regions, left = yield from halving(*regions_of(arrays), mlp_steps)
        value = added([(terms, left) for terms in regions], True)
        crossed = yield value, [swap(value[0], "wide", 2)]
        blocks = added([
            (terms + [(crossed[0], n * left, [(0, 0, False)])], left) for n, terms in enumerate(finish(own)[0])
        ])
        blocks = yield from whole_sum(blocks, mlp_steps)
        return (yield from joining(blocks, mlp_steps))

    own.turn()
    grad_far = gate(grad_far, own.sent)
    far = Chain(far_steps([grad_far[0], swap(grad_far[1], "wide", 1)]))

    shape = (frames, seq_pad, width)
    per_frame = (
        hidden_res, acc.reshape(shape), gacc.reshape(shape), mlp_normed, mlp_inv, cot, normed, inv, heads, prob
    )
    *blocks, proj, low, sums = attn_backward(
        patches, place, scale, (attn_gain, mlp_gain), per_frame, packs, [sum_up, sum_up_far], attn_weights,
        own.sent + far.sent,
    )
    count = 8 + wide
    others = [swap(sums, "wide", k) for k in range(1, wide)]
    message_bits = list(bits)
    last, attn = [low], None
    for step in ORDER:
        if step == "o":
            last = own.turn(*last)
        elif step == "f":
            last = far.turn(*last)
        elif step == "a":
            last = attn.turn(*last)
        elif step == "T":
            grad_attn = attn_grads(attn_in, proj, low, mix, last + own.sent + far.sent)
            last = grad_attn[:1]
        elif step == "g":
            grad_attn = gate(grad_attn, last)
            attn_next, attn_last = (swap(grad_attn[k], "wide", 1) for k in (1, 3))
            last = added([([(grad_attn[2], 0, []), (attn_last, 0, [])], 4 * part)])
            attn_received = swap(last[0], "wide", 2)
        elif step == "A":
            attn_received, attn_next = gate([attn_received, attn_next], last)
            attn = Chain(narrow_sum([grad_attn[0], attn_next, attn_received], attn_count))
            last = attn.sent
        elif step == "w":
            merged = merge(place, count, [sums] + gate(others, last), True)
            last = [merged]
        elif step == "m":
            bit = message_bits.pop(0)
            merged = merge(place, count, [merged] + gate([swap(merged, "narrow", bit)], last))
            last = [merged]
        elif step == "M":
            for bit in message_bits:
                merged = merge(place, count, [merged] + gate([swap(merged, "narrow", bit)], last))
            (merged,) = gate([merged], last)
            grad_cross_flat, grad_cross_proj, sum_cross_grad, sum_cross, back = message_backward(
                count, merged, msg_in, cross_heads, cross_prob, cross_mix, cross_flat, cross_proj
            )
            last = [back]
        elif step == "B":
            for bit in bits_of(wide)[:-1]:
                back = back + gate([swap(back, "wide", bit)], last)[0]
            other = swap(back.astype(LOW), "wide", bits_of(wide)[-1])
            last = [back]
        elif step == "P":
            blocks = gate(blocks, last)
            pieces = [piece if k == 0 else swap(piece, "wide", k) for k, piece in enumerate(blocks)]
        elif step == "E":
            grad_message_weight, msg_sums, grad_cls = message_end(
                chunk, group, count, merged, back, gate([other], last)[0], msg_normed, msg_inv, message_gain, cls_rows,
                message_weight,
            )
            last = [grad_message_weight]
        elif step == "C":
            output_tokens, grad_tokens = collect(place, pieces[:1] + gate(pieces[1:], last), grad_cls)
            last = [grad_tokens]
    while attn.value is None or far.value is None:
        last = far.turn(*attn.turn(*last))
    far_value = far.value
    grad_attn_own = jnp.concatenate(attn.value, axis=0)
    sums = merged[:count].reshape(count, width)
    grad_up_bias = lax.dynamic_slice_in_dim(sums[6 : 6 + wide].reshape(-1), wide_idx * hidden, hidden, 0)

    return (
        output_tokens.transpose(0, 2, 1),
        grad_tokens.transpose(0, 2, 1),
        grad_message_weight,
        msg_sums[0],
        msg_sums[1],
        msg_sums[2],
        grad_cross_flat.reshape(3, part, width).transpose(2, 0, 1),
        jnp.stack([sum_cross[0, :part], sum_cross[0, 2 * part :]]),
        grad_cross_proj,
        sum_cross_grad[0],
        sums[4],
        sums[5],
        grad_attn_own[: 3 * part].reshape(3, part, width).transpose(2, 0, 1),
        own_cols(sums[count - 2 :]),
        grad_attn_own[3 * part :],
        own_cols(sums[3]),
        sums[1],
        sums[2],
        far_value[0],
        grad_up_bias,
        far_value[1],
        own_cols(sums[0]),
    )


def solution(mesh):
    return jax.shard_map(
        body,
        mesh=mesh,
        in_specs=(
            P("narrow", None, "wide"),
            P("narrow", None, "wide"),
            P(),
            P(),
            P(),
            P(),
            P(),
            P(),
            P(None, None, "wide"),
            P(None, "wide"),
            P("wide", None),
            P(),
            P(),
            P(),
            P(None, None, "wide"),
            P(None, "wide"),
            P("wide", None),
            P("wide"),
            P(),
            P(),
            P(None, "wide"),
            P("wide"),
            P("wide", None),
            P("wide"),
        ),
        out_specs=(
            P("narrow", None, "wide"),
            P("narrow", None, "wide"),
            P(),
            P(),
            P(),
            P(),
            P(None, None, "wide"),
            P(None, "wide"),
            P("wide", None),
            P(),
            P(),
            P(),
            P(None, None, "wide"),
            P(None, "wide"),
            P("wide", None),
            P("wide"),
            P(),
            P(),
            P(None, "wide"),
            P("wide"),
            P("wide", None),
            P("wide"),
        ),
        check_vma=False,
    )
```

```python
import functools
import jax
import jax.numpy as jnp
from jax import lax
from jax.experimental import pallas as pl
from jax.experimental.pallas import tpu as pltpu
from jax.sharding import PartitionSpec as P

VIDEO_FRAMES = 8
HD = 64
EPS = 1e-05
ROW_TILE = 16
LOW = jnp.bfloat16
F32 = jnp.float32
VMEM_LIMIT = 56 * 1024 * 1024
ANY = pl.BlockSpec(memory_space=pl.ANY)
VMEM = pl.BlockSpec(memory_space=pltpu.VMEM)
SMEM = pl.BlockSpec(memory_space=pltpu.SMEM)


def dot(left, right, dims):
    return lax.dot_general(left, right, (dims, ((), ())), preferred_element_type=F32)


def mat_mul(left, right):
    return dot(left, right, ((1,), (0,)))


def mat_tn(left, right):
    return dot(left, right, ((0,), (0,)))


def mat_nt(left, right):
    return dot(left, right, ((1,), (1,)))


def normalize(values):
    row_mean = jnp.mean(values, axis=-1, keepdims=True)
    centred = values - row_mean
    inv_std = lax.rsqrt(jnp.mean(centred * centred, axis=-1, keepdims=True) + EPS)
    return (centred * inv_std, inv_std)


def norm_back(grad_norm, normed, inv_std, norm_gain):
    scaled = grad_norm * norm_gain
    return inv_std * (
        scaled
        - jnp.mean(scaled, axis=-1, keepdims=True)
        - normed * jnp.mean(scaled * normed, axis=-1, keepdims=True)
    )


def bits_of(size):
    return [1 << b for b in range(size.bit_length() - 1)]


def reorder(parts, index):
    parts = list(parts)
    for bit in bits_of(len(parts)):
        odd = (index & bit) != 0
        parts = [jnp.where(odd, parts[k ^ bit], parts[k]) for k in range(len(parts))]
    return parts


def call(kernel, name, micros=0.0, **options):
    return pl.pallas_call(
        kernel,
        name=name,
        compiler_params=pltpu.CompilerParams(vmem_limit_bytes=VMEM_LIMIT),
        cost_estimate=pl.CostEstimate(
            flops=int(micros * 1.0e9), bytes_accessed=int(micros * 3.0e6), transcendentals=0
        ),
        **options,
    )


def shaped(shape, dtype):
    return jax.ShapeDtypeStruct(tuple(shape), dtype)


def whole(array):
    return pl.BlockSpec(array.shape, lambda *_: (0,) * array.ndim)


def fixed(shape):
    return pl.BlockSpec(tuple(shape), lambda *_: (0,) * len(shape))


def per_step(shape):
    return pl.BlockSpec((1,) + tuple(shape[1:]), lambda f: (f,) + (0,) * (len(shape) - 1))


def row_of(ref):
    return ref[...].reshape(1, -1)


def head_masks(width):
    lane = lax.broadcasted_iota(jnp.int32, (1, width), 1) // HD
    return [lane == h for h in range(width // HD)]


def stack_heads(values, masks, scale=1.0):
    return jnp.concatenate([values * jnp.where(m, scale, 0.0).astype(values.dtype) for m in masks], axis=0)


def pick_heads(values, masks):
    size = values.shape[0] // len(masks)
    picked = values[:size]
    for h in range(1, len(masks)):
        picked = jnp.where(masks[h], values[h * size : (h + 1) * size], picked)
    return picked


def weight_copies(refs, shards, place_ref, buf, sem):
    whole_count = 2 * shards - len(refs)
    odd = place_ref[1]
    copies = []
    for j in range(whole_count):
        copies.append([pltpu.make_async_copy(refs[j], buf.at[j], sem.at[j, 0])])
    rest = refs[whole_count:]
    for i in range(len(rest) // 2):
        half = rest[2 * i].shape[0]
        at = pl.multiple_of(odd * half, half)
        other = pl.multiple_of((1 - odd) * half, half)
        j = whole_count + i
        copies.append([
            pltpu.make_async_copy(rest[2 * i], buf.at[j, pl.ds(at, half)], sem.at[j, 0]),
            pltpu.make_async_copy(rest[2 * i + 1], buf.at[j, pl.ds(other, half)], sem.at[j, 1]),
        ])
    return copies


def start_all(copies):
    for group in copies:
        for copy in group:
            copy.start()


def wait_all(copies):
    for group in copies:
        for copy in group:
            copy.wait()


def attn_forward_kernel(waits, place_ref, gain_ref, shift_ref, mlp_gain_ref, mlp_shift_ref, base_ref, *refs):
    shards = refs[-3].shape[0]
    toks, refs = refs[:shards], refs[shards:]
    sums, refs = refs[:shards], refs[shards:]
    packs, refs = refs[:shards], refs[shards:]
    weights, refs = refs[: -14 - waits], refs[-14:]
    (normed_ref, inv_ref, attn_in_ref, heads_ref, prob_ref, mix_ref, hidden_ref, mlp_normed_ref,
     mlp_inv_ref, mlp_in_ref, tok_buf, w_buf, w_sem, msg_buf) = refs
    part, patches = toks[0].shape[1], toks[0].shape[2]
    seq_pad, width = normed_ref.shape[1], normed_ref.shape[2]
    frames = pl.num_programs(0)
    frame = pl.program_id(0)
    wide_idx = place_ref[0]
    copies = weight_copies(weights, shards, place_ref, w_buf, w_sem)

    @pl.when(frame == 0)
    def _():
        start_all(copies)
        tok_buf[...] = jnp.zeros_like(tok_buf)
        total = base_ref[...]
        for ref in sums:
            total += ref[...]
        msg_buf[...] = total

    for k in range(shards):
        at = pl.multiple_of((wide_idx ^ k) * part, part)
        at_frame = (wide_idx & 1) * frames + frame if k == 2 else 0
        tok_buf[pl.ds(at, part), :patches] = toks[k][at_frame]
    tokens = tok_buf[...].T[:seq_pad].astype(F32)
    group = msg_buf[...]
    own = lax.broadcasted_iota(jnp.int32, (group.shape[0], 1), 0) == wide_idx * frames + frame
    message = jnp.sum(jnp.where(own, group, 0.0), axis=0, keepdims=True)
    row = lax.broadcasted_iota(jnp.int32, (seq_pad, 1), 0)
    full = jnp.where(row == patches, message, tokens)
    normed, inv = normalize(full)
    normed_ref[0] = normed
    inv_ref[0] = inv
    gain, shift, mlp_gain, mlp_shift = map(row_of, (gain_ref, shift_ref, mlp_gain_ref, mlp_shift_ref))
    attn_in = (normed * gain + shift).astype(LOW)
    attn_in_ref[0] = attn_in
    masks = head_masks(part)
    live = lax.broadcasted_iota(jnp.int32, (1, seq_pad), 1) <= patches
    total = full + jnp.concatenate(reorder([p[1:2, 2 * part : 3 * part] for p in packs], wide_idx), axis=1)

    @pl.when(frame == 0)
    def _():
        wait_all(copies)

    heads = []
    for k in range(shards):
        proj = mat_nt(attn_in, w_buf[k, : 3 * part])
        queries = (proj[:, :part] + packs[k][1:2, :part]).astype(LOW)
        keys = proj[:, part : 2 * part].astype(LOW)
        values = (proj[:, 2 * part :] + packs[k][1:2, part : 2 * part]).astype(LOW)
        heads_ref[0, k, 0] = queries
        heads_ref[0, k, 1] = keys
        heads_ref[0, k, 2] = values
        heads.append((queries, keys, values))

    def score(k):
        queries, keys, _ = heads[k]
        return mat_nt(stack_heads(queries, masks, HD ** (-0.5)), keys)

    def finish_shard(k):
        mix_ref[0, k] = pick_heads(mat_mul(prob_ref[0, k], heads[k][2]), masks).astype(LOW)

    scores = [score(0)]
    for k in range(shards):
        if k + 1 < shards:
            scores.append(score(k + 1))
        if k > 0:
            finish_shard(k - 1)
        live_scores = jnp.where(live, scores[k], -1e30)
        exps = jnp.exp(live_scores - jnp.max(live_scores, axis=-1, keepdims=True))
        prob_ref[0, k] = (exps * (1.0 / jnp.sum(exps, axis=-1, keepdims=True))).astype(LOW)
    finish_shard(shards - 1)
    for k in range(shards):
        total += mat_mul(mix_ref[0, k], w_buf[k, 3 * part :])
    hidden_ref[0] = total
    mlp_normed, mlp_inv = normalize(total.astype(LOW).astype(F32))
    mlp_normed_ref[0] = mlp_normed
    mlp_inv_ref[0] = mlp_inv
    mlp_in_ref[0] = (mlp_normed * mlp_gain + mlp_shift).astype(LOW)


def attn_forward(seq_pad, place, vecs, base, toks, sums, packs, weights, after):
    frames, part, patches = toks[0].shape
    shards = len(toks)
    width = part * shards
    heads = part // HD
    seq_lanes = -(-seq_pad // 128) * 128
    shapes = [
        ((frames, seq_pad, width), F32),
        ((frames, seq_pad, 1), F32),
        ((frames, seq_pad, width), LOW),
        ((frames, shards, 3, seq_pad, part), LOW),
        ((frames, shards, heads * seq_pad, seq_pad), LOW),
        ((frames, shards, seq_pad, part), LOW),
        ((frames, seq_pad, width), F32),
        ((frames, seq_pad, width), F32),
        ((frames, seq_pad, 1), F32),
        ((frames, seq_pad, width), LOW),
    ]
    return call(
        functools.partial(attn_forward_kernel, len(after)),
        "attn_forward",
        0.0,
        grid=(frames,),
        in_specs=[SMEM] + [whole(v) for v in vecs] + [whole(base)]
        + [per_step(v.shape) if v.shape[0] == frames else whole(v) for v in toks]
        + [whole(v) for v in list(sums) + list(packs)]
        + [ANY] * (len(weights) + len(after)),
        out_specs=[per_step(s) for s, _ in shapes],
        out_shape=[shaped(s, d) for s, d in shapes],
        scratch_shapes=[
            pltpu.VMEM((width, seq_lanes), LOW),
            pltpu.VMEM((shards, 4 * part, width), LOW),
            pltpu.SemaphoreType.DMA((shards, 2)),
            pltpu.VMEM(base.shape, F32),
        ],
    )(place, *vecs, base, *toks, *sums, *packs, *weights, *after)


def mlp_kernel(frames, count, first, waits, place_ref, scale_ref, mlp_in_ref, *refs):
    packs, refs = refs[:count], refs[count:]
    if first:
        shards = 2 * count
        cots, refs = refs[:shards], refs[shards:]
    else:
        (grad_ref, acc_in, gacc_in), refs = refs[:3], refs[3:]
    each = 2 if first else 4
    weights, refs = refs[: each * count], refs[each * count + waits :]
    if first:
        (cot_ref, grad_ref), refs = refs[:2], refs[2:]
    acc_ref, gacc_ref, sums_ref = refs[:3]
    g_refs, refs = refs[3 : 3 + count], refs[3 + count :]
    w_buf, g_buf, act_buf, pre_buf, in_sem, out_sem, acc_buf, gacc_buf, sum_sem, acc_sem = refs[:10]
    rows, width = mlp_in_ref.shape
    hidden = act_buf.shape[1]
    step = rows // frames
    loads = []
    for i in range(count):
        if first:
            for j, ref in ((2 * i, weights[i]), (2 * i + 1, weights[count + i])):
                loads.append([pltpu.make_async_copy(ref, w_buf.at[j], in_sem.at[j, 0])])
        else:
            near, far = weights[4 * i : 4 * i + 2], weights[4 * i + 2 : 4 * i + 4]
            half = far[0].shape[0]
            at, other = (pl.multiple_of(odd * half, half) for odd in (place_ref[1], 1 - place_ref[1]))
            for j in range(2):
                to = w_buf.at[2 * i + j]
                loads.append([
                    pltpu.make_async_copy(near[j], to.at[pl.ds(at, half)], in_sem.at[2 * i + j, 0]),
                    pltpu.make_async_copy(far[j], to.at[pl.ds(other, half)], in_sem.at[2 * i + j, 1]),
                ])
    start_all(loads)
    carried = []
    if not first:
        carried = [
            pltpu.make_async_copy(acc_in, acc_buf, sum_sem.at[0]),
            pltpu.make_async_copy(gacc_in, gacc_buf, sum_sem.at[1]),
        ]
    start_all([carried])
    stores = [
        pltpu.make_async_copy(g_buf.at[2 * i + j], g_refs[i].at[pl.ds(j * width, width)], out_sem.at[2 * i + j])
        for i in range(count) for j in range(2)
    ]
    if first:
        cot_buf = refs[10]
        cot_buf[...] = jnp.zeros_like(cot_buf)
        part, patches = cots[0].shape[1:]
        for f in range(frames):
            for k in range(shards):
                at = pl.multiple_of((place_ref[0] ^ k) * part, part)
                at_frame = (place_ref[0] & 1) * frames + f if k == 2 else f
                cot_buf[pl.ds(at, part), :patches] = cots[k][at_frame]
            cot = cot_buf[...].T[:step]
            cot_ref[f] = cot
            grad_ref[f * step : (f + 1) * step] = (cot.astype(F32) * scale_ref[f]).astype(LOW)
    def before(i, f):
        at = slice(f * step, (f + 1) * step)
        return mat_mul(mlp_in_ref[at], w_buf[2 * i]), mat_nt(grad_ref[at], w_buf[2 * i + 1])

    def weight_grads(i):
        rows_of = slice(i * rows, (i + 1) * rows)
        up, down = 2 * i, 2 * i + 1
        for c in range(0, width, 256):
            yield
            g_buf[up, c : c + 256] = mat_tn(mlp_in_ref[:, c : c + 256], pre_buf[rows_of]).astype(LOW)
        stores[up].start()
        for c in range(0, hidden, 256):
            yield
            g_buf[down, c : c + 256] = mat_tn(act_buf[rows_of, c : c + 256], grad_ref[...]).astype(LOW)
        stores[down].start()

    pending = iter(())
    for i in range(count):
        up, down = 2 * i, 2 * i + 1
        wait_all(loads[up : down + 1])
        bias = packs[i][0:1]
        total = jnp.zeros((1, hidden), F32)
        ahead = [before(i, 0)]
        for f in range(frames):
            at = slice(f * step, (f + 1) * step)
            kept = slice(i * rows + f * step, i * rows + (f + 1) * step)
            if f + 1 < frames:
                ahead.append(before(i, f + 1))
            next(pending, None)
            next(pending, None)
            pre, grad_act = ahead[f]
            pre = pre + bias
            sig = 0.5 + 0.5 * jnp.tanh(0.851 * pre)
            act = pre * sig
            act_buf[kept] = act.astype(LOW)
            grad_pre = (grad_act * (sig + 1.702 * act * (1.0 - sig))).astype(LOW)
            pre_buf[kept] = grad_pre
            total += jnp.sum(grad_pre.astype(F32), axis=0, keepdims=True)
        sums_ref[i] = total
        for _ in pending:
            pass
        if i == 0:
            wait_all([carried])
        for f in range(frames):
            at = slice(f * step, (f + 1) * step)
            kept = slice(i * rows + f * step, i * rows + (f + 1) * step)
            out = mat_mul(act_buf[kept], w_buf[down])
            back = mat_nt(pre_buf[kept], w_buf[up])
            if i > 0 or not first:
                acc_buf[at] += out
                gacc_buf[at] += back
            else:
                acc_buf[at] = out
                gacc_buf[at] = back
            if i == count - 1:
                for n, (buf, ref) in enumerate(((acc_buf, acc_ref), (gacc_buf, gacc_ref))):
                    store = pltpu.make_async_copy(buf.at[pl.ds(f * step, step)], ref.at[pl.ds(f * step, step)], acc_sem.at[n, f])
                    store.start()
                    stores.append(store)
        pending = weight_grads(i)
    for _ in pending:
        pass
    for store in stores:
        store.wait()


def mlp_step(frames, place, scale, mlp_in, packs, weights, cots=None, carried=None, after=()):
    rows, width = mlp_in.shape
    count = len(packs)
    first = cots is not None
    hidden = packs[0].shape[1]
    step = rows // frames
    ins = [place, scale, mlp_in, *packs, *(cots if first else carried)]
    shapes = [shaped((frames, step, width), LOW), shaped((rows, width), LOW)] if first else []
    shapes += [shaped((rows, width), F32)] * 2 + [shaped((count, 1, hidden), F32)]
    grads = [shaped((width + hidden, width), LOW)] * count
    scratch = [
        pltpu.VMEM((2 * count, width, hidden), LOW),
        pltpu.VMEM((2 * count, width, hidden), LOW),
        pltpu.VMEM((count * rows, hidden), LOW),
        pltpu.VMEM((count * rows, hidden), LOW),
        pltpu.SemaphoreType.DMA((2 * count, 2)),
        pltpu.SemaphoreType.DMA((2 * count,)),
        pltpu.VMEM((rows, width), F32),
        pltpu.VMEM((rows, width), F32),
        pltpu.SemaphoreType.DMA((2,)),
        pltpu.SemaphoreType.DMA((2, frames)),
    ]
    if first:
        scratch.append(pltpu.VMEM((width, -(-step // 128) * 128), LOW))
    return call(
        functools.partial(mlp_kernel, frames, count, first, len(after)),
        "mlp",
        18.5,
        in_specs=[SMEM, SMEM, VMEM]
        + [VMEM] * (len(ins) - 3 if first else count + 1)
        + [ANY] * ((0 if first else 2) + len(weights) + len(after)),
        out_specs=[VMEM] * (len(shapes) - 3) + [ANY] * 2 + [VMEM] + [ANY] * len(grads),
        out_shape=shapes + grads,
        scratch_shapes=scratch,
    )(*ins, *weights, *after)


def attn_backward_kernel(
    shards, waits, place_ref, scale_ref, gain_ref, mlp_gain_ref, res_ref, acc_ref, gacc_ref, mlp_normed_ref, mlp_inv_ref, cot_ref,
    normed_ref, inv_ref, heads_ref, prob_ref, *refs
):
    packs, refs = refs[:shards], refs[shards:]
    ups, refs = refs[: shards // 2], refs[shards // 2 :]
    outs = shards + 3 + 2
    weights, refs = refs[: len(refs) - outs - waits], refs[len(refs) - outs :]
    pieces, refs = refs[:shards], refs[shards:]
    proj_ref, low_ref, sums_ref, w_buf, w_sem = refs
    part = heads_ref.shape[4]
    patches = pieces[0].shape[3]
    seq_pad, width = res_ref.shape[1:]
    gain, mlp_gain = row_of(gain_ref), row_of(mlp_gain_ref)
    frame = pl.program_id(0)
    wide_idx = place_ref[0]
    copies = weight_copies(weights, shards, place_ref, w_buf, w_sem)

    @pl.when(frame == 0)
    def _():
        start_all(copies)
        sums_ref[...] = jnp.zeros_like(sums_ref)
        rows = [ref[i] for ref in ups for i in range(2)]
        for k, values in enumerate(reorder(rows, wide_idx)):
            sums_ref[6 + k] = values

    def columns(values, i):
        blocks = values.T
        blocks = reorder([blocks[j * part : (j + 1) * part, :patches] for j in range(shards)], wide_idx)
        for ref, block in zip(pieces, blocks):
            ref[0, i] = block

    down_bias = jnp.concatenate(reorder([p[1:2, 3 * part : 4 * part] for p in packs], wide_idx), axis=1)
    columns((res_ref[0] + acc_ref[0] + down_bias).astype(LOW), 0)
    grad_res = cot_ref[0].astype(F32) * scale_ref[frame]
    gacc, mlp_normed = gacc_ref[0], mlp_normed_ref[0]
    hidden = grad_res + norm_back(gacc, mlp_normed, mlp_inv_ref[0], mlp_gain)

    def add_sum(row, values):
        sums_ref[row] += jnp.sum(values, axis=0, keepdims=True)

    add_sum(0, grad_res)
    add_sum(1, gacc * mlp_normed)
    add_sum(2, gacc)
    add_sum(3, hidden)
    low = hidden.astype(LOW)
    low_ref[0] = low
    masks = head_masks(part)
    scale = HD ** (-0.5)
    back = jnp.zeros(hidden.shape, F32)
    bias_sums = []

    @pl.when(frame == 0)
    def _():
        wait_all(copies)

    mixes = [stack_heads(mat_nt(low, w_buf[k, 3 * part :]).astype(LOW), masks) for k in range(shards)]

    def grad_prob_of(k):
        return mat_nt(mixes[k], heads_ref[0, k, 2])

    def finish_shard(k, grad_score):
        prob_low = prob_ref[0, k]
        grad_value = mat_tn(prob_low, mixes[k])
        grad_query = pick_heads(mat_mul(grad_score, heads_ref[0, k, 1]), masks)
        grad_key = mat_tn(grad_score, stack_heads(heads_ref[0, k, 0], masks))
        proj = jnp.concatenate([grad_query * scale, grad_key * scale, grad_value], axis=1).astype(LOW)
        proj_ref[0, k] = proj
        bias_sums.append(jnp.sum(proj.astype(F32), axis=0, keepdims=True))

    grad_probs = [grad_prob_of(0)]
    grad_score = None
    for k in range(shards):
        if k + 1 < shards:
            grad_probs.append(grad_prob_of(k + 1))
        if k > 0:
            finish_shard(k - 1, grad_score)
        prob = prob_ref[0, k].astype(F32)
        weighted = prob * grad_probs[k]
        grad_score = (weighted - prob * jnp.sum(weighted, axis=-1, keepdims=True)).astype(LOW)
    finish_shard(shards - 1, grad_score)
    for k in range(shards):
        back += mat_mul(proj_ref[0, k], w_buf[k, : 3 * part])
    for i, at in ((6 + shards, 0), (7 + shards, 2 * part)):
        own = reorder([values[:, at : at + part] for values in bias_sums], wide_idx)
        sums_ref[i] += jnp.concatenate(own, axis=1)
    normed = normed_ref[0]
    add_sum(4, back * normed)
    add_sum(5, back)
    total = hidden + norm_back(back, normed, inv_ref[0], gain)
    row = lax.broadcasted_iota(jnp.int32, (seq_pad, 1), 0)
    sums_ref[8 + shards + frame] = jnp.sum(jnp.where(row == patches, total, 0.0), axis=0, keepdims=True)
    columns(total.astype(LOW), 1)


def attn_backward(patches, place, scale, vecs, per_frame, packs, ups, weights, after):
    frames, seq_pad, width = per_frame[0].shape
    heads = per_frame[8]
    shards, part = heads.shape[1], heads.shape[4]
    blocks = [(frames, 2, part, patches)] * shards
    proj = (frames, shards, seq_pad, 3 * part)
    return call(
        functools.partial(attn_backward_kernel, shards, len(after)),
        "attn_backward",
        20.3,
        grid=(frames,),
        in_specs=[SMEM, SMEM]
        + [whole(v) for v in vecs]
        + [per_step(v.shape) for v in per_frame]
        + [whole(v) for v in list(packs) + list(ups)]
        + [ANY] * (len(weights) + len(after)),
        out_specs=[per_step(b) for b in blocks]
        + [per_step(proj), per_step((frames, seq_pad, width)), fixed((8 + shards + frames, 1, width))],
        out_shape=[shaped(b, LOW) for b in blocks]
        + [
            shaped(proj, LOW),
            shaped((frames, seq_pad, width), LOW),
            shaped((8 + shards + frames, 1, width), F32),
        ],
        scratch_shapes=[
            pltpu.VMEM((shards, 4 * part, width), LOW),
            pltpu.SemaphoreType.DMA((shards, 2)),
        ],
    )(place, scale, *vecs, *per_frame, *packs, *ups, *weights, *after)


def attn_grads_kernel(waits, attn_in_ref, low_ref, proj_ref, mix_ref, *refs):
    grad_refs, (proj_buf, mix_buf) = refs[waits:-2], refs[-2:]
    count = len(grad_refs)
    frames, seq_pad, part = mix_ref.shape[0], mix_ref.shape[2], mix_ref.shape[3]
    for i in range(count):
        for f in range(frames):
            at = slice(f * seq_pad, (f + 1) * seq_pad)
            proj_buf[at] = proj_ref[f, i]
            mix_buf[at] = mix_ref[f, i]
        for c in range(0, 3 * part, part):
            grad_refs[i][c : c + part] = mat_tn(proj_buf[:, c : c + part], attn_in_ref[...]).astype(LOW)
        grad_refs[i][3 * part :] = mat_tn(mix_buf[...], low_ref[...]).astype(LOW)


def attn_grads(attn_in, proj, low, mix, after):
    frames, shards, seq_pad, part = mix.shape
    width = attn_in.shape[-1]
    rows = frames * seq_pad
    return call(
        functools.partial(attn_grads_kernel, len(after)),
        "attn_grads",
        0.0,
        grid=(1,),
        in_specs=[fixed((rows, width)), fixed((rows, width)), fixed(proj.shape), fixed(mix.shape)] + [ANY] * len(after),
        out_specs=[fixed((4 * part, width))] * shards,
        out_shape=[shaped((4 * part, width), LOW)] * shards,
        scratch_shapes=[pltpu.VMEM((rows, 3 * part), LOW), pltpu.VMEM((rows, part), LOW)],
    )(attn_in.reshape(rows, width), low.reshape(rows, width), proj, mix, *after)


def same_video(place_ref, group, rows, columns):
    first = pl.program_id(0) * columns

    def video(position):
        position = position + first
        return (((position // group) ^ place_ref[2]) * group + position % group) // VIDEO_FRAMES

    row = lax.broadcasted_iota(jnp.int32, (rows, columns), 0) % columns
    column = lax.broadcasted_iota(jnp.int32, (rows, columns), 1)
    return video(row) == video(column)


def message_forward_kernel(
    group, waits, place_ref, cls_ref, weight_ref, m_bias_ref, gain_ref, shift_ref, offset_ref, flat_ref, bias_ref,
    proj_ref, *refs
):
    normed_ref, inv_ref, in_ref, heads_ref, prob_ref, mix_ref, base_ref, sum_ref = refs[waits:]
    part = proj_ref.shape[0]
    chunk = cls_ref.shape[0]
    message = mat_mul(cls_ref[...], weight_ref[...]) + row_of(m_bias_ref)
    normed, inv = normalize(message)
    normed_ref[...] = normed
    inv_ref[...] = inv
    msg_in = (normed * row_of(gain_ref) + row_of(shift_ref)).astype(LOW)
    in_ref[...] = msg_in
    proj = mat_nt(msg_in, flat_ref[...])
    queries = (proj[:, :part] + bias_ref[0:1]).astype(LOW)
    keys = proj[:, part : 2 * part].astype(LOW)
    values = (proj[:, 2 * part :] + bias_ref[1:2]).astype(LOW)
    heads_ref[0, 0] = queries
    heads_ref[0, 1] = keys
    heads_ref[0, 2] = values
    masks = head_masks(part)
    scores = mat_nt(stack_heads(queries, masks, HD ** (-0.5)), keys)
    scores = jnp.where(same_video(place_ref, group, len(masks) * chunk, chunk), scores, -1e30)
    exps = jnp.exp(scores - jnp.max(scores, axis=-1, keepdims=True))
    prob = exps / jnp.sum(exps, axis=-1, keepdims=True)
    prob_ref[0] = prob
    mix = pick_heads(mat_mul(prob.astype(LOW), values), masks).astype(LOW)
    mix_ref[...] = mix

    @pl.when(pl.program_id(0) == 0)
    def _():
        base_ref[...] = message[:group] + row_of(offset_ref)
        sum_ref[...] = mat_mul(mix, proj_ref[...])[:group]


def message_forward(chunk, group, place, cls_rows, weight, vecs, flat, bias, proj, after):
    count, width = cls_rows.shape
    part = proj.shape[0]
    heads = part // HD
    chunks = count // chunk
    rows = lambda columns: pl.BlockSpec((chunk, columns), lambda c: (c, 0))
    return call(
        functools.partial(message_forward_kernel, group, len(after)),
        "message_forward",
        4.2,
        grid=(chunks,),
        in_specs=[SMEM, rows(width)]
        + [whole(v) for v in (weight, *vecs, flat, bias, proj)]
        + [ANY] * len(after),
        out_specs=[
            rows(width), rows(1), rows(width),
            per_step((chunks, 3, chunk, part)), per_step((chunks, heads * chunk, chunk)),
            rows(part), fixed((group, width)), fixed((group, width)),
        ],
        out_shape=[
            shaped((count, width), F32),
            shaped((count, 1), F32),
            shaped((count, width), LOW),
            shaped((chunks, 3, chunk, part), LOW),
            shaped((chunks, heads * chunk, chunk), F32),
            shaped((count, part), LOW),
            shaped((group, width), F32),
            shaped((group, width), F32),
        ],
    )(place, cls_rows, weight, *vecs, flat, bias, proj, *after)


def message_rows(all_ref, count, chunk):
    return all_ref[pl.ds(count + pl.program_id(0) * chunk, chunk)][:, 0]


def message_backward_kernel(
    count, all_ref, in_ref, heads_ref, prob_ref, mix_ref, flat_ref, proj_ref, grad_flat_ref, grad_proj_ref,
    sum_grad_ref, sum_cross_ref, back_ref
):
    @pl.when(pl.program_id(0) == 0)
    def _():
        for ref in (grad_flat_ref, grad_proj_ref, sum_grad_ref, sum_cross_ref):
            ref[...] = jnp.zeros_like(ref)

    part = proj_ref.shape[0]
    masks = head_masks(part)
    grad = message_rows(all_ref, count, in_ref.shape[0]).astype(LOW)
    sum_grad_ref[...] += jnp.sum(grad.astype(F32), axis=0, keepdims=True)
    grad_proj_ref[...] += mat_tn(mix_ref[...], grad)
    grad_mix = mat_nt(grad, proj_ref[...]).astype(LOW)
    mix_heads = stack_heads(grad_mix, masks)
    queries, keys, values = heads_ref[0, 0], heads_ref[0, 1], heads_ref[0, 2]
    prob = prob_ref[0]
    grad_prob = mat_nt(mix_heads, values)
    grad_score = prob * (grad_prob - jnp.sum(prob * grad_prob, axis=-1, keepdims=True))
    score_low = grad_score.astype(LOW)
    grad_query = pick_heads(mat_mul(score_low, keys), masks) * HD ** (-0.5)
    grad_key = mat_tn(score_low, stack_heads(queries, masks)) * HD ** (-0.5)
    grad_value = mat_tn(prob.astype(LOW), mix_heads)
    cross = jnp.concatenate([grad_query, grad_key, grad_value], axis=1).astype(LOW)
    sum_cross_ref[...] += jnp.sum(cross.astype(F32), axis=0, keepdims=True)
    grad_flat_ref[...] += mat_tn(cross, in_ref[...])
    back_ref[...] = mat_mul(cross, flat_ref[...])


def message_backward(count, merged, msg_in, heads, prob, mix, flat, proj):
    total, width = msg_in.shape
    part = proj.shape[0]
    chunks, _, chunk, _ = heads.shape
    rows = lambda columns: pl.BlockSpec((chunk, columns), lambda c: (c, 0))
    shapes = [(3 * part, width), (part, width), (1, width), (1, 3 * part)]
    return call(
        functools.partial(message_backward_kernel, count),
        "message_backward",
        0.0,
        grid=(chunks,),
        in_specs=[whole(merged), rows(width), per_step(heads.shape), per_step(prob.shape), rows(part)]
        + [whole(flat), whole(proj)],
        out_specs=[fixed(s) for s in shapes] + [rows(width)],
        out_shape=[shaped(s, F32) for s in shapes + [(total, width)]],
    )(merged, msg_in, heads, prob, mix, flat, proj)


def message_end_kernel(
    group, count, all_ref, back_ref, other_ref, normed_ref, inv_ref, gain_ref, cls_ref, weight_ref, grad_weight_ref,
    sums_ref, grad_cls_ref
):
    @pl.when(pl.program_id(0) == 0)
    def _():
        grad_weight_ref[...] = jnp.zeros_like(grad_weight_ref)
        sums_ref[...] = jnp.zeros_like(sums_ref)

    back = back_ref[...] + other_ref[...].astype(F32)
    normed = normed_ref[...]
    grad = message_rows(all_ref, count, back.shape[0]) + norm_back(back, normed, inv_ref[...], row_of(gain_ref))
    low = grad.astype(LOW)
    for row, values in enumerate((low.astype(F32), back * normed, back)):
        sums_ref[row : row + 1] += jnp.sum(values, axis=0, keepdims=True)
    grad_weight_ref[...] += mat_tn(cls_ref[...], low)

    @pl.when(pl.program_id(0) == 0)
    def _():
        grad_cls_ref[...] = mat_nt(weight_ref[...], low)[:, :group]


def message_end(chunk, group, count, merged, back, other, normed, inv, gain, cls_rows, weight):
    total, width = back.shape
    rows = lambda columns: pl.BlockSpec((chunk, columns), lambda c: (c, 0))
    return call(
        functools.partial(message_end_kernel, group, count),
        "message_end",
        0.0,
        grid=(total // chunk,),
        in_specs=[whole(merged)] + [rows(width)] * 3 + [rows(1), whole(gain), rows(width), whole(weight)],
        out_specs=[fixed((width, width)), fixed((8, width)), fixed((width, group))],
        out_shape=[shaped((width, width), F32), shaped((8, width), F32), shaped((width, group), F32)],
    )(merged, back, other, normed, inv, gain, cls_rows, weight)


def merge_kernel(count, ordered, place_ref, *refs):
    refs, out_ref = refs[:-1], refs[-1]
    size = refs[0].shape[0] - count
    total = refs[0][:count]
    for ref in refs[1:]:
        total += ref[:count]
    out_ref[:count] = total
    for k, ref in enumerate(refs):
        at = (place_ref[0] ^ k) if ordered else k
        out_ref[pl.ds(count + at * size, size)] = ref[count:]


def merge(place, count, buffers, ordered=False):
    rows, one, width = buffers[0].shape
    return call(
        functools.partial(merge_kernel, count, ordered),
        "merge",
        0.0,
        in_specs=[SMEM] + [VMEM] * len(buffers),
        out_specs=VMEM,
        out_shape=shaped((count + (rows - count) * len(buffers), one, width), F32),
    )(place, *buffers)


def collect_kernel(place_ref, *refs):
    *pieces, grad_cls_ref, tok_ref, grad_ref = refs
    frames, _, part, patches = pieces[0].shape
    own = grad_cls_ref[pl.ds(pl.multiple_of(place_ref[0] * part, part), part), :]
    lane = lax.broadcasted_iota(jnp.int32, (part, patches), 1)
    for j, piece in enumerate(reorder([ref[...] for ref in pieces], place_ref[0])):
        for f in range(frames):
            i = j * frames + f
            tok_ref[i] = piece[f, 0]
            grad = piece[f, 1].astype(F32)
            grad_ref[i] = jnp.where(lane == 0, grad + own[:, i : i + 1], grad).astype(LOW)


def collect(place, pieces, grad_cls):
    frames, _, part, patches = pieces[0].shape
    shape = (frames * len(pieces), part, patches)
    return call(
        collect_kernel,
        "collect",
        0.0,
        in_specs=[SMEM] + [VMEM] * (len(pieces) + 1),
        out_specs=[VMEM] * 2,
        out_shape=[shaped(shape, LOW)] * 2,
    )(place, *pieces, grad_cls)


def swap(block, axis, flip):
    return lax.ppermute(block, axis, [(i, i ^ flip) for i in range(lax.axis_size(axis))])


def gate(arrays, after):
    return list(lax.optimization_barrier((tuple(arrays), tuple(after)))[0])


def frames_in(block, after):
    index = lax.axis_index("wide")
    part = block.shape[0] // lax.axis_size("wide")
    (block,) = gate([block], after)
    crossed = swap(lax.dynamic_slice_in_dim(block, ((index ^ 2) & 2) * part, 2 * part, 0), "wide", 2)
    own = lax.dynamic_slice_in_dim(block, index * part, part, 0)
    near = swap(lax.dynamic_slice_in_dim(block, (index ^ 1) * part, part, 0), "wide", 1)
    return [own, near, crossed]


def frames_end(pieces, after):
    own, near, crossed = pieces
    (crossed,) = gate([crossed], after)
    part = own.shape[0]
    index = lax.axis_index("wide")
    far = swap(lax.dynamic_slice_in_dim(crossed, ((index & 1) ^ 1) * part, part, 0), "wide", 1)
    return [own, near, crossed, far]


def send_half(block, after):
    odd = lax.axis_index("narrow") & 1
    half = block.shape[0] // 2
    sent = lax.dynamic_slice_in_dim(gate([block], after)[0], odd * half, half, 0)
    return [swap(sent, "wide", bit) for bit in bits_of(lax.axis_size("wide"))[1:]]


def near_shards(block):
    return [block, swap(block, "wide", 1)]


def far_shards(near, far):
    return [near, far, swap(near, "wide", 1), swap(far, "wide", 1)]


def row_at(base, moves):
    at = base
    for bit, rows, flipped in moves:
        is_set = ((lax.axis_index("narrow") & bit) != 0).astype(jnp.int32)
        at = at + rows * ((1 - is_set) if flipped else is_set)
    return at


def added(sums, together=False):
    blocks = []
    for terms, size in sums:
        rows = [
            array if not moves and array.shape[0] == size else lax.dynamic_slice_in_dim(array, row_at(base, moves), size, 0)
            for array, base, moves in terms
        ]
        blocks.append(sum(row.astype(F32) for row in rows).astype(LOW))
    return [jnp.concatenate(blocks, axis=0)] if together else blocks


def joined(pairs, bits):
    odds = [(lax.axis_index("narrow") & bit) != 0 for bit in bits]
    return [
        jnp.where(odd, jnp.concatenate([other, block], axis=0), jnp.concatenate([block, other], axis=0))
        for (block, other), odd in zip(pairs, odds)
    ]


def orders(count):
    bits = bits_of(lax.axis_size("narrow"))[:count]
    return [bits, bits[1:] + bits[:1]]


def regions_of(arrays, base=0):
    half = arrays[0].shape[0] // 2
    return [[(array, n * half, []) for array in arrays] for n in range(2)], half


def halving(regions, size, steps):
    for at in range(steps):
        bits = [order[at] for order in orders(steps)]
        size = size // 2
        sent = added([
            ([(array, base, moves + [(bit, size, True)]) for array, base, moves in terms], size)
            for bit, terms in zip(bits, regions)
        ])
        received = yield sent, [swap(block, "narrow", bit) for block, bit in zip(sent, bits)]
        regions = [
            [(array, base, moves + [(bit, size, False)]) for array, base, moves in terms] + [(block, 0, [])]
            for bit, terms, block in zip(bits, regions, received)
        ]
    return regions, size


def joining(blocks, steps):
    for at in reversed(range(steps)):
        bits = [order[at] for order in orders(steps)]
        others = yield blocks, [swap(block, "narrow", bit) for block, bit in zip(blocks, bits)]
        blocks = joined(list(zip(blocks, others)), bits)
    return [block.astype(F32) for block in blocks]


def whole_sum(blocks, steps):
    for bit in bits_of(lax.axis_size("narrow"))[steps:]:
        others = yield blocks, [swap(block, "narrow", bit) for block in blocks]
        blocks = added([([(a, 0, []), (b, 0, [])], a.shape[0]) for a, b in zip(blocks, others)])
    return blocks


def narrow_sum(arrays, steps):
    regions, left = yield from halving(*regions_of(arrays), steps)
    blocks = added([(terms, left) for terms in regions])
    blocks = yield from whole_sum(blocks, steps)
    return (yield from joining(blocks, steps))


class Chain:
    def __init__(self, steps):
        self.steps = steps
        self.value = None
        self.sent, self.received = next(steps)

    def turn(self, *after):
        if self.value is not None:
            return list(after)
        received = gate(self.received, after) if after else self.received
        try:
            self.sent, self.received = self.steps.send(received)
        except StopIteration as end:
            self.value = end.value
            return received
        return self.sent


def finish(chain):
    while chain.value is None:
        chain.turn()
    return chain.value


ORDER = "ofTwfmgfmAofmMaBPfaEfaCaf"


def body(
    frame_tokens,
    cotangent,
    caption_count,
    caption_len,
    message_weight,
    message_bias,
    message_gain,
    message_shift,
    cross_qkv,
    cross_bias,
    cross_proj,
    cross_offset,
    attn_gain,
    attn_shift,
    qkv_weight,
    qkv_bias,
    out_weight,
    out_bias,
    mlp_gain,
    mlp_shift,
    up_weight,
    up_bias,
    down_weight,
    down_bias,
):
    group, patches, part = frame_tokens.shape
    width = message_weight.shape[0]
    hidden = up_weight.shape[1]
    wide = lax.axis_size("wide")
    narrow = lax.axis_size("narrow")
    wide_idx = lax.axis_index("wide")
    narrow_idx = lax.axis_index("narrow")
    frames = group // wide
    seq_pad = -(-(patches + 1) // ROW_TILE) * ROW_TILE
    rows = frames * seq_pad
    all_frames = group * narrow
    chunk = max(c for c in range(VIDEO_FRAMES, 129, VIDEO_FRAMES) if all_frames % c == 0 and c % group == 0)
    place = jnp.stack([wide_idx, narrow_idx & 1, narrow_idx]).astype(jnp.int32)

    def own_cols(values):
        return lax.dynamic_slice_in_dim(values, wide_idx * part, part, values.ndim - 1)

    tokens_t = frame_tokens.transpose(0, 2, 1)
    pack = jnp.concatenate(
        [up_bias, qkv_bias.reshape(-1), out_bias, down_bias, frame_tokens[:, 0, :].astype(F32).reshape(-1)]
    ).reshape(-1, width)
    packs = [pack] + [swap(pack, "wide", k) for k in range(1, wide)]
    cls_rows = jnp.concatenate(
        reorder([p[2:].reshape(group, part).astype(LOW) for p in packs], wide_idx), axis=1
    )
    cls_own = cls_rows
    toks = frames_in(tokens_t, [cls_own])
    attn_own = jnp.concatenate(
        [qkv_weight.transpose(1, 2, 0).reshape(3 * part, width), out_weight], axis=0
    )
    attn_near = send_half(attn_own, [cls_own])
    narrow_bits = bits_of(narrow)
    cls_rows = jnp.concatenate([cls_rows, swap(cls_rows, "narrow", 1)], axis=0)
    attn_near = gate(attn_near, [cls_rows])
    attn_far = [swap(near, "narrow", 1) for near in attn_near]
    (cls_rows,) = gate([cls_rows], attn_near)
    for bit in narrow_bits[1:]:
        cls_rows = jnp.concatenate([cls_rows, swap(cls_rows, "narrow", bit)], axis=0)
    attn_far = gate(attn_far, [cls_rows])
    toks = frames_end(toks, [cls_rows])
    attn_weights = near_shards(attn_own)
    for near, far in zip(attn_near, attn_far):
        attn_weights += far_shards(near, far)
    cots = frames_in(cotangent.transpose(0, 2, 1), attn_far)

    caption_slot = jnp.arange(caption_len.shape[1])
    word_total = jnp.sum(
        jnp.where(caption_slot[None, :] < caption_count[:, None], caption_len, 0), axis=1
    ).astype(F32)
    video_scale = word_total / jnp.mean(word_total)
    own_video = (narrow_idx * group + wide_idx * frames + jnp.arange(frames)) // VIDEO_FRAMES
    video_match = own_video[:, None] == jnp.arange(video_scale.shape[0])[None, :]
    scale = jnp.sum(jnp.where(video_match, video_scale[None, :], 0.0), axis=1)

    up_shards, down_shards = near_shards(up_weight), near_shards(down_weight)

    cross_flat = cross_qkv.transpose(1, 2, 0).reshape(3 * part, width)
    msg_normed, msg_inv, msg_in, cross_heads, cross_prob, cross_mix, base, group_sum = message_forward(
        chunk, group, place, cls_rows, message_weight,
        (message_bias, message_gain, message_shift, cross_offset), cross_flat, cross_bias, cross_proj,
        toks[1:] + attn_weights[1:2] + attn_weights[4:5] + [up_shards[1], down_shards[1]],
    )
    group_sums = [group_sum] + [swap(group_sum, "wide", k) for k in range(1, wide)]

    odd = narrow_idx & 1
    half = width // 2

    def half_of(weight, after):
        return lax.dynamic_slice_in_dim(gate([weight], after)[0], odd * half, half, 0)

    near_parts = [
        swap(half_of(up_weight, toks[2:3]), "wide", 2),
        swap(half_of(down_weight, group_sums[2:]), "wide", 2),
    ]
    (near_parts[0],) = gate(near_parts[:1], group_sums[2:] + attn_far)
    near_other = [swap(near_parts[0], "wide", 1)]
    far_parts = [swap(near_parts[0], "narrow", 1)]

    forward = attn_forward(
        seq_pad, place, (attn_gain, attn_shift, mlp_gain, mlp_shift), base, toks, group_sums, packs, attn_weights,
        [up_shards[1], down_shards[1], near_other[0]],
    )
    (normed, inv, attn_in, heads, prob, mix, hidden_res, mlp_normed, mlp_inv, mlp_in) = gate(
        forward, far_parts + near_parts[1:]
    )
    mlp_in = mlp_in.reshape(rows, width)
    bits = bits_of(narrow)
    size = width + hidden
    cots = frames_end(cots, [mlp_in])
    (near_parts[1],) = gate(near_parts[1:], [mlp_in])
    far_parts.append(swap(near_parts[1], "narrow", 1))
    near_other.append(swap(near_parts[1], "wide", 1))
    (far_parts[0],) = gate(far_parts[:1], [mlp_in])
    far_other = [swap(far_parts[0], "wide", 1)]
    cot, grad_rows, acc, gacc, sum_up, *grad_own = mlp_step(
        frames, place, scale, mlp_in, packs[:2], up_shards + down_shards, cots=cots,
        after=[near_other[1]] + far_other,
    )
    acc, gacc, grad_rows, cot, *grad_own = gate([acc, gacc, grad_rows, cot] + grad_own, far_parts[1:])
    far_other.append(swap(far_parts[1], "wide", 1))
    grad_next = grad_own[1]

    def split_steps(rows):
        count = 0
        while count < len(bits) and rows % (2 * ROW_TILE) == 0:
            rows, count = rows // 2, count + 1
        return count

    mlp_steps, attn_count = split_steps(size // 2), split_steps(2 * part)
    own = Chain(halving(*regions_of([grad_own[0], swap(grad_next, "wide", 1)]), mlp_steps))
    mlp_weights = near_parts + far_parts + near_other + far_other
    acc, gacc, sum_up_far, *grad_far = mlp_step(
        frames, place, scale, mlp_in, packs[2:], mlp_weights, carried=(grad_rows, acc, gacc), after=own.sent
    )

    def far_steps(arrays):
        regions, left = yield from halving(*regions_of(arrays), mlp_steps)
        value = added([(terms, left) for terms in regions], True)
        crossed = yield value, [swap(value[0], "wide", 2)]
        blocks = added([
            (terms + [(crossed[0], n * left, [(0, 0, False)])], left) for n, terms in enumerate(finish(own)[0])
        ])
        blocks = yield from whole_sum(blocks, mlp_steps)
        return (yield from joining(blocks, mlp_steps))

    own.turn()
    grad_far = gate(grad_far, own.sent)
    far = Chain(far_steps([grad_far[0], swap(grad_far[1], "wide", 1)]))

    shape = (frames, seq_pad, width)
    per_frame = (
        hidden_res, acc.reshape(shape), gacc.reshape(shape), mlp_normed, mlp_inv, cot, normed, inv, heads, prob
    )
    *blocks, proj, low, sums = attn_backward(
        patches, place, scale, (attn_gain, mlp_gain), per_frame, packs, [sum_up, sum_up_far], attn_weights,
        own.sent + far.sent,
    )
    count = 8 + wide
    others = [swap(sums, "wide", k) for k in range(1, wide)]
    message_bits = list(bits)
    last, attn = [low], None
    for step in ORDER:
        if step == "o":
            last = own.turn(*last)
        elif step == "f":
            last = far.turn(*last)
        elif step == "a":
            last = attn.turn(*last)
        elif step == "T":
            grad_attn = attn_grads(attn_in, proj, low, mix, last + own.sent + far.sent)
            last = grad_attn[:1]
        elif step == "g":
            grad_attn = gate(grad_attn, last)
            attn_next, attn_last = (swap(grad_attn[k], "wide", 1) for k in (1, 3))
            last = added([([(grad_attn[2], 0, []), (attn_last, 0, [])], 4 * part)])
            attn_received = swap(last[0], "wide", 2)
        elif step == "A":
            attn_received, attn_next = gate([attn_received, attn_next], last)
            attn = Chain(narrow_sum([grad_attn[0], attn_next, attn_received], attn_count))
            last = attn.sent
        elif step == "w":
            merged = merge(place, count, [sums] + gate(others, last), True)
            last = [merged]
        elif step == "m":
            bit = message_bits.pop(0)
            merged = merge(place, count, [merged] + gate([swap(merged, "narrow", bit)], last))
            last = [merged]
        elif step == "M":
            for bit in message_bits:
                merged = merge(place, count, [merged] + gate([swap(merged, "narrow", bit)], last))
            (merged,) = gate([merged], last)
            grad_cross_flat, grad_cross_proj, sum_cross_grad, sum_cross, back = message_backward(
                count, merged, msg_in, cross_heads, cross_prob, cross_mix, cross_flat, cross_proj
            )
            last = [back]
        elif step == "B":
            for bit in bits_of(wide)[:-1]:
                back = back + gate([swap(back, "wide", bit)], last)[0]
            other = swap(back.astype(LOW), "wide", bits_of(wide)[-1])
            last = [back]
        elif step == "P":
            blocks = gate(blocks, last)
            pieces = [piece if k == 0 else swap(piece, "wide", k) for k, piece in enumerate(blocks)]
        elif step == "E":
            grad_message_weight, msg_sums, grad_cls = message_end(
                chunk, group, count, merged, back, gate([other], last)[0], msg_normed, msg_inv, message_gain, cls_rows,
                message_weight,
            )
            last = [grad_message_weight]
        elif step == "C":
            output_tokens, grad_tokens = collect(place, pieces[:1] + gate(pieces[1:], last), grad_cls)
            last = [grad_tokens]
    while attn.value is None or far.value is None:
        last = far.turn(*attn.turn(*last))
    far_value = far.value
    grad_attn_own = jnp.concatenate(attn.value, axis=0)
    sums = merged[:count].reshape(count, width)
    grad_up_bias = lax.dynamic_slice_in_dim(sums[6 : 6 + wide].reshape(-1), wide_idx * hidden, hidden, 0)

    return (
        output_tokens.transpose(0, 2, 1),
        grad_tokens.transpose(0, 2, 1),
        grad_message_weight,
        msg_sums[0],
        msg_sums[1],
        msg_sums[2],
        grad_cross_flat.reshape(3, part, width).transpose(2, 0, 1),
        jnp.stack([sum_cross[0, :part], sum_cross[0, 2 * part :]]),
        grad_cross_proj,
        sum_cross_grad[0],
        sums[4],
        sums[5],
        grad_attn_own[: 3 * part].reshape(3, part, width).transpose(2, 0, 1),
        own_cols(sums[count - 2 :]),
        grad_attn_own[3 * part :],
        own_cols(sums[3]),
        sums[1],
        sums[2],
        far_value[0],
        grad_up_bias,
        far_value[1],
        own_cols(sums[0]),
    )


def solution(mesh):
    return jax.shard_map(
        body,
        mesh=mesh,
        in_specs=(
            P("narrow", None, "wide"),
            P("narrow", None, "wide"),
            P(),
            P(),
            P(),
            P(),
            P(),
            P(),
            P(None, None, "wide"),
            P(None, "wide"),
            P("wide", None),
            P(),
            P(),
            P(),
            P(None, None, "wide"),
            P(None, "wide"),
            P("wide", None),
            P("wide"),
            P(),
            P(),
            P(None, "wide"),
            P("wide"),
            P("wide", None),
            P("wide"),
        ),
        out_specs=(
            P("narrow", None, "wide"),
            P("narrow", None, "wide"),
            P(),
            P(),
            P(),
            P(),
            P(None, None, "wide"),
            P(None, "wide"),
            P("wide", None),
            P(),
            P(),
            P(),
            P(None, None, "wide"),
            P(None, "wide"),
            P("wide", None),
            P("wide"),
            P(),
            P(),
            P(None, "wide"),
            P("wide"),
            P("wide", None),
            P("wide"),
        ),
        check_vma=False,
    )
```

```python
import functools
import jax
import jax.numpy as jnp
from jax import lax
from jax.experimental import pallas as pl
from jax.experimental.pallas import tpu as pltpu
from jax.sharding import PartitionSpec as P

VIDEO_FRAMES = 8
HD = 64
EPS = 1e-05
ROW_TILE = 16
LOW = jnp.bfloat16
F32 = jnp.float32
VMEM_LIMIT = 56 * 1024 * 1024
ANY = pl.BlockSpec(memory_space=pl.ANY)
VMEM = pl.BlockSpec(memory_space=pltpu.VMEM)
SMEM = pl.BlockSpec(memory_space=pltpu.SMEM)


def dot(left, right, dims):
    return lax.dot_general(left, right, (dims, ((), ())), preferred_element_type=F32)


def mat_mul(left, right):
    return dot(left, right, ((1,), (0,)))


def mat_tn(left, right):
    return dot(left, right, ((0,), (0,)))


def mat_nt(left, right):
    return dot(left, right, ((1,), (1,)))


def normalize(values):
    row_mean = jnp.mean(values, axis=-1, keepdims=True)
    centred = values - row_mean
    inv_std = lax.rsqrt(jnp.mean(centred * centred, axis=-1, keepdims=True) + EPS)
    return (centred * inv_std, inv_std)


def norm_back(grad_norm, normed, inv_std, norm_gain):
    scaled = grad_norm * norm_gain
    return inv_std * (
        scaled
        - jnp.mean(scaled, axis=-1, keepdims=True)
        - normed * jnp.mean(scaled * normed, axis=-1, keepdims=True)
    )


def bits_of(size):
    return [1 << b for b in range(size.bit_length() - 1)]


def reorder(parts, index):
    parts = list(parts)
    for bit in bits_of(len(parts)):
        odd = (index & bit) != 0
        parts = [jnp.where(odd, parts[k ^ bit], parts[k]) for k in range(len(parts))]
    return parts


def call(kernel, name, micros=0.0, **options):
    return pl.pallas_call(
        kernel,
        name=name,
        compiler_params=pltpu.CompilerParams(vmem_limit_bytes=VMEM_LIMIT),
        cost_estimate=pl.CostEstimate(
            flops=int(micros * 1.0e9), bytes_accessed=int(micros * 3.0e6), transcendentals=0
        ),
        **options,
    )


def shaped(shape, dtype):
    return jax.ShapeDtypeStruct(tuple(shape), dtype)


def whole(array):
    return pl.BlockSpec(array.shape, lambda *_: (0,) * array.ndim)


def fixed(shape):
    return pl.BlockSpec(tuple(shape), lambda *_: (0,) * len(shape))


def per_step(shape):
    return pl.BlockSpec((1,) + tuple(shape[1:]), lambda f: (f,) + (0,) * (len(shape) - 1))


def row_of(ref):
    return ref[...].reshape(1, -1)


def head_masks(width):
    lane = lax.broadcasted_iota(jnp.int32, (1, width), 1) // HD
    return [lane == h for h in range(width // HD)]


def stack_heads(values, masks, scale=1.0):
    return jnp.concatenate([values * jnp.where(m, scale, 0.0).astype(values.dtype) for m in masks], axis=0)


def pick_heads(values, masks):
    size = values.shape[0] // len(masks)
    picked = values[:size]
    for h in range(1, len(masks)):
        picked = jnp.where(masks[h], values[h * size : (h + 1) * size], picked)
    return picked


def weight_copies(refs, shards, place_ref, buf, sem):
    whole_count = 2 * shards - len(refs)
    odd = place_ref[1]
    copies = []
    for j in range(whole_count):
        copies.append([pltpu.make_async_copy(refs[j], buf.at[j], sem.at[j, 0])])
    rest = refs[whole_count:]
    for i in range(len(rest) // 2):
        half = rest[2 * i].shape[0]
        at = pl.multiple_of(odd * half, half)
        other = pl.multiple_of((1 - odd) * half, half)
        j = whole_count + i
        copies.append([
            pltpu.make_async_copy(rest[2 * i], buf.at[j, pl.ds(at, half)], sem.at[j, 0]),
            pltpu.make_async_copy(rest[2 * i + 1], buf.at[j, pl.ds(other, half)], sem.at[j, 1]),
        ])
    return copies


def start_all(copies):
    for group in copies:
        for copy in group:
            copy.start()


def wait_all(copies):
    for group in copies:
        for copy in group:
            copy.wait()


def attn_forward_kernel(waits, place_ref, gain_ref, shift_ref, mlp_gain_ref, mlp_shift_ref, base_ref, *refs):
    shards = refs[-3].shape[0]
    toks, refs = refs[:shards], refs[shards:]
    sums, refs = refs[:shards], refs[shards:]
    packs, refs = refs[:shards], refs[shards:]
    weights, refs = refs[: -14 - waits], refs[-14:]
    (normed_ref, inv_ref, attn_in_ref, heads_ref, prob_ref, mix_ref, hidden_ref, mlp_normed_ref,
     mlp_inv_ref, mlp_in_ref, tok_buf, w_buf, w_sem, msg_buf) = refs
    part, patches = toks[0].shape[1], toks[0].shape[2]
    seq_pad, width = normed_ref.shape[1], normed_ref.shape[2]
    frames = pl.num_programs(0)
    frame = pl.program_id(0)
    wide_idx = place_ref[0]
    copies = weight_copies(weights, shards, place_ref, w_buf, w_sem)

    @pl.when(frame == 0)
    def _():
        start_all(copies)
        tok_buf[...] = jnp.zeros_like(tok_buf)
        total = base_ref[...]
        for ref in sums:
            total += ref[...]
        msg_buf[...] = total

    for k in range(shards):
        at = pl.multiple_of((wide_idx ^ k) * part, part)
        at_frame = (wide_idx & 1) * frames + frame if k == 2 else 0
        tok_buf[pl.ds(at, part), :patches] = toks[k][at_frame]
    tokens = tok_buf[...].T[:seq_pad].astype(F32)
    group = msg_buf[...]
    own = lax.broadcasted_iota(jnp.int32, (group.shape[0], 1), 0) == wide_idx * frames + frame
    message = jnp.sum(jnp.where(own, group, 0.0), axis=0, keepdims=True)
    row = lax.broadcasted_iota(jnp.int32, (seq_pad, 1), 0)
    full = jnp.where(row == patches, message, tokens)
    normed, inv = normalize(full)
    normed_ref[0] = normed
    inv_ref[0] = inv
    gain, shift, mlp_gain, mlp_shift = map(row_of, (gain_ref, shift_ref, mlp_gain_ref, mlp_shift_ref))
    attn_in = (normed * gain + shift).astype(LOW)
    attn_in_ref[0] = attn_in
    masks = head_masks(part)
    live = lax.broadcasted_iota(jnp.int32, (1, seq_pad), 1) <= patches
    total = full + jnp.concatenate(reorder([p[1:2, 2 * part : 3 * part] for p in packs], wide_idx), axis=1)

    @pl.when(frame == 0)
    def _():
        wait_all(copies)

    heads = []
    for k in range(shards):
        proj = mat_nt(attn_in, w_buf[k, : 3 * part])
        queries = (proj[:, :part] + packs[k][1:2, :part]).astype(LOW)
        keys = proj[:, part : 2 * part].astype(LOW)
        values = (proj[:, 2 * part :] + packs[k][1:2, part : 2 * part]).astype(LOW)
        heads_ref[0, k, 0] = queries
        heads_ref[0, k, 1] = keys
        heads_ref[0, k, 2] = values
        heads.append((queries, keys, values))

    def score(k):
        queries, keys, _ = heads[k]
        return mat_nt(stack_heads(queries, masks, HD ** (-0.5)), keys)

    def finish_shard(k):
        mix_ref[0, k] = pick_heads(mat_mul(prob_ref[0, k], heads[k][2]), masks).astype(LOW)

    scores = [score(0)]
    for k in range(shards):
        if k + 1 < shards:
            scores.append(score(k + 1))
        if k > 0:
            finish_shard(k - 1)
        live_scores = jnp.where(live, scores[k], -1e30)
        exps = jnp.exp(live_scores - jnp.max(live_scores, axis=-1, keepdims=True))
        prob_ref[0, k] = (exps * (1.0 / jnp.sum(exps, axis=-1, keepdims=True))).astype(LOW)
    finish_shard(shards - 1)
    for k in range(shards):
        total += mat_mul(mix_ref[0, k], w_buf[k, 3 * part :])
    hidden_ref[0] = total
    mlp_normed, mlp_inv = normalize(total.astype(LOW).astype(F32))
    mlp_normed_ref[0] = mlp_normed
    mlp_inv_ref[0] = mlp_inv
    mlp_in_ref[0] = (mlp_normed * mlp_gain + mlp_shift).astype(LOW)


def attn_forward(seq_pad, place, vecs, base, toks, sums, packs, weights, after):
    frames, part, patches = toks[0].shape
    shards = len(toks)
    width = part * shards
    heads = part // HD
    seq_lanes = -(-seq_pad // 128) * 128
    shapes = [
        ((frames, seq_pad, width), F32),
        ((frames, seq_pad, 1), F32),
        ((frames, seq_pad, width), LOW),
        ((frames, shards, 3, seq_pad, part), LOW),
        ((frames, shards, heads * seq_pad, seq_pad), LOW),
        ((frames, shards, seq_pad, part), LOW),
        ((frames, seq_pad, width), F32),
        ((frames, seq_pad, width), F32),
        ((frames, seq_pad, 1), F32),
        ((frames, seq_pad, width), LOW),
    ]
    return call(
        functools.partial(attn_forward_kernel, len(after)),
        "attn_forward",
        0.0,
        grid=(frames,),
        in_specs=[SMEM] + [whole(v) for v in vecs] + [whole(base)]
        + [per_step(v.shape) if v.shape[0] == frames else whole(v) for v in toks]
        + [whole(v) for v in list(sums) + list(packs)]
        + [ANY] * (len(weights) + len(after)),
        out_specs=[per_step(s) for s, _ in shapes],
        out_shape=[shaped(s, d) for s, d in shapes],
        scratch_shapes=[
            pltpu.VMEM((width, seq_lanes), LOW),
            pltpu.VMEM((shards, 4 * part, width), LOW),
            pltpu.SemaphoreType.DMA((shards, 2)),
            pltpu.VMEM(base.shape, F32),
        ],
    )(place, *vecs, base, *toks, *sums, *packs, *weights, *after)


def mlp_kernel(frames, count, first, waits, place_ref, scale_ref, mlp_in_ref, *refs):
    packs, refs = refs[:count], refs[count:]
    if first:
        shards = 2 * count
        cots, refs = refs[:shards], refs[shards:]
    else:
        (grad_ref, acc_in, gacc_in), refs = refs[:3], refs[3:]
    each = 2 if first else 4
    weights, refs = refs[: each * count], refs[each * count + waits :]
    if first:
        (cot_ref, grad_ref), refs = refs[:2], refs[2:]
    acc_ref, gacc_ref, sums_ref = refs[:3]
    g_refs, refs = refs[3 : 3 + count], refs[3 + count :]
    w_buf, g_buf, act_buf, pre_buf, in_sem, out_sem, acc_buf, gacc_buf, sum_sem, acc_sem = refs[:10]
    rows, width = mlp_in_ref.shape
    hidden = act_buf.shape[1]
    step = rows // frames
    loads = []
    for i in range(count):
        if first:
            for j, ref in ((2 * i, weights[i]), (2 * i + 1, weights[count + i])):
                loads.append([pltpu.make_async_copy(ref, w_buf.at[j], in_sem.at[j, 0])])
        else:
            near, far = weights[4 * i : 4 * i + 2], weights[4 * i + 2 : 4 * i + 4]
            half = far[0].shape[0]
            at, other = (pl.multiple_of(odd * half, half) for odd in (place_ref[1], 1 - place_ref[1]))
            for j in range(2):
                to = w_buf.at[2 * i + j]
                loads.append([
                    pltpu.make_async_copy(near[j], to.at[pl.ds(at, half)], in_sem.at[2 * i + j, 0]),
                    pltpu.make_async_copy(far[j], to.at[pl.ds(other, half)], in_sem.at[2 * i + j, 1]),
                ])
    start_all(loads)
    carried = []
    if not first:
        carried = [
            pltpu.make_async_copy(acc_in, acc_buf, sum_sem.at[0]),
            pltpu.make_async_copy(gacc_in, gacc_buf, sum_sem.at[1]),
        ]
    start_all([carried])
    stores = [
        pltpu.make_async_copy(g_buf.at[2 * i + j], g_refs[i].at[pl.ds(j * width, width)], out_sem.at[2 * i + j])
        for i in range(count) for j in range(2)
    ]
    if first:
        cot_buf = refs[10]
        cot_buf[...] = jnp.zeros_like(cot_buf)
        part, patches = cots[0].shape[1:]
        for f in range(frames):
            for k in range(shards):
                at = pl.multiple_of((place_ref[0] ^ k) * part, part)
                at_frame = (place_ref[0] & 1) * frames + f if k == 2 else f
                cot_buf[pl.ds(at, part), :patches] = cots[k][at_frame]
            cot = cot_buf[...].T[:step]
            cot_ref[f] = cot
            grad_ref[f * step : (f + 1) * step] = (cot.astype(F32) * scale_ref[f]).astype(LOW)
    def before(i, f):
        at = slice(f * step, (f + 1) * step)
        return mat_mul(mlp_in_ref[at], w_buf[2 * i]), mat_nt(grad_ref[at], w_buf[2 * i + 1])

    def weight_grads(i):
        rows_of = slice(i * rows, (i + 1) * rows)
        up, down = 2 * i, 2 * i + 1
        for c in range(0, width, 256):
            yield
            g_buf[up, c : c + 256] = mat_tn(mlp_in_ref[:, c : c + 256], pre_buf[rows_of]).astype(LOW)
        stores[up].start()
        for c in range(0, hidden, 256):
            yield
            g_buf[down, c : c + 256] = mat_tn(act_buf[rows_of, c : c + 256], grad_ref[...]).astype(LOW)
        stores[down].start()

    pending = iter(())
    for i in range(count):
        up, down = 2 * i, 2 * i + 1
        wait_all(loads[up : down + 1])
        bias = packs[i][0:1]
        total = jnp.zeros((1, hidden), F32)
        ahead = [before(i, 0)]
        for f in range(frames):
            at = slice(f * step, (f + 1) * step)
            kept = slice(i * rows + f * step, i * rows + (f + 1) * step)
            if f + 1 < frames:
                ahead.append(before(i, f + 1))
            next(pending, None)
            next(pending, None)
            pre, grad_act = ahead[f]
            pre = pre + bias
            sig = 0.5 + 0.5 * jnp.tanh(0.851 * pre)
            act = pre * sig
            act_buf[kept] = act.astype(LOW)
            grad_pre = (grad_act * (sig + 1.702 * act * (1.0 - sig))).astype(LOW)
            pre_buf[kept] = grad_pre
            total += jnp.sum(grad_pre.astype(F32), axis=0, keepdims=True)
        sums_ref[i] = total
        for _ in pending:
            pass
        if i == 0:
            wait_all([carried])
        for f in range(frames):
            at = slice(f * step, (f + 1) * step)
            kept = slice(i * rows + f * step, i * rows + (f + 1) * step)
            out = mat_mul(act_buf[kept], w_buf[down])
            back = mat_nt(pre_buf[kept], w_buf[up])
            if i > 0 or not first:
                acc_buf[at] += out
                gacc_buf[at] += back
            else:
                acc_buf[at] = out
                gacc_buf[at] = back
            if i == count - 1:
                for n, (buf, ref) in enumerate(((acc_buf, acc_ref), (gacc_buf, gacc_ref))):
                    store = pltpu.make_async_copy(buf.at[pl.ds(f * step, step)], ref.at[pl.ds(f * step, step)], acc_sem.at[n, f])
                    store.start()
                    stores.append(store)
        pending = weight_grads(i)
    for _ in pending:
        pass
    for store in stores:
        store.wait()


def mlp_step(frames, place, scale, mlp_in, packs, weights, cots=None, carried=None, after=()):
    rows, width = mlp_in.shape
    count = len(packs)
    first = cots is not None
    hidden = packs[0].shape[1]
    step = rows // frames
    ins = [place, scale, mlp_in, *packs, *(cots if first else carried)]
    shapes = [shaped((frames, step, width), LOW), shaped((rows, width), LOW)] if first else []
    shapes += [shaped((rows, width), F32)] * 2 + [shaped((count, 1, hidden), F32)]
    grads = [shaped((width + hidden, width), LOW)] * count
    scratch = [
        pltpu.VMEM((2 * count, width, hidden), LOW),
        pltpu.VMEM((2 * count, width, hidden), LOW),
        pltpu.VMEM((count * rows, hidden), LOW),
        pltpu.VMEM((count * rows, hidden), LOW),
        pltpu.SemaphoreType.DMA((2 * count, 2)),
        pltpu.SemaphoreType.DMA((2 * count,)),
        pltpu.VMEM((rows, width), F32),
        pltpu.VMEM((rows, width), F32),
        pltpu.SemaphoreType.DMA((2,)),
        pltpu.SemaphoreType.DMA((2, frames)),
    ]
    if first:
        scratch.append(pltpu.VMEM((width, -(-step // 128) * 128), LOW))
    return call(
        functools.partial(mlp_kernel, frames, count, first, len(after)),
        "mlp",
        18.5,
        in_specs=[SMEM, SMEM, VMEM]
        + [VMEM] * (len(ins) - 3 if first else count + 1)
        + [ANY] * ((0 if first else 2) + len(weights) + len(after)),
        out_specs=[VMEM] * (len(shapes) - 3) + [ANY] * 2 + [VMEM] + [ANY] * len(grads),
        out_shape=shapes + grads,
        scratch_shapes=scratch,
    )(*ins, *weights, *after)


def attn_backward_kernel(
    shards, waits, place_ref, scale_ref, gain_ref, mlp_gain_ref, res_ref, acc_ref, gacc_ref, mlp_normed_ref, mlp_inv_ref, cot_ref,
    normed_ref, inv_ref, heads_ref, prob_ref, *refs
):
    packs, refs = refs[:shards], refs[shards:]
    ups, refs = refs[: shards // 2], refs[shards // 2 :]
    outs = shards + 3 + 2
    weights, refs = refs[: len(refs) - outs - waits], refs[len(refs) - outs :]
    pieces, refs = refs[:shards], refs[shards:]
    proj_ref, low_ref, sums_ref, w_buf, w_sem = refs
    part = heads_ref.shape[4]
    patches = pieces[0].shape[3]
    seq_pad, width = res_ref.shape[1:]
    gain, mlp_gain = row_of(gain_ref), row_of(mlp_gain_ref)
    frame = pl.program_id(0)
    wide_idx = place_ref[0]
    copies = weight_copies(weights, shards, place_ref, w_buf, w_sem)

    @pl.when(frame == 0)
    def _():
        start_all(copies)
        sums_ref[...] = jnp.zeros_like(sums_ref)
        rows = [ref[i] for ref in ups for i in range(2)]
        for k, values in enumerate(reorder(rows, wide_idx)):
            sums_ref[6 + k] = values

    def columns(values, i):
        blocks = values.T
        blocks = reorder([blocks[j * part : (j + 1) * part, :patches] for j in range(shards)], wide_idx)
        for ref, block in zip(pieces, blocks):
            ref[0, i] = block

    down_bias = jnp.concatenate(reorder([p[1:2, 3 * part : 4 * part] for p in packs], wide_idx), axis=1)
    columns((res_ref[0] + acc_ref[0] + down_bias).astype(LOW), 0)
    grad_res = cot_ref[0].astype(F32) * scale_ref[frame]
    gacc, mlp_normed = gacc_ref[0], mlp_normed_ref[0]
    hidden = grad_res + norm_back(gacc, mlp_normed, mlp_inv_ref[0], mlp_gain)

    def add_sum(row, values):
        sums_ref[row] += jnp.sum(values, axis=0, keepdims=True)

    add_sum(0, grad_res)
    add_sum(1, gacc * mlp_normed)
    add_sum(2, gacc)
    add_sum(3, hidden)
    low = hidden.astype(LOW)
    low_ref[0] = low
    masks = head_masks(part)
    scale = HD ** (-0.5)
    back = jnp.zeros(hidden.shape, F32)
    bias_sums = []

    @pl.when(frame == 0)
    def _():
        wait_all(copies)

    mixes = [stack_heads(mat_nt(low, w_buf[k, 3 * part :]).astype(LOW), masks) for k in range(shards)]

    def grad_prob_of(k):
        return mat_nt(mixes[k], heads_ref[0, k, 2])

    def finish_shard(k, grad_score):
        prob_low = prob_ref[0, k]
        grad_value = mat_tn(prob_low, mixes[k])
        grad_query = pick_heads(mat_mul(grad_score, heads_ref[0, k, 1]), masks)
        grad_key = mat_tn(grad_score, stack_heads(heads_ref[0, k, 0], masks))
        proj = jnp.concatenate([grad_query * scale, grad_key * scale, grad_value], axis=1).astype(LOW)
        proj_ref[0, k] = proj
        bias_sums.append(jnp.sum(proj.astype(F32), axis=0, keepdims=True))

    grad_probs = [grad_prob_of(0)]
    grad_score = None
    for k in range(shards):
        if k + 1 < shards:
            grad_probs.append(grad_prob_of(k + 1))
        if k > 0:
            finish_shard(k - 1, grad_score)
        prob = prob_ref[0, k].astype(F32)
        weighted = prob * grad_probs[k]
        grad_score = (weighted - prob * jnp.sum(weighted, axis=-1, keepdims=True)).astype(LOW)
    finish_shard(shards - 1, grad_score)
    for k in range(shards):
        back += mat_mul(proj_ref[0, k], w_buf[k, : 3 * part])
    for i, at in ((6 + shards, 0), (7 + shards, 2 * part)):
        own = reorder([values[:, at : at + part] for values in bias_sums], wide_idx)
        sums_ref[i] += jnp.concatenate(own, axis=1)
    normed = normed_ref[0]
    add_sum(4, back * normed)
    add_sum(5, back)
    total = hidden + norm_back(back, normed, inv_ref[0], gain)
    row = lax.broadcasted_iota(jnp.int32, (seq_pad, 1), 0)
    sums_ref[8 + shards + frame] = jnp.sum(jnp.where(row == patches, total, 0.0), axis=0, keepdims=True)
    columns(total.astype(LOW), 1)


def attn_backward(patches, place, scale, vecs, per_frame, packs, ups, weights, after):
    frames, seq_pad, width = per_frame[0].shape
    heads = per_frame[8]
    shards, part = heads.shape[1], heads.shape[4]
    blocks = [(frames, 2, part, patches)] * shards
    proj = (frames, shards, seq_pad, 3 * part)
    return call(
        functools.partial(attn_backward_kernel, shards, len(after)),
        "attn_backward",
        20.3,
        grid=(frames,),
        in_specs=[SMEM, SMEM]
        + [whole(v) for v in vecs]
        + [per_step(v.shape) for v in per_frame]
        + [whole(v) for v in list(packs) + list(ups)]
        + [ANY] * (len(weights) + len(after)),
        out_specs=[per_step(b) for b in blocks]
        + [per_step(proj), per_step((frames, seq_pad, width)), fixed((8 + shards + frames, 1, width))],
        out_shape=[shaped(b, LOW) for b in blocks]
        + [
            shaped(proj, LOW),
            shaped((frames, seq_pad, width), LOW),
            shaped((8 + shards + frames, 1, width), F32),
        ],
        scratch_shapes=[
            pltpu.VMEM((shards, 4 * part, width), LOW),
            pltpu.SemaphoreType.DMA((shards, 2)),
        ],
    )(place, scale, *vecs, *per_frame, *packs, *ups, *weights, *after)


def attn_grads_kernel(waits, attn_in_ref, low_ref, proj_ref, mix_ref, *refs):
    grad_refs, (proj_buf, mix_buf) = refs[waits:-2], refs[-2:]
    count = len(grad_refs)
    frames, seq_pad, part = mix_ref.shape[0], mix_ref.shape[2], mix_ref.shape[3]
    for i in range(count):
        for f in range(frames):
            at = slice(f * seq_pad, (f + 1) * seq_pad)
            proj_buf[at] = proj_ref[f, i]
            mix_buf[at] = mix_ref[f, i]
        for c in range(0, 3 * part, part):
            grad_refs[i][c : c + part] = mat_tn(proj_buf[:, c : c + part], attn_in_ref[...]).astype(LOW)
        grad_refs[i][3 * part :] = mat_tn(mix_buf[...], low_ref[...]).astype(LOW)


def attn_grads(attn_in, proj, low, mix, after):
    frames, shards, seq_pad, part = mix.shape
    width = attn_in.shape[-1]
    rows = frames * seq_pad
    return call(
        functools.partial(attn_grads_kernel, len(after)),
        "attn_grads",
        0.0,
        grid=(1,),
        in_specs=[fixed((rows, width)), fixed((rows, width)), fixed(proj.shape), fixed(mix.shape)] + [ANY] * len(after),
        out_specs=[fixed((4 * part, width))] * shards,
        out_shape=[shaped((4 * part, width), LOW)] * shards,
        scratch_shapes=[pltpu.VMEM((rows, 3 * part), LOW), pltpu.VMEM((rows, part), LOW)],
    )(attn_in.reshape(rows, width), low.reshape(rows, width), proj, mix, *after)


def same_video(place_ref, group, rows, columns):
    first = pl.program_id(0) * columns

    def video(position):
        position = position + first
        return (((position // group) ^ place_ref[2]) * group + position % group) // VIDEO_FRAMES

    row = lax.broadcasted_iota(jnp.int32, (rows, columns), 0) % columns
    column = lax.broadcasted_iota(jnp.int32, (rows, columns), 1)
    return video(row) == video(column)


def message_forward_kernel(
    group, waits, place_ref, cls_ref, weight_ref, m_bias_ref, gain_ref, shift_ref, offset_ref, flat_ref, bias_ref,
    proj_ref, *refs
):
    normed_ref, inv_ref, in_ref, heads_ref, prob_ref, mix_ref, base_ref, sum_ref = refs[waits:]
    part = proj_ref.shape[0]
    chunk = cls_ref.shape[0]
    message = mat_mul(cls_ref[...], weight_ref[...]) + row_of(m_bias_ref)
    normed, inv = normalize(message)
    normed_ref[...] = normed
    inv_ref[...] = inv
    msg_in = (normed * row_of(gain_ref) + row_of(shift_ref)).astype(LOW)
    in_ref[...] = msg_in
    proj = mat_nt(msg_in, flat_ref[...])
    queries = (proj[:, :part] + bias_ref[0:1]).astype(LOW)
    keys = proj[:, part : 2 * part].astype(LOW)
    values = (proj[:, 2 * part :] + bias_ref[1:2]).astype(LOW)
    heads_ref[0, 0] = queries
    heads_ref[0, 1] = keys
    heads_ref[0, 2] = values
    masks = head_masks(part)
    scores = mat_nt(stack_heads(queries, masks, HD ** (-0.5)), keys)
    scores = jnp.where(same_video(place_ref, group, len(masks) * chunk, chunk), scores, -1e30)
    exps = jnp.exp(scores - jnp.max(scores, axis=-1, keepdims=True))
    prob = exps / jnp.sum(exps, axis=-1, keepdims=True)
    prob_ref[0] = prob
    mix = pick_heads(mat_mul(prob.astype(LOW), values), masks).astype(LOW)
    mix_ref[...] = mix

    @pl.when(pl.program_id(0) == 0)
    def _():
        base_ref[...] = message[:group] + row_of(offset_ref)
        sum_ref[...] = mat_mul(mix, proj_ref[...])[:group]


def message_forward(chunk, group, place, cls_rows, weight, vecs, flat, bias, proj, after):
    count, width = cls_rows.shape
    part = proj.shape[0]
    heads = part // HD
    chunks = count // chunk
    rows = lambda columns: pl.BlockSpec((chunk, columns), lambda c: (c, 0))
    return call(
        functools.partial(message_forward_kernel, group, len(after)),
        "message_forward",
        0.0,
        grid=(chunks,),
        in_specs=[SMEM, rows(width)]
        + [whole(v) for v in (weight, *vecs, flat, bias, proj)]
        + [ANY] * len(after),
        out_specs=[
            rows(width), rows(1), rows(width),
            per_step((chunks, 3, chunk, part)), per_step((chunks, heads * chunk, chunk)),
            rows(part), fixed((group, width)), fixed((group, width)),
        ],
        out_shape=[
            shaped((count, width), F32),
            shaped((count, 1), F32),
            shaped((count, width), LOW),
            shaped((chunks, 3, chunk, part), LOW),
            shaped((chunks, heads * chunk, chunk), F32),
            shaped((count, part), LOW),
            shaped((group, width), F32),
            shaped((group, width), F32),
        ],
    )(place, cls_rows, weight, *vecs, flat, bias, proj, *after)


def message_rows(all_ref, count, chunk):
    return all_ref[pl.ds(count + pl.program_id(0) * chunk, chunk)][:, 0]


def message_backward_kernel(
    count, all_ref, in_ref, heads_ref, prob_ref, mix_ref, flat_ref, proj_ref, grad_flat_ref, grad_proj_ref,
    sum_grad_ref, sum_cross_ref, back_ref
):
    @pl.when(pl.program_id(0) == 0)
    def _():
        for ref in (grad_flat_ref, grad_proj_ref, sum_grad_ref, sum_cross_ref):
            ref[...] = jnp.zeros_like(ref)

    part = proj_ref.shape[0]
    masks = head_masks(part)
    grad = message_rows(all_ref, count, in_ref.shape[0]).astype(LOW)
    sum_grad_ref[...] += jnp.sum(grad.astype(F32), axis=0, keepdims=True)
    grad_proj_ref[...] += mat_tn(mix_ref[...], grad)
    grad_mix = mat_nt(grad, proj_ref[...]).astype(LOW)
    mix_heads = stack_heads(grad_mix, masks)
    queries, keys, values = heads_ref[0, 0], heads_ref[0, 1], heads_ref[0, 2]
    prob = prob_ref[0]
    grad_prob = mat_nt(mix_heads, values)
    grad_score = prob * (grad_prob - jnp.sum(prob * grad_prob, axis=-1, keepdims=True))
    score_low = grad_score.astype(LOW)
    grad_query = pick_heads(mat_mul(score_low, keys), masks) * HD ** (-0.5)
    grad_key = mat_tn(score_low, stack_heads(queries, masks)) * HD ** (-0.5)
    grad_value = mat_tn(prob.astype(LOW), mix_heads)
    cross = jnp.concatenate([grad_query, grad_key, grad_value], axis=1).astype(LOW)
    sum_cross_ref[...] += jnp.sum(cross.astype(F32), axis=0, keepdims=True)
    grad_flat_ref[...] += mat_tn(cross, in_ref[...])
    back_ref[...] = mat_mul(cross, flat_ref[...])


def message_backward(count, merged, msg_in, heads, prob, mix, flat, proj):
    total, width = msg_in.shape
    part = proj.shape[0]
    chunks, _, chunk, _ = heads.shape
    rows = lambda columns: pl.BlockSpec((chunk, columns), lambda c: (c, 0))
    shapes = [(3 * part, width), (part, width), (1, width), (1, 3 * part)]
    return call(
        functools.partial(message_backward_kernel, count),
        "message_backward",
        0.0,
        grid=(chunks,),
        in_specs=[whole(merged), rows(width), per_step(heads.shape), per_step(prob.shape), rows(part)]
        + [whole(flat), whole(proj)],
        out_specs=[fixed(s) for s in shapes] + [rows(width)],
        out_shape=[shaped(s, F32) for s in shapes + [(total, width)]],
    )(merged, msg_in, heads, prob, mix, flat, proj)


def message_end_kernel(
    group, count, all_ref, back_ref, other_ref, normed_ref, inv_ref, gain_ref, cls_ref, weight_ref, grad_weight_ref,
    sums_ref, grad_cls_ref
):
    @pl.when(pl.program_id(0) == 0)
    def _():
        grad_weight_ref[...] = jnp.zeros_like(grad_weight_ref)
        sums_ref[...] = jnp.zeros_like(sums_ref)

    back = back_ref[...] + other_ref[...].astype(F32)
    normed = normed_ref[...]
    grad = message_rows(all_ref, count, back.shape[0]) + norm_back(back, normed, inv_ref[...], row_of(gain_ref))
    low = grad.astype(LOW)
    for row, values in enumerate((low.astype(F32), back * normed, back)):
        sums_ref[row : row + 1] += jnp.sum(values, axis=0, keepdims=True)
    grad_weight_ref[...] += mat_tn(cls_ref[...], low)

    @pl.when(pl.program_id(0) == 0)
    def _():
        grad_cls_ref[...] = mat_nt(weight_ref[...], low)[:, :group]


def message_end(chunk, group, count, merged, back, other, normed, inv, gain, cls_rows, weight):
    total, width = back.shape
    rows = lambda columns: pl.BlockSpec((chunk, columns), lambda c: (c, 0))
    return call(
        functools.partial(message_end_kernel, group, count),
        "message_end",
        0.0,
        grid=(total // chunk,),
        in_specs=[whole(merged)] + [rows(width)] * 3 + [rows(1), whole(gain), rows(width), whole(weight)],
        out_specs=[fixed((width, width)), fixed((8, width)), fixed((width, group))],
        out_shape=[shaped((width, width), F32), shaped((8, width), F32), shaped((width, group), F32)],
    )(merged, back, other, normed, inv, gain, cls_rows, weight)


def merge_kernel(count, ordered, place_ref, *refs):
    refs, out_ref = refs[:-1], refs[-1]
    size = refs[0].shape[0] - count
    total = refs[0][:count]
    for ref in refs[1:]:
        total += ref[:count]
    out_ref[:count] = total
    for k, ref in enumerate(refs):
        at = (place_ref[0] ^ k) if ordered else k
        out_ref[pl.ds(count + at * size, size)] = ref[count:]


def merge(place, count, buffers, ordered=False):
    rows, one, width = buffers[0].shape
    return call(
        functools.partial(merge_kernel, count, ordered),
        "merge",
        1.6,
        in_specs=[SMEM] + [VMEM] * len(buffers),
        out_specs=VMEM,
        out_shape=shaped((count + (rows - count) * len(buffers), one, width), F32),
    )(place, *buffers)


def collect_kernel(place_ref, *refs):
    *pieces, grad_cls_ref, tok_ref, grad_ref = refs
    frames, _, part, patches = pieces[0].shape
    own = grad_cls_ref[pl.ds(pl.multiple_of(place_ref[0] * part, part), part), :]
    lane = lax.broadcasted_iota(jnp.int32, (part, patches), 1)
    for j, piece in enumerate(reorder([ref[...] for ref in pieces], place_ref[0])):
        for f in range(frames):
            i = j * frames + f
            tok_ref[i] = piece[f, 0]
            grad = piece[f, 1].astype(F32)
            grad_ref[i] = jnp.where(lane == 0, grad + own[:, i : i + 1], grad).astype(LOW)


def collect(place, pieces, grad_cls):
    frames, _, part, patches = pieces[0].shape
    shape = (frames * len(pieces), part, patches)
    return call(
        collect_kernel,
        "collect",
        0.0,
        in_specs=[SMEM] + [VMEM] * (len(pieces) + 1),
        out_specs=[VMEM] * 2,
        out_shape=[shaped(shape, LOW)] * 2,
    )(place, *pieces, grad_cls)


def swap(block, axis, flip):
    return lax.ppermute(block, axis, [(i, i ^ flip) for i in range(lax.axis_size(axis))])


def gate(arrays, after):
    return list(lax.optimization_barrier((tuple(arrays), tuple(after)))[0])


def frames_in(block, after):
    index = lax.axis_index("wide")
    part = block.shape[0] // lax.axis_size("wide")
    (block,) = gate([block], after)
    crossed = swap(lax.dynamic_slice_in_dim(block, ((index ^ 2) & 2) * part, 2 * part, 0), "wide", 2)
    own = lax.dynamic_slice_in_dim(block, index * part, part, 0)
    near = swap(lax.dynamic_slice_in_dim(block, (index ^ 1) * part, part, 0), "wide", 1)
    return [own, near, crossed]


def frames_end(pieces, after):
    own, near, crossed = pieces
    (crossed,) = gate([crossed], after)
    part = own.shape[0]
    index = lax.axis_index("wide")
    far = swap(lax.dynamic_slice_in_dim(crossed, ((index & 1) ^ 1) * part, part, 0), "wide", 1)
    return [own, near, crossed, far]


def send_half(block, after):
    odd = lax.axis_index("narrow") & 1
    half = block.shape[0] // 2
    sent = lax.dynamic_slice_in_dim(gate([block], after)[0], odd * half, half, 0)
    return [swap(sent, "wide", bit) for bit in bits_of(lax.axis_size("wide"))[1:]]


def near_shards(block):
    return [block, swap(block, "wide", 1)]


def far_shards(near, far):
    return [near, far, swap(near, "wide", 1), swap(far, "wide", 1)]


def row_at(base, moves):
    at = base
    for bit, rows, flipped in moves:
        is_set = ((lax.axis_index("narrow") & bit) != 0).astype(jnp.int32)
        at = at + rows * ((1 - is_set) if flipped else is_set)
    return at


def added(sums, together=False):
    blocks = []
    for terms, size in sums:
        rows = [
            array if not moves and array.shape[0] == size else lax.dynamic_slice_in_dim(array, row_at(base, moves), size, 0)
            for array, base, moves in terms
        ]
        blocks.append(sum(row.astype(F32) for row in rows).astype(LOW))
    return [jnp.concatenate(blocks, axis=0)] if together else blocks


def joined(pairs, bits):
    odds = [(lax.axis_index("narrow") & bit) != 0 for bit in bits]
    return [
        jnp.where(odd, jnp.concatenate([other, block], axis=0), jnp.concatenate([block, other], axis=0))
        for (block, other), odd in zip(pairs, odds)
    ]


def orders(count):
    bits = bits_of(lax.axis_size("narrow"))[:count]
    return [bits, bits[1:] + bits[:1]]


def regions_of(arrays, base=0):
    half = arrays[0].shape[0] // 2
    return [[(array, n * half, []) for array in arrays] for n in range(2)], half


def halving(regions, size, steps):
    for at in range(steps):
        bits = [order[at] for order in orders(steps)]
        size = size // 2
        sent = added([
            ([(array, base, moves + [(bit, size, True)]) for array, base, moves in terms], size)
            for bit, terms in zip(bits, regions)
        ])
        received = yield sent, [swap(block, "narrow", bit) for block, bit in zip(sent, bits)]
        regions = [
            [(array, base, moves + [(bit, size, False)]) for array, base, moves in terms] + [(block, 0, [])]
            for bit, terms, block in zip(bits, regions, received)
        ]
    return regions, size


def joining(blocks, steps):
    for at in reversed(range(steps)):
        bits = [order[at] for order in orders(steps)]
        others = yield blocks, [swap(block, "narrow", bit) for block, bit in zip(blocks, bits)]
        blocks = joined(list(zip(blocks, others)), bits)
    return [block.astype(F32) for block in blocks]


def whole_sum(blocks, steps):
    for bit in bits_of(lax.axis_size("narrow"))[steps:]:
        others = yield blocks, [swap(block, "narrow", bit) for block in blocks]
        blocks = added([([(a, 0, []), (b, 0, [])], a.shape[0]) for a, b in zip(blocks, others)])
    return blocks


def narrow_sum(arrays, steps):
    regions, left = yield from halving(*regions_of(arrays), steps)
    blocks = added([(terms, left) for terms in regions])
    blocks = yield from whole_sum(blocks, steps)
    return (yield from joining(blocks, steps))


class Chain:
    def __init__(self, steps):
        self.steps = steps
        self.value = None
        self.sent, self.received = next(steps)

    def turn(self, *after):
        if self.value is not None:
            return list(after)
        received = gate(self.received, after) if after else self.received
        try:
            self.sent, self.received = self.steps.send(received)
        except StopIteration as end:
            self.value = end.value
            return received
        return self.sent


def finish(chain):
    while chain.value is None:
        chain.turn()
    return chain.value


ORDER = "ofTwfmgfmAmofMaBPfaEfaCaf"


def body(
    frame_tokens,
    cotangent,
    caption_count,
    caption_len,
    message_weight,
    message_bias,
    message_gain,
    message_shift,
    cross_qkv,
    cross_bias,
    cross_proj,
    cross_offset,
    attn_gain,
    attn_shift,
    qkv_weight,
    qkv_bias,
    out_weight,
    out_bias,
    mlp_gain,
    mlp_shift,
    up_weight,
    up_bias,
    down_weight,
    down_bias,
):
    group, patches, part = frame_tokens.shape
    width = message_weight.shape[0]
    hidden = up_weight.shape[1]
    wide = lax.axis_size("wide")
    narrow = lax.axis_size("narrow")
    wide_idx = lax.axis_index("wide")
    narrow_idx = lax.axis_index("narrow")
    frames = group // wide
    seq_pad = -(-(patches + 1) // ROW_TILE) * ROW_TILE
    rows = frames * seq_pad
    all_frames = group * narrow
    chunk = max(c for c in range(VIDEO_FRAMES, 129, VIDEO_FRAMES) if all_frames % c == 0 and c % group == 0)
    place = jnp.stack([wide_idx, narrow_idx & 1, narrow_idx]).astype(jnp.int32)

    def own_cols(values):
        return lax.dynamic_slice_in_dim(values, wide_idx * part, part, values.ndim - 1)

    tokens_t = frame_tokens.transpose(0, 2, 1)
    pack = jnp.concatenate(
        [up_bias, qkv_bias.reshape(-1), out_bias, down_bias, frame_tokens[:, 0, :].astype(F32).reshape(-1)]
    ).reshape(-1, width)
    packs = [pack] + [swap(pack, "wide", k) for k in range(1, wide)]
    cls_rows = jnp.concatenate(
        reorder([p[2:].reshape(group, part).astype(LOW) for p in packs], wide_idx), axis=1
    )
    cls_own = cls_rows
    toks = frames_in(tokens_t, [cls_own])
    attn_own = jnp.concatenate(
        [qkv_weight.transpose(1, 2, 0).reshape(3 * part, width), out_weight], axis=0
    )
    attn_near = send_half(attn_own, [cls_own])
    narrow_bits = bits_of(narrow)
    cls_rows = jnp.concatenate([cls_rows, swap(cls_rows, "narrow", 1)], axis=0)
    attn_near = gate(attn_near, [cls_rows])
    attn_far = [swap(near, "narrow", 1) for near in attn_near]
    (cls_rows,) = gate([cls_rows], attn_near)
    for bit in narrow_bits[1:]:
        cls_rows = jnp.concatenate([cls_rows, swap(cls_rows, "narrow", bit)], axis=0)
    attn_far = gate(attn_far, [cls_rows])
    toks = frames_end(toks, [cls_rows])
    attn_weights = near_shards(attn_own)
    for near, far in zip(attn_near, attn_far):
        attn_weights += far_shards(near, far)
    cots = frames_in(cotangent.transpose(0, 2, 1), attn_far)

    caption_slot = jnp.arange(caption_len.shape[1])
    word_total = jnp.sum(
        jnp.where(caption_slot[None, :] < caption_count[:, None], caption_len, 0), axis=1
    ).astype(F32)
    video_scale = word_total / jnp.mean(word_total)
    own_video = (narrow_idx * group + wide_idx * frames + jnp.arange(frames)) // VIDEO_FRAMES
    video_match = own_video[:, None] == jnp.arange(video_scale.shape[0])[None, :]
    scale = jnp.sum(jnp.where(video_match, video_scale[None, :], 0.0), axis=1)

    up_shards, down_shards = near_shards(up_weight), near_shards(down_weight)

    cross_flat = cross_qkv.transpose(1, 2, 0).reshape(3 * part, width)
    msg_normed, msg_inv, msg_in, cross_heads, cross_prob, cross_mix, base, group_sum = message_forward(
        chunk, group, place, cls_rows, message_weight,
        (message_bias, message_gain, message_shift, cross_offset), cross_flat, cross_bias, cross_proj,
        toks[1:] + attn_weights[1:2] + attn_weights[4:5] + [up_shards[1], down_shards[1]],
    )
    group_sums = [group_sum] + [swap(group_sum, "wide", k) for k in range(1, wide)]

    odd = narrow_idx & 1
    half = width // 2

    def half_of(weight, after):
        return lax.dynamic_slice_in_dim(gate([weight], after)[0], odd * half, half, 0)

    near_parts = [
        swap(half_of(up_weight, toks[2:3]), "wide", 2),
        swap(half_of(down_weight, group_sums[2:]), "wide", 2),
    ]
    (near_parts[0],) = gate(near_parts[:1], group_sums[2:] + attn_far)
    near_other = [swap(near_parts[0], "wide", 1)]
    far_parts = [swap(near_parts[0], "narrow", 1)]

    forward = attn_forward(
        seq_pad, place, (attn_gain, attn_shift, mlp_gain, mlp_shift), base, toks, group_sums, packs, attn_weights,
        [up_shards[1], down_shards[1], near_other[0]],
    )
    (normed, inv, attn_in, heads, prob, mix, hidden_res, mlp_normed, mlp_inv, mlp_in) = gate(
        forward, far_parts + near_parts[1:]
    )
    mlp_in = mlp_in.reshape(rows, width)
    bits = bits_of(narrow)
    size = width + hidden
    cots = frames_end(cots, [mlp_in])
    (near_parts[1],) = gate(near_parts[1:], [mlp_in])
    far_parts.append(swap(near_parts[1], "narrow", 1))
    near_other.append(swap(near_parts[1], "wide", 1))
    (far_parts[0],) = gate(far_parts[:1], [mlp_in])
    far_other = [swap(far_parts[0], "wide", 1)]
    cot, grad_rows, acc, gacc, sum_up, *grad_own = mlp_step(
        frames, place, scale, mlp_in, packs[:2], up_shards + down_shards, cots=cots,
        after=[near_other[1]] + far_other,
    )
    acc, gacc, grad_rows, cot, *grad_own = gate([acc, gacc, grad_rows, cot] + grad_own, far_parts[1:])
    far_other.append(swap(far_parts[1], "wide", 1))
    grad_next = grad_own[1]

    def split_steps(rows):
        count = 0
        while count < len(bits) and rows % (2 * ROW_TILE) == 0:
            rows, count = rows // 2, count + 1
        return count

    mlp_steps, attn_count = split_steps(size // 2), split_steps(2 * part)
    own = Chain(halving(*regions_of([grad_own[0], swap(grad_next, "wide", 1)]), mlp_steps))
    mlp_weights = near_parts + far_parts + near_other + far_other
    acc, gacc, sum_up_far, *grad_far = mlp_step(
        frames, place, scale, mlp_in, packs[2:], mlp_weights, carried=(grad_rows, acc, gacc), after=own.sent
    )

    def far_steps(arrays):
        regions, left = yield from halving(*regions_of(arrays), mlp_steps)
        value = added([(terms, left) for terms in regions], True)
        crossed = yield value, [swap(value[0], "wide", 2)]
        blocks = added([
            (terms + [(crossed[0], n * left, [(0, 0, False)])], left) for n, terms in enumerate(finish(own)[0])
        ])
        blocks = yield from whole_sum(blocks, mlp_steps)
        return (yield from joining(blocks, mlp_steps))

    own.turn()
    grad_far = gate(grad_far, own.sent)
    far = Chain(far_steps([grad_far[0], swap(grad_far[1], "wide", 1)]))

    shape = (frames, seq_pad, width)
    per_frame = (
        hidden_res, acc.reshape(shape), gacc.reshape(shape), mlp_normed, mlp_inv, cot, normed, inv, heads, prob
    )
    *blocks, proj, low, sums = attn_backward(
        patches, place, scale, (attn_gain, mlp_gain), per_frame, packs, [sum_up, sum_up_far], attn_weights,
        own.sent + far.sent,
    )
    count = 8 + wide
    others = [swap(sums, "wide", k) for k in range(1, wide)]
    message_bits = list(bits)
    last, attn = [low], None
    for step in ORDER:
        if step == "o":
            last = own.turn(*last)
        elif step == "f":
            last = far.turn(*last)
        elif step == "a":
            last = attn.turn(*last)
        elif step == "T":
            grad_attn = attn_grads(attn_in, proj, low, mix, last + own.sent + far.sent)
            last = grad_attn[:1]
        elif step == "g":
            grad_attn = gate(grad_attn, last)
            attn_next, attn_last = (swap(grad_attn[k], "wide", 1) for k in (1, 3))
            last = added([([(grad_attn[2], 0, []), (attn_last, 0, [])], 4 * part)])
            attn_received = swap(last[0], "wide", 2)
        elif step == "A":
            attn_received, attn_next = gate([attn_received, attn_next], last)
            attn = Chain(narrow_sum([grad_attn[0], attn_next, attn_received], attn_count))
            last = attn.sent
        elif step == "w":
            merged = merge(place, count, [sums] + gate(others, last), True)
            last = [merged]
        elif step == "m":
            bit = message_bits.pop(0)
            merged = merge(place, count, [merged] + gate([swap(merged, "narrow", bit)], last))
            last = [merged]
        elif step == "M":
            for bit in message_bits:
                merged = merge(place, count, [merged] + gate([swap(merged, "narrow", bit)], last))
            (merged,) = gate([merged], last)
            grad_cross_flat, grad_cross_proj, sum_cross_grad, sum_cross, back = message_backward(
                count, merged, msg_in, cross_heads, cross_prob, cross_mix, cross_flat, cross_proj
            )
            last = [back]
        elif step == "B":
            for bit in bits_of(wide)[:-1]:
                back = back + gate([swap(back, "wide", bit)], last)[0]
            other = swap(back.astype(LOW), "wide", bits_of(wide)[-1])
            last = [back]
        elif step == "P":
            blocks = gate(blocks, last)
            pieces = [piece if k == 0 else swap(piece, "wide", k) for k, piece in enumerate(blocks)]
        elif step == "E":
            grad_message_weight, msg_sums, grad_cls = message_end(
                chunk, group, count, merged, back, gate([other], last)[0], msg_normed, msg_inv, message_gain, cls_rows,
                message_weight,
            )
            last = [grad_message_weight]
        elif step == "C":
            output_tokens, grad_tokens = collect(place, pieces[:1] + gate(pieces[1:], last), grad_cls)
            last = [grad_tokens]
    while attn.value is None or far.value is None:
        last = far.turn(*attn.turn(*last))
    far_value = far.value
    grad_attn_own = jnp.concatenate(attn.value, axis=0)
    sums = merged[:count].reshape(count, width)
    grad_up_bias = lax.dynamic_slice_in_dim(sums[6 : 6 + wide].reshape(-1), wide_idx * hidden, hidden, 0)

    return (
        output_tokens.transpose(0, 2, 1),
        grad_tokens.transpose(0, 2, 1),
        grad_message_weight,
        msg_sums[0],
        msg_sums[1],
        msg_sums[2],
        grad_cross_flat.reshape(3, part, width).transpose(2, 0, 1),
        jnp.stack([sum_cross[0, :part], sum_cross[0, 2 * part :]]),
        grad_cross_proj,
        sum_cross_grad[0],
        sums[4],
        sums[5],
        grad_attn_own[: 3 * part].reshape(3, part, width).transpose(2, 0, 1),
        own_cols(sums[count - 2 :]),
        grad_attn_own[3 * part :],
        own_cols(sums[3]),
        sums[1],
        sums[2],
        far_value[0],
        grad_up_bias,
        far_value[1],
        own_cols(sums[0]),
    )


def solution(mesh):
    return jax.shard_map(
        body,
        mesh=mesh,
        in_specs=(
            P("narrow", None, "wide"),
            P("narrow", None, "wide"),
            P(),
            P(),
            P(),
            P(),
            P(),
            P(),
            P(None, None, "wide"),
            P(None, "wide"),
            P("wide", None),
            P(),
            P(),
            P(),
            P(None, None, "wide"),
            P(None, "wide"),
            P("wide", None),
            P("wide"),
            P(),
            P(),
            P(None, "wide"),
            P("wide"),
            P("wide", None),
            P("wide"),
        ),
        out_specs=(
            P("narrow", None, "wide"),
            P("narrow", None, "wide"),
            P(),
            P(),
            P(),
            P(),
            P(None, None, "wide"),
            P(None, "wide"),
            P("wide", None),
            P(),
            P(),
            P(),
            P(None, None, "wide"),
            P(None, "wide"),
            P("wide", None),
            P("wide"),
            P(),
            P(),
            P(None, "wide"),
            P("wide"),
            P("wide", None),
            P("wide"),
        ),
        check_vma=False,
    )
```
